128 devices in a mesh: gx: 16 (over z, y), gy: 8 (over x, core).
Axes of the slice: x: 4, y: 4, z: 4, core: 2. Of those that a mesh axis runs over, the one named last changes fastest.
Arguments:
- tracer: float32 [16, 20, 64, 2048], P(None, None, 'gy', 'gx'), may hold values from -6 to 6
- east_vel: float32 [20, 64, 2048], P(None, 'gy', 'gx'), may hold values from -0.5 to 0.5
- north_vel: float32 [20, 64, 2048], P(None, 'gy', 'gx'), may hold values from -0.5 to 0.5
- diffusion: float32 [20, 64, 2048], P(None, 'gy', 'gx'), may hold values from 0.01 to 0.1
- mixing: float32 [20, 64, 2048], P(None, 'gy', 'gx'), may hold values from 0.1 to 10
- level_count: int32 [64, 2048], P('gy', 'gx'), may hold values from 0 to 20, as said below
- fold_map: int32 [2048], replicated, may hold values from 0 to 2047, as said below
- surface_term: float32 [64, 2048], P('gy', 'gx'), may hold values from 0.02 to 0.2
Outputs:
- mixed: float32 [16, 20, 64, 2048], P(None, None, 'gy', 'gx')
- pressure: float32 [64, 2048], P('gy', 'gx')
- residual: float32 [64, 2048], P('gy', 'gx')
The draws below stay inside these ranges and needn't reach their ends.
Inputs may be any that keep to these rules, and one draw needn't show every extreme that they name: level_count is each column's number of ocean levels; 0 marks land. fold_map[i] = (2 p - 1 - i) mod 2048 for one column p, so it is its own inverse and fixes no column.
All inputs are finite; a program needn't handle non-finite values.
Results may differ from the reference program's by a relative error of at most 0.0003.
Values sent between devices are 32-bit elements; how exact they have to be, the bound alone decides.
No kernel may reach another device: no remote copies, remote signals or barrier semaphores. Data moves between devices by JAX's collectives and lax.ppermute only.
A program may use at most 128 MiB of HBM per device.

```python
import math
import jax
import jax.numpy as jnp

NTR = 16
L = 20
CY = 8
CX = 128
ITERS = 4
NY = 64
NX = 2048


def draw_level_count(key, part):
    key = jax.random.fold_in(key, 11)
    key_cap, key_depth, key_land = jax.random.split(key, 3)
    blocks_y = NY // CY
    blocks_x = NX // CX
    cap = jax.random.randint(key_cap, (blocks_y, 1, blocks_x, 1), L // 4, L + 1)
    depth = jax.random.randint(key_depth, (blocks_y, CY, blocks_x, CX), 1, L + 1)
    depth = jnp.minimum(depth, cap)
    land = jax.random.randint(key_land, (blocks_y, CY, blocks_x, CX), 0, 5) == 0
    counts = jnp.where(land, 0, depth).reshape(NY, NX)
    counts = counts.at[0, 0].set(L)
    counts = counts.at[0, 1].set(0)
    return counts.astype(jnp.int32)


def draw_fold_map(key, part):
    key = jax.random.fold_in(key, 23)
    pole = jax.random.randint(key, (), 0, NX)
    index_row = jnp.arange(NX, dtype=jnp.int32)
    return ((2 * pole - 1 - index_row) % NX).astype(jnp.int32)


def level_of(stream_key, extent, cuts, smallest, high):
    gain = 1.0
    for axis_at, blocks in cuts:
        draws = jax.random.uniform(jax.random.fold_in(jax.random.fold_in(stream_key, 6), axis_at), (blocks,), jnp.float32, smallest / len(cuts), high / len(cuts))
        gain = gain * jnp.repeat(jnp.exp(draws), extent[axis_at] // blocks).reshape((-1,) + (1,) * (len(extent) - 1 - axis_at))
    return gain


def noise(own_key, dims, width, limit, cuts=(), kind=jnp.bfloat16):
    array = width * jax.random.normal(own_key, dims, jnp.float32)
    if cuts:
        array = array * level_of(own_key, dims, cuts, -0.22, 0.18)
    return jnp.clip(array, -limit, limit).astype(kind)


def setup_inputs(seed: int = 0) -> dict:
    arg_keys = jax.random.split(jax.random.key(seed), 9)
    return {
        "tracer": noise(arg_keys[0], (NTR, L, NY, NX), 1.0, 6.0, ((2, 8), (3, 16)), jnp.float32),
        "east_vel": jnp.clip(jax.random.uniform(arg_keys[1], (L, NY, NX), jnp.float32, -0.5, 0.5) * level_of(arg_keys[1], (L, NY, NX), ((1, 8), (2, 16)), -0.4, 0.0), -0.5, 0.5),
        "north_vel": jnp.clip(jax.random.uniform(arg_keys[2], (L, NY, NX), jnp.float32, -0.5, 0.5) * level_of(arg_keys[2], (L, NY, NX), ((1, 8), (2, 16)), -0.4, 0.0), -0.5, 0.5),
        "diffusion": jnp.clip(jnp.exp(math.log(0.1) - 2.3025851 * jax.random.uniform(arg_keys[3], (L, NY, NX), jnp.float32) ** level_of(arg_keys[3], (L, NY, NX), ((1, 8), (2, 16)), -0.2, 0.2)), 0.01, 0.1),
        "mixing": jnp.clip(jnp.exp(math.log(10.0) - 4.6051702 * jax.random.uniform(arg_keys[4], (L, NY, NX), jnp.float32) ** level_of(arg_keys[4], (L, NY, NX), ((1, 8), (2, 16)), -0.2, 0.2)), 0.1, 10.0),
        "level_count": draw_level_count(jax.random.fold_in(arg_keys[8], 71), 0),
        "fold_map": draw_fold_map(jax.random.fold_in(arg_keys[8], 71), 0),
        "surface_term": jnp.clip(jnp.exp(math.log(0.2) - 2.3025851 * jax.random.uniform(arg_keys[7], (NY, NX), jnp.float32) ** level_of(arg_keys[7], (NY, NX), ((0, 8), (1, 16)), -0.2, 0.2)), 0.02, 0.2),
    }


def extend(field, fold_map):
    top_row = jnp.take(field[..., -1, :], fold_map, axis=-1)
    zero_row = jnp.zeros_like(field[..., :1, :])
    tall = jnp.concatenate([zero_row, field, top_row[..., None, :]], axis=-2)
    return jnp.concatenate([tall[..., -1:], tall, tall[..., :1]], axis=-1)


def columns(explicit, coupling):
    levels_count = coupling.shape[0]
    c_prev = jnp.zeros_like(coupling[0])
    r_prev = jnp.zeros_like(explicit[:, 0])
    a_prev = jnp.zeros_like(coupling[0])
    c_list = []
    r_list = []
    for level in range(levels_count):
        a_now = coupling[level]
        lower = -a_prev
        denominator = (1.0 + a_prev + a_now) - lower * c_prev
        c_now = -a_now / denominator
        r_now = (explicit[:, level] - lower * r_prev) / denominator
        c_list.append(c_now)
        r_list.append(r_now)
        c_prev, r_prev, a_prev = c_now, r_now, a_now
    x_next = jnp.zeros_like(explicit[:, 0])
    outs_list = [None] * levels_count
    for level in range(levels_count - 1, -1, -1):
        x_next = r_list[level] - c_list[level] * x_next
        outs_list[level] = x_next
    return jnp.stack(outs_list, axis=1)


NEIGHBOURS = [(0, 1, 1.0), (0, -1, 1.0), (1, 0, 1.0), (-1, 0, 1.0), (1, 1, 0.5), (1, -1, 0.5), (-1, 1, 0.5), (-1, -1, 0.5)]


def window(padded, row_off, col_off):
    rows = padded.shape[0] - 2
    cols = padded.shape[1] - 2
    return padded[1 + row_off:1 + row_off + rows, 1 + col_off:1 + col_off + cols]


def reference(tracer, east_vel, north_vel, diffusion, mixing, level_count, fold_map, surface_term):
    levels = jnp.arange(L, dtype=jnp.int32)[:, None, None]
    level_mask = (levels < level_count[None]).astype(jnp.float32)
    masked = tracer * level_mask[None]
    padded = extend(masked, fold_map)
    east_side = padded[:, :, 1:-1, 2:]
    west_side = padded[:, :, 1:-1, :-2]
    north_side = padded[:, :, 2:, 1:-1]
    south_side = padded[:, :, :-2, 1:-1]
    explicit = masked + level_mask * (-0.5 * east_vel * (east_side - west_side) - 0.5 * north_vel * (north_side - south_side) + diffusion * (east_side + west_side + north_side + south_side - 4.0 * masked))
    coupling = mixing * (levels + 1 < level_count[None]).astype(jnp.float32)
    mixed = columns(explicit, coupling)
    thickness = (0.5 + 1.5 * jnp.arange(L).astype(jnp.float32) / (L - 1)).astype(jnp.float32)[:, None, None]
    depth = jnp.sum(thickness * level_mask, axis=0) / L
    wet_cells = level_count > 0
    rhs = jnp.where(wet_cells, 0.25 * jnp.sum(thickness * (mixed[0] - mixed[1]), axis=0), 0.0)
    depth_pad = extend(depth, fold_map)
    couplings = [weight * jnp.minimum(depth, window(depth_pad, row_off, col_off)) for row_off, col_off, weight in NEIGHBOURS]
    total = jnp.zeros_like(depth)
    for entry in couplings:
        total = total + entry
    diag = jnp.where(wet_cells, surface_term + total, 1.0)

    def apply(field):
        field_pad = extend(field, fold_map)
        summed = jnp.zeros_like(field)
        for entry, (row_off, col_off, weight) in zip(couplings, NEIGHBOURS):
            summed = summed + entry * window(field_pad, row_off, col_off)
        return jnp.where(wet_cells, diag * field - summed, field)

    pressure = jnp.zeros_like(rhs)
    residual = rhs
    scaled = residual / diag
    direction = scaled
    energy = jnp.sum(residual * scaled)
    for step in range(ITERS):
        image = apply(direction)
        step_size = energy / jnp.sum(direction * image)
        pressure = pressure + step_size * direction
        residual = residual - step_size * image
        if step + 1 < ITERS:
            scaled = residual / diag
            energy_new = jnp.sum(residual * scaled)
            direction = scaled + (energy_new / energy) * direction
            energy = energy_new
    return mixed, pressure, residual
```

```python
import functools

import jax
import jax.numpy as jnp
from jax import lax
from jax.experimental import pallas as pl
from jax.experimental.pallas import tpu as pltpu
from jax.sharding import PartitionSpec as P

ITERS = 4
TRACERS, LEVELS, ROWS, COLS = 16, 20, 8, 128
GROUP = 4
BOTH = ("gx", "gy")
VMEM_LIMIT = 40 * 1024 * 1024

COL_TRACER, COL_DEEP, COL_SIZE = 0, 32, 72
ROW_TRACER, ROW_EAST, ROW_WEST, ROW_DIFF, ROW_FIELD, ROW_COUNT, ROW_SURFACE, ROW_SIZE = 0, 320, 360, 400, 560, 880, 888, 896
DEEP_SIZE = ROW_SIZE - ROW_EAST
COUNT_LANE, SURFACE_LANE = 100, 105

SCALAR_BOUND, FIELD_BOUND = 1500.0, 1.0e5

NEIGHBOURS = [
    (0, 1, 1.0),
    (0, -1, 1.0),
    (1, 0, 1.0),
    (-1, 0, 1.0),
    (1, 1, 0.5),
    (1, -1, 0.5),
    (-1, 1, 0.5),
    (-1, -1, 0.5),
]


def params():
    return pltpu.CompilerParams(vmem_limit_bytes=VMEM_LIMIT)


def whole():
    return pl.BlockSpec(memory_space=pltpu.VMEM)


def lanes():
    return lax.broadcasted_iota(jnp.int32, (ROWS, COLS), 1)


def sublanes():
    return lax.broadcasted_iota(jnp.int32, (ROWS, COLS), 0)


def roll(tile, shift, axis):
    size = tile.shape[axis]
    shift = shift % size
    return tile if shift == 0 else pltpu.roll(tile, shift, axis)


def turned(tile):
    return jnp.take_along_axis(tile, ROWS - 1 - sublanes(), axis=0)


def thickness(level):
    return 0.5 + 1.5 * level / (LEVELS - 1)


def pack_columns(items, lane):
    west = jnp.zeros((ROWS, COLS), jnp.float32)
    east = jnp.zeros((ROWS, COLS), jnp.float32)
    for tile, width, first in items:
        here = (lane >= first) & (lane < first + width)
        west = jnp.where(here, roll(tile, first, 1), west)
        east = jnp.where(here, roll(tile, first + width, 1), east)
    return west, east


def columns_kernel(tracer, east_vel, north_vel, diffusion, mixing, count, surface, to_west, to_east):
    lane = lanes()
    levels = count[...]

    def put(row, items):
        west, east = pack_columns(items, lane)
        to_west[row : row + ROWS, :] = west
        to_east[row : row + ROWS, :] = east

    for group in range(TRACERS // GROUP):
        put(
            COL_TRACER + group * ROWS,
            [
                (jnp.where(k < levels, tracer[group * GROUP + t, k], 0.0), 1, t * LEVELS + k)
                for t in range(GROUP)
                for k in range(LEVELS)
            ],
        )
    difference = [(jnp.where(k < levels, tracer[0, k] - tracer[1, k], 0.0), 5, 5 * k) for k in range(LEVELS)]
    put(
        COL_DEEP,
        difference + [(levels.astype(jnp.float32), 5, COUNT_LANE), (surface[...], 4, SURFACE_LANE)],
    )
    for at, field in enumerate((east_vel, north_vel, diffusion, mixing)):
        put(COL_DEEP + (1 + at) * ROWS, [(field[k], 4, 4 * k) for k in range(LEVELS)])


def pack_rows(kind, out, tracer, fields, count, surface):
    edge = 0 if kind == "south" else ROWS - 1
    turn = turned if kind == "fold" else (lambda tile: tile)
    low = sublanes() < 4
    levels = count[...]
    per = 2 * LEVELS
    level_row = lax.broadcasted_iota(jnp.int32, (per, COLS), 0)
    level_row = jnp.where(level_row >= LEVELS, level_row - LEVELS, level_row)
    wet = level_row < jnp.broadcast_to(levels[edge : edge + 1, :], (per, COLS))
    for at in range(TRACERS * LEVELS // per):
        rows = tracer[pl.ds(edge + ROWS * per * at, per, stride=ROWS), :]
        out[ROW_TRACER + per * at : ROW_TRACER + per * (at + 1), :] = jnp.where(wet, rows, 0.0)
    for k in range(LEVELS):
        one, two = ROWS * k, ROWS * (LEVELS + k)
        tile = jnp.where(k < levels, tracer[one : one + ROWS, :] - tracer[two : two + ROWS, :], 0.0)
        out[ROW_DIFF + ROWS * k : ROW_DIFF + ROWS * (k + 1), :] = turn(tile)
    for at, field in enumerate(fields):
        for m in range(LEVELS // 2):
            first, second = turn(field[2 * m]), turn(field[2 * m + 1])
            if kind == "north":
                tile = jnp.where(low, roll(first, 4, 0), second)
            else:
                tile = jnp.where(low, first, roll(second, 4, 0))
            row = ROW_FIELD + ROWS * (at * (LEVELS // 2) + m)
            out[row : row + ROWS, :] = tile
    out[ROW_COUNT : ROW_COUNT + ROWS, :] = turn(levels.astype(jnp.float32))
    out[ROW_SURFACE : ROW_SURFACE + ROWS, :] = turn(surface[...])


def rows_kernel(tracer, east_vel, north_vel, diffusion, mixing, count, surface, near, far):
    here = lax.axis_index("gy")
    top = lax.axis_size("gy") - 1
    rest = (tracer, (east_vel, north_vel, diffusion, mixing), count, surface)

    @pl.when(here % 2 == 0)
    def _():
        pack_rows("north", near, *rest)
        pack_rows("south", far, *rest)

    @pl.when(here % 2 == 1)
    def _():
        pack_rows("south", near, *rest)

    @pl.when((here % 2 == 1) & (here != top))
    def _():
        pack_rows("north", far, *rest)

    @pl.when(here == top)
    def _():
        pack_rows("fold", far, *rest)


def corners_kernel(east, west, near_in, far_in, near, far):
    del near_in, far_in
    here = lax.axis_index("gy")
    top = lax.axis_size("gy") - 1
    half = ROW_WEST - ROW_EAST
    near[:half, :] = east[COL_DEEP:, :]
    near[half:, :] = west[COL_DEEP:, :]

    @pl.when(here != top)
    def _():
        far[:half, :] = east[COL_DEEP:, :]
        far[half:, :] = west[COL_DEEP:, :]

    @pl.when(here == top)
    def _():
        for row in range(0, half, ROWS):
            far[row : row + ROWS, :] = turned(east[COL_DEEP + row : COL_DEEP + row + ROWS, :])
            far[half + row : half + row + ROWS, :] = turned(west[COL_DEEP + row : COL_DEEP + row + ROWS, :])


def pole_of(fold_map):
    return (fold_map[0] + 1) % (COLS * lax.axis_size("gx"))


def fold_index(offset, lane):
    return (offset - 1 - lane) & (COLS - 1)


def unpack(east, west, first, width, lane):
    right = roll(east, -first, 1)
    left = roll(west, -width - first, 1)
    return jnp.where(lane < width, right, jnp.where(lane >= COLS - width, left, 0.0))


def east_of(one, two, lane):
    a, b = roll(one, -1, 1), roll(two, -1, 1)
    return jnp.where(lane == COLS - 1, b, a), jnp.where(lane == COLS - 1, a, b)


def west_of(one, two, lane):
    a, b = roll(one, 1, 1), roll(two, 1, 1)
    return jnp.where(lane == 0, b, a), jnp.where(lane == 0, a, b)


def krylov_kernel(
    fold_map, tracer, east_vel, north_vel, diffusion, mixing, count, surface, from_east, from_west, near, far, extra,
    vectors, diagonal, right_side, partial,
    north_buf, south_buf, other_buf, halo_main, halo_side, diff_main, diff_side, misc,
):
    here = lax.axis_index("gy")
    top = lax.axis_size("gy") - 1
    lane, sub = lanes(), sublanes()
    low = sub < 4
    pole = pole_of(fold_map)
    offset = pole & (COLS - 1)
    odd_block = (pole // COLS) % 2 == 1
    fields = (east_vel, north_vel, diffusion, mixing)

    def at(ref, row):
        return ref[row - ROW_EAST : row - ROW_EAST + ROWS, :]

    @pl.when(here % 2 == 0)
    def _():
        north_buf[...] = near[ROW_EAST:, :]
        south_buf[...] = far[ROW_EAST:, :]

    @pl.when(here % 2 == 1)
    def _():
        south_buf[...] = near[ROW_EAST:, :]

    @pl.when((here % 2 == 1) & ((here != top) | odd_block))
    def _():
        north_buf[...] = far[ROW_EAST:, :]
        other_buf[...] = extra[ROW_EAST:, :]

    @pl.when((here == top) & jnp.logical_not(odd_block))
    def _():
        north_buf[...] = extra[ROW_EAST:, :]
        other_buf[...] = far[ROW_EAST:, :]

    def north_field(ref, f, k):
        tile = at(ref, ROW_FIELD + ROWS * (f * (LEVELS // 2) + k // 2))
        return roll(tile, 4 * (k % 2), 0)

    def south_field(f, k):
        tile = at(south_buf, ROW_FIELD + ROWS * (f * (LEVELS // 2) + k // 2))
        return roll(tile, 4 * (1 - k % 2), 0)

    def side(ref, f, first, width):
        return unpack(at(ref, ROW_EAST + ROWS * f), at(ref, ROW_WEST + ROWS * f), first, width, lane)

    @pl.when(here != top)
    def _():
        for f in range(4):
            east = jnp.where(low, at(north_buf, ROW_EAST + ROWS * (1 + f)), at(south_buf, ROW_EAST + ROWS * (1 + f)))
            west = jnp.where(low, at(north_buf, ROW_WEST + ROWS * (1 + f)), at(south_buf, ROW_WEST + ROWS * (1 + f)))
            for k in range(LEVELS):
                halo_main[f, k] = jnp.where(low, north_field(north_buf, f, k), south_field(f, k))
                halo_side[f, k] = unpack(east, west, 4 * k, 4, lane)
        for k in range(LEVELS):
            diff_main[k] = at(north_buf, ROW_DIFF + ROWS * k)
            diff_side[k] = side(north_buf, 0, 5 * k, 5)
        misc[0] = at(north_buf, ROW_COUNT)
        misc[1] = side(north_buf, 0, COUNT_LANE, 5)
        misc[2] = at(north_buf, ROW_SURFACE)
        misc[3] = side(north_buf, 0, SURFACE_LANE, 4)

    @pl.when(here == top)
    def _():
        index = fold_index(offset, lane)

        def folded(a_main, a_side, b_main, b_side):
            a, b = jnp.take_along_axis(a_main, index, axis=1), jnp.take_along_axis(b_main, index, axis=1)
            c, d = jnp.take_along_axis(a_side, index, axis=1), jnp.take_along_axis(b_side, index, axis=1)
            first = jnp.where(lane >= offset, a, b)
            right = jnp.where(lane < offset, a, c)
            left = jnp.where(lane >= offset, b, d)
            return first, jnp.where(lane < COLS // 2, right, left)

        for f in range(4):
            sign = -1.0 if f < 2 else 1.0
            for k in range(LEVELS):
                one, two = folded(
                    north_field(north_buf, f, k),
                    side(north_buf, 1 + f, 4 * k, 4),
                    north_field(other_buf, f, k),
                    side(other_buf, 1 + f, 4 * k, 4),
                )
                halo_main[f, k] = jnp.where(low, sign * one, south_field(f, k))
                halo_side[f, k] = jnp.where(low, sign * two, side(south_buf, 1 + f, 4 * k, 4))
        for k in range(LEVELS):
            diff_main[k], diff_side[k] = folded(
                at(north_buf, ROW_DIFF + ROWS * k),
                side(north_buf, 0, 5 * k, 5),
                at(other_buf, ROW_DIFF + ROWS * k),
                side(other_buf, 0, 5 * k, 5),
            )
        misc[0], misc[1] = folded(
            at(north_buf, ROW_COUNT),
            side(north_buf, 0, COUNT_LANE, 5),
            at(other_buf, ROW_COUNT),
            side(other_buf, 0, COUNT_LANE, 5),
        )
        misc[2], misc[3] = folded(
            at(north_buf, ROW_SURFACE),
            side(north_buf, 0, SURFACE_LANE, 4),
            at(other_buf, ROW_SURFACE),
            side(other_buf, 0, SURFACE_LANE, 4),
        )

    def column(f):
        row = COL_DEEP + ROWS * f
        return from_east[row : row + ROWS, :], from_west[row : row + ROWS, :]

    def neighbours_across(own, north, south):
        up, up_n, up_s = roll(own, -1, 0), roll(north, -1, 0), roll(south, -1, 0)
        down, down_n, down_s = roll(own, 1, 0), roll(north, 1, 0), roll(south, 1, 0)
        return (
            jnp.where(sub == 7, up_n, up),
            jnp.where(low, up_n, jnp.where(sub == 7, up, up_s)),
            jnp.where(sub == 0, down_s, down),
            jnp.where(sub == 0, down, jnp.where(low, down_n, down_s)),
        )

    def halo(pair):
        return jnp.where(low, pair[0], pair[1])

    counts_own = (count[...].astype(jnp.float32), unpack(*column(0), COUNT_LANE, 5, lane))
    counts_north = (misc[0], misc[1])
    counts_south = (at(south_buf, ROW_COUNT), side(south_buf, 0, COUNT_LANE, 5))
    counts = (counts_own[0], counts_own[1], halo((counts_north[0], counts_south[0])), halo((counts_north[1], counts_south[1])))
    surfaces = (
        surface[...],
        unpack(*column(0), SURFACE_LANE, 4, lane),
        halo((misc[2], at(south_buf, ROW_SURFACE))),
        halo((misc[3], side(south_buf, 0, SURFACE_LANE, 4))),
    )

    zero = jnp.zeros((ROWS, COLS), jnp.float32)
    c_prev, r_prev, a_prev = [zero] * 4, [zero] * 4, [zero] * 4
    c_list, r_list = [], []
    for k in range(LEVELS):
        own = (jnp.where(k < counts[0], tracer[0, k] - tracer[1, k], 0.0), unpack(*column(0), 5 * k, 5, lane))
        north = (diff_main[k], diff_side[k])
        south = (at(south_buf, ROW_DIFF + ROWS * k), side(south_buf, 0, 5 * k, 5))
        halos = (halo((north[0], south[0])), halo((north[1], south[1])))
        centre = (own[0], own[1], halos[0], halos[1])
        easts = east_of(*own, lane) + east_of(*halos, lane)
        wests = west_of(*own, lane) + west_of(*halos, lane)
        first = neighbours_across(own[0], north[0], south[0])
        second = neighbours_across(own[1], north[1], south[1])
        norths = (first[0], second[0], first[1], second[1])
        souths = (first[2], second[2], first[3], second[3])
        values = [
            (field[k], unpack(*column(1 + f), 4 * k, 4, lane), halo_main[f, k], halo_side[f, k])
            for f, field in enumerate(fields)
        ]
        c_now, r_now, a_now = [], [], []
        for i in range(4):
            u, v, spread, mix = (value[i] for value in values)
            change = (
                -0.5 * u * (easts[i] - wests[i])
                - 0.5 * v * (norths[i] - souths[i])
                + spread * (easts[i] + wests[i] + norths[i] + souths[i] - 4.0 * centre[i])
            )
            explicit = centre[i] + jnp.where(k < counts[i], change, 0.0)
            a = jnp.where(k + 1 < counts[i], mix, 0.0)
            inverse = 1.0 / (1.0 + a_prev[i] + a + a_prev[i] * c_prev[i])
            c_now.append(-a * inverse)
            r_now.append((explicit + a_prev[i] * r_prev[i]) * inverse)
            a_now.append(a)
        c_prev, r_prev, a_prev = c_now, r_now, a_now
        c_list.append(c_now)
        r_list.append(r_now)
    total, x_next = [zero] * 4, [zero] * 4
    for k in range(LEVELS - 1, -1, -1):
        x_next = [r_list[k][i] - c_list[k][i] * x_next[i] for i in range(4)]
        total = [total[i] + thickness(k) * x_next[i] for i in range(4)]
    rhs = [jnp.where(counts[i] > 0, 0.25 * total[i], 0.0) for i in range(4)]

    def depth_of(levels):
        depth = zero
        for k in range(LEVELS):
            depth = depth + jnp.where(k < levels, thickness(k), 0.0)
        return depth / LEVELS

    own = tuple(depth_of(levels) for levels in counts_own)
    north = tuple(depth_of(levels) for levels in counts_north)
    south = tuple(depth_of(levels) for levels in counts_south)
    depths = (own[0], own[1], halo((north[0], south[0])), halo((north[1], south[1])))

    def rows_of(own, north, south):
        first = neighbours_across(own[0], north[0], south[0])
        second = neighbours_across(own[1], north[1], south[1])
        return (first[0], second[0], first[1], second[1]), (first[2], second[2], first[3], second[3])

    def coupled(others, weight):
        return [weight * jnp.minimum(depths[i], others[i]) for i in range(4)]

    own_e, north_e, south_e = (east_of(*pair, lane) for pair in (own, north, south))
    own_w, north_w, south_w = (west_of(*pair, lane) for pair in (own, north, south))
    halo_e = (halo((north_e[0], south_e[0])), halo((north_e[1], south_e[1])))
    halo_w = (halo((north_w[0], south_w[0])), halo((north_w[1], south_w[1])))
    mid = rows_of(own, north, south)
    mid_e = rows_of(own_e, north_e, south_e)
    mid_w = rows_of(own_w, north_w, south_w)
    couplings = [
        coupled(own_e + halo_e, 1.0),
        coupled(own_w + halo_w, 1.0),
        coupled(mid[0], 1.0),
        coupled(mid[1], 1.0),
        coupled(mid_e[0], 0.5),
        coupled(mid_w[0], 0.5),
        coupled(mid_e[1], 0.5),
        coupled(mid_w[1], 0.5),
    ]
    diag = [
        jnp.where(counts[i] > 0, surfaces[i] + sum(entry[i] for entry in couplings), 1.0) for i in range(4)
    ]
    inverse = [1.0 / diag[i] for i in range(4)]
    couplings = [[entry[i] * inverse[i] for i in range(4)] for entry in couplings]

    def shifted_rows(tiles):
        north, south = [None] * 4, [None] * 4
        for i in range(2):
            a, b = roll(tiles[i], -1, 0), roll(tiles[i + 2], -1, 0)
            north[i], north[i + 2] = jnp.where(sub == 7, b, a), jnp.where(sub == 7, a, b)
            a, b = roll(tiles[i], 1, 0), roll(tiles[i + 2], 1, 0)
            south[i], south[i + 2] = jnp.where(sub == 0, b, a), jnp.where(sub == 0, a, b)
        return north, south

    def spread_out(tiles):
        east = east_of(tiles[0], tiles[1], lane) + east_of(tiles[2], tiles[3], lane)
        west = west_of(tiles[0], tiles[1], lane) + west_of(tiles[2], tiles[3], lane)
        mid_n, mid_s = shifted_rows(tiles)
        east_n, east_s = shifted_rows(east)
        west_n, west_s = shifted_rows(west)
        around = (east, west, mid_n, mid_s, east_n, west_n, east_s, west_s)
        return [sum(entry[i] * values[i] for entry, values in zip(couplings, around)) for i in range(4)]

    found = [[rhs[i] * inverse[i] for i in range(4)]]
    found.append(spread_out(found[0]))
    for _ in range(2, ITERS + 1):
        ahead = spread_out(found[-1])
        found.append([2.0 * ahead[i] - found[-2][i] for i in range(4)])
    for j in range(ITERS + 1):
        vectors[j] = found[j][0]
    diagonal[...] = diag[0]
    right_side[...] = rhs[0]
    weighted = [diag[0] * found[j][0] for j in range(ITERS + 1)]
    sums = [weighted[j] * found[j][0] for j in range(ITERS + 1)]
    sums += [weighted[j] * found[j + 1][0] for j in range(ITERS)]
    row = jnp.zeros((1, COLS), jnp.float32)
    for j, entry in enumerate(sums):
        row = jnp.where(lane[:1, :] == j, jnp.sum(entry, keepdims=True), row)
    partial[...] = jnp.broadcast_to(row, partial.shape)


def combine_kernel(moments, vectors, diagonal, pressure, residual, good):
    size = ITERS + 1
    sums = jnp.sum(moments[...], axis=0, keepdims=True)

    def lane_of(j):
        return jnp.broadcast_to(sums[:, j : j + 1], (ROWS, COLS))

    even = [lane_of(j) for j in range(size)]
    odd = [lane_of(size + j) for j in range(ITERS)]
    mu = []
    for j in range(size):
        mu.append(even[0] if j == 0 else 2.0 * even[j] - even[0])
        if j < ITERS:
            mu.append(odd[0] if j == 0 else 2.0 * odd[j] - odd[0])

    def mass(i, j):
        return 0.5 * (mu[i + j] + mu[abs(i - j)])

    def stiffness(i, j):
        i, j = min(i, j), max(i, j)
        if j == 0:
            return mu[0] - mu[1]
        return mass(i, j) - 0.5 * (mass(i, j + 1) + mass(i, j - 1))

    def form(values, entry):
        out = None
        for i in range(len(values)):
            inner = values[i] * entry(i, i)
            for j in range(i + 1, len(values)):
                inner = inner + 2.0 * values[j] * entry(i, j)
            out = values[i] * inner if out is None else out + values[i] * inner
        return out

    def applied(values):
        out = [value for value in values] + [jnp.zeros_like(values[0])]
        out[1] = out[1] - values[0]
        for j in range(1, len(values)):
            out[j + 1] = out[j + 1] - 0.5 * values[j]
            out[j - 1] = out[j - 1] - 0.5 * values[j]
        return out

    def amplified(values, result):
        total = sum(jnp.abs(value) for value in values)
        return total * total * mu[0] / result

    scaled = [jnp.ones((ROWS, COLS), jnp.float32)]
    direction = list(scaled)
    solution_at = []
    energy = mu[0]
    worst = jnp.zeros((ROWS, COLS), jnp.float32)
    fine = energy > 0.0
    for step in range(ITERS):
        image = applied(direction)
        curvature = form(direction, stiffness)
        step_size = energy / curvature
        fine = fine & (amplified(direction, curvature) <= SCALAR_BOUND) & (curvature > 0.0)
        solution_at = [
            step_size * value + (solution_at[j] if j < len(solution_at) else 0.0) for j, value in enumerate(direction)
        ]
        scaled = [
            (scaled[j] if j < len(scaled) else 0.0) - step_size * value for j, value in enumerate(image)
        ]
        energy_new = form(scaled, mass)
        bound = SCALAR_BOUND if step + 1 < ITERS else FIELD_BOUND
        fine = fine & (amplified(scaled, energy_new) <= bound) & (energy_new > 0.0)
        if step + 1 < ITERS:
            ratio = energy_new / energy
            direction = [
                scaled[j] + (ratio * direction[j] if j < len(direction) else 0.0) for j in range(len(scaled))
            ]
            energy = energy_new
    del worst
    pressure[...] = sum(solution_at[j] * vectors[j] for j in range(len(solution_at)))
    residual[...] = diagonal[...] * sum(scaled[j] * vectors[j] for j in range(len(scaled)))
    good[0] = jnp.min(jnp.where(fine, 1, 0).astype(jnp.int32))


def tracers_kernel(
    fold_map, tracer, east_vel, north_vel, diffusion, mixing, count, from_east, from_west, near, far, extra,
    mixed,
    north_rows, south_rows, factors,
):
    here = lax.axis_index("gy")
    top = lax.axis_size("gy") - 1
    lane, sub = lanes(), sublanes()
    levels = count[...]
    group = pl.program_id(0)

    @pl.when(group == 0)
    def _():
        @pl.when(here % 2 == 0)
        def _():
            north_rows[...] = near[...]
            south_rows[...] = far[...]

        @pl.when(here % 2 == 1)
        def _():
            south_rows[...] = near[...]

        @pl.when((here % 2 == 1) & (here != top))
        def _():
            north_rows[...] = far[...]

        @pl.when(here == top)
        def _():
            pole = pole_of(fold_map)
            offset = pole & (COLS - 1)
            odd_block = (pole // COLS) % 2 == 1
            index = fold_index(offset, lane)
            from_far = (lane >= offset) == odd_block
            for row in range(0, TRACERS * LEVELS, ROWS):
                a = jnp.take_along_axis(far[row : row + ROWS, :], index, axis=1)
                b = jnp.take_along_axis(extra[row : row + ROWS, :], index, axis=1)
                north_rows[row : row + ROWS, :] = jnp.where(from_far, a, b)

        c_prev = jnp.zeros((ROWS, COLS), jnp.float32)
        a_prev = jnp.zeros((ROWS, COLS), jnp.float32)
        for k in range(LEVELS):
            wet = jnp.where(k < levels, 1.0, 0.0)
            u, v, spread = 0.5 * wet * east_vel[k], 0.5 * wet * north_vel[k], wet * diffusion[k]
            a = jnp.where(k + 1 < levels, mixing[k], 0.0)
            inverse = 1.0 / (1.0 + a_prev + a + a_prev * c_prev)
            c_prev = -a * inverse
            factors[0, k] = 1.0 - 4.0 * spread
            factors[1, k] = spread - u
            factors[2, k] = spread + u
            factors[3, k] = spread - v
            factors[4, k] = spread + v
            factors[5, k] = inverse
            factors[6, k] = a_prev
            factors[7, k] = c_prev
            a_prev = a

    row = pl.multiple_of(group * ROWS, ROWS)
    columns_east = from_east[pl.ds(row, ROWS), :]
    columns_west = from_west[pl.ds(row, ROWS), :]
    r_prev = [jnp.zeros((ROWS, COLS), jnp.float32)] * GROUP
    for k in range(LEVELS):
        centre, to_e, to_w, to_n, to_s, inverse, above = (factors[j, k] for j in range(7))
        wet = k < levels
        for t in range(GROUP):
            cell = jnp.where(wet, tracer[t, k], 0.0)
            at = t * LEVELS + k
            halo_row = group * (GROUP * LEVELS) + at
            east = jnp.where(lane == COLS - 1, roll(columns_east, -1 - at, 1), roll(cell, -1, 1))
            west = jnp.where(lane == 0, roll(columns_west, -at, 1), roll(cell, 1, 1))
            north = jnp.where(sub == ROWS - 1, north_rows[pl.ds(halo_row, 1), :], roll(cell, -1, 0))
            south = jnp.where(sub == 0, south_rows[pl.ds(halo_row, 1), :], roll(cell, 1, 0))
            explicit = centre * cell + to_e * east + to_w * west + to_n * north + to_s * south
            r_prev[t] = (explicit + above * r_prev[t]) * inverse
            mixed[t, k] = r_prev[t]
    x_next = r_prev
    for k in range(LEVELS - 2, -1, -1):
        below = factors[7, k]
        for t in range(GROUP):
            x_next[t] = mixed[t, k] - below * x_next[t]
            mixed[t, k] = x_next[t]


def extended(cells, sides, width):
    for axis, dim in sides:
        count = lax.axis_size(axis)
        head = lax.slice_in_dim(cells, 0, width, axis=dim)
        tail = lax.slice_in_dim(cells, cells.shape[dim] - width, cells.shape[dim], axis=dim)
        cells = jnp.concatenate(
            [
                lax.ppermute(tail, axis, [(i, (i + 1) % count) for i in range(count)]),
                cells,
                lax.ppermute(head, axis, [((i + 1) % count, i) for i in range(count)]),
            ],
            axis=dim,
        )
    return cells


def extend(field, fold_map):
    rows, cols = field.shape
    padded = extended(field, (("gx", 1), ("gy", 0)), 1)
    total_cols = fold_map.shape[0]
    whole_row = lax.all_gather(field[rows - 1, :], "gx", axis=0, tiled=True)
    start = lax.axis_index("gx") * cols
    wanted = (start - 1 + jnp.arange(cols + 2, dtype=jnp.int32)) % total_cols
    folded = jnp.take(whole_row, jnp.take(fold_map, wanted), axis=0)
    row_index = lax.axis_index("gy")
    upper = jnp.where(row_index == lax.axis_size("gy") - 1, folded, padded[rows + 1, :])
    lower = jnp.where(row_index == 0, 0.0, padded[0, :])
    return jnp.concatenate([lower[None, :], padded[1 : rows + 1, :], upper[None, :]], axis=0)


def window(padded, row_off, col_off):
    rows = padded.shape[0] - 2
    cols = padded.shape[1] - 2
    return padded[1 + row_off : 1 + row_off + rows, 1 + col_off : 1 + col_off + cols]


def total_of(value):
    return lax.psum(jnp.sum(value), BOTH)


def direct_gradients(rhs, level_count, fold_map, surface_term):
    levels = jnp.arange(LEVELS, dtype=jnp.int32)[:, None, None]
    level_mask = (levels < level_count[None]).astype(jnp.float32)
    thick = (0.5 + 1.5 * jnp.arange(LEVELS).astype(jnp.float32) / (LEVELS - 1))[:, None, None]
    depth = jnp.sum(thick * level_mask, axis=0) / LEVELS
    wet_cells = level_count > 0
    depth_pad = extend(depth, fold_map)
    couplings = [
        weight * jnp.minimum(depth, window(depth_pad, row_off, col_off)) for row_off, col_off, weight in NEIGHBOURS
    ]
    diag = jnp.where(wet_cells, surface_term + sum(couplings), 1.0)

    def step(_, state):
        pressure, residual, direction, energy = state
        field_pad = extend(direction, fold_map)
        summed = jnp.zeros_like(direction)
        for entry, (row_off, col_off, _weight) in zip(couplings, NEIGHBOURS):
            summed = summed + entry * window(field_pad, row_off, col_off)
        image = jnp.where(wet_cells, diag * direction - summed, direction)
        step_size = energy / total_of(direction * image)
        pressure = pressure + step_size * direction
        residual = residual - step_size * image
        scaled = residual / diag
        energy_new = total_of(residual * scaled)
        return pressure, residual, scaled + energy_new / energy * direction, energy_new

    scaled = rhs / diag
    state = (jnp.zeros_like(rhs), rhs, scaled, total_of(rhs * scaled))
    state = lax.fori_loop(0, ITERS, step, state)
    return state[0], state[1]


def shards(sizes, tracer, east_vel, north_vel, diffusion, mixing, level_count, fold_map, surface_term):
    nx, ny = sizes
    f32 = jnp.float32

    def device(x, y):
        return (x % nx) * ny + y

    def kernel(body, **rest):
        return pl.pallas_call(body, compiler_params=params(), **rest)

    def shape(*dims):
        return jax.ShapeDtypeStruct(dims, f32)

    fields = (east_vel, north_vel, diffusion, mixing)

    to_west, to_east = kernel(
        columns_kernel,
        out_shape=(shape(COL_SIZE, COLS), shape(COL_SIZE, COLS)),
        in_specs=[whole()] * 7,
        out_specs=(whole(), whole()),
        name="pack_columns",
    )(tracer, *fields, level_count, surface_term)
    from_east = lax.ppermute(to_west, BOTH, [(device(x + 1, y), device(x, y)) for x in range(nx) for y in range(ny)])
    from_west = lax.ppermute(to_east, BOTH, [(device(x - 1, y), device(x, y)) for x in range(nx) for y in range(ny)])

    flat = tracer.reshape(TRACERS * LEVELS * ROWS, COLS)
    near, far = kernel(
        rows_kernel,
        out_shape=(shape(ROW_SIZE, COLS), shape(ROW_SIZE, COLS)),
        in_specs=[whole()] * 7,
        out_specs=(whole(), whole()),
        cost_estimate=pl.CostEstimate(flops=1000000, bytes_accessed=4000000, transcendentals=0),
        name="pack_rows",
    )(flat, *fields, level_count, surface_term)

    corner = pl.BlockSpec((ROW_DIFF - ROW_EAST, COLS), lambda i: (ROW_EAST // (ROW_DIFF - ROW_EAST), 0))
    column = pl.BlockSpec((COL_SIZE, COLS), lambda i: (0, 0))
    near, far = kernel(
        corners_kernel,
        grid=(1,),
        out_shape=(shape(ROW_SIZE, COLS), shape(ROW_SIZE, COLS)),
        in_specs=[column, column, pl.BlockSpec(memory_space=pl.ANY), pl.BlockSpec(memory_space=pl.ANY)],
        out_specs=(corner, corner),
        input_output_aliases={2: 0, 3: 1},
        name="put_corners",
    )(from_east, from_west, near, far)

    near = lax.ppermute(near, BOTH, [(device(x, y ^ 1), device(x, y)) for x in range(nx) for y in range(ny)])
    inner = [
        (device(x, y + 1 if y % 2 else y - 1), device(x, y)) for x in range(nx) for y in range(1, ny - 1)
    ]

    def across(turn):
        return [(device(turn - x, ny - 1), device(x, ny - 1)) for x in range(nx)]

    def exchange(block, rows):
        turns = ((block - 1) % nx, block)
        even, odd = turns if turns[0] % 2 == 0 else turns[::-1]
        return lax.ppermute(rows, BOTH, inner + across(even)), lax.ppermute(rows, BOTH, across(odd))

    block = (pole_of(fold_map) // COLS) % nx
    far, extra = lax.switch(block, [functools.partial(exchange, i) for i in range(nx)], far)

    smem = pl.BlockSpec(memory_space=pltpu.SMEM)
    pair = pl.BlockSpec((2, LEVELS, ROWS, COLS), lambda i: (0, 0, 0, 0))

    def all_of(array):
        return pl.BlockSpec(array.shape, lambda i: (0,) * array.ndim)

    rest = (*fields, level_count, surface_term, from_east, from_west, near, far, extra)
    vectors, diagonal, rhs, partial = kernel(
        krylov_kernel,
        grid=(1,),
        out_shape=(shape(ITERS + 1, ROWS, COLS), shape(ROWS, COLS), shape(ROWS, COLS), shape(nx * ny, COLS)),
        in_specs=[smem, pair] + [all_of(array) for array in rest],
        out_specs=tuple(
            pl.BlockSpec(dims, lambda i, n=len(dims): (0,) * n)
            for dims in ((ITERS + 1, ROWS, COLS), (ROWS, COLS), (ROWS, COLS), (nx * ny, COLS))
        ),
        scratch_shapes=[
            pltpu.VMEM((DEEP_SIZE, COLS), f32),
            pltpu.VMEM((DEEP_SIZE, COLS), f32),
            pltpu.VMEM((DEEP_SIZE, COLS), f32),
            pltpu.VMEM((4, LEVELS, ROWS, COLS), f32),
            pltpu.VMEM((4, LEVELS, ROWS, COLS), f32),
            pltpu.VMEM((LEVELS, ROWS, COLS), f32),
            pltpu.VMEM((LEVELS, ROWS, COLS), f32),
            pltpu.VMEM((4, ROWS, COLS), f32),
        ],
        name="krylov",
    )(fold_map, tracer, *rest)

    moments = lax.all_to_all(partial, BOTH, 0, 0)

    batch = pl.BlockSpec((GROUP, LEVELS, ROWS, COLS), lambda i: (i, 0, 0, 0))
    edge = pl.BlockSpec((TRACERS * LEVELS, COLS), lambda i: (0, 0))
    tiles = pl.BlockSpec((COL_DEEP, COLS), lambda i: (0, 0))
    mixed = kernel(
        tracers_kernel,
        grid=(TRACERS // GROUP,),
        out_shape=shape(TRACERS, LEVELS, ROWS, COLS),
        in_specs=[smem, batch] + [all_of(array) for array in (*fields, level_count)] + [tiles, tiles, edge, edge, edge],
        out_specs=batch,
        scratch_shapes=[
            pltpu.VMEM((TRACERS * LEVELS, COLS), f32),
            pltpu.VMEM((TRACERS * LEVELS, COLS), f32),
            pltpu.VMEM((8, LEVELS, ROWS, COLS), f32),
        ],
        name="tracers",
    )(fold_map, tracer, *fields, level_count, from_east, from_west, near, far, extra)

    pressure, residual, good = kernel(
        combine_kernel,
        out_shape=(shape(ROWS, COLS), shape(ROWS, COLS), jax.ShapeDtypeStruct((1,), jnp.int32)),
        in_specs=[whole()] * 3,
        out_specs=(whole(), whole(), smem),
        name="combine",
    )(moments, vectors, diagonal)

    pressure, residual = lax.cond(
        good[0] == 1,
        lambda pressure, residual, rhs, count, surface, fold: (pressure, residual),
        lambda pressure, residual, rhs, count, surface, fold: direct_gradients(rhs, count, fold, surface),
        pressure,
        residual,
        rhs,
        level_count,
        surface_term,
        fold_map,
    )
    return mixed, pressure, residual


def solution(mesh):
    in_specs = (
        P(None, None, "gy", "gx"),
        P(None, "gy", "gx"),
        P(None, "gy", "gx"),
        P(None, "gy", "gx"),
        P(None, "gy", "gx"),
        P("gy", "gx"),
        P(),
        P("gy", "gx"),
    )
    out_specs = (P(None, None, "gy", "gx"), P("gy", "gx"), P("gy", "gx"))
    body = functools.partial(shards, (mesh.shape["gx"], mesh.shape["gy"]))
    return jax.shard_map(body, mesh=mesh, in_specs=in_specs, out_specs=out_specs, check_vma=False)
```

```python
import functools

import jax
import jax.numpy as jnp
from jax import lax
from jax.experimental import pallas as pl
from jax.experimental.pallas import tpu as pltpu
from jax.sharding import PartitionSpec as P

ITERS = 4
TRACERS, LEVELS, ROWS, COLS = 16, 20, 8, 128
GROUP = 4
GROUPS = TRACERS // GROUP
EDGE = TRACERS * LEVELS
BOTH = ("gx", "gy")
VMEM_LIMIT = 40 * 1024 * 1024


def params():
    return pltpu.CompilerParams(vmem_limit_bytes=VMEM_LIMIT)


def whole():
    return pl.BlockSpec(memory_space=pltpu.VMEM)


def lanes():
    return lax.broadcasted_iota(jnp.int32, (ROWS, COLS), 1)


def sublanes():
    return lax.broadcasted_iota(jnp.int32, (ROWS, COLS), 0)


def roll(tile, shift, axis):
    size = tile.shape[axis]
    shift = shift % size
    return tile if shift == 0 else pltpu.roll(tile, shift, axis)


def east_of(tile, beyond, lane):
    return roll(jnp.where(lane == 0, beyond, tile), -1, 1)


def west_of(tile, beyond, lane):
    return roll(jnp.where(lane == COLS - 1, beyond, tile), 1, 1)


def north_of(tile, beyond, sub):
    return roll(jnp.where(sub == 0, beyond, tile), -1, 0)


def south_of(tile, beyond, sub):
    return roll(jnp.where(sub == ROWS - 1, beyond, tile), 1, 0)


def thickness(level):
    return 0.5 + 1.5 * level / (LEVELS - 1)


def pack_kernel(
    tracer, count, surface,
    to_west, to_east, near, far, shared,
    cells, levels_ref, surface_ref, ready,
):
    lane = lanes()
    size = GROUP * LEVELS * ROWS
    small = [
        pltpu.make_async_copy(count, levels_ref, ready.at[GROUPS]),
        pltpu.make_async_copy(surface, surface_ref, ready.at[GROUPS + 1]),
    ]
    large = [
        pltpu.make_async_copy(tracer.at[pl.ds(g * size, size)], cells.at[pl.ds(g * size, size)], ready.at[g])
        for g in range(GROUPS)
    ]
    for copy in small + large:
        copy.start()
    even = lax.axis_index("gy") % 2 == 0
    for copy in small:
        copy.wait()
    levels = levels_ref[...]
    depth = jnp.zeros((ROWS, COLS), jnp.float32)
    for k in range(LEVELS):
        depth = depth + jnp.where(k < levels, thickness(k), 0.0)
    shared[:, :ROWS, :] = jnp.broadcast_to((depth / LEVELS)[None], (shared.shape[0], ROWS, COLS))
    shared[:, ROWS:, :] = jnp.broadcast_to(surface_ref[...][None], (shared.shape[0], ROWS, COLS))

    per = 2 * LEVELS
    level_row = lax.broadcasted_iota(jnp.int32, (per, COLS), 0)
    level_row = jnp.where(level_row >= LEVELS, level_row - LEVELS, level_row)
    wet_south = level_row < jnp.broadcast_to(levels[:1, :], (per, COLS))
    wet_north = level_row < jnp.broadcast_to(levels[ROWS - 1 :, :], (per, COLS))
    for g in range(GROUPS):
        large[g].wait()
        west = jnp.zeros((ROWS, COLS), jnp.float32)
        east = jnp.zeros((ROWS, COLS), jnp.float32)
        for t in range(GROUP):
            for k in range(LEVELS):
                row, first = ((g * GROUP + t) * LEVELS + k) * ROWS, t * LEVELS + k
                tile = jnp.where(k < levels, cells[row : row + ROWS, :], 0.0)
                west = jnp.where(lane == first, roll(tile, first, 1), west)
                east = jnp.where(lane == first, roll(tile, first + 1, 1), east)
        to_west[g * ROWS : (g + 1) * ROWS, :] = west
        to_east[g * ROWS : (g + 1) * ROWS, :] = east
        for half in range(GROUP * LEVELS // per):
            at = g * GROUP * LEVELS + half * per
            south = jnp.where(wet_south, cells[pl.ds(at * ROWS, per, stride=ROWS), :], 0.0)
            north = jnp.where(wet_north, cells[pl.ds(at * ROWS + ROWS - 1, per, stride=ROWS), :], 0.0)
            near[at : at + per, :] = jnp.where(even, north, south)
            far[at : at + per, :] = jnp.where(even, south, north)


def pole_of(fold_map):
    return (fold_map[0] + 1) & (COLS * lax.axis_size("gx") - 1)


def halo_rows(fold_map, near, far, extra, north_rows, south_rows):
    here = lax.axis_index("gy")
    top = lax.axis_size("gy") - 1

    @pl.when(here % 2 == 0)
    def _():
        north_rows[...] = near[...]
        south_rows[...] = far[...]

    @pl.when(here % 2 == 1)
    def _():
        south_rows[...] = near[...]

    @pl.when((here % 2 == 1) & (here != top))
    def _():
        north_rows[...] = far[...]

    @pl.when(here == top)
    def _():
        lane = lanes()
        pole = pole_of(fold_map)
        offset = pole & (COLS - 1)
        index = (offset - 1 - lane) & (COLS - 1)
        from_far = (lane >= offset) == ((pole & COLS) != 0)
        for row in range(0, north_rows.shape[0], ROWS):
            a = jnp.take_along_axis(far[row : row + ROWS, :], index, axis=1)
            b = jnp.take_along_axis(extra[row : row + ROWS, :], index, axis=1)
            north_rows[row : row + ROWS, :] = jnp.where(from_far, a, b)


def right_side_kernel(
    fold_map, tracer, east_vel, north_vel, diffusion, mixing, count, from_east, from_west, near, far, extra,
    rhs,
    north_rows, south_rows,
):
    lane, sub = lanes(), sublanes()
    levels = count[...]
    halo_rows(fold_map, near, far, extra, north_rows, south_rows)

    def gap(rows, k):
        return rows[k : k + 1, :] - rows[LEVELS + k : LEVELS + k + 1, :]

    columns_east = from_east[...] - roll(from_east[...], -LEVELS, 1)
    columns_west = from_west[...] - roll(from_west[...], -LEVELS, 1)
    zero = jnp.zeros((ROWS, COLS), jnp.float32)
    c_prev, r_prev, a_prev = zero, zero, zero
    c_list, r_list = [], []
    for k in range(LEVELS):
        wet = k < levels
        cell = jnp.where(wet, tracer[0, k] - tracer[1, k], 0.0)
        east = east_of(cell, roll(columns_east, -k, 1), lane)
        west = west_of(cell, roll(columns_west, COLS - 1 - k, 1), lane)
        north = north_of(cell, gap(north_rows, k), sub)
        south = south_of(cell, gap(south_rows, k), sub)
        change = (
            -0.5 * east_vel[k] * (east - west)
            - 0.5 * north_vel[k] * (north - south)
            + diffusion[k] * (east + west + north + south - 4.0 * cell)
        )
        explicit = cell + jnp.where(wet, change, 0.0)
        a = jnp.where(k + 1 < levels, mixing[k], 0.0)
        inverse = 1.0 / (1.0 + a_prev + a + a_prev * c_prev)
        c_prev = -a * inverse
        r_prev = (explicit + a_prev * r_prev) * inverse
        a_prev = a
        c_list.append(c_prev)
        r_list.append(r_prev)
    total, x_next = zero, zero
    for k in range(LEVELS - 1, -1, -1):
        x_next = r_list[k] - c_list[k] * x_next
        total = total + thickness(k) * x_next
    value = jnp.where(levels > 0, 0.25 * total, 0.0)
    rhs[...] = jnp.broadcast_to(value[None], rhs.shape)


def gradients_kernel(
    fold_map, rhs, shared,
    pressure, residual,
    to_e, to_w, from_n, from_ne, from_nw, from_s, from_se, from_sw, diagonal, inverse, scaled, field, image, ghost,
):
    nx, ny = lax.axis_size("gx"), lax.axis_size("gy")
    lane, sub = lanes(), sublanes()
    zero = jnp.zeros((ROWS, COLS), jnp.float32)
    pole = pole_of(fold_map)

    def tile(ref, x, y):
        return ref[pl.ds(pl.multiple_of((x * ny + y) * ROWS, ROWS), ROWS), :]

    def put(ref, x, y, value):
        ref[pl.ds(pl.multiple_of((x * ny + y) * ROWS, ROWS), ROWS), :] = value

    def strip(ref, x):
        return [tile(ref, x, y) for y in range(ny)]

    def beside(ref, x):
        own = strip(ref, x)
        after, before = strip(ref, (x + 1) & (nx - 1)), strip(ref, (x - 1) & (nx - 1))
        east = [east_of(own[y], after[y], lane) for y in range(ny)]
        west = [west_of(own[y], before[y], lane) for y in range(ny)]
        return own, east, west

    def moved_south(tiles, last):
        return [north_of(tiles[y], tiles[y + 1] if y + 1 < ny else last, sub) for y in range(ny)]

    def moved_north(tiles):
        return [south_of(tiles[y], tiles[y - 1] if y else zero, sub) for y in range(ny)]

    def over_fold(ref, shift):
        turn = (pole - 1 - shift) & (nx * COLS - 1)
        offset, block = (turn + 1) & (COLS - 1), ((turn + 1) >> (COLS.bit_length() - 1)) & (nx - 1)
        rows = ref[pl.ds(ny * ROWS - 1, nx, stride=ny * ROWS), :]
        index = (offset - 1 - lane) & (COLS - 1)
        halves = [jnp.take_along_axis(rows[h : h + ROWS, :], index, axis=1) for h in range(0, nx, ROWS)]
        out = []
        for h in range(0, nx, ROWS):
            ends = []
            for turned in (block - 1, block):
                source = (turned - h - sub) & (nx - 1)
                value = jnp.take_along_axis(halves[0], source & (ROWS - 1), axis=0)
                for at in range(1, nx // ROWS):
                    other = jnp.take_along_axis(halves[at], source & (ROWS - 1), axis=0)
                    value = jnp.where(source >= at * ROWS, other, value)
                ends.append(value)
            out.append(jnp.where(lane >= offset, ends[0], ends[1]))
        return out

    def last_rows(ref):
        rows = ref[pl.ds(ny * ROWS - 1, nx, stride=ny * ROWS), :]
        return [rows[h : h + ROWS, :] for h in range(0, nx, ROWS)]

    def put_ghost(values):
        for at, value in enumerate(values):
            ghost[at * ROWS : (at + 1) * ROWS, :] = value

    def total(value):
        return jnp.broadcast_to(jnp.sum(value, keepdims=True), (ROWS, COLS))

    def spread(x, carry):
        for y in range(ny):
            put(field, x, y, shared[x * ny + y, :ROWS, :])
        return carry

    lax.fori_loop(0, nx, spread, 0)
    edge, beyond = last_rows(field), over_fold(field, 0)
    beyond_e, beyond_w = over_fold(field, 1), over_fold(field, -1)
    fold_n = [jnp.minimum(a, b) for a, b in zip(edge, beyond)]
    fold_ne = [0.5 * jnp.minimum(a, b) for a, b in zip(edge, beyond_e)]
    fold_nw = [0.5 * jnp.minimum(a, b) for a, b in zip(edge, beyond_w)]
    put_ghost([a + b + c for a, b, c in zip(fold_n, fold_ne, fold_nw)])

    def couple(x, energy):
        own, east, west = beside(field, x)
        above = moved_south(own, zero)
        below = moved_north(own)
        side, ahead, behind = [], [], []
        for y in range(ny):
            e, w = jnp.minimum(own[y], east[y]), jnp.minimum(own[y], west[y])
            n, ne, nw = (
                jnp.minimum(below[y], own[y]),
                0.5 * jnp.minimum(below[y], east[y]),
                0.5 * jnp.minimum(below[y], west[y]),
            )
            s, se, sw = (
                jnp.minimum(above[y], own[y]),
                0.5 * jnp.minimum(above[y], east[y]),
                0.5 * jnp.minimum(above[y], west[y]),
            )
            for ref, value in zip(
                (to_e, to_w, from_n, from_ne, from_nw, from_s, from_se, from_sw), (e, w, n, ne, nw, s, se, sw)
            ):
                put(ref, x, y, value)
            side.append(e + w)
            ahead.append(n + ne + nw)
            behind.append(s + se + sw)
        ahead = moved_south(ahead, ghost[pl.ds(x, 1), :])
        behind = moved_north(behind)
        for y in range(ny):
            term = shared[x * ny + y, ROWS:, :] + (side[y] + ahead[y] + behind[y])
            diag = jnp.where(own[y] > 0.0, term, 1.0)
            inv = 1.0 / diag
            resid = tile(rhs, x, y)
            first = resid * inv
            put(diagonal, x, y, diag)
            put(inverse, x, y, inv)
            put(scaled, x, y, first)
            energy = energy + resid * first
        return energy

    energy = total(lax.fori_loop(0, nx, couple, zero))

    def start(x, carry):
        for y in range(ny):
            put(field, x, y, tile(scaled, x, y))
            put(scaled, x, y, tile(rhs, x, y))
        return carry

    lax.fori_loop(0, nx, start, 0)

    my_x, my_y = lax.axis_index("gx"), lax.axis_index("gy")
    mine = zero
    for step in range(ITERS):
        beyond = zip(fold_n, over_fold(field, 0), fold_ne, over_fold(field, 1), fold_nw, over_fold(field, -1))
        put_ghost([a * p + b * q + c * r for a, p, b, q, c, r in beyond])

        def apply(x, product):
            own, east, west = beside(field, x)
            ahead, behind = [], []
            for y in range(ny):
                ahead.append(
                    tile(from_n, x, y) * own[y] + tile(from_ne, x, y) * east[y] + tile(from_nw, x, y) * west[y]
                )
                behind.append(
                    tile(from_s, x, y) * own[y] + tile(from_se, x, y) * east[y] + tile(from_sw, x, y) * west[y]
                )
            ahead = moved_south(ahead, ghost[pl.ds(x, 1), :])
            behind = moved_north(behind)
            for y in range(ny):
                side = tile(to_e, x, y) * east[y] + tile(to_w, x, y) * west[y]
                value = tile(diagonal, x, y) * own[y] - (side + ahead[y] + behind[y])
                put(image, x, y, value)
                product = product + own[y] * value
            return product

        step_size = energy / total(lax.fori_loop(0, nx, apply, zero))
        mine = mine + step_size * tile(field, my_x, my_y)
        if step + 1 == ITERS:
            break

        def reduce(x, sums):
            for y in range(ny):
                resid = tile(scaled, x, y) - step_size * tile(image, x, y)
                put(scaled, x, y, resid)
                sums = sums + resid * (resid * tile(inverse, x, y))
            return sums

        energy_new = total(lax.fori_loop(0, nx, reduce, zero))
        ratio = energy_new / energy
        energy = energy_new

        def turn(x, carry):
            for y in range(ny):
                put(field, x, y, tile(scaled, x, y) * tile(inverse, x, y) + ratio * tile(field, x, y))
            return carry

        lax.fori_loop(0, nx, turn, 0)
    pressure[...] = mine
    residual[...] = tile(scaled, my_x, my_y) - step_size * tile(image, my_x, my_y)


def tracers_kernel(
    fold_map, tracer, east_vel, north_vel, diffusion, mixing, count, from_east, from_west, near, far, extra,
    mixed,
    north_rows, south_rows, factors,
):
    lane, sub = lanes(), sublanes()
    levels = count[...]
    group = pl.program_id(0)

    @pl.when(group == 0)
    def _():
        halo_rows(fold_map, near, far, extra, north_rows, south_rows)
        c_prev = jnp.zeros((ROWS, COLS), jnp.float32)
        a_prev = jnp.zeros((ROWS, COLS), jnp.float32)
        for k in range(LEVELS):
            wet = jnp.where(k < levels, 1.0, 0.0)
            u, v, spread = 0.5 * wet * east_vel[k], 0.5 * wet * north_vel[k], wet * diffusion[k]
            a = jnp.where(k + 1 < levels, mixing[k], 0.0)
            inverse = 1.0 / (1.0 + a_prev + a + a_prev * c_prev)
            c_prev = -a * inverse
            factors[0, k] = 1.0 - 4.0 * spread
            factors[1, k] = spread - u
            factors[2, k] = spread + u
            factors[3, k] = spread - v
            factors[4, k] = spread + v
            factors[5, k] = inverse
            factors[6, k] = a_prev
            factors[7, k] = c_prev
            a_prev = a

    row = pl.multiple_of(group * ROWS, ROWS)
    columns_east = from_east[pl.ds(row, ROWS), :]
    columns_west = from_west[pl.ds(row, ROWS), :]
    r_prev = [jnp.zeros((ROWS, COLS), jnp.float32)] * GROUP
    for k in range(LEVELS):
        centre, to_e, to_w, to_n, to_s, inverse, above = (factors[j, k] for j in range(7))
        wet = k < levels
        for t in range(GROUP):
            cell = jnp.where(wet, tracer[t, k], 0.0)
            at = t * LEVELS + k
            halo_row = group * (GROUP * LEVELS) + at
            east = east_of(cell, roll(columns_east, -at, 1), lane)
            west = west_of(cell, roll(columns_west, COLS - 1 - at, 1), lane)
            north = north_of(cell, north_rows[pl.ds(halo_row, 1), :], sub)
            south = south_of(cell, south_rows[pl.ds(halo_row, 1), :], sub)
            explicit = centre * cell + to_e * east + to_w * west + to_n * north + to_s * south
            r_prev[t] = (explicit + above * r_prev[t]) * inverse
            mixed[t, k] = r_prev[t]
    x_next = r_prev
    for k in range(LEVELS - 2, -1, -1):
        below = factors[7, k]
        for t in range(GROUP):
            x_next[t] = mixed[t, k] - below * x_next[t]
            mixed[t, k] = x_next[t]


def shards(sizes, tracer, east_vel, north_vel, diffusion, mixing, level_count, fold_map, surface_term):
    nx, ny = sizes
    f32 = jnp.float32
    grid_rows = nx * ny * ROWS

    def device(x, y):
        return (x % nx) * ny + y

    def kernel(body, **rest):
        return pl.pallas_call(body, compiler_params=params(), **rest)

    def shape(*dims):
        return jax.ShapeDtypeStruct(dims, f32)

    def vmem(*dims):
        return pltpu.VMEM(dims, f32)

    def all_of(array):
        return pl.BlockSpec(array.shape, lambda i: (0,) * array.ndim)

    smem = pl.BlockSpec(memory_space=pltpu.SMEM)
    hbm = pl.BlockSpec(memory_space=pltpu.HBM)
    fields = (east_vel, north_vel, diffusion, mixing)
    flat = tracer.reshape(EDGE * ROWS, COLS)

    to_west, to_east, near, far, shared = kernel(
        pack_kernel,
        out_shape=(
            shape(GROUPS * ROWS, COLS),
            shape(GROUPS * ROWS, COLS),
            shape(EDGE, COLS),
            shape(EDGE, COLS),
            shape(nx * ny, 2 * ROWS, COLS),
        ),
        in_specs=[hbm] * 3,
        out_specs=(whole(),) * 5,
        scratch_shapes=[
            vmem(EDGE * ROWS, COLS),
            pltpu.VMEM((ROWS, COLS), jnp.int32),
            vmem(ROWS, COLS),
            pltpu.SemaphoreType.DMA((GROUPS + 2,)),
        ],
        name="pack",
    )(flat, level_count, surface_term)

    from_east = lax.ppermute(to_west, BOTH, [(device(x + 1, y), device(x, y)) for x in range(nx) for y in range(ny)])
    from_west = lax.ppermute(to_east, BOTH, [(device(x - 1, y), device(x, y)) for x in range(nx) for y in range(ny)])
    near = lax.ppermute(near, BOTH, [(device(x, y ^ 1), device(x, y)) for x in range(nx) for y in range(ny)])
    inner = [(device(x, y + 1 if y % 2 else y - 1), device(x, y)) for x in range(nx) for y in range(1, ny - 1)]
    shared = lax.all_to_all(shared, BOTH, 0, 0)

    def across(turn):
        return [(device(turn - x, ny - 1), device(x, ny - 1)) for x in range(nx)]

    def exchange(block, rows):
        turns = ((block - 1) % nx, block)
        even, odd = turns if turns[0] % 2 == 0 else turns[::-1]
        return lax.ppermute(rows, BOTH, inner + across(even)), lax.ppermute(rows, BOTH, across(odd))

    block = pole_of(fold_map) >> (COLS.bit_length() - 1)
    far, extra = lax.switch(block, [functools.partial(exchange, i) for i in range(nx)], far)

    pair = pl.BlockSpec((2, LEVELS, ROWS, COLS), lambda i: (0, 0, 0, 0))
    two = pl.BlockSpec((2 * LEVELS, COLS), lambda i: (0, 0))
    tile = pl.BlockSpec((ROWS, COLS), lambda i: (0, 0))
    rhs = kernel(
        right_side_kernel,
        grid=(1,),
        out_shape=shape(nx * ny, ROWS, COLS),
        in_specs=[smem, pair] + [all_of(array) for array in (*fields, level_count)] + [tile, tile, two, two, two],
        out_specs=pl.BlockSpec((nx * ny, ROWS, COLS), lambda i: (0, 0, 0)),
        scratch_shapes=[vmem(2 * LEVELS, COLS), vmem(2 * LEVELS, COLS)],
        name="right_side",
    )(fold_map, tracer, *fields, level_count, from_east, from_west, near, far, extra)
    rhs = lax.all_to_all(rhs, BOTH, 0, 0).reshape(grid_rows, COLS)

    batch = pl.BlockSpec((GROUP, LEVELS, ROWS, COLS), lambda i: (i, 0, 0, 0))
    edge = pl.BlockSpec((EDGE, COLS), lambda i: (0, 0))
    tiles = pl.BlockSpec((GROUPS * ROWS, COLS), lambda i: (0, 0))
    mixed = kernel(
        tracers_kernel,
        grid=(GROUPS,),
        out_shape=shape(TRACERS, LEVELS, ROWS, COLS),
        in_specs=[smem, batch] + [all_of(array) for array in (*fields, level_count)] + [tiles, tiles, edge, edge, edge],
        out_specs=batch,
        scratch_shapes=[vmem(EDGE, COLS), vmem(EDGE, COLS), vmem(8, LEVELS, ROWS, COLS)],
        name="tracers",
    )(fold_map, tracer, *fields, level_count, from_east, from_west, near, far, extra)

    pressure, residual = kernel(
        gradients_kernel,
        out_shape=(shape(ROWS, COLS), shape(ROWS, COLS)),
        in_specs=[smem, whole(), whole()],
        out_specs=(whole(), whole()),
        scratch_shapes=[vmem(grid_rows, COLS) for _ in range(13)] + [vmem(nx, COLS)],
        name="gradients",
    )(fold_map, rhs, shared)
    return mixed, pressure, residual


def solution(mesh):
    in_specs = (
        P(None, None, "gy", "gx"),
        P(None, "gy", "gx"),
        P(None, "gy", "gx"),
        P(None, "gy", "gx"),
        P(None, "gy", "gx"),
        P("gy", "gx"),
        P(),
        P("gy", "gx"),
    )
    out_specs = (P(None, None, "gy", "gx"), P("gy", "gx"), P("gy", "gx"))
    body = functools.partial(shards, (mesh.shape["gx"], mesh.shape["gy"]))
    return jax.shard_map(body, mesh=mesh, in_specs=in_specs, out_specs=out_specs, check_vma=False)
```

```python
import functools

import jax
import jax.numpy as jnp
from jax import lax
from jax.experimental import pallas as pl
from jax.experimental.pallas import tpu as pltpu
from jax.sharding import PartitionSpec as P

ITERS = 4
TRACERS, LEVELS, ROWS, COLS = 16, 20, 8, 128
GROUP = 4
GROUPS = TRACERS // GROUP
EDGE = TRACERS * LEVELS
BOTH = ("gx", "gy")
VMEM_LIMIT = 40 * 1024 * 1024
PACK_VMEM_LIMIT = 63 * 1024 * 1024

COL_DEEP, COL_SIZE = GROUPS * ROWS, (GROUPS + 5) * ROWS
COUNT_LANE, SURFACE_LANE = 100, 105
ROW_EAST, ROW_WEST, ROW_DIFF, ROW_COUNT, ROW_SURFACE, ROW_SIZE = 0, 8, 16, 40, 48, 56

SCALAR_BOUND, FIELD_BOUND = 1500.0, 1.0e5

NEIGHBOURS = [
    (0, 1, 1.0),
    (0, -1, 1.0),
    (1, 0, 1.0),
    (-1, 0, 1.0),
    (1, 1, 0.5),
    (1, -1, 0.5),
    (-1, 1, 0.5),
    (-1, -1, 0.5),
]


def params(limit=VMEM_LIMIT):
    return pltpu.CompilerParams(vmem_limit_bytes=limit)


def whole():
    return pl.BlockSpec(memory_space=pltpu.VMEM)


def lanes():
    return lax.broadcasted_iota(jnp.int32, (ROWS, COLS), 1)


def sublanes():
    return lax.broadcasted_iota(jnp.int32, (ROWS, COLS), 0)


def roll(tile, shift, axis):
    size = tile.shape[axis]
    shift = shift % size
    return tile if shift == 0 else pltpu.roll(tile, shift, axis)


def east_of(tile, beyond, lane):
    return roll(jnp.where(lane == 0, beyond, tile), -1, 1)


def west_of(tile, beyond, lane):
    return roll(jnp.where(lane == COLS - 1, beyond, tile), 1, 1)


def north_of(tile, beyond, sub):
    return roll(jnp.where(sub == 0, beyond, tile), -1, 0)


def south_of(tile, beyond, sub):
    return roll(jnp.where(sub == ROWS - 1, beyond, tile), 1, 0)


def thickness(level):
    return 0.5 + 1.5 * level / (LEVELS - 1)


def turned(tile):
    return jnp.take_along_axis(tile, ROWS - 1 - sublanes(), axis=0)


def pack_kernel(
    tracer, east_vel, north_vel, diffusion, mixing, count, surface,
    to_west, to_east, near, far, near_rows, far_rows,
    cells, fields, levels_ref, surface_ref, ready,
):
    lane = lanes()
    size = GROUP * LEVELS * ROWS
    pairs = [(count, levels_ref), (surface, surface_ref)]
    pairs += [(tracer.at[pl.ds(g * size, size)], cells.at[pl.ds(g * size, size)]) for g in range(GROUPS)]
    pairs += [(field, fields.at[f]) for f, field in enumerate((east_vel, north_vel, diffusion, mixing))]
    copies = [pltpu.make_async_copy(source, target, ready.at[i]) for i, (source, target) in enumerate(pairs)]
    for copy in copies:
        copy.start()
    here = lax.axis_index("gy")
    even = here % 2 == 0
    is_top = here == lax.axis_size("gy") - 1

    def put(row, items):
        west = jnp.zeros((ROWS, COLS), jnp.float32)
        east = jnp.zeros((ROWS, COLS), jnp.float32)
        for tile, width, first in items:
            chosen = lane == first if width == 1 else (lane >= first) & (lane < first + width)
            west = jnp.where(chosen, roll(tile, first, 1), west)
            east = jnp.where(chosen, roll(tile, first + width, 1), east)
        to_west[row : row + ROWS, :] = west
        to_east[row : row + ROWS, :] = east

    copies[0].wait()
    copies[1].wait()
    levels, surfaces = levels_ref[...], surface_ref[...]
    depths = levels.astype(jnp.float32)
    for row, value in ((ROW_COUNT, depths), (ROW_SURFACE, surfaces)):
        near_rows[row : row + ROWS, :] = value
        far_rows[row : row + ROWS, :] = jnp.where(is_top, turned(value), value)
    per = 2 * LEVELS
    level_row = lax.broadcasted_iota(jnp.int32, (per, COLS), 0)
    level_row = jnp.where(level_row >= LEVELS, level_row - LEVELS, level_row)
    wet_south = level_row < jnp.broadcast_to(levels[:1, :], (per, COLS))
    wet_north = level_row < jnp.broadcast_to(levels[ROWS - 1 :, :], (per, COLS))
    for g in range(GROUPS):
        copies[2 + g].wait()

        def cell(t, k):
            row = (t * LEVELS + k) * ROWS
            return jnp.where(k < levels, cells[row : row + ROWS, :], 0.0)

        put(g * ROWS, [(cell(g * GROUP + t, k), 1, t * LEVELS + k) for t in range(GROUP) for k in range(LEVELS)])
        if g == 0:
            difference = [(cell(0, k) - cell(1, k), 5, 5 * k) for k in range(LEVELS)]
            put(COL_DEEP, difference + [(depths, 5, COUNT_LANE), (surfaces, 4, SURFACE_LANE)])
        for half in range(GROUP * LEVELS // per):
            at = g * GROUP * LEVELS + half * per
            south = jnp.where(wet_south, cells[pl.ds(at * ROWS, per, stride=ROWS), :], 0.0)
            north = jnp.where(wet_north, cells[pl.ds(at * ROWS + ROWS - 1, per, stride=ROWS), :], 0.0)
            near[at : at + per, :] = jnp.where(even, north, south)
            far[at : at + per, :] = jnp.where(even, south, north)
    for edge in (near, far):
        rows = near_rows if edge is near else far_rows
        rows[ROW_DIFF : ROW_DIFF + LEVELS, :] = edge[:LEVELS, :] - edge[LEVELS : 2 * LEVELS, :]
        rows[ROW_DIFF + LEVELS : ROW_COUNT, :] = jnp.zeros((ROW_COUNT - ROW_DIFF - LEVELS, COLS), jnp.float32)
    for f in range(4):
        copies[2 + GROUPS + f].wait()
        put(COL_DEEP + (1 + f) * ROWS, [(fields[f, k], 4, 4 * k) for k in range(LEVELS)])


def corners_kernel(east, west, near_in, far_in, near, far):
    del near_in, far_in
    is_top = lax.axis_index("gy") == lax.axis_size("gy") - 1
    for row, value in ((ROW_EAST, east[...]), (ROW_WEST, west[...])):
        near[row : row + ROWS, :] = value
        far[row : row + ROWS, :] = jnp.where(is_top, turned(value), value)


def pole_of(fold_map):
    return (fold_map[0] + 1) & (COLS * lax.axis_size("gx") - 1)


def folded(offset, a_main, a_side, b_main, b_side):
    lane = lanes()
    index = (offset - 1 - lane) & (COLS - 1)
    a, b, c, d = (jnp.take_along_axis(tile, index, axis=1) for tile in (a_main, b_main, a_side, b_side))
    right = jnp.where(lane < offset, a, c)
    left = jnp.where(lane >= offset, b, d)
    return jnp.where(lane >= offset, a, b), jnp.where(lane < COLS // 2, right, left)


class Rows:
    def __init__(self, fold_map, near, far, extra):
        here = lax.axis_index("gy")
        pole = pole_of(fold_map)
        self.near, self.far, self.extra = near, far, extra
        self.even = here % 2 == 0
        self.is_top = here == lax.axis_size("gy") - 1
        self.offset = pole & (COLS - 1)
        self.first_in_far = (pole & COLS) != 0

    def at(self, ref, row):
        return ref[row : row + ROWS, :]

    def south(self, row):
        return jnp.where(self.even, self.at(self.far, row), self.at(self.near, row))

    def north(self, row):
        return jnp.where(self.even, self.at(self.near, row), self.at(self.far, row))

    def blocks(self, row):
        far, extra = self.at(self.far, row), self.at(self.extra, row)
        return jnp.where(self.first_in_far, far, extra), jnp.where(self.first_in_far, extra, far)


def halo_rows(fold_map, near, far, extra, north_rows, south_rows):
    here = lax.axis_index("gy")
    top = lax.axis_size("gy") - 1

    @pl.when(here % 2 == 0)
    def _():
        north_rows[...] = near[...]
        south_rows[...] = far[...]

    @pl.when(here % 2 == 1)
    def _():
        south_rows[...] = near[...]

    @pl.when((here % 2 == 1) & (here != top))
    def _():
        north_rows[...] = far[...]

    @pl.when(here == top)
    def _():
        lane = lanes()
        pole = pole_of(fold_map)
        offset = pole & (COLS - 1)
        index = (offset - 1 - lane) & (COLS - 1)
        from_far = (lane >= offset) == ((pole & COLS) != 0)
        for row in range(0, north_rows.shape[0], ROWS):
            a = jnp.take_along_axis(far[row : row + ROWS, :], index, axis=1)
            b = jnp.take_along_axis(extra[row : row + ROWS, :], index, axis=1)
            north_rows[row : row + ROWS, :] = jnp.where(from_far, a, b)


def unpack(east, west, first, width, lane):
    right = roll(east, -first, 1)
    left = roll(west, -width - first, 1)
    return jnp.where(lane < width, right, jnp.where(lane >= COLS - width, left, 0.0))


def both_east(one, two, lane):
    return east_of(one, two, lane), east_of(two, one, lane)


def both_west(one, two, lane):
    return west_of(one, two, lane), west_of(two, one, lane)


def right_side_kernel(
    fold_map, tracer, east_vel, north_vel, diffusion, mixing, count, from_east, from_west, near, far, extra,
    rhs, rhs_far,
    beyond_main, beyond_side,
):
    lane, sub = lanes(), sublanes()
    low = sub < ROWS // 2
    rows = Rows(fold_map, near, far, extra)
    south_east, south_west = rows.south(ROW_EAST), rows.south(ROW_WEST)
    south_rows = [rows.south(ROW_DIFF + row) for row in range(0, ROW_COUNT - ROW_DIFF, ROWS)]

    def row_of(tiles, k):
        return jnp.broadcast_to(tiles[k // ROWS][k % ROWS : k % ROWS + 1, :], (ROWS, COLS))

    @pl.when(jnp.logical_not(rows.is_top))
    def _():
        east = jnp.where(low, rows.north(ROW_EAST), south_east)
        west = jnp.where(low, rows.north(ROW_WEST), south_west)
        north_rows = [rows.north(ROW_DIFF + row) for row in range(0, ROW_COUNT - ROW_DIFF, ROWS)]
        for k in range(LEVELS):
            beyond_main[k] = jnp.where(low, row_of(north_rows, k), row_of(south_rows, k))
            beyond_side[k] = unpack(east, west, 5 * k, 5, lane)

    @pl.when(rows.is_top)
    def _():
        (a_east, b_east), (a_west, b_west) = rows.blocks(ROW_EAST), rows.blocks(ROW_WEST)
        pairs = [rows.blocks(ROW_DIFF + row) for row in range(0, ROW_COUNT - ROW_DIFF, ROWS)]
        a_rows, b_rows = [pair[0] for pair in pairs], [pair[1] for pair in pairs]
        for k in range(LEVELS):
            main, side = folded(
                rows.offset,
                row_of(a_rows, k),
                unpack(a_east, a_west, 5 * k, 5, lane),
                row_of(b_rows, k),
                unpack(b_east, b_west, 5 * k, 5, lane),
            )
            beyond_main[k] = jnp.where(low, main, row_of(south_rows, k))
            beyond_side[k] = jnp.where(low, side, unpack(south_east, south_west, 5 * k, 5, lane))

    def column(f):
        row = COL_DEEP + ROWS * f
        return from_east[row : row + ROWS, :], from_west[row : row + ROWS, :]

    columns = [column(f) for f in range(5)]
    counts = (count[...].astype(jnp.float32), unpack(*columns[0], COUNT_LANE, 5, lane))
    zero = jnp.zeros((ROWS, COLS), jnp.float32)
    c_prev, r_prev, a_prev = [zero] * 2, [zero] * 2, [zero] * 2
    c_list, r_list = [], []
    for k in range(LEVELS):
        centre = (jnp.where(k < counts[0], tracer[0, k] - tracer[1, k], 0.0), unpack(*columns[0], 5 * k, 5, lane))
        easts, wests = both_east(*centre, lane), both_west(*centre, lane)
        beyond = (beyond_main[k], beyond_side[k])
        values = [
            (field[k], unpack(*columns[1 + f], 4 * k, 4, lane))
            for f, field in enumerate((east_vel, north_vel, diffusion, mixing))
        ]
        c_now, r_now, a_now = [], [], []
        for i in range(2):
            u, v, spread, mix = (value[i] for value in values)
            north, south = north_of(centre[i], beyond[i], sub), south_of(centre[i], beyond[i], sub)
            change = (
                -0.5 * u * (easts[i] - wests[i])
                - 0.5 * v * (north - south)
                + spread * (easts[i] + wests[i] + north + south - 4.0 * centre[i])
            )
            explicit = centre[i] + jnp.where(k < counts[i], change, 0.0)
            a = jnp.where(k + 1 < counts[i], mix, 0.0)
            inverse = 1.0 / (1.0 + a_prev[i] + a + a_prev[i] * c_prev[i])
            c_now.append(-a * inverse)
            r_now.append((explicit + a_prev[i] * r_prev[i]) * inverse)
            a_now.append(a)
        c_prev, r_prev, a_prev = c_now, r_now, a_now
        c_list.append(c_now)
        r_list.append(r_now)
    total, x_next = [zero] * 2, [zero] * 2
    for k in range(LEVELS - 1, -1, -1):
        x_next = [r_list[k][i] - c_list[k][i] * x_next[i] for i in range(2)]
        total = [total[i] + thickness(k) * x_next[i] for i in range(2)]
    for i in range(2):
        value = jnp.where(counts[i] > 0, 0.25 * total[i], 0.0)
        rhs[i * ROWS : (i + 1) * ROWS, :] = value
        rhs_far[i * ROWS : (i + 1) * ROWS, :] = jnp.where(rows.is_top, turned(value), value)


def couplings_kernel(
    fold_map, count, surface, from_east, from_west, near, far, extra,
    coupling, inverse, diagonal,
):
    lane, sub = lanes(), sublanes()
    low = sub < ROWS // 2
    rows = Rows(fold_map, near, far, extra)

    def halo(pair):
        return jnp.where(low, pair[0], pair[1])

    def side_of(packed, first, width):
        return unpack(packed[0], packed[1], first, width, lane)

    south_packed = rows.south(ROW_EAST), rows.south(ROW_WEST)
    north_packed = rows.north(ROW_EAST), rows.north(ROW_WEST)
    (a_east, b_east), (a_west, b_west) = rows.blocks(ROW_EAST), rows.blocks(ROW_WEST)

    def norths(row, first, width):
        a, b = rows.blocks(row)
        main, side = folded(
            rows.offset, a, side_of((a_east, a_west), first, width), b, side_of((b_east, b_west), first, width)
        )
        return (
            jnp.where(rows.is_top, main, rows.north(row)),
            jnp.where(rows.is_top, side, side_of(north_packed, first, width)),
        )

    counts_own = (count[...].astype(jnp.float32), unpack(from_east[...], from_west[...], COUNT_LANE, 5, lane))
    counts_north = norths(ROW_COUNT, COUNT_LANE, 5)
    counts_south = (rows.south(ROW_COUNT), side_of(south_packed, COUNT_LANE, 5))
    counts = counts_own + tuple(halo(pair) for pair in zip(counts_north, counts_south))
    surface_south = (rows.south(ROW_SURFACE), side_of(south_packed, SURFACE_LANE, 4))
    surfaces = (surface[...], unpack(from_east[...], from_west[...], SURFACE_LANE, 4, lane)) + tuple(
        halo(pair) for pair in zip(norths(ROW_SURFACE, SURFACE_LANE, 4), surface_south)
    )

    def neighbours_across(own, north, south):
        up, up_n, up_s = roll(own, -1, 0), roll(north, -1, 0), roll(south, -1, 0)
        down, down_n, down_s = roll(own, 1, 0), roll(north, 1, 0), roll(south, 1, 0)
        return (
            jnp.where(sub == 7, up_n, up),
            jnp.where(low, up_n, jnp.where(sub == 7, up, up_s)),
            jnp.where(sub == 0, down_s, down),
            jnp.where(sub == 0, down, jnp.where(low, down_n, down_s)),
        )

    zero = jnp.zeros((ROWS, COLS), jnp.float32)
    def depth_of(levels):
        depth = zero
        for k in range(LEVELS):
            depth = depth + jnp.where(k < levels, thickness(k), 0.0)
        return depth / LEVELS

    own = tuple(depth_of(levels) for levels in counts_own)
    north = tuple(depth_of(levels) for levels in counts_north)
    south = tuple(depth_of(levels) for levels in counts_south)
    depths = (own[0], own[1], halo((north[0], south[0])), halo((north[1], south[1])))

    def rows_of(own, north, south):
        first = neighbours_across(own[0], north[0], south[0])
        second = neighbours_across(own[1], north[1], south[1])
        return (first[0], second[0], first[1], second[1]), (first[2], second[2], first[3], second[3])

    def coupled(others, weight):
        return [weight * jnp.minimum(depths[i], others[i]) for i in range(4)]

    own_e, north_e, south_e = (both_east(*pair, lane) for pair in (own, north, south))
    own_w, north_w, south_w = (both_west(*pair, lane) for pair in (own, north, south))
    halo_e = (halo((north_e[0], south_e[0])), halo((north_e[1], south_e[1])))
    halo_w = (halo((north_w[0], south_w[0])), halo((north_w[1], south_w[1])))
    mid = rows_of(own, north, south)
    mid_e = rows_of(own_e, north_e, south_e)
    mid_w = rows_of(own_w, north_w, south_w)
    couplings = [
        coupled(own_e + halo_e, 1.0),
        coupled(own_w + halo_w, 1.0),
        coupled(mid[0], 1.0),
        coupled(mid[1], 1.0),
        coupled(mid_e[0], 0.5),
        coupled(mid_w[0], 0.5),
        coupled(mid_e[1], 0.5),
        coupled(mid_w[1], 0.5),
    ]
    diag = [
        jnp.where(counts[i] > 0, surfaces[i] + sum(entry[i] for entry in couplings), 1.0) for i in range(4)
    ]
    for i in range(4):
        inv = 1.0 / diag[i]
        inverse[i] = inv
        for at, entry in enumerate(couplings):
            coupling[at, i] = entry[i] * inv
    diagonal[...] = diag[0]


def krylov_kernel(
    fold_map, coupling, inverse, diagonal, rhs, near, far, extra,
    vectors, partial,
):
    lane, sub = lanes(), sublanes()
    low = sub < ROWS // 2
    rows = Rows(fold_map, near, far, extra)
    (a_main, b_main), (a_side, b_side) = rows.blocks(0), rows.blocks(ROWS)
    north = folded(rows.offset, a_main, a_side, b_main, b_side)
    start = [rhs[:ROWS, :], rhs[ROWS:, :]]
    for i in range(2):
        value = jnp.where(rows.is_top, north[i], rows.north(i * ROWS))
        start.append(jnp.where(low, value, rows.south(i * ROWS)))

    def shifted_rows(tiles):
        north, south = [None] * 4, [None] * 4
        for i in range(2):
            a, b = roll(tiles[i], -1, 0), roll(tiles[i + 2], -1, 0)
            north[i], north[i + 2] = jnp.where(sub == 7, b, a), jnp.where(sub == 7, a, b)
            a, b = roll(tiles[i], 1, 0), roll(tiles[i + 2], 1, 0)
            south[i], south[i + 2] = jnp.where(sub == 0, b, a), jnp.where(sub == 0, a, b)
        return north, south

    def spread_out(tiles):
        east = both_east(tiles[0], tiles[1], lane) + both_east(tiles[2], tiles[3], lane)
        west = both_west(tiles[0], tiles[1], lane) + both_west(tiles[2], tiles[3], lane)
        mid_n, mid_s = shifted_rows(tiles)
        east_n, east_s = shifted_rows(east)
        west_n, west_s = shifted_rows(west)
        around = (east, west, mid_n, mid_s, east_n, west_n, east_s, west_s)
        return [sum(coupling[at, i] * values[i] for at, values in enumerate(around)) for i in range(4)]

    found = [[start[i] * inverse[i] for i in range(4)]]
    found.append(spread_out(found[0]))
    for _ in range(2, ITERS + 1):
        ahead = spread_out(found[-1])
        found.append([2.0 * ahead[i] - found[-2][i] for i in range(4)])
    for j in range(ITERS + 1):
        vectors[j] = found[j][0]
    weighted = [diagonal[...] * found[j][0] for j in range(ITERS + 1)]
    sums = [weighted[j] * found[j][0] for j in range(ITERS + 1)]
    sums += [weighted[j] * found[j + 1][0] for j in range(ITERS)]
    row = jnp.zeros((1, COLS), jnp.float32)
    for j, entry in enumerate(sums):
        row = jnp.where(lane[:1, :] == j, jnp.sum(entry, keepdims=True), row)
    partial[...] = jnp.broadcast_to(row, partial.shape)


def combine_kernel(moments, vectors, diagonal, pressure, residual, good):
    size = ITERS + 1
    sums = jnp.sum(moments[...], axis=0, keepdims=True)

    def lane_of(j):
        return jnp.broadcast_to(sums[:, j : j + 1], (ROWS, COLS))

    even = [lane_of(j) for j in range(size)]
    odd = [lane_of(size + j) for j in range(ITERS)]
    mu = []
    for j in range(size):
        mu.append(even[0] if j == 0 else 2.0 * even[j] - even[0])
        if j < ITERS:
            mu.append(odd[0] if j == 0 else 2.0 * odd[j] - odd[0])

    def mass(i, j):
        return 0.5 * (mu[i + j] + mu[abs(i - j)])

    def stiffness(i, j):
        i, j = min(i, j), max(i, j)
        if j == 0:
            return mu[0] - mu[1]
        return mass(i, j) - 0.5 * (mass(i, j + 1) + mass(i, j - 1))

    def form(values, entry):
        out = None
        for i in range(len(values)):
            inner = values[i] * entry(i, i)
            for j in range(i + 1, len(values)):
                inner = inner + 2.0 * values[j] * entry(i, j)
            out = values[i] * inner if out is None else out + values[i] * inner
        return out

    def applied(values):
        out = [value for value in values] + [jnp.zeros_like(values[0])]
        out[1] = out[1] - values[0]
        for j in range(1, len(values)):
            out[j + 1] = out[j + 1] - 0.5 * values[j]
            out[j - 1] = out[j - 1] - 0.5 * values[j]
        return out

    def amplified(values, result):
        total = sum(jnp.abs(value) for value in values)
        return total * total * mu[0] / result

    scaled = [jnp.ones((ROWS, COLS), jnp.float32)]
    direction = list(scaled)
    solution_at = []
    energy = mu[0]
    fine = energy > 0.0
    for step in range(ITERS):
        image = applied(direction)
        curvature = form(direction, stiffness)
        step_size = energy / curvature
        fine = fine & (amplified(direction, curvature) <= SCALAR_BOUND) & (curvature > 0.0)
        solution_at = [
            step_size * value + (solution_at[j] if j < len(solution_at) else 0.0) for j, value in enumerate(direction)
        ]
        scaled = [
            (scaled[j] if j < len(scaled) else 0.0) - step_size * value for j, value in enumerate(image)
        ]
        energy_new = form(scaled, mass)
        bound = SCALAR_BOUND if step + 1 < ITERS else FIELD_BOUND
        fine = fine & (amplified(scaled, energy_new) <= bound) & (energy_new > 0.0)
        if step + 1 < ITERS:
            ratio = energy_new / energy
            direction = [
                scaled[j] + (ratio * direction[j] if j < len(direction) else 0.0) for j in range(len(scaled))
            ]
            energy = energy_new
    pressure[...] = sum(solution_at[j] * vectors[j] for j in range(len(solution_at)))
    residual[...] = diagonal[...] * sum(scaled[j] * vectors[j] for j in range(len(scaled)))
    good[0] = jnp.min(jnp.where(fine, 1, 0).astype(jnp.int32))


def tracers_kernel(
    fold_map, tracer, east_vel, north_vel, diffusion, mixing, count, from_east, from_west, near, far, extra,
    mixed,
    north_rows, south_rows, factors,
):
    lane, sub = lanes(), sublanes()
    levels = count[...]
    group = pl.program_id(0)

    @pl.when(group == 0)
    def _():
        halo_rows(fold_map, near, far, extra, north_rows, south_rows)
        c_prev = jnp.zeros((ROWS, COLS), jnp.float32)
        a_prev = jnp.zeros((ROWS, COLS), jnp.float32)
        for k in range(LEVELS):
            wet = jnp.where(k < levels, 1.0, 0.0)
            u, v, spread = 0.5 * wet * east_vel[k], 0.5 * wet * north_vel[k], wet * diffusion[k]
            a = jnp.where(k + 1 < levels, mixing[k], 0.0)
            inverse = 1.0 / (1.0 + a_prev + a + a_prev * c_prev)
            c_prev = -a * inverse
            factors[0, k] = 1.0 - 4.0 * spread
            factors[1, k] = spread - u
            factors[2, k] = spread + u
            factors[3, k] = spread - v
            factors[4, k] = spread + v
            factors[5, k] = inverse
            factors[6, k] = a_prev
            factors[7, k] = c_prev
            a_prev = a

    row = pl.multiple_of(group * ROWS, ROWS)
    columns_east = from_east[pl.ds(row, ROWS), :]
    columns_west = from_west[pl.ds(row, ROWS), :]
    r_prev = [jnp.zeros((ROWS, COLS), jnp.float32)] * GROUP
    for k in range(LEVELS):
        centre, to_e, to_w, to_n, to_s, inverse, above = (factors[j, k] for j in range(7))
        wet = k < levels
        for t in range(GROUP):
            cell = jnp.where(wet, tracer[t, k], 0.0)
            at = t * LEVELS + k
            halo_row = group * (GROUP * LEVELS) + at
            east = east_of(cell, roll(columns_east, -at, 1), lane)
            west = west_of(cell, roll(columns_west, COLS - 1 - at, 1), lane)
            north = north_of(cell, north_rows[pl.ds(halo_row, 1), :], sub)
            south = south_of(cell, south_rows[pl.ds(halo_row, 1), :], sub)
            explicit = centre * cell + to_e * east + to_w * west + to_n * north + to_s * south
            r_prev[t] = (explicit + above * r_prev[t]) * inverse
            mixed[t, k] = r_prev[t]
    x_next = r_prev
    for k in range(LEVELS - 2, -1, -1):
        below = factors[7, k]
        for t in range(GROUP):
            x_next[t] = mixed[t, k] - below * x_next[t]
            mixed[t, k] = x_next[t]


def extended(cells, sides, width):
    for axis, dim in sides:
        count = lax.axis_size(axis)
        head = lax.slice_in_dim(cells, 0, width, axis=dim)
        tail = lax.slice_in_dim(cells, cells.shape[dim] - width, cells.shape[dim], axis=dim)
        cells = jnp.concatenate(
            [
                lax.ppermute(tail, axis, [(i, (i + 1) % count) for i in range(count)]),
                cells,
                lax.ppermute(head, axis, [((i + 1) % count, i) for i in range(count)]),
            ],
            axis=dim,
        )
    return cells


def extend(field, fold_map):
    rows, cols = field.shape
    padded = extended(field, (("gx", 1), ("gy", 0)), 1)
    total_cols = fold_map.shape[0]
    whole_row = lax.all_gather(field[rows - 1, :], "gx", axis=0, tiled=True)
    start = lax.axis_index("gx") * cols
    wanted = (start - 1 + jnp.arange(cols + 2, dtype=jnp.int32)) % total_cols
    folded = jnp.take(whole_row, jnp.take(fold_map, wanted), axis=0)
    row_index = lax.axis_index("gy")
    upper = jnp.where(row_index == lax.axis_size("gy") - 1, folded, padded[rows + 1, :])
    lower = jnp.where(row_index == 0, 0.0, padded[0, :])
    return jnp.concatenate([lower[None, :], padded[1 : rows + 1, :], upper[None, :]], axis=0)


def window(padded, row_off, col_off):
    rows = padded.shape[0] - 2
    cols = padded.shape[1] - 2
    return padded[1 + row_off : 1 + row_off + rows, 1 + col_off : 1 + col_off + cols]


def total_of(value):
    return lax.psum(jnp.sum(value), BOTH)


def direct_gradients(rhs, level_count, fold_map, surface_term):
    levels = jnp.arange(LEVELS, dtype=jnp.int32)[:, None, None]
    level_mask = (levels < level_count[None]).astype(jnp.float32)
    thick = (0.5 + 1.5 * jnp.arange(LEVELS).astype(jnp.float32) / (LEVELS - 1))[:, None, None]
    depth = jnp.sum(thick * level_mask, axis=0) / LEVELS
    wet_cells = level_count > 0
    depth_pad = extend(depth, fold_map)
    couplings = [
        weight * jnp.minimum(depth, window(depth_pad, row_off, col_off)) for row_off, col_off, weight in NEIGHBOURS
    ]
    diag = jnp.where(wet_cells, surface_term + sum(couplings), 1.0)

    def step(_, state):
        pressure, residual, direction, energy = state
        field_pad = extend(direction, fold_map)
        summed = jnp.zeros_like(direction)
        for entry, (row_off, col_off, _weight) in zip(couplings, NEIGHBOURS):
            summed = summed + entry * window(field_pad, row_off, col_off)
        image = jnp.where(wet_cells, diag * direction - summed, direction)
        step_size = energy / total_of(direction * image)
        pressure = pressure + step_size * direction
        residual = residual - step_size * image
        scaled = residual / diag
        energy_new = total_of(residual * scaled)
        return pressure, residual, scaled + energy_new / energy * direction, energy_new

    scaled = rhs / diag
    state = (jnp.zeros_like(rhs), rhs, scaled, total_of(rhs * scaled))
    state = lax.fori_loop(0, ITERS, step, state)
    return state[0], state[1]


def kernel(body, limit=VMEM_LIMIT, **rest):
    return pl.pallas_call(body, compiler_params=params(limit), **rest)


def shape(*dims):
    return jax.ShapeDtypeStruct(dims, jnp.float32)


def vmem(*dims):
    return pltpu.VMEM(dims, jnp.float32)


def all_of(array):
    return pl.BlockSpec(array.shape, lambda i: (0,) * array.ndim)


def block_of(dims, at=0):
    return pl.BlockSpec(dims, lambda i: (at,) + (0,) * (len(dims) - 1))


def step_at(block, sizes, tracer, fields, count, surface, fold_map, to_west, to_east, near, far, near_rows, far_rows):
    nx, ny = sizes
    smem = pl.BlockSpec(memory_space=pltpu.SMEM)

    def device(x, y):
        return (x % nx) * ny + y

    turns = ((block - 1) % nx, block)
    even, odd = turns if turns[0] % 2 == 0 else turns[::-1]
    pair = [(device(x, y ^ 1), device(x, y)) for x in range(nx) for y in range(ny)]
    inner = [(device(x, y + 1 if y % 2 else y - 1), device(x, y)) for x in range(nx) for y in range(1, ny - 1)]
    across_even, across_odd = (
        [(device(turn - x, ny - 1), device(x, ny - 1)) for x in range(nx)] for turn in (even, odd)
    )

    def exchange(near, far):
        return (
            lax.ppermute(near, BOTH, pair),
            lax.ppermute(far, BOTH, inner + across_even),
            lax.ppermute(far, BOTH, across_odd),
        )

    from_east = lax.ppermute(to_west, BOTH, [(device(x + 1, y), device(x, y)) for x in range(nx) for y in range(ny)])
    from_west = lax.ppermute(to_east, BOTH, [(device(x - 1, y), device(x, y)) for x in range(nx) for y in range(ny)])
    deep = block_of((ROWS, COLS), COL_DEEP // ROWS)
    corner = block_of((ROW_DIFF, COLS))
    near_rows, far_rows = kernel(
        corners_kernel,
        grid=(1,),
        out_shape=(shape(ROW_SIZE, COLS), shape(ROW_SIZE, COLS)),
        in_specs=[deep, deep, pl.BlockSpec(memory_space=pl.ANY), pl.BlockSpec(memory_space=pl.ANY)],
        out_specs=(corner, corner),
        input_output_aliases={2: 0, 3: 1},
        name="put_corners",
    )(from_east, from_west, near_rows, far_rows)
    edges = exchange(near_rows, far_rows)

    columns = block_of((COL_SIZE, COLS))
    own_rows = [block_of((ROW_SIZE, COLS))] * 3
    rhs, rhs_far = kernel(
        right_side_kernel,
        grid=(1,),
        out_shape=(shape(2 * ROWS, COLS), shape(2 * ROWS, COLS)),
        in_specs=[smem, block_of((2, LEVELS, ROWS, COLS))]
        + [all_of(array) for array in (*fields, count)]
        + [columns, columns]
        + own_rows,
        out_specs=(block_of((2 * ROWS, COLS)), block_of((2 * ROWS, COLS))),
        scratch_shapes=[vmem(LEVELS, ROWS, COLS), vmem(LEVELS, ROWS, COLS)],
        name="right_side",
    )(fold_map, tracer, *fields, count, from_east, from_west, *edges)
    rhs_edges = exchange(rhs, rhs_far)
    coupling, inverse, diagonal = kernel(
        couplings_kernel,
        grid=(1,),
        out_shape=(shape(8, 4, ROWS, COLS), shape(4, ROWS, COLS), shape(ROWS, COLS)),
        in_specs=[smem, all_of(count), all_of(surface), deep, deep] + own_rows,
        out_specs=(block_of((8, 4, ROWS, COLS)), block_of((4, ROWS, COLS)), block_of((ROWS, COLS))),
        cost_estimate=pl.CostEstimate(flops=2000000, bytes_accessed=2000000, transcendentals=0),
        name="couplings",
    )(fold_map, count, surface, from_east, from_west, *edges)
    vectors, partial = kernel(
        krylov_kernel,
        out_shape=(shape(ITERS + 1, ROWS, COLS), shape(nx * ny, COLS)),
        in_specs=[smem] + [whole()] * 7,
        out_specs=(whole(), whole()),
        name="krylov",
    )(fold_map, coupling, inverse, diagonal, rhs, *rhs_edges)

    near, far, partial = lax.optimization_barrier((near, far, partial))
    moments = lax.all_to_all(partial, BOTH, 0, 0)
    tracer_edges = exchange(near, far)
    batch = pl.BlockSpec((GROUP, LEVELS, ROWS, COLS), lambda i: (i, 0, 0, 0))
    mixed = kernel(
        tracers_kernel,
        grid=(GROUPS,),
        out_shape=shape(TRACERS, LEVELS, ROWS, COLS),
        in_specs=[smem, batch]
        + [all_of(array) for array in (*fields, count)]
        + [block_of((COL_DEEP, COLS))] * 2
        + [block_of((EDGE, COLS))] * 3,
        out_specs=batch,
        scratch_shapes=[vmem(EDGE, COLS), vmem(EDGE, COLS), vmem(8, LEVELS, ROWS, COLS)],
        name="tracers",
    )(fold_map, tracer, *fields, count, from_east, from_west, *tracer_edges)

    pressure, residual, good = kernel(
        combine_kernel,
        out_shape=(shape(ROWS, COLS), shape(ROWS, COLS), jax.ShapeDtypeStruct((1,), jnp.int32)),
        in_specs=[whole()] * 3,
        out_specs=(whole(), whole(), smem),
        name="combine",
    )(moments, vectors, diagonal)
    return mixed, pressure, residual, rhs[:ROWS], good


def shards(sizes, tracer, east_vel, north_vel, diffusion, mixing, count, fold_map, surface):
    nx, _ = sizes
    hbm = pl.BlockSpec(memory_space=pltpu.HBM)
    fields = (east_vel, north_vel, diffusion, mixing)
    packed = kernel(
        pack_kernel,
        limit=PACK_VMEM_LIMIT,
        out_shape=(
            shape(COL_SIZE, COLS),
            shape(COL_SIZE, COLS),
            shape(EDGE, COLS),
            shape(EDGE, COLS),
            shape(ROW_SIZE, COLS),
            shape(ROW_SIZE, COLS),
        ),
        in_specs=[hbm] * 7,
        out_specs=(whole(),) * 6,
        scratch_shapes=[
            vmem(EDGE * ROWS, COLS),
            vmem(4, LEVELS, ROWS, COLS),
            pltpu.VMEM((ROWS, COLS), jnp.int32),
            vmem(ROWS, COLS),
            pltpu.SemaphoreType.DMA((GROUPS + 6,)),
        ],
        name="pack",
    )(tracer.reshape(EDGE * ROWS, COLS), *fields, count, surface)

    block = pole_of(fold_map) >> (COLS.bit_length() - 1)
    mixed, pressure, residual, rhs, good = lax.switch(
        block, [functools.partial(step_at, at, sizes) for at in range(nx)],
        tracer, fields, count, surface, fold_map, *packed,
    )
    pressure, residual = lax.cond(
        good[0] == 1,
        lambda pressure, residual, rhs, count, surface, fold: (pressure, residual),
        lambda pressure, residual, rhs, count, surface, fold: direct_gradients(rhs, count, fold, surface),
        pressure,
        residual,
        rhs,
        count,
        surface,
        fold_map,
    )
    return mixed, pressure, residual


def solution(mesh):
    in_specs = (
        P(None, None, "gy", "gx"),
        P(None, "gy", "gx"),
        P(None, "gy", "gx"),
        P(None, "gy", "gx"),
        P(None, "gy", "gx"),
        P("gy", "gx"),
        P(),
        P("gy", "gx"),
    )
    out_specs = (P(None, None, "gy", "gx"), P("gy", "gx"), P("gy", "gx"))
    body = functools.partial(shards, (mesh.shape["gx"], mesh.shape["gy"]))
    return jax.shard_map(body, mesh=mesh, in_specs=in_specs, out_specs=out_specs, check_vma=False)
```

```python
import functools

import jax
import jax.numpy as jnp
from jax import lax
from jax.experimental import pallas as pl
from jax.experimental.pallas import tpu as pltpu
from jax.sharding import PartitionSpec as P

ITERS = 4
TRACERS, LEVELS, ROWS, COLS = 16, 20, 8, 128
GROUP = 4
GROUPS = TRACERS // GROUP
EDGE = TRACERS * LEVELS
BOTH = ("gx", "gy")
VMEM_LIMIT = 40 * 1024 * 1024
PACK_VMEM_LIMIT = 63 * 1024 * 1024

COL_DEEP, COL_SIZE = GROUPS * ROWS, (GROUPS + 5) * ROWS
COUNT_LANE, SURFACE_LANE = 100, 105
ROW_EAST, ROW_WEST, ROW_DIFF, ROW_FIELD, ROW_COUNT, ROW_SURFACE, ROW_SIZE = 0, 40, 80, 240, 560, 568, 576

SCALAR_BOUND, FIELD_BOUND = 1500.0, 1.0e5

NEIGHBOURS = [
    (0, 1, 1.0),
    (0, -1, 1.0),
    (1, 0, 1.0),
    (-1, 0, 1.0),
    (1, 1, 0.5),
    (1, -1, 0.5),
    (-1, 1, 0.5),
    (-1, -1, 0.5),
]


def params(limit=VMEM_LIMIT):
    return pltpu.CompilerParams(vmem_limit_bytes=limit)


def whole():
    return pl.BlockSpec(memory_space=pltpu.VMEM)


def lanes():
    return lax.broadcasted_iota(jnp.int32, (ROWS, COLS), 1)


def sublanes():
    return lax.broadcasted_iota(jnp.int32, (ROWS, COLS), 0)


def roll(tile, shift, axis):
    size = tile.shape[axis]
    shift = shift % size
    return tile if shift == 0 else pltpu.roll(tile, shift, axis)


def east_of(tile, beyond, lane):
    return roll(jnp.where(lane == 0, beyond, tile), -1, 1)


def west_of(tile, beyond, lane):
    return roll(jnp.where(lane == COLS - 1, beyond, tile), 1, 1)


def north_of(tile, beyond, sub):
    return roll(jnp.where(sub == 0, beyond, tile), -1, 0)


def south_of(tile, beyond, sub):
    return roll(jnp.where(sub == ROWS - 1, beyond, tile), 1, 0)


def thickness(level):
    return 0.5 + 1.5 * level / (LEVELS - 1)


def turned(tile):
    return jnp.take_along_axis(tile, ROWS - 1 - sublanes(), axis=0)


def pack_kernel(
    tracer, east_vel, north_vel, diffusion, mixing, count, surface,
    to_west, to_east, near, far, near_rows, far_rows,
    cells, fields, levels_ref, surface_ref, ready,
):
    lane = lanes()
    low = sublanes() < ROWS // 2
    size = GROUP * LEVELS * ROWS
    pairs = [(count, levels_ref), (surface, surface_ref)]
    pairs += [(tracer.at[pl.ds(g * size, size)], cells.at[pl.ds(g * size, size)]) for g in range(GROUPS)]
    pairs += [(field, fields.at[f]) for f, field in enumerate((east_vel, north_vel, diffusion, mixing))]
    copies = [pltpu.make_async_copy(source, target, ready.at[i]) for i, (source, target) in enumerate(pairs)]
    for copy in copies:
        copy.start()
    here = lax.axis_index("gy")
    even = here % 2 == 0
    is_top = here == lax.axis_size("gy") - 1

    def put(row, items):
        west = jnp.zeros((ROWS, COLS), jnp.float32)
        east = jnp.zeros((ROWS, COLS), jnp.float32)
        for tile, width, first in items:
            chosen = lane == first if width == 1 else (lane >= first) & (lane < first + width)
            west = jnp.where(chosen, roll(tile, first, 1), west)
            east = jnp.where(chosen, roll(tile, first + width, 1), east)
        to_west[row : row + ROWS, :] = west
        to_east[row : row + ROWS, :] = east

    copies[0].wait()
    copies[1].wait()
    levels, surfaces = levels_ref[...], surface_ref[...]
    depths = levels.astype(jnp.float32)
    per = 2 * LEVELS
    level_row = lax.broadcasted_iota(jnp.int32, (per, COLS), 0)
    level_row = jnp.where(level_row >= LEVELS, level_row - LEVELS, level_row)
    wet_south = level_row < jnp.broadcast_to(levels[:1, :], (per, COLS))
    wet_north = level_row < jnp.broadcast_to(levels[ROWS - 1 :, :], (per, COLS))

    def cell(t, k):
        row = (t * LEVELS + k) * ROWS
        return jnp.where(k < levels, cells[row : row + ROWS, :], 0.0)

    for g in range(GROUPS):
        copies[2 + g].wait()
        put(g * ROWS, [(cell(g * GROUP + t, k), 1, t * LEVELS + k) for t in range(GROUP) for k in range(LEVELS)])
        if g == 0:
            difference = [(cell(0, k) - cell(1, k), 5, 5 * k) for k in range(LEVELS)]
            put(COL_DEEP, difference + [(depths, 5, COUNT_LANE), (surfaces, 4, SURFACE_LANE)])
        for half in range(GROUP * LEVELS // per):
            at = g * GROUP * LEVELS + half * per
            south = jnp.where(wet_south, cells[pl.ds(at * ROWS, per, stride=ROWS), :], 0.0)
            north = jnp.where(wet_north, cells[pl.ds(at * ROWS + ROWS - 1, per, stride=ROWS), :], 0.0)
            near[at : at + per, :] = jnp.where(even, north, south)
            far[at : at + per, :] = jnp.where(even, south, north)
    for f in range(4):
        copies[2 + GROUPS + f].wait()
        put(COL_DEEP + (1 + f) * ROWS, [(fields[f, k], 4, 4 * k) for k in range(LEVELS)])

    def pack(kind, out):
        turn = turned if kind == "fold" else (lambda tile: tile)
        for k in range(LEVELS):
            out[ROW_DIFF + ROWS * k : ROW_DIFF + ROWS * (k + 1), :] = turn(cell(0, k) - cell(1, k))
        for f in range(4):
            for m in range(LEVELS // 2):
                first, second = turn(fields[f, 2 * m]), turn(fields[f, 2 * m + 1])
                if kind == "north":
                    tile = jnp.where(low, roll(first, 4, 0), second)
                else:
                    tile = jnp.where(low, first, roll(second, 4, 0))
                row = ROW_FIELD + ROWS * (f * (LEVELS // 2) + m)
                out[row : row + ROWS, :] = tile
        out[ROW_COUNT : ROW_COUNT + ROWS, :] = turn(depths)
        out[ROW_SURFACE : ROW_SURFACE + ROWS, :] = turn(surfaces)

    @pl.when(even)
    def _():
        pack("north", near_rows)
        pack("south", far_rows)

    @pl.when(jnp.logical_not(even))
    def _():
        pack("south", near_rows)

    @pl.when(jnp.logical_not(even) & jnp.logical_not(is_top))
    def _():
        pack("north", far_rows)

    @pl.when(is_top)
    def _():
        pack("fold", far_rows)


def corners_kernel(east, west, near_in, far_in, near, far):
    del near_in, far_in
    is_top = lax.axis_index("gy") == lax.axis_size("gy") - 1
    for base, ref in ((ROW_EAST, east), (ROW_WEST, west)):
        for row in range(0, ROW_WEST, ROWS):
            value = ref[COL_DEEP + row : COL_DEEP + row + ROWS, :]
            near[base + row : base + row + ROWS, :] = value
            far[base + row : base + row + ROWS, :] = jnp.where(is_top, turned(value), value)


def pole_of(fold_map):
    return (fold_map[0] + 1) & (COLS * lax.axis_size("gx") - 1)


def halo_rows(fold_map, near, far, first, second, north_rows, south_rows):
    here = lax.axis_index("gy")
    top = lax.axis_size("gy") - 1

    @pl.when(here % 2 == 0)
    def _():
        north_rows[...] = near[...]
        south_rows[...] = far[...]

    @pl.when(here % 2 == 1)
    def _():
        south_rows[...] = near[...]

    @pl.when((here % 2 == 1) & (here != top))
    def _():
        north_rows[...] = far[...]

    @pl.when(here == top)
    def _():
        lane = lanes()
        offset = pole_of(fold_map) & (COLS - 1)
        index = (offset - 1 - lane) & (COLS - 1)
        for row in range(0, north_rows.shape[0], ROWS):
            a = jnp.take_along_axis(first[row : row + ROWS, :], index, axis=1)
            b = jnp.take_along_axis(second[row : row + ROWS, :], index, axis=1)
            north_rows[row : row + ROWS, :] = jnp.where(lane >= offset, a, b)


def unfold(offset, first, second, out):
    lane = lanes()
    index = (offset - 1 - lane) & (COLS - 1)
    zero = jnp.zeros((ROWS, COLS), jnp.float32)

    def tile(ref, row):
        return ref[row : row + ROWS, :]

    def flipped(row, sign):
        a = sign * jnp.take_along_axis(tile(first, row), index, axis=1)
        b = sign * jnp.take_along_axis(tile(second, row), index, axis=1)
        out[row : row + ROWS, :] = jnp.where(lane >= offset, a, b)
        return a, b

    def collect(packed, a, b, width, at):
        chosen = (lane >= at) & (lane < at + width)
        return jnp.where(chosen, roll(a, at, 1), packed[0]), jnp.where(chosen, roll(b, at + width, 1), packed[1])

    def finish(row, packed, sign, width, within):
        beside = (lane + (offset - 1) + width - 2 * within) & (COLS - 1)
        right = sign * jnp.take_along_axis(tile(first, ROW_WEST + row), beside, axis=1)
        beside = (lane + (offset - 1 - COLS) + width - 2 * within) & (COLS - 1)
        left = sign * jnp.take_along_axis(tile(second, ROW_EAST + row), beside, axis=1)
        out[ROW_EAST + row : ROW_EAST + row + ROWS, :] = jnp.where(within < offset, packed[0], right)
        out[ROW_WEST + row : ROW_WEST + row + ROWS, :] = jnp.where(within >= offset + width - COLS, packed[1], left)

    packed = (zero, zero)
    for k in range(LEVELS):
        packed = collect(packed, *flipped(ROW_DIFF + ROWS * k, 1.0), 5, 5 * k)
    packed = collect(packed, *flipped(ROW_COUNT, 1.0), 5, COUNT_LANE)
    packed = collect(packed, *flipped(ROW_SURFACE, 1.0), 4, SURFACE_LANE)
    fifth = lane - 5 * ((lane * 205) >> 10)
    finish(0, packed, 1.0, jnp.where(lane >= SURFACE_LANE, 4, 5), fifth)
    for f in range(4):
        sign = -1.0 if f < 2 else 1.0
        packed = (zero, zero)
        for m in range(LEVELS // 2):
            a, b = flipped(ROW_FIELD + ROWS * (f * (LEVELS // 2) + m), sign)
            packed = collect(packed, a, b, 4, 8 * m)
            packed = collect(packed, roll(a, 4, 0), roll(b, 4, 0), 4, 8 * m + 4)
        finish((1 + f) * ROWS, packed, sign, 4, lane & 3)


def unpack(east, west, first, width, lane):
    right = roll(east, -first, 1)
    left = roll(west, -width - first, 1)
    return jnp.where(lane < width, right, jnp.where(lane >= COLS - width, left, 0.0))


def both_east(one, two, lane):
    return east_of(one, two, lane), east_of(two, one, lane)


def both_west(one, two, lane):
    return west_of(one, two, lane), west_of(two, one, lane)


def krylov_kernel(
    fold_map, tracer, east_vel, north_vel, diffusion, mixing, count, surface, from_east, from_west,
    near, far, first_rows, second_rows,
    vectors, diagonal, right_side, partial,
    north_buf, south_buf,
):
    here = lax.axis_index("gy")
    top = lax.axis_size("gy") - 1
    lane, sub = lanes(), sublanes()
    low = sub < 4
    fields = (east_vel, north_vel, diffusion, mixing)

    @pl.when(here % 2 == 0)
    def _():
        north_buf[...] = near[...]
        south_buf[...] = far[...]

    @pl.when(here % 2 == 1)
    def _():
        south_buf[...] = near[...]

    @pl.when((here % 2 == 1) & (here != top))
    def _():
        north_buf[...] = far[...]

    @pl.when(here == top)
    def _():
        unfold(pole_of(fold_map) & (COLS - 1), first_rows, second_rows, north_buf)

    def at(ref, row):
        return ref[row : row + ROWS, :]

    def field_tile(ref, f, k):
        return at(ref, ROW_FIELD + ROWS * (f * (LEVELS // 2) + k // 2))

    def halo_main(f, k):
        north, south = field_tile(north_buf, f, k), field_tile(south_buf, f, k)
        return jnp.where(low, roll(north, 4 * (k % 2), 0), roll(south, 4 * (1 - k % 2), 0))

    def side(ref, f, first, width):
        return unpack(at(ref, ROW_EAST + ROWS * f), at(ref, ROW_WEST + ROWS * f), first, width, lane)

    halo_packed = [
        [
            jnp.where(low, at(north_buf, base + ROWS * (1 + f)), at(south_buf, base + ROWS * (1 + f)))
            for base in (ROW_EAST, ROW_WEST)
        ]
        for f in range(4)
    ]

    def column(f):
        row = COL_DEEP + ROWS * f
        return from_east[row : row + ROWS, :], from_west[row : row + ROWS, :]

    def neighbours_across(own, north, south):
        up, up_n, up_s = roll(own, -1, 0), roll(north, -1, 0), roll(south, -1, 0)
        down, down_n, down_s = roll(own, 1, 0), roll(north, 1, 0), roll(south, 1, 0)
        return (
            jnp.where(sub == 7, up_n, up),
            jnp.where(low, up_n, jnp.where(sub == 7, up, up_s)),
            jnp.where(sub == 0, down_s, down),
            jnp.where(sub == 0, down, jnp.where(low, down_n, down_s)),
        )

    def halo(pair):
        return jnp.where(low, pair[0], pair[1])

    counts_own = (count[...].astype(jnp.float32), unpack(*column(0), COUNT_LANE, 5, lane))
    counts_north = (at(north_buf, ROW_COUNT), side(north_buf, 0, COUNT_LANE, 5))
    counts_south = (at(south_buf, ROW_COUNT), side(south_buf, 0, COUNT_LANE, 5))
    counts = (counts_own[0], counts_own[1], halo((counts_north[0], counts_south[0])), halo((counts_north[1], counts_south[1])))
    surfaces = (
        surface[...],
        unpack(*column(0), SURFACE_LANE, 4, lane),
        halo((at(north_buf, ROW_SURFACE), at(south_buf, ROW_SURFACE))),
        halo((side(north_buf, 0, SURFACE_LANE, 4), side(south_buf, 0, SURFACE_LANE, 4))),
    )

    zero = jnp.zeros((ROWS, COLS), jnp.float32)
    c_prev, r_prev, a_prev = [zero] * 4, [zero] * 4, [zero] * 4
    c_list, r_list = [], []
    for k in range(LEVELS):
        own = (jnp.where(k < counts[0], tracer[0, k] - tracer[1, k], 0.0), unpack(*column(0), 5 * k, 5, lane))
        north = (at(north_buf, ROW_DIFF + ROWS * k), side(north_buf, 0, 5 * k, 5))
        south = (at(south_buf, ROW_DIFF + ROWS * k), side(south_buf, 0, 5 * k, 5))
        halos = (halo((north[0], south[0])), halo((north[1], south[1])))
        centre = (own[0], own[1], halos[0], halos[1])
        easts = both_east(*own, lane) + both_east(*halos, lane)
        wests = both_west(*own, lane) + both_west(*halos, lane)
        first = neighbours_across(own[0], north[0], south[0])
        second = neighbours_across(own[1], north[1], south[1])
        norths = (first[0], second[0], first[1], second[1])
        souths = (first[2], second[2], first[3], second[3])
        values = [
            (field[k], unpack(*column(1 + f), 4 * k, 4, lane), halo_main(f, k), unpack(*halo_packed[f], 4 * k, 4, lane))
            for f, field in enumerate(fields)
        ]
        c_now, r_now, a_now = [], [], []
        for i in range(4):
            u, v, spread, mix = (value[i] for value in values)
            change = (
                -0.5 * u * (easts[i] - wests[i])
                - 0.5 * v * (norths[i] - souths[i])
                + spread * (easts[i] + wests[i] + norths[i] + souths[i] - 4.0 * centre[i])
            )
            explicit = centre[i] + jnp.where(k < counts[i], change, 0.0)
            a = jnp.where(k + 1 < counts[i], mix, 0.0)
            inverse = 1.0 / (1.0 + a_prev[i] + a + a_prev[i] * c_prev[i])
            c_now.append(-a * inverse)
            r_now.append((explicit + a_prev[i] * r_prev[i]) * inverse)
            a_now.append(a)
        c_prev, r_prev, a_prev = c_now, r_now, a_now
        c_list.append(c_now)
        r_list.append(r_now)
    total, x_next = [zero] * 4, [zero] * 4
    for k in range(LEVELS - 1, -1, -1):
        x_next = [r_list[k][i] - c_list[k][i] * x_next[i] for i in range(4)]
        total = [total[i] + thickness(k) * x_next[i] for i in range(4)]
    rhs = [jnp.where(counts[i] > 0, 0.25 * total[i], 0.0) for i in range(4)]

    def depth_of(levels):
        depth = zero
        for k in range(LEVELS):
            depth = depth + jnp.where(k < levels, thickness(k), 0.0)
        return depth / LEVELS

    own = tuple(depth_of(levels) for levels in counts_own)
    north = tuple(depth_of(levels) for levels in counts_north)
    south = tuple(depth_of(levels) for levels in counts_south)
    depths = (own[0], own[1], halo((north[0], south[0])), halo((north[1], south[1])))

    def rows_of(own, north, south):
        first = neighbours_across(own[0], north[0], south[0])
        second = neighbours_across(own[1], north[1], south[1])
        return (first[0], second[0], first[1], second[1]), (first[2], second[2], first[3], second[3])

    def coupled(others, weight):
        return [weight * jnp.minimum(depths[i], others[i]) for i in range(4)]

    own_e, north_e, south_e = (both_east(*pair, lane) for pair in (own, north, south))
    own_w, north_w, south_w = (both_west(*pair, lane) for pair in (own, north, south))
    halo_e = (halo((north_e[0], south_e[0])), halo((north_e[1], south_e[1])))
    halo_w = (halo((north_w[0], south_w[0])), halo((north_w[1], south_w[1])))
    mid = rows_of(own, north, south)
    mid_e = rows_of(own_e, north_e, south_e)
    mid_w = rows_of(own_w, north_w, south_w)
    couplings = [
        coupled(own_e + halo_e, 1.0),
        coupled(own_w + halo_w, 1.0),
        coupled(mid[0], 1.0),
        coupled(mid[1], 1.0),
        coupled(mid_e[0], 0.5),
        coupled(mid_w[0], 0.5),
        coupled(mid_e[1], 0.5),
        coupled(mid_w[1], 0.5),
    ]
    diag = [
        jnp.where(counts[i] > 0, surfaces[i] + sum(entry[i] for entry in couplings), 1.0) for i in range(4)
    ]
    inverse = [1.0 / diag[i] for i in range(4)]
    couplings = [[entry[i] * inverse[i] for i in range(4)] for entry in couplings]

    def shifted_rows(tiles):
        north, south = [None] * 4, [None] * 4
        for i in range(2):
            a, b = roll(tiles[i], -1, 0), roll(tiles[i + 2], -1, 0)
            north[i], north[i + 2] = jnp.where(sub == 7, b, a), jnp.where(sub == 7, a, b)
            a, b = roll(tiles[i], 1, 0), roll(tiles[i + 2], 1, 0)
            south[i], south[i + 2] = jnp.where(sub == 0, b, a), jnp.where(sub == 0, a, b)
        return north, south

    def spread_out(tiles):
        east = both_east(tiles[0], tiles[1], lane) + both_east(tiles[2], tiles[3], lane)
        west = both_west(tiles[0], tiles[1], lane) + both_west(tiles[2], tiles[3], lane)
        mid_n, mid_s = shifted_rows(tiles)
        east_n, east_s = shifted_rows(east)
        west_n, west_s = shifted_rows(west)
        around = (east, west, mid_n, mid_s, east_n, west_n, east_s, west_s)
        return [sum(entry[i] * values[i] for entry, values in zip(couplings, around)) for i in range(4)]

    found = [[rhs[i] * inverse[i] for i in range(4)]]
    found.append(spread_out(found[0]))
    for _ in range(2, ITERS + 1):
        ahead = spread_out(found[-1])
        found.append([2.0 * ahead[i] - found[-2][i] for i in range(4)])
    for j in range(ITERS + 1):
        vectors[j] = found[j][0]
    diagonal[...] = diag[0]
    right_side[...] = rhs[0]
    weighted = [diag[0] * found[j][0] for j in range(ITERS + 1)]
    sums = [weighted[j] * found[j][0] for j in range(ITERS + 1)]
    sums += [weighted[j] * found[j + 1][0] for j in range(ITERS)]
    row = jnp.zeros((1, COLS), jnp.float32)
    for j, entry in enumerate(sums):
        row = jnp.where(lane[:1, :] == j, jnp.sum(entry, keepdims=True), row)
    partial[...] = jnp.broadcast_to(row, partial.shape)


def combine_kernel(moments, vectors, diagonal, pressure, residual, good):
    size = ITERS + 1
    sums = jnp.sum(moments[...], axis=0, keepdims=True)

    def lane_of(j):
        return jnp.broadcast_to(sums[:, j : j + 1], (ROWS, COLS))

    even = [lane_of(j) for j in range(size)]
    odd = [lane_of(size + j) for j in range(ITERS)]
    mu = []
    for j in range(size):
        mu.append(even[0] if j == 0 else 2.0 * even[j] - even[0])
        if j < ITERS:
            mu.append(odd[0] if j == 0 else 2.0 * odd[j] - odd[0])

    def mass(i, j):
        return 0.5 * (mu[i + j] + mu[abs(i - j)])

    def stiffness(i, j):
        i, j = min(i, j), max(i, j)
        if j == 0:
            return mu[0] - mu[1]
        return mass(i, j) - 0.5 * (mass(i, j + 1) + mass(i, j - 1))

    def form(values, entry):
        out = None
        for i in range(len(values)):
            inner = values[i] * entry(i, i)
            for j in range(i + 1, len(values)):
                inner = inner + 2.0 * values[j] * entry(i, j)
            out = values[i] * inner if out is None else out + values[i] * inner
        return out

    def applied(values):
        out = [value for value in values] + [jnp.zeros_like(values[0])]
        out[1] = out[1] - values[0]
        for j in range(1, len(values)):
            out[j + 1] = out[j + 1] - 0.5 * values[j]
            out[j - 1] = out[j - 1] - 0.5 * values[j]
        return out

    def amplified(values, result):
        total = sum(jnp.abs(value) for value in values)
        return total * total * mu[0] / result

    scaled = [jnp.ones((ROWS, COLS), jnp.float32)]
    direction = list(scaled)
    solution_at = []
    energy = mu[0]
    fine = energy > 0.0
    for step in range(ITERS):
        image = applied(direction)
        curvature = form(direction, stiffness)
        step_size = energy / curvature
        fine = fine & (amplified(direction, curvature) <= SCALAR_BOUND) & (curvature > 0.0)
        solution_at = [
            step_size * value + (solution_at[j] if j < len(solution_at) else 0.0) for j, value in enumerate(direction)
        ]
        scaled = [
            (scaled[j] if j < len(scaled) else 0.0) - step_size * value for j, value in enumerate(image)
        ]
        energy_new = form(scaled, mass)
        bound = SCALAR_BOUND if step + 1 < ITERS else FIELD_BOUND
        fine = fine & (amplified(scaled, energy_new) <= bound) & (energy_new > 0.0)
        if step + 1 < ITERS:
            ratio = energy_new / energy
            direction = [
                scaled[j] + (ratio * direction[j] if j < len(direction) else 0.0) for j in range(len(scaled))
            ]
            energy = energy_new
    pressure[...] = sum(solution_at[j] * vectors[j] for j in range(len(solution_at)))
    residual[...] = diagonal[...] * sum(scaled[j] * vectors[j] for j in range(len(scaled)))
    good[0] = jnp.min(jnp.where(fine, 1, 0).astype(jnp.int32))


def tracers_kernel(
    fold_map, tracer, east_vel, north_vel, diffusion, mixing, count, from_east, from_west, near, far, first, second,
    mixed,
    north_rows, south_rows, factors,
):
    lane, sub = lanes(), sublanes()
    levels = count[...]
    group = pl.program_id(0)

    @pl.when(group == 0)
    def _():
        halo_rows(fold_map, near, far, first, second, north_rows, south_rows)
        c_prev = jnp.zeros((ROWS, COLS), jnp.float32)
        a_prev = jnp.zeros((ROWS, COLS), jnp.float32)
        for k in range(LEVELS):
            wet = jnp.where(k < levels, 1.0, 0.0)
            u, v, spread = 0.5 * wet * east_vel[k], 0.5 * wet * north_vel[k], wet * diffusion[k]
            a = jnp.where(k + 1 < levels, mixing[k], 0.0)
            inverse = 1.0 / (1.0 + a_prev + a + a_prev * c_prev)
            c_prev = -a * inverse
            factors[0, k] = 1.0 - 4.0 * spread
            factors[1, k] = spread - u
            factors[2, k] = spread + u
            factors[3, k] = spread - v
            factors[4, k] = spread + v
            factors[5, k] = inverse
            factors[6, k] = a_prev
            factors[7, k] = c_prev
            a_prev = a

    row = pl.multiple_of(group * ROWS, ROWS)
    columns_east = from_east[pl.ds(row, ROWS), :]
    columns_west = from_west[pl.ds(row, ROWS), :]
    r_prev = [jnp.zeros((ROWS, COLS), jnp.float32)] * GROUP
    for k in range(LEVELS):
        centre, to_e, to_w, to_n, to_s, inverse, above = (factors[j, k] for j in range(7))
        wet = k < levels
        for t in range(GROUP):
            cell = jnp.where(wet, tracer[t, k], 0.0)
            at = t * LEVELS + k
            halo_row = group * (GROUP * LEVELS) + at
            east = east_of(cell, roll(columns_east, -at, 1), lane)
            west = west_of(cell, roll(columns_west, COLS - 1 - at, 1), lane)
            north = north_of(cell, north_rows[pl.ds(halo_row, 1), :], sub)
            south = south_of(cell, south_rows[pl.ds(halo_row, 1), :], sub)
            explicit = centre * cell + to_e * east + to_w * west + to_n * north + to_s * south
            r_prev[t] = (explicit + above * r_prev[t]) * inverse
            mixed[t, k] = r_prev[t]
    x_next = r_prev
    for k in range(LEVELS - 2, -1, -1):
        below = factors[7, k]
        for t in range(GROUP):
            x_next[t] = mixed[t, k] - below * x_next[t]
            mixed[t, k] = x_next[t]


def extended(cells, sides, width):
    for axis, dim in sides:
        count = lax.axis_size(axis)
        head = lax.slice_in_dim(cells, 0, width, axis=dim)
        tail = lax.slice_in_dim(cells, cells.shape[dim] - width, cells.shape[dim], axis=dim)
        cells = jnp.concatenate(
            [
                lax.ppermute(tail, axis, [(i, (i + 1) % count) for i in range(count)]),
                cells,
                lax.ppermute(head, axis, [((i + 1) % count, i) for i in range(count)]),
            ],
            axis=dim,
        )
    return cells


def extend(field, fold_map):
    rows, cols = field.shape
    padded = extended(field, (("gx", 1), ("gy", 0)), 1)
    total_cols = fold_map.shape[0]
    whole_row = lax.all_gather(field[rows - 1, :], "gx", axis=0, tiled=True)
    start = lax.axis_index("gx") * cols
    wanted = (start - 1 + jnp.arange(cols + 2, dtype=jnp.int32)) % total_cols
    folded = jnp.take(whole_row, jnp.take(fold_map, wanted), axis=0)
    row_index = lax.axis_index("gy")
    upper = jnp.where(row_index == lax.axis_size("gy") - 1, folded, padded[rows + 1, :])
    lower = jnp.where(row_index == 0, 0.0, padded[0, :])
    return jnp.concatenate([lower[None, :], padded[1 : rows + 1, :], upper[None, :]], axis=0)


def window(padded, row_off, col_off):
    rows = padded.shape[0] - 2
    cols = padded.shape[1] - 2
    return padded[1 + row_off : 1 + row_off + rows, 1 + col_off : 1 + col_off + cols]


def total_of(value):
    return lax.psum(jnp.sum(value), BOTH)


def direct_gradients(rhs, level_count, fold_map, surface_term):
    levels = jnp.arange(LEVELS, dtype=jnp.int32)[:, None, None]
    level_mask = (levels < level_count[None]).astype(jnp.float32)
    thick = (0.5 + 1.5 * jnp.arange(LEVELS).astype(jnp.float32) / (LEVELS - 1))[:, None, None]
    depth = jnp.sum(thick * level_mask, axis=0) / LEVELS
    wet_cells = level_count > 0
    depth_pad = extend(depth, fold_map)
    couplings = [
        weight * jnp.minimum(depth, window(depth_pad, row_off, col_off)) for row_off, col_off, weight in NEIGHBOURS
    ]
    diag = jnp.where(wet_cells, surface_term + sum(couplings), 1.0)

    def step(_, state):
        pressure, residual, direction, energy = state
        field_pad = extend(direction, fold_map)
        summed = jnp.zeros_like(direction)
        for entry, (row_off, col_off, _weight) in zip(couplings, NEIGHBOURS):
            summed = summed + entry * window(field_pad, row_off, col_off)
        image = jnp.where(wet_cells, diag * direction - summed, direction)
        step_size = energy / total_of(direction * image)
        pressure = pressure + step_size * direction
        residual = residual - step_size * image
        scaled = residual / diag
        energy_new = total_of(residual * scaled)
        return pressure, residual, scaled + energy_new / energy * direction, energy_new

    scaled = rhs / diag
    state = (jnp.zeros_like(rhs), rhs, scaled, total_of(rhs * scaled))
    state = lax.fori_loop(0, ITERS, step, state)
    return state[0], state[1]


def kernel(body, limit=VMEM_LIMIT, **rest):
    return pl.pallas_call(body, compiler_params=params(limit), **rest)


def shape(*dims):
    return jax.ShapeDtypeStruct(dims, jnp.float32)


def vmem(*dims):
    return pltpu.VMEM(dims, jnp.float32)


def block_of(dims, at=0):
    return pl.BlockSpec(dims, lambda i: (at,) + (0,) * (len(dims) - 1))


def all_of(array):
    return block_of(array.shape)


def shards(sizes, tracer, east_vel, north_vel, diffusion, mixing, count, fold_map, surface):
    nx, ny = sizes
    hbm = pl.BlockSpec(memory_space=pltpu.HBM)
    smem = pl.BlockSpec(memory_space=pltpu.SMEM)
    fields = (east_vel, north_vel, diffusion, mixing)

    def device(x, y):
        return (x % nx) * ny + y

    to_west, to_east, near_edge, far_edge, near, far = kernel(
        pack_kernel,
        limit=PACK_VMEM_LIMIT,
        out_shape=(
            shape(COL_SIZE, COLS),
            shape(COL_SIZE, COLS),
            shape(EDGE, COLS),
            shape(EDGE, COLS),
            shape(ROW_SIZE, COLS),
            shape(ROW_SIZE, COLS),
        ),
        in_specs=[hbm] * 7,
        out_specs=(whole(),) * 6,
        scratch_shapes=[
            vmem(EDGE * ROWS, COLS),
            vmem(4, LEVELS, ROWS, COLS),
            pltpu.VMEM((ROWS, COLS), jnp.int32),
            vmem(ROWS, COLS),
            pltpu.SemaphoreType.DMA((GROUPS + 6,)),
        ],
        name="pack",
    )(tracer.reshape(EDGE * ROWS, COLS), *fields, count, surface)

    pairs = [(device(x, y ^ 1), device(x, y)) for x in range(nx) for y in range(ny)]
    inner = [(device(x, y + 1 if y % 2 else y - 1), device(x, y)) for x in range(nx) for y in range(1, ny - 1)]
    block = pole_of(fold_map) >> (COLS.bit_length() - 1)

    def across(turn, rows):
        return lax.ppermute(rows, BOTH, [(device(turn - x, ny - 1), device(x, ny - 1)) for x in range(nx)])

    def over_fold(rows):
        return lax.switch(block, [lambda rows, at=at: (across(at - 1, rows), across(at, rows)) for at in range(nx)], rows)

    from_east = lax.ppermute(to_west, BOTH, [(device(x + 1, y), device(x, y)) for x in range(nx) for y in range(ny)])
    from_west = lax.ppermute(to_east, BOTH, [(device(x - 1, y), device(x, y)) for x in range(nx) for y in range(ny)])
    fold_edges = over_fold(far_edge)
    near_edge, far_edge = lax.ppermute(near_edge, BOTH, pairs), lax.ppermute(far_edge, BOTH, inner)

    columns = block_of((COL_SIZE, COLS))
    corner = block_of((ROW_DIFF, COLS))
    near, far = kernel(
        corners_kernel,
        grid=(1,),
        out_shape=(shape(ROW_SIZE, COLS), shape(ROW_SIZE, COLS)),
        in_specs=[columns, columns, pl.BlockSpec(memory_space=pl.ANY), pl.BlockSpec(memory_space=pl.ANY)],
        out_specs=(corner, corner),
        input_output_aliases={2: 0, 3: 1},
        name="put_corners",
    )(from_east, from_west, near, far)
    from_near, from_far = lax.ppermute(near, BOTH, pairs), lax.ppermute(far, BOTH, inner)
    fold_rows = over_fold(far)

    rest = (*fields, count, surface, from_east, from_west, from_near, from_far, *fold_rows)
    vectors, diagonal, rhs, partial = kernel(
        krylov_kernel,
        grid=(1,),
        out_shape=(shape(ITERS + 1, ROWS, COLS), shape(ROWS, COLS), shape(ROWS, COLS), shape(nx * ny, COLS)),
        in_specs=[smem, block_of((2, LEVELS, ROWS, COLS))] + [all_of(array) for array in rest],
        out_specs=(
            block_of((ITERS + 1, ROWS, COLS)),
            block_of((ROWS, COLS)),
            block_of((ROWS, COLS)),
            block_of((nx * ny, COLS)),
        ),
        scratch_shapes=[vmem(ROW_SIZE, COLS), vmem(ROW_SIZE, COLS)],
        name="krylov",
    )(fold_map, tracer, *rest)

    moments = lax.all_to_all(partial, BOTH, 0, 0)

    batch = pl.BlockSpec((GROUP, LEVELS, ROWS, COLS), lambda i: (i, 0, 0, 0))
    mixed = kernel(
        tracers_kernel,
        grid=(GROUPS,),
        out_shape=shape(TRACERS, LEVELS, ROWS, COLS),
        in_specs=[smem, batch]
        + [all_of(array) for array in (*fields, count)]
        + [block_of((COL_DEEP, COLS))] * 2
        + [block_of((EDGE, COLS))] * 4,
        out_specs=batch,
        scratch_shapes=[vmem(EDGE, COLS), vmem(EDGE, COLS), vmem(8, LEVELS, ROWS, COLS)],
        name="tracers",
    )(fold_map, tracer, *fields, count, from_east, from_west, near_edge, far_edge, *fold_edges)

    pressure, residual, good = kernel(
        combine_kernel,
        out_shape=(shape(ROWS, COLS), shape(ROWS, COLS), jax.ShapeDtypeStruct((1,), jnp.int32)),
        in_specs=[whole()] * 3,
        out_specs=(whole(), whole(), smem),
        name="combine",
    )(moments, vectors, diagonal)
    pressure, residual = lax.cond(
        good[0] == 1,
        lambda pressure, residual, rhs, count, surface, fold: (pressure, residual),
        lambda pressure, residual, rhs, count, surface, fold: direct_gradients(rhs, count, fold, surface),
        pressure,
        residual,
        rhs,
        count,
        surface,
        fold_map,
    )
    return mixed, pressure, residual


def solution(mesh):
    in_specs = (
        P(None, None, "gy", "gx"),
        P(None, "gy", "gx"),
        P(None, "gy", "gx"),
        P(None, "gy", "gx"),
        P(None, "gy", "gx"),
        P("gy", "gx"),
        P(),
        P("gy", "gx"),
    )
    out_specs = (P(None, None, "gy", "gx"), P("gy", "gx"), P("gy", "gx"))
    body = functools.partial(shards, (mesh.shape["gx"], mesh.shape["gy"]))
    return jax.shard_map(body, mesh=mesh, in_specs=in_specs, out_specs=out_specs, check_vma=False)
```

```python
import functools

import jax
import jax.numpy as jnp
from jax import lax
from jax.experimental import pallas as pl
from jax.experimental.pallas import tpu as pltpu
from jax.sharding import PartitionSpec as P

ITERS = 4
TRACERS, LEVELS, ROWS, COLS = 16, 20, 8, 128
GROUP = 4
GROUPS = TRACERS // GROUP
EDGE = TRACERS * LEVELS
BOTH = ("gx", "gy")
VMEM_LIMIT = 40 * 1024 * 1024
PACK_VMEM_LIMIT = 63 * 1024 * 1024

COL_DEEP, COL_SIZE = GROUPS * ROWS, (GROUPS + 5) * ROWS
COUNT_LANE, SURFACE_LANE = 100, 105
ROW_EAST, ROW_WEST, ROW_DIFF, ROW_FIELD, ROW_COUNT, ROW_SURFACE, ROW_SIZE = 0, 40, 80, 240, 560, 568, 576

SCALAR_BOUND, FIELD_BOUND = 1500.0, 1.0e5

NEIGHBOURS = [
    (0, 1, 1.0),
    (0, -1, 1.0),
    (1, 0, 1.0),
    (-1, 0, 1.0),
    (1, 1, 0.5),
    (1, -1, 0.5),
    (-1, 1, 0.5),
    (-1, -1, 0.5),
]


def params(limit=VMEM_LIMIT):
    return pltpu.CompilerParams(vmem_limit_bytes=limit)


def whole():
    return pl.BlockSpec(memory_space=pltpu.VMEM)


def lanes():
    return lax.broadcasted_iota(jnp.int32, (ROWS, COLS), 1)


def sublanes():
    return lax.broadcasted_iota(jnp.int32, (ROWS, COLS), 0)


def roll(tile, shift, axis):
    size = tile.shape[axis]
    shift = shift % size
    return tile if shift == 0 else pltpu.roll(tile, shift, axis)


def east_of(tile, beyond, lane):
    return roll(jnp.where(lane == 0, beyond, tile), -1, 1)


def west_of(tile, beyond, lane):
    return roll(jnp.where(lane == COLS - 1, beyond, tile), 1, 1)


def north_of(tile, beyond, sub):
    return roll(jnp.where(sub == 0, beyond, tile), -1, 0)


def south_of(tile, beyond, sub):
    return roll(jnp.where(sub == ROWS - 1, beyond, tile), 1, 0)


def thickness(level):
    return 0.5 + 1.5 * level / (LEVELS - 1)


def turned(tile):
    return jnp.take_along_axis(tile, ROWS - 1 - sublanes(), axis=0)


def start_copies(pairs, ready):
    copies = [pltpu.make_async_copy(source, target, ready.at[i]) for i, (source, target) in enumerate(pairs)]
    for copy in copies:
        copy.start()
    return copies


def columns_kernel(
    tracer, east_vel, north_vel, diffusion, mixing, count, surface,
    to_west, to_east,
    cells, fields, levels_ref, surface_ref, ready,
):
    lane = lanes()
    size = GROUP * LEVELS * ROWS
    pairs = [(count, levels_ref), (surface, surface_ref)]
    pairs += [(tracer.at[pl.ds(g * size, size)], cells.at[pl.ds(g * size, size)]) for g in range(GROUPS)]
    pairs += [(field, fields.at[f]) for f, field in enumerate((east_vel, north_vel, diffusion, mixing))]
    copies = start_copies(pairs, ready)

    def put(row, items):
        west = jnp.zeros((ROWS, COLS), jnp.float32)
        east = jnp.zeros((ROWS, COLS), jnp.float32)
        for tile, width, first in items:
            chosen = lane == first if width == 1 else (lane >= first) & (lane < first + width)
            west = jnp.where(chosen, roll(tile, first, 1), west)
            east = jnp.where(chosen, roll(tile, first + width, 1), east)
        to_west[row : row + ROWS, :] = west
        to_east[row : row + ROWS, :] = east

    copies[0].wait()
    copies[1].wait()
    levels, surfaces = levels_ref[...], surface_ref[...]

    def cell(t, k):
        row = (t * LEVELS + k) * ROWS
        return jnp.where(k < levels, cells[row : row + ROWS, :], 0.0)

    for g in range(GROUPS):
        copies[2 + g].wait()
        put(g * ROWS, [(cell(g * GROUP + t, k), 1, t * LEVELS + k) for t in range(GROUP) for k in range(LEVELS)])
        if g == 0:
            difference = [(cell(0, k) - cell(1, k), 5, 5 * k) for k in range(LEVELS)]
            put(COL_DEEP, difference + [(levels.astype(jnp.float32), 5, COUNT_LANE), (surfaces, 4, SURFACE_LANE)])
    for f in range(4):
        copies[2 + GROUPS + f].wait()
        put(COL_DEEP + (1 + f) * ROWS, [(fields[f, k], 4, 4 * k) for k in range(LEVELS)])


def rows_kernel(
    fold_map, tracer, east_vel, north_vel, diffusion, mixing, count, surface,
    near, far, near_rows, far_rows, difference, block,
    cells, fields, levels_ref, surface_ref, ready,
):
    low = sublanes() < ROWS // 2
    pairs = [(count, levels_ref), (surface, surface_ref), (tracer, cells)]
    pairs += [(field, fields.at[f]) for f, field in enumerate((east_vel, north_vel, diffusion, mixing))]
    copies = start_copies(pairs, ready)
    here = lax.axis_index("gy")
    even = here % 2 == 0
    is_top = here == lax.axis_size("gy") - 1
    block[0] = pole_of(fold_map) >> (COLS.bit_length() - 1)
    copies[0].wait()
    copies[1].wait()
    levels, surfaces = levels_ref[...], surface_ref[...]
    depths = levels.astype(jnp.float32)
    per = 2 * LEVELS
    level_row = lax.broadcasted_iota(jnp.int32, (per, COLS), 0)
    level_row = jnp.where(level_row >= LEVELS, level_row - LEVELS, level_row)
    wet_south = level_row < jnp.broadcast_to(levels[:1, :], (per, COLS))
    wet_north = level_row < jnp.broadcast_to(levels[ROWS - 1 :, :], (per, COLS))
    copies[2].wait()
    for at in range(0, EDGE, per):
        south = jnp.where(wet_south, cells[pl.ds(at * ROWS, per, stride=ROWS), :], 0.0)
        north = jnp.where(wet_north, cells[pl.ds(at * ROWS + ROWS - 1, per, stride=ROWS), :], 0.0)
        near[at : at + per, :] = jnp.where(even, north, south)
        far[at : at + per, :] = jnp.where(even, south, north)
    for k in range(LEVELS):
        one, two = ROWS * k, ROWS * (LEVELS + k)
        difference[k] = jnp.where(k < levels, cells[one : one + ROWS, :] - cells[two : two + ROWS, :], 0.0)
    for copy in copies[3:]:
        copy.wait()

    def pack(kind, out):
        turn = turned if kind == "fold" else (lambda tile: tile)
        for k in range(LEVELS):
            out[ROW_DIFF + ROWS * k : ROW_DIFF + ROWS * (k + 1), :] = turn(difference[k])
        for f in range(4):
            for m in range(LEVELS // 2):
                first, second = turn(fields[f, 2 * m]), turn(fields[f, 2 * m + 1])
                if kind == "north":
                    tile = jnp.where(low, roll(first, 4, 0), second)
                else:
                    tile = jnp.where(low, first, roll(second, 4, 0))
                row = ROW_FIELD + ROWS * (f * (LEVELS // 2) + m)
                out[row : row + ROWS, :] = tile
        out[ROW_COUNT : ROW_COUNT + ROWS, :] = turn(depths)
        out[ROW_SURFACE : ROW_SURFACE + ROWS, :] = turn(surfaces)

    @pl.when(even)
    def _():
        pack("north", near_rows)
        pack("south", far_rows)

    @pl.when(jnp.logical_not(even))
    def _():
        pack("south", near_rows)

    @pl.when(jnp.logical_not(even) & jnp.logical_not(is_top))
    def _():
        pack("north", far_rows)

    @pl.when(is_top)
    def _():
        pack("fold", far_rows)


def corners_kernel(east, west, near_in, far_in, near_edge, far_edge, near, far):
    del near_in, far_in, near_edge, far_edge
    is_top = lax.axis_index("gy") == lax.axis_size("gy") - 1
    for base, ref in ((ROW_EAST, east), (ROW_WEST, west)):
        for row in range(0, ROW_WEST, ROWS):
            value = ref[COL_DEEP + row : COL_DEEP + row + ROWS, :]
            near[base + row : base + row + ROWS, :] = value
            far[base + row : base + row + ROWS, :] = jnp.where(is_top, turned(value), value)


def pole_of(fold_map):
    return (fold_map[0] + 1) & (COLS * lax.axis_size("gx") - 1)


def halo_rows(fold_map, near, far, first, second, north_rows, south_rows):
    here = lax.axis_index("gy")
    top = lax.axis_size("gy") - 1

    @pl.when(here % 2 == 0)
    def _():
        north_rows[...] = near[...]
        south_rows[...] = far[...]

    @pl.when(here % 2 == 1)
    def _():
        south_rows[...] = near[...]

    @pl.when((here % 2 == 1) & (here != top))
    def _():
        north_rows[...] = far[...]

    @pl.when(here == top)
    def _():
        lane = lanes()
        offset = pole_of(fold_map) & (COLS - 1)
        index = (offset - 1 - lane) & (COLS - 1)
        for row in range(0, north_rows.shape[0], ROWS):
            a = jnp.take_along_axis(first[row : row + ROWS, :], index, axis=1)
            b = jnp.take_along_axis(second[row : row + ROWS, :], index, axis=1)
            north_rows[row : row + ROWS, :] = jnp.where(lane >= offset, a, b)


def unfold(offset, first, second, out):
    lane = lanes()
    index = (offset - 1 - lane) & (COLS - 1)
    zero = jnp.zeros((ROWS, COLS), jnp.float32)

    def tile(ref, row):
        return ref[row : row + ROWS, :]

    def flipped(row, sign):
        a = sign * jnp.take_along_axis(tile(first, row), index, axis=1)
        b = sign * jnp.take_along_axis(tile(second, row), index, axis=1)
        out[row : row + ROWS, :] = jnp.where(lane >= offset, a, b)
        return a, b

    def collect(packed, a, b, width, at):
        chosen = (lane >= at) & (lane < at + width)
        return jnp.where(chosen, roll(a, at, 1), packed[0]), jnp.where(chosen, roll(b, at + width, 1), packed[1])

    def finish(row, packed, sign, width, within):
        beside = (lane + (offset - 1) + width - 2 * within) & (COLS - 1)
        right = sign * jnp.take_along_axis(tile(first, ROW_WEST + row), beside, axis=1)
        beside = (lane + (offset - 1 - COLS) + width - 2 * within) & (COLS - 1)
        left = sign * jnp.take_along_axis(tile(second, ROW_EAST + row), beside, axis=1)
        out[ROW_EAST + row : ROW_EAST + row + ROWS, :] = jnp.where(within < offset, packed[0], right)
        out[ROW_WEST + row : ROW_WEST + row + ROWS, :] = jnp.where(within >= offset + width - COLS, packed[1], left)

    packed = (zero, zero)
    for k in range(LEVELS):
        packed = collect(packed, *flipped(ROW_DIFF + ROWS * k, 1.0), 5, 5 * k)
    packed = collect(packed, *flipped(ROW_COUNT, 1.0), 5, COUNT_LANE)
    packed = collect(packed, *flipped(ROW_SURFACE, 1.0), 4, SURFACE_LANE)
    fifth = lane - 5 * ((lane * 205) >> 10)
    finish(0, packed, 1.0, jnp.where(lane >= SURFACE_LANE, 4, 5), fifth)
    for f in range(4):
        sign = -1.0 if f < 2 else 1.0
        packed = (zero, zero)
        for m in range(LEVELS // 2):
            a, b = flipped(ROW_FIELD + ROWS * (f * (LEVELS // 2) + m), sign)
            packed = collect(packed, a, b, 4, 8 * m)
            packed = collect(packed, roll(a, 4, 0), roll(b, 4, 0), 4, 8 * m + 4)
        finish((1 + f) * ROWS, packed, sign, 4, lane & 3)


def unpack(east, west, first, width, lane):
    right = roll(east, -first, 1)
    left = roll(west, -width - first, 1)
    return jnp.where(lane < width, right, jnp.where(lane >= COLS - width, left, 0.0))


def both_east(one, two, lane):
    return east_of(one, two, lane), east_of(two, one, lane)


def both_west(one, two, lane):
    return west_of(one, two, lane), west_of(two, one, lane)


def krylov_kernel(
    fold_map, difference, east_vel, north_vel, diffusion, mixing, count, surface, from_east, from_west,
    near, far, first_rows, second_rows,
    vectors, diagonal, right_side, partial,
    north_buf, south_buf,
):
    here = lax.axis_index("gy")
    top = lax.axis_size("gy") - 1
    lane, sub = lanes(), sublanes()
    low = sub < 4
    fields = (east_vel, north_vel, diffusion, mixing)

    @pl.when(here % 2 == 0)
    def _():
        north_buf[...] = near[...]
        south_buf[...] = far[...]

    @pl.when(here % 2 == 1)
    def _():
        south_buf[...] = near[...]

    @pl.when((here % 2 == 1) & (here != top))
    def _():
        north_buf[...] = far[...]

    @pl.when(here == top)
    def _():
        unfold(pole_of(fold_map) & (COLS - 1), first_rows, second_rows, north_buf)

    def at(ref, row):
        return ref[row : row + ROWS, :]

    def field_tile(ref, f, k):
        return at(ref, ROW_FIELD + ROWS * (f * (LEVELS // 2) + k // 2))

    def halo_main(f, k):
        north, south = field_tile(north_buf, f, k), field_tile(south_buf, f, k)
        return jnp.where(low, roll(north, 4 * (k % 2), 0), roll(south, 4 * (1 - k % 2), 0))

    def side(ref, f, first, width):
        return unpack(at(ref, ROW_EAST + ROWS * f), at(ref, ROW_WEST + ROWS * f), first, width, lane)

    halo_packed = [
        [
            jnp.where(low, at(north_buf, base + ROWS * (1 + f)), at(south_buf, base + ROWS * (1 + f)))
            for base in (ROW_EAST, ROW_WEST)
        ]
        for f in range(4)
    ]

    def column(f):
        row = COL_DEEP + ROWS * f
        return from_east[row : row + ROWS, :], from_west[row : row + ROWS, :]

    def neighbours_across(own, north, south):
        up, up_n, up_s = roll(own, -1, 0), roll(north, -1, 0), roll(south, -1, 0)
        down, down_n, down_s = roll(own, 1, 0), roll(north, 1, 0), roll(south, 1, 0)
        return (
            jnp.where(sub == 7, up_n, up),
            jnp.where(low, up_n, jnp.where(sub == 7, up, up_s)),
            jnp.where(sub == 0, down_s, down),
            jnp.where(sub == 0, down, jnp.where(low, down_n, down_s)),
        )

    def halo(pair):
        return jnp.where(low, pair[0], pair[1])

    counts_own = (count[...].astype(jnp.float32), unpack(*column(0), COUNT_LANE, 5, lane))
    counts_north = (at(north_buf, ROW_COUNT), side(north_buf, 0, COUNT_LANE, 5))
    counts_south = (at(south_buf, ROW_COUNT), side(south_buf, 0, COUNT_LANE, 5))
    counts = (counts_own[0], counts_own[1], halo((counts_north[0], counts_south[0])), halo((counts_north[1], counts_south[1])))
    surfaces = (
        surface[...],
        unpack(*column(0), SURFACE_LANE, 4, lane),
        halo((at(north_buf, ROW_SURFACE), at(south_buf, ROW_SURFACE))),
        halo((side(north_buf, 0, SURFACE_LANE, 4), side(south_buf, 0, SURFACE_LANE, 4))),
    )

    zero = jnp.zeros((ROWS, COLS), jnp.float32)
    c_prev, r_prev, a_prev = [zero] * 4, [zero] * 4, [zero] * 4
    c_list, r_list = [], []
    for k in range(LEVELS):
        own = (difference[k], unpack(*column(0), 5 * k, 5, lane))
        north = (at(north_buf, ROW_DIFF + ROWS * k), side(north_buf, 0, 5 * k, 5))
        south = (at(south_buf, ROW_DIFF + ROWS * k), side(south_buf, 0, 5 * k, 5))
        halos = (halo((north[0], south[0])), halo((north[1], south[1])))
        centre = (own[0], own[1], halos[0], halos[1])
        easts = both_east(*own, lane) + both_east(*halos, lane)
        wests = both_west(*own, lane) + both_west(*halos, lane)
        first = neighbours_across(own[0], north[0], south[0])
        second = neighbours_across(own[1], north[1], south[1])
        norths = (first[0], second[0], first[1], second[1])
        souths = (first[2], second[2], first[3], second[3])
        values = [
            (field[k], unpack(*column(1 + f), 4 * k, 4, lane), halo_main(f, k), unpack(*halo_packed[f], 4 * k, 4, lane))
            for f, field in enumerate(fields)
        ]
        c_now, r_now, a_now = [], [], []
        for i in range(4):
            u, v, spread, mix = (value[i] for value in values)
            change = (
                -0.5 * u * (easts[i] - wests[i])
                - 0.5 * v * (norths[i] - souths[i])
                + spread * (easts[i] + wests[i] + norths[i] + souths[i] - 4.0 * centre[i])
            )
            explicit = centre[i] + jnp.where(k < counts[i], change, 0.0)
            a = jnp.where(k + 1 < counts[i], mix, 0.0)
            inverse = 1.0 / (1.0 + a_prev[i] + a + a_prev[i] * c_prev[i])
            c_now.append(-a * inverse)
            r_now.append((explicit + a_prev[i] * r_prev[i]) * inverse)
            a_now.append(a)
        c_prev, r_prev, a_prev = c_now, r_now, a_now
        c_list.append(c_now)
        r_list.append(r_now)
    total, x_next = [zero] * 4, [zero] * 4
    for k in range(LEVELS - 1, -1, -1):
        x_next = [r_list[k][i] - c_list[k][i] * x_next[i] for i in range(4)]
        total = [total[i] + thickness(k) * x_next[i] for i in range(4)]
    rhs = [jnp.where(counts[i] > 0, 0.25 * total[i], 0.0) for i in range(4)]

    def depth_of(levels):
        depth = zero
        for k in range(LEVELS):
            depth = depth + jnp.where(k < levels, thickness(k), 0.0)
        return depth / LEVELS

    own = tuple(depth_of(levels) for levels in counts_own)
    north = tuple(depth_of(levels) for levels in counts_north)
    south = tuple(depth_of(levels) for levels in counts_south)
    depths = (own[0], own[1], halo((north[0], south[0])), halo((north[1], south[1])))

    def rows_of(own, north, south):
        first = neighbours_across(own[0], north[0], south[0])
        second = neighbours_across(own[1], north[1], south[1])
        return (first[0], second[0], first[1], second[1]), (first[2], second[2], first[3], second[3])

    def coupled(others, weight):
        return [weight * jnp.minimum(depths[i], others[i]) for i in range(4)]

    own_e, north_e, south_e = (both_east(*pair, lane) for pair in (own, north, south))
    own_w, north_w, south_w = (both_west(*pair, lane) for pair in (own, north, south))
    halo_e = (halo((north_e[0], south_e[0])), halo((north_e[1], south_e[1])))
    halo_w = (halo((north_w[0], south_w[0])), halo((north_w[1], south_w[1])))
    mid = rows_of(own, north, south)
    mid_e = rows_of(own_e, north_e, south_e)
    mid_w = rows_of(own_w, north_w, south_w)
    couplings = [
        coupled(own_e + halo_e, 1.0),
        coupled(own_w + halo_w, 1.0),
        coupled(mid[0], 1.0),
        coupled(mid[1], 1.0),
        coupled(mid_e[0], 0.5),
        coupled(mid_w[0], 0.5),
        coupled(mid_e[1], 0.5),
        coupled(mid_w[1], 0.5),
    ]
    diag = [
        jnp.where(counts[i] > 0, surfaces[i] + sum(entry[i] for entry in couplings), 1.0) for i in range(4)
    ]
    inverse = [1.0 / diag[i] for i in range(4)]
    couplings = [[entry[i] * inverse[i] for i in range(4)] for entry in couplings]

    def shifted_rows(tiles):
        north, south = [None] * 4, [None] * 4
        for i in range(2):
            a, b = roll(tiles[i], -1, 0), roll(tiles[i + 2], -1, 0)
            north[i], north[i + 2] = jnp.where(sub == 7, b, a), jnp.where(sub == 7, a, b)
            a, b = roll(tiles[i], 1, 0), roll(tiles[i + 2], 1, 0)
            south[i], south[i + 2] = jnp.where(sub == 0, b, a), jnp.where(sub == 0, a, b)
        return north, south

    def spread_out(tiles):
        east = both_east(tiles[0], tiles[1], lane) + both_east(tiles[2], tiles[3], lane)
        west = both_west(tiles[0], tiles[1], lane) + both_west(tiles[2], tiles[3], lane)
        mid_n, mid_s = shifted_rows(tiles)
        east_n, east_s = shifted_rows(east)
        west_n, west_s = shifted_rows(west)
        around = (east, west, mid_n, mid_s, east_n, west_n, east_s, west_s)
        return [sum(entry[i] * values[i] for entry, values in zip(couplings, around)) for i in range(4)]

    found = [[rhs[i] * inverse[i] for i in range(4)]]
    found.append(spread_out(found[0]))
    for _ in range(2, ITERS + 1):
        ahead = spread_out(found[-1])
        found.append([2.0 * ahead[i] - found[-2][i] for i in range(4)])
    for j in range(ITERS + 1):
        vectors[j] = found[j][0]
    diagonal[...] = diag[0]
    right_side[...] = rhs[0]
    weighted = [diag[0] * found[j][0] for j in range(ITERS + 1)]
    sums = [weighted[j] * found[j][0] for j in range(ITERS + 1)]
    sums += [weighted[j] * found[j + 1][0] for j in range(ITERS)]
    row = jnp.zeros((1, COLS), jnp.float32)
    for j, entry in enumerate(sums):
        row = jnp.where(lane[:1, :] == j, jnp.sum(entry, keepdims=True), row)
    partial[...] = jnp.broadcast_to(row, partial.shape)


def combine_kernel(moments, vectors, diagonal, pressure, residual, good):
    size = ITERS + 1
    sums = jnp.sum(moments[...], axis=0, keepdims=True)

    def lane_of(j):
        return jnp.broadcast_to(sums[:, j : j + 1], (ROWS, COLS))

    even = [lane_of(j) for j in range(size)]
    odd = [lane_of(size + j) for j in range(ITERS)]
    mu = []
    for j in range(size):
        mu.append(even[0] if j == 0 else 2.0 * even[j] - even[0])
        if j < ITERS:
            mu.append(odd[0] if j == 0 else 2.0 * odd[j] - odd[0])

    def mass(i, j):
        return 0.5 * (mu[i + j] + mu[abs(i - j)])

    def stiffness(i, j):
        i, j = min(i, j), max(i, j)
        if j == 0:
            return mu[0] - mu[1]
        return mass(i, j) - 0.5 * (mass(i, j + 1) + mass(i, j - 1))

    def form(values, entry):
        out = None
        for i in range(len(values)):
            inner = values[i] * entry(i, i)
            for j in range(i + 1, len(values)):
                inner = inner + 2.0 * values[j] * entry(i, j)
            out = values[i] * inner if out is None else out + values[i] * inner
        return out

    def applied(values):
        out = [value for value in values] + [jnp.zeros_like(values[0])]
        out[1] = out[1] - values[0]
        for j in range(1, len(values)):
            out[j + 1] = out[j + 1] - 0.5 * values[j]
            out[j - 1] = out[j - 1] - 0.5 * values[j]
        return out

    def amplified(values, result):
        total = sum(jnp.abs(value) for value in values)
        return total * total * mu[0] / result

    scaled = [jnp.ones((ROWS, COLS), jnp.float32)]
    direction = list(scaled)
    solution_at = []
    energy = mu[0]
    fine = energy > 0.0
    for step in range(ITERS):
        image = applied(direction)
        curvature = form(direction, stiffness)
        step_size = energy / curvature
        fine = fine & (amplified(direction, curvature) <= SCALAR_BOUND) & (curvature > 0.0)
        solution_at = [
            step_size * value + (solution_at[j] if j < len(solution_at) else 0.0) for j, value in enumerate(direction)
        ]
        scaled = [
            (scaled[j] if j < len(scaled) else 0.0) - step_size * value for j, value in enumerate(image)
        ]
        energy_new = form(scaled, mass)
        bound = SCALAR_BOUND if step + 1 < ITERS else FIELD_BOUND
        fine = fine & (amplified(scaled, energy_new) <= bound) & (energy_new > 0.0)
        if step + 1 < ITERS:
            ratio = energy_new / energy
            direction = [
                scaled[j] + (ratio * direction[j] if j < len(direction) else 0.0) for j in range(len(scaled))
            ]
            energy = energy_new
    pressure[...] = sum(solution_at[j] * vectors[j] for j in range(len(solution_at)))
    residual[...] = diagonal[...] * sum(scaled[j] * vectors[j] for j in range(len(scaled)))
    good[0] = jnp.min(jnp.where(fine, 1, 0).astype(jnp.int32))


def tracers_kernel(
    fold_map, tracer, east_vel, north_vel, diffusion, mixing, count, from_east, from_west, near, far, first, second,
    mixed,
    north_rows, south_rows, factors,
):
    lane, sub = lanes(), sublanes()
    levels = count[...]
    group = pl.program_id(0)

    @pl.when(group == 0)
    def _():
        halo_rows(fold_map, near, far, first, second, north_rows, south_rows)
        c_prev = jnp.zeros((ROWS, COLS), jnp.float32)
        a_prev = jnp.zeros((ROWS, COLS), jnp.float32)
        for k in range(LEVELS):
            wet = jnp.where(k < levels, 1.0, 0.0)
            u, v, spread = 0.5 * wet * east_vel[k], 0.5 * wet * north_vel[k], wet * diffusion[k]
            a = jnp.where(k + 1 < levels, mixing[k], 0.0)
            inverse = 1.0 / (1.0 + a_prev + a + a_prev * c_prev)
            c_prev = -a * inverse
            factors[0, k] = 1.0 - 4.0 * spread
            factors[1, k] = spread - u
            factors[2, k] = spread + u
            factors[3, k] = spread - v
            factors[4, k] = spread + v
            factors[5, k] = inverse
            factors[6, k] = a_prev
            factors[7, k] = c_prev
            a_prev = a

    row = pl.multiple_of(group * ROWS, ROWS)
    columns_east = from_east[pl.ds(row, ROWS), :]
    columns_west = from_west[pl.ds(row, ROWS), :]
    r_prev = [jnp.zeros((ROWS, COLS), jnp.float32)] * GROUP
    for k in range(LEVELS):
        centre, to_e, to_w, to_n, to_s, inverse, above = (factors[j, k] for j in range(7))
        wet = k < levels
        for t in range(GROUP):
            cell = jnp.where(wet, tracer[t, k], 0.0)
            at = t * LEVELS + k
            halo_row = group * (GROUP * LEVELS) + at
            east = east_of(cell, roll(columns_east, -at, 1), lane)
            west = west_of(cell, roll(columns_west, COLS - 1 - at, 1), lane)
            north = north_of(cell, north_rows[pl.ds(halo_row, 1), :], sub)
            south = south_of(cell, south_rows[pl.ds(halo_row, 1), :], sub)
            explicit = centre * cell + to_e * east + to_w * west + to_n * north + to_s * south
            r_prev[t] = (explicit + above * r_prev[t]) * inverse
            mixed[t, k] = r_prev[t]
    x_next = r_prev
    for k in range(LEVELS - 2, -1, -1):
        below = factors[7, k]
        for t in range(GROUP):
            x_next[t] = mixed[t, k] - below * x_next[t]
            mixed[t, k] = x_next[t]


def extended(cells, sides, width):
    for axis, dim in sides:
        count = lax.axis_size(axis)
        head = lax.slice_in_dim(cells, 0, width, axis=dim)
        tail = lax.slice_in_dim(cells, cells.shape[dim] - width, cells.shape[dim], axis=dim)
        cells = jnp.concatenate(
            [
                lax.ppermute(tail, axis, [(i, (i + 1) % count) for i in range(count)]),
                cells,
                lax.ppermute(head, axis, [((i + 1) % count, i) for i in range(count)]),
            ],
            axis=dim,
        )
    return cells


def extend(field, fold_map):
    rows, cols = field.shape
    padded = extended(field, (("gx", 1), ("gy", 0)), 1)
    total_cols = fold_map.shape[0]
    whole_row = lax.all_gather(field[rows - 1, :], "gx", axis=0, tiled=True)
    start = lax.axis_index("gx") * cols
    wanted = (start - 1 + jnp.arange(cols + 2, dtype=jnp.int32)) % total_cols
    folded = jnp.take(whole_row, jnp.take(fold_map, wanted), axis=0)
    row_index = lax.axis_index("gy")
    upper = jnp.where(row_index == lax.axis_size("gy") - 1, folded, padded[rows + 1, :])
    lower = jnp.where(row_index == 0, 0.0, padded[0, :])
    return jnp.concatenate([lower[None, :], padded[1 : rows + 1, :], upper[None, :]], axis=0)


def window(padded, row_off, col_off):
    rows = padded.shape[0] - 2
    cols = padded.shape[1] - 2
    return padded[1 + row_off : 1 + row_off + rows, 1 + col_off : 1 + col_off + cols]


def total_of(value):
    return lax.psum(jnp.sum(value), BOTH)


def direct_gradients(rhs, level_count, fold_map, surface_term):
    levels = jnp.arange(LEVELS, dtype=jnp.int32)[:, None, None]
    level_mask = (levels < level_count[None]).astype(jnp.float32)
    thick = (0.5 + 1.5 * jnp.arange(LEVELS).astype(jnp.float32) / (LEVELS - 1))[:, None, None]
    depth = jnp.sum(thick * level_mask, axis=0) / LEVELS
    wet_cells = level_count > 0
    depth_pad = extend(depth, fold_map)
    couplings = [
        weight * jnp.minimum(depth, window(depth_pad, row_off, col_off)) for row_off, col_off, weight in NEIGHBOURS
    ]
    diag = jnp.where(wet_cells, surface_term + sum(couplings), 1.0)

    def step(_, state):
        pressure, residual, direction, energy = state
        field_pad = extend(direction, fold_map)
        summed = jnp.zeros_like(direction)
        for entry, (row_off, col_off, _weight) in zip(couplings, NEIGHBOURS):
            summed = summed + entry * window(field_pad, row_off, col_off)
        image = jnp.where(wet_cells, diag * direction - summed, direction)
        step_size = energy / total_of(direction * image)
        pressure = pressure + step_size * direction
        residual = residual - step_size * image
        scaled = residual / diag
        energy_new = total_of(residual * scaled)
        return pressure, residual, scaled + energy_new / energy * direction, energy_new

    scaled = rhs / diag
    state = (jnp.zeros_like(rhs), rhs, scaled, total_of(rhs * scaled))
    state = lax.fori_loop(0, ITERS, step, state)
    return state[0], state[1]


def kernel(body, limit=VMEM_LIMIT, **rest):
    return pl.pallas_call(body, compiler_params=params(limit), **rest)


def shape(*dims):
    return jax.ShapeDtypeStruct(dims, jnp.float32)


def vmem(*dims):
    return pltpu.VMEM(dims, jnp.float32)


def block_of(dims, at=0):
    return pl.BlockSpec(dims, lambda i: (at,) + (0,) * (len(dims) - 1))


def all_of(array):
    return block_of(array.shape)


def shards(sizes, tracer, east_vel, north_vel, diffusion, mixing, count, fold_map, surface):
    nx, ny = sizes
    hbm = pl.BlockSpec(memory_space=pltpu.HBM)
    smem = pl.BlockSpec(memory_space=pltpu.SMEM)
    fields = (east_vel, north_vel, diffusion, mixing)

    def device(x, y):
        return (x % nx) * ny + y

    flat = tracer.reshape(EDGE * ROWS, COLS)
    scratch = [
        vmem(EDGE * ROWS, COLS),
        vmem(4, LEVELS, ROWS, COLS),
        pltpu.VMEM((ROWS, COLS), jnp.int32),
        vmem(ROWS, COLS),
        pltpu.SemaphoreType.DMA((GROUPS + 6,)),
    ]
    to_west, to_east = kernel(
        columns_kernel,
        limit=PACK_VMEM_LIMIT,
        out_shape=(shape(COL_SIZE, COLS), shape(COL_SIZE, COLS)),
        in_specs=[hbm] * 7,
        out_specs=(whole(),) * 2,
        scratch_shapes=scratch,
        name="pack_columns",
    )(flat, *fields, count, surface)

    from_east = lax.ppermute(to_west, BOTH, [(device(x + 1, y), device(x, y)) for x in range(nx) for y in range(ny)])
    from_west = lax.ppermute(to_east, BOTH, [(device(x - 1, y), device(x, y)) for x in range(nx) for y in range(ny)])

    near_edge, far_edge, near, far, difference, block = kernel(
        rows_kernel,
        limit=PACK_VMEM_LIMIT,
        out_shape=(
            shape(EDGE, COLS),
            shape(EDGE, COLS),
            shape(ROW_SIZE, COLS),
            shape(ROW_SIZE, COLS),
            shape(LEVELS, ROWS, COLS),
            jax.ShapeDtypeStruct((1,), jnp.int32),
        ),
        in_specs=[smem] + [hbm] * 7,
        out_specs=(whole(),) * 5 + (smem,),
        scratch_shapes=scratch,
        cost_estimate=pl.CostEstimate(flops=4000000, bytes_accessed=8000000, transcendentals=0),
        name="pack_rows",
    )(fold_map, flat, *fields, count, surface)

    pairs = [(device(x, y ^ 1), device(x, y)) for x in range(nx) for y in range(ny)]
    inner = [(device(x, y + 1 if y % 2 else y - 1), device(x, y)) for x in range(nx) for y in range(1, ny - 1)]

    def across(turn, rows):
        return lax.ppermute(rows, BOTH, [(device(turn - x, ny - 1), device(x, ny - 1)) for x in range(nx)])

    def by_block(branch, *operands):
        return lax.switch(block[0], [functools.partial(branch, at) for at in range(nx)], *operands)

    fold_edges = by_block(lambda at, rows: (across(at - 1, rows), across(at, rows)), far_edge)
    near_edge, far_edge = lax.ppermute(near_edge, BOTH, pairs), lax.ppermute(far_edge, BOTH, inner)

    columns = block_of((COL_SIZE, COLS))
    corner = block_of((ROW_DIFF, COLS))
    near, far = kernel(
        corners_kernel,
        grid=(1,),
        out_shape=(shape(ROW_SIZE, COLS), shape(ROW_SIZE, COLS)),
        in_specs=[columns, columns] + [pl.BlockSpec(memory_space=pl.ANY)] * 4,
        out_specs=(corner, corner),
        input_output_aliases={2: 0, 3: 1},
        name="put_corners",
    )(from_east, from_west, near, far, near_edge, far_edge)
    from_near, from_far, *fold_rows = by_block(
        lambda at, near, far: (
            lax.ppermute(near, BOTH, pairs),
            lax.ppermute(far, BOTH, inner),
            across(at - 1, far),
            across(at, far),
        ),
        near,
        far,
    )

    rest = (*fields, count, surface, from_east, from_west, from_near, from_far, *fold_rows)
    vectors, diagonal, rhs, partial = kernel(
        krylov_kernel,
        grid=(1,),
        out_shape=(shape(ITERS + 1, ROWS, COLS), shape(ROWS, COLS), shape(ROWS, COLS), shape(nx * ny, COLS)),
        in_specs=[smem, all_of(difference)] + [all_of(array) for array in rest],
        out_specs=(
            block_of((ITERS + 1, ROWS, COLS)),
            block_of((ROWS, COLS)),
            block_of((ROWS, COLS)),
            block_of((nx * ny, COLS)),
        ),
        scratch_shapes=[vmem(ROW_SIZE, COLS), vmem(ROW_SIZE, COLS)],
        name="krylov",
    )(fold_map, difference, *rest)

    moments = lax.all_to_all(partial, BOTH, 0, 0)

    batch = pl.BlockSpec((GROUP, LEVELS, ROWS, COLS), lambda i: (i, 0, 0, 0))
    mixed = kernel(
        tracers_kernel,
        grid=(GROUPS,),
        out_shape=shape(TRACERS, LEVELS, ROWS, COLS),
        in_specs=[smem, batch]
        + [all_of(array) for array in (*fields, count)]
        + [block_of((COL_DEEP, COLS))] * 2
        + [block_of((EDGE, COLS))] * 4,
        out_specs=batch,
        scratch_shapes=[vmem(EDGE, COLS), vmem(EDGE, COLS), vmem(8, LEVELS, ROWS, COLS)],
        name="tracers",
    )(fold_map, tracer, *fields, count, from_east, from_west, near_edge, far_edge, *fold_edges)

    pressure, residual, good = kernel(
        combine_kernel,
        out_shape=(shape(ROWS, COLS), shape(ROWS, COLS), jax.ShapeDtypeStruct((1,), jnp.int32)),
        in_specs=[whole()] * 3,
        out_specs=(whole(), whole(), smem),
        name="combine",
    )(moments, vectors, diagonal)
    pressure, residual = lax.cond(
        good[0] == 1,
        lambda pressure, residual, rhs, count, surface, fold: (pressure, residual),
        lambda pressure, residual, rhs, count, surface, fold: direct_gradients(rhs, count, fold, surface),
        pressure,
        residual,
        rhs,
        count,
        surface,
        fold_map,
    )
    return mixed, pressure, residual


def solution(mesh):
    in_specs = (
        P(None, None, "gy", "gx"),
        P(None, "gy", "gx"),
        P(None, "gy", "gx"),
        P(None, "gy", "gx"),
        P(None, "gy", "gx"),
        P("gy", "gx"),
        P(),
        P("gy", "gx"),
    )
    out_specs = (P(None, None, "gy", "gx"), P("gy", "gx"), P("gy", "gx"))
    body = functools.partial(shards, (mesh.shape["gx"], mesh.shape["gy"]))
    return jax.shard_map(body, mesh=mesh, in_specs=in_specs, out_specs=out_specs, check_vma=False)
```

```python
import functools

import jax
import jax.numpy as jnp
from jax import lax
from jax.experimental import pallas as pl
from jax.experimental.pallas import tpu as pltpu
from jax.sharding import PartitionSpec as P

ITERS = 4
TRACERS, LEVELS, ROWS, COLS = 16, 20, 8, 128
GROUP = 4
GROUPS = TRACERS // GROUP
EDGE = TRACERS * LEVELS
BOTH = ("gx", "gy")
VMEM_LIMIT = 40 * 1024 * 1024
PACK_VMEM_LIMIT = 63 * 1024 * 1024

COL_DEEP, COL_SIZE = GROUPS * ROWS, (GROUPS + 5) * ROWS
COUNT_LANE, SURFACE_LANE = 100, 105
ROW_EAST, ROW_WEST, ROW_DIFF, ROW_FIELD, ROW_COUNT, ROW_SURFACE, ROW_SIZE = 320, 360, 400, 560, 880, 888, 896
DEEP_SIZE = ROW_SIZE - ROW_EAST

SCALAR_BOUND, FIELD_BOUND = 1500.0, 1.0e5

NEIGHBOURS = [
    (0, 1, 1.0),
    (0, -1, 1.0),
    (1, 0, 1.0),
    (-1, 0, 1.0),
    (1, 1, 0.5),
    (1, -1, 0.5),
    (-1, 1, 0.5),
    (-1, -1, 0.5),
]


def params(limit=VMEM_LIMIT):
    return pltpu.CompilerParams(vmem_limit_bytes=limit)


def whole():
    return pl.BlockSpec(memory_space=pltpu.VMEM)


def lanes():
    return lax.broadcasted_iota(jnp.int32, (ROWS, COLS), 1)


def sublanes():
    return lax.broadcasted_iota(jnp.int32, (ROWS, COLS), 0)


def roll(tile, shift, axis):
    size = tile.shape[axis]
    shift = shift % size
    return tile if shift == 0 else pltpu.roll(tile, shift, axis)


def east_of(tile, beyond, lane):
    return roll(jnp.where(lane == 0, beyond, tile), -1, 1)


def west_of(tile, beyond, lane):
    return roll(jnp.where(lane == COLS - 1, beyond, tile), 1, 1)


def north_of(tile, beyond, sub):
    return roll(jnp.where(sub == 0, beyond, tile), -1, 0)


def south_of(tile, beyond, sub):
    return roll(jnp.where(sub == ROWS - 1, beyond, tile), 1, 0)


def thickness(level):
    return 0.5 + 1.5 * level / (LEVELS - 1)


def turned(tile):
    return jnp.take_along_axis(tile, ROWS - 1 - sublanes(), axis=0)


def start_copies(pairs, ready):
    copies = [pltpu.make_async_copy(source, target, ready.at[i]) for i, (source, target) in enumerate(pairs)]
    for copy in copies:
        copy.start()
    return copies


def columns_kernel(
    tracer, east_vel, north_vel, diffusion, mixing, count, surface,
    to_west, to_east,
    cells, fields, levels_ref, surface_ref, ready,
):
    lane = lanes()
    size = GROUP * LEVELS * ROWS
    pairs = [(count, levels_ref), (surface, surface_ref)]
    pairs += [(tracer.at[pl.ds(g * size, size)], cells.at[pl.ds(g * size, size)]) for g in range(GROUPS)]
    pairs += [(field, fields.at[f]) for f, field in enumerate((east_vel, north_vel, diffusion, mixing))]
    copies = start_copies(pairs, ready)

    def put(row, items):
        west = jnp.zeros((ROWS, COLS), jnp.float32)
        east = jnp.zeros((ROWS, COLS), jnp.float32)
        for tile, width, first in items:
            chosen = lane == first if width == 1 else (lane >= first) & (lane < first + width)
            west = jnp.where(chosen, roll(tile, first, 1), west)
            east = jnp.where(chosen, roll(tile, first + width, 1), east)
        to_west[row : row + ROWS, :] = west
        to_east[row : row + ROWS, :] = east

    copies[0].wait()
    copies[1].wait()
    levels, surfaces = levels_ref[...], surface_ref[...]

    def cell(t, k):
        row = (t * LEVELS + k) * ROWS
        return jnp.where(k < levels, cells[row : row + ROWS, :], 0.0)

    for g in range(GROUPS):
        copies[2 + g].wait()
        put(g * ROWS, [(cell(g * GROUP + t, k), 1, t * LEVELS + k) for t in range(GROUP) for k in range(LEVELS)])
        if g == 0:
            difference = [(cell(0, k) - cell(1, k), 5, 5 * k) for k in range(LEVELS)]
            put(COL_DEEP, difference + [(levels.astype(jnp.float32), 5, COUNT_LANE), (surfaces, 4, SURFACE_LANE)])
    for f in range(4):
        copies[2 + GROUPS + f].wait()
        put(COL_DEEP + (1 + f) * ROWS, [(fields[f, k], 4, 4 * k) for k in range(LEVELS)])


def rows_kernel(
    fold_map, tracer, east_vel, north_vel, diffusion, mixing, count, surface,
    near_rows, far_rows, difference, block,
    cells, fields, levels_ref, surface_ref, ready,
):
    low = sublanes() < ROWS // 2
    pairs = [(count, levels_ref), (surface, surface_ref), (tracer, cells)]
    pairs += [(field, fields.at[f]) for f, field in enumerate((east_vel, north_vel, diffusion, mixing))]
    copies = start_copies(pairs, ready)
    here = lax.axis_index("gy")
    even = here % 2 == 0
    is_top = here == lax.axis_size("gy") - 1
    block[0] = pole_of(fold_map) >> (COLS.bit_length() - 1)
    copies[0].wait()
    copies[1].wait()
    levels, surfaces = levels_ref[...], surface_ref[...]
    depths = levels.astype(jnp.float32)
    per = 2 * LEVELS
    level_row = lax.broadcasted_iota(jnp.int32, (per, COLS), 0)
    level_row = jnp.where(level_row >= LEVELS, level_row - LEVELS, level_row)
    wet_south = level_row < jnp.broadcast_to(levels[:1, :], (per, COLS))
    wet_north = level_row < jnp.broadcast_to(levels[ROWS - 1 :, :], (per, COLS))
    copies[2].wait()
    for at in range(0, EDGE, per):
        south = jnp.where(wet_south, cells[pl.ds(at * ROWS, per, stride=ROWS), :], 0.0)
        north = jnp.where(wet_north, cells[pl.ds(at * ROWS + ROWS - 1, per, stride=ROWS), :], 0.0)
        near_rows[at : at + per, :] = jnp.where(even, north, south)
        far_rows[at : at + per, :] = jnp.where(even, south, north)
    for k in range(LEVELS):
        one, two = ROWS * k, ROWS * (LEVELS + k)
        difference[k] = jnp.where(k < levels, cells[one : one + ROWS, :] - cells[two : two + ROWS, :], 0.0)
    for copy in copies[3:]:
        copy.wait()

    def pack(kind, out):
        turn = turned if kind == "fold" else (lambda tile: tile)
        for k in range(LEVELS):
            out[ROW_DIFF + ROWS * k : ROW_DIFF + ROWS * (k + 1), :] = turn(difference[k])
        for f in range(4):
            for m in range(LEVELS // 2):
                first, second = turn(fields[f, 2 * m]), turn(fields[f, 2 * m + 1])
                if kind == "north":
                    tile = jnp.where(low, roll(first, 4, 0), second)
                else:
                    tile = jnp.where(low, first, roll(second, 4, 0))
                row = ROW_FIELD + ROWS * (f * (LEVELS // 2) + m)
                out[row : row + ROWS, :] = tile
        out[ROW_COUNT : ROW_COUNT + ROWS, :] = turn(depths)
        out[ROW_SURFACE : ROW_SURFACE + ROWS, :] = turn(surfaces)

    @pl.when(even)
    def _():
        pack("north", near_rows)
        pack("south", far_rows)

    @pl.when(jnp.logical_not(even))
    def _():
        pack("south", near_rows)

    @pl.when(jnp.logical_not(even) & jnp.logical_not(is_top))
    def _():
        pack("north", far_rows)

    @pl.when(is_top)
    def _():
        pack("fold", far_rows)


def corners_kernel(east, west, near_in, far_in, near, far):
    del near_in, far_in
    is_top = lax.axis_index("gy") == lax.axis_size("gy") - 1
    for base, ref in ((0, east), (ROW_WEST - ROW_EAST, west)):
        for row in range(0, ROW_WEST - ROW_EAST, ROWS):
            value = ref[COL_DEEP + row : COL_DEEP + row + ROWS, :]
            near[base + row : base + row + ROWS, :] = value
            far[base + row : base + row + ROWS, :] = jnp.where(is_top, turned(value), value)


def pole_of(fold_map):
    return (fold_map[0] + 1) & (COLS * lax.axis_size("gx") - 1)


def halo_rows(fold_map, near, far, extra, north_rows, south_rows):
    here = lax.axis_index("gy")
    top = lax.axis_size("gy") - 1

    @pl.when(here % 2 == 0)
    def _():
        north_rows[...] = near[...]
        south_rows[...] = far[...]

    @pl.when(here % 2 == 1)
    def _():
        south_rows[...] = near[...]

    @pl.when((here % 2 == 1) & (here != top))
    def _():
        north_rows[...] = far[...]

    @pl.when(here == top)
    def _():
        lane = lanes()
        pole = pole_of(fold_map)
        offset = pole & (COLS - 1)
        index = (offset - 1 - lane) & (COLS - 1)
        from_far = (lane >= offset) == ((pole & COLS) != 0)
        for row in range(0, north_rows.shape[0], ROWS):
            a = jnp.take_along_axis(far[row : row + ROWS, :], index, axis=1)
            b = jnp.take_along_axis(extra[row : row + ROWS, :], index, axis=1)
            north_rows[row : row + ROWS, :] = jnp.where(from_far, a, b)


def unfold(offset, first_in_far, far, extra, out):
    lane = lanes()
    index = (offset - 1 - lane) & (COLS - 1)
    zero = jnp.zeros((ROWS, COLS), jnp.float32)

    def first(row):
        return jnp.where(first_in_far, far[row : row + ROWS, :], extra[row : row + ROWS, :])

    def second(row):
        return jnp.where(first_in_far, extra[row : row + ROWS, :], far[row : row + ROWS, :])

    def store(row, value):
        out[row - ROW_EAST : row - ROW_EAST + ROWS, :] = value

    def flipped(row, sign):
        a = sign * jnp.take_along_axis(first(row), index, axis=1)
        b = sign * jnp.take_along_axis(second(row), index, axis=1)
        store(row, jnp.where(lane >= offset, a, b))
        return a, b

    def collect(packed, a, b, width, at):
        chosen = (lane >= at) & (lane < at + width)
        return jnp.where(chosen, roll(a, at, 1), packed[0]), jnp.where(chosen, roll(b, at + width, 1), packed[1])

    def finish(row, packed, sign, width, within):
        beside = (lane + (offset - 1) + width - 2 * within) & (COLS - 1)
        right = sign * jnp.take_along_axis(first(ROW_WEST + row), beside, axis=1)
        beside = (lane + (offset - 1 - COLS) + width - 2 * within) & (COLS - 1)
        left = sign * jnp.take_along_axis(second(ROW_EAST + row), beside, axis=1)
        store(ROW_EAST + row, jnp.where(within < offset, packed[0], right))
        store(ROW_WEST + row, jnp.where(within >= offset + width - COLS, packed[1], left))

    packed = (zero, zero)
    for k in range(LEVELS):
        packed = collect(packed, *flipped(ROW_DIFF + ROWS * k, 1.0), 5, 5 * k)
    packed = collect(packed, *flipped(ROW_COUNT, 1.0), 5, COUNT_LANE)
    packed = collect(packed, *flipped(ROW_SURFACE, 1.0), 4, SURFACE_LANE)
    fifth = lane - 5 * ((lane * 205) >> 10)
    finish(0, packed, 1.0, jnp.where(lane >= SURFACE_LANE, 4, 5), fifth)
    for f in range(4):
        sign = -1.0 if f < 2 else 1.0
        packed = (zero, zero)
        for m in range(LEVELS // 2):
            a, b = flipped(ROW_FIELD + ROWS * (f * (LEVELS // 2) + m), sign)
            packed = collect(packed, a, b, 4, 8 * m)
            packed = collect(packed, roll(a, 4, 0), roll(b, 4, 0), 4, 8 * m + 4)
        finish((1 + f) * ROWS, packed, sign, 4, lane & 3)


def unpack(east, west, first, width, lane):
    right = roll(east, -first, 1)
    left = roll(west, -width - first, 1)
    return jnp.where(lane < width, right, jnp.where(lane >= COLS - width, left, 0.0))


def both_east(one, two, lane):
    return east_of(one, two, lane), east_of(two, one, lane)


def both_west(one, two, lane):
    return west_of(one, two, lane), west_of(two, one, lane)


def krylov_kernel(
    fold_map, difference, east_vel, north_vel, diffusion, mixing, count, surface, from_east, from_west,
    near, far, extra,
    vectors, diagonal, right_side, partial,
    north_buf, south_buf,
):
    here = lax.axis_index("gy")
    top = lax.axis_size("gy") - 1
    lane, sub = lanes(), sublanes()
    low = sub < 4
    fields = (east_vel, north_vel, diffusion, mixing)

    @pl.when(here % 2 == 0)
    def _():
        north_buf[...] = near[ROW_EAST:, :]
        south_buf[...] = far[ROW_EAST:, :]

    @pl.when(here % 2 == 1)
    def _():
        south_buf[...] = near[ROW_EAST:, :]

    @pl.when((here % 2 == 1) & (here != top))
    def _():
        north_buf[...] = far[ROW_EAST:, :]

    @pl.when(here == top)
    def _():
        pole = pole_of(fold_map)
        unfold(pole & (COLS - 1), (pole & COLS) != 0, far, extra, north_buf)

    def at(ref, row):
        return ref[row - ROW_EAST : row - ROW_EAST + ROWS, :]

    def field_tile(ref, f, k):
        return at(ref, ROW_FIELD + ROWS * (f * (LEVELS // 2) + k // 2))

    def halo_main(f, k):
        north, south = field_tile(north_buf, f, k), field_tile(south_buf, f, k)
        return jnp.where(low, roll(north, 4 * (k % 2), 0), roll(south, 4 * (1 - k % 2), 0))

    def side(ref, f, first, width):
        return unpack(at(ref, ROW_EAST + ROWS * f), at(ref, ROW_WEST + ROWS * f), first, width, lane)

    halo_packed = [
        [
            jnp.where(low, at(north_buf, base + ROWS * (1 + f)), at(south_buf, base + ROWS * (1 + f)))
            for base in (ROW_EAST, ROW_WEST)
        ]
        for f in range(4)
    ]

    def column(f):
        row = COL_DEEP + ROWS * f
        return from_east[row : row + ROWS, :], from_west[row : row + ROWS, :]

    def neighbours_across(own, north, south):
        up, up_n, up_s = roll(own, -1, 0), roll(north, -1, 0), roll(south, -1, 0)
        down, down_n, down_s = roll(own, 1, 0), roll(north, 1, 0), roll(south, 1, 0)
        return (
            jnp.where(sub == 7, up_n, up),
            jnp.where(low, up_n, jnp.where(sub == 7, up, up_s)),
            jnp.where(sub == 0, down_s, down),
            jnp.where(sub == 0, down, jnp.where(low, down_n, down_s)),
        )

    def halo(pair):
        return jnp.where(low, pair[0], pair[1])

    counts_own = (count[...].astype(jnp.float32), unpack(*column(0), COUNT_LANE, 5, lane))
    counts_north = (at(north_buf, ROW_COUNT), side(north_buf, 0, COUNT_LANE, 5))
    counts_south = (at(south_buf, ROW_COUNT), side(south_buf, 0, COUNT_LANE, 5))
    counts = (counts_own[0], counts_own[1], halo((counts_north[0], counts_south[0])), halo((counts_north[1], counts_south[1])))
    surfaces = (
        surface[...],
        unpack(*column(0), SURFACE_LANE, 4, lane),
        halo((at(north_buf, ROW_SURFACE), at(south_buf, ROW_SURFACE))),
        halo((side(north_buf, 0, SURFACE_LANE, 4), side(south_buf, 0, SURFACE_LANE, 4))),
    )

    zero = jnp.zeros((ROWS, COLS), jnp.float32)
    c_prev, r_prev, a_prev = [zero] * 4, [zero] * 4, [zero] * 4
    c_list, r_list = [], []
    for k in range(LEVELS):
        own = (difference[k], unpack(*column(0), 5 * k, 5, lane))
        north = (at(north_buf, ROW_DIFF + ROWS * k), side(north_buf, 0, 5 * k, 5))
        south = (at(south_buf, ROW_DIFF + ROWS * k), side(south_buf, 0, 5 * k, 5))
        halos = (halo((north[0], south[0])), halo((north[1], south[1])))
        centre = (own[0], own[1], halos[0], halos[1])
        easts = both_east(*own, lane) + both_east(*halos, lane)
        wests = both_west(*own, lane) + both_west(*halos, lane)
        first = neighbours_across(own[0], north[0], south[0])
        second = neighbours_across(own[1], north[1], south[1])
        norths = (first[0], second[0], first[1], second[1])
        souths = (first[2], second[2], first[3], second[3])
        values = [
            (field[k], unpack(*column(1 + f), 4 * k, 4, lane), halo_main(f, k), unpack(*halo_packed[f], 4 * k, 4, lane))
            for f, field in enumerate(fields)
        ]
        c_now, r_now, a_now = [], [], []
        for i in range(4):
            u, v, spread, mix = (value[i] for value in values)
            change = (
                -0.5 * u * (easts[i] - wests[i])
                - 0.5 * v * (norths[i] - souths[i])
                + spread * (easts[i] + wests[i] + norths[i] + souths[i] - 4.0 * centre[i])
            )
            explicit = centre[i] + jnp.where(k < counts[i], change, 0.0)
            a = jnp.where(k + 1 < counts[i], mix, 0.0)
            inverse = 1.0 / (1.0 + a_prev[i] + a + a_prev[i] * c_prev[i])
            c_now.append(-a * inverse)
            r_now.append((explicit + a_prev[i] * r_prev[i]) * inverse)
            a_now.append(a)
        c_prev, r_prev, a_prev = c_now, r_now, a_now
        c_list.append(c_now)
        r_list.append(r_now)
    total, x_next = [zero] * 4, [zero] * 4
    for k in range(LEVELS - 1, -1, -1):
        x_next = [r_list[k][i] - c_list[k][i] * x_next[i] for i in range(4)]
        total = [total[i] + thickness(k) * x_next[i] for i in range(4)]
    rhs = [jnp.where(counts[i] > 0, 0.25 * total[i], 0.0) for i in range(4)]

    def depth_of(levels):
        depth = zero
        for k in range(LEVELS):
            depth = depth + jnp.where(k < levels, thickness(k), 0.0)
        return depth / LEVELS

    own = tuple(depth_of(levels) for levels in counts_own)
    north = tuple(depth_of(levels) for levels in counts_north)
    south = tuple(depth_of(levels) for levels in counts_south)
    depths = (own[0], own[1], halo((north[0], south[0])), halo((north[1], south[1])))

    def rows_of(own, north, south):
        first = neighbours_across(own[0], north[0], south[0])
        second = neighbours_across(own[1], north[1], south[1])
        return (first[0], second[0], first[1], second[1]), (first[2], second[2], first[3], second[3])

    def coupled(others, weight):
        return [weight * jnp.minimum(depths[i], others[i]) for i in range(4)]

    own_e, north_e, south_e = (both_east(*pair, lane) for pair in (own, north, south))
    own_w, north_w, south_w = (both_west(*pair, lane) for pair in (own, north, south))
    halo_e = (halo((north_e[0], south_e[0])), halo((north_e[1], south_e[1])))
    halo_w = (halo((north_w[0], south_w[0])), halo((north_w[1], south_w[1])))
    mid = rows_of(own, north, south)
    mid_e = rows_of(own_e, north_e, south_e)
    mid_w = rows_of(own_w, north_w, south_w)
    couplings = [
        coupled(own_e + halo_e, 1.0),
        coupled(own_w + halo_w, 1.0),
        coupled(mid[0], 1.0),
        coupled(mid[1], 1.0),
        coupled(mid_e[0], 0.5),
        coupled(mid_w[0], 0.5),
        coupled(mid_e[1], 0.5),
        coupled(mid_w[1], 0.5),
    ]
    diag = [
        jnp.where(counts[i] > 0, surfaces[i] + sum(entry[i] for entry in couplings), 1.0) for i in range(4)
    ]
    inverse = [1.0 / diag[i] for i in range(4)]
    couplings = [[entry[i] * inverse[i] for i in range(4)] for entry in couplings]

    def shifted_rows(tiles):
        north, south = [None] * 4, [None] * 4
        for i in range(2):
            a, b = roll(tiles[i], -1, 0), roll(tiles[i + 2], -1, 0)
            north[i], north[i + 2] = jnp.where(sub == 7, b, a), jnp.where(sub == 7, a, b)
            a, b = roll(tiles[i], 1, 0), roll(tiles[i + 2], 1, 0)
            south[i], south[i + 2] = jnp.where(sub == 0, b, a), jnp.where(sub == 0, a, b)
        return north, south

    def spread_out(tiles):
        east = both_east(tiles[0], tiles[1], lane) + both_east(tiles[2], tiles[3], lane)
        west = both_west(tiles[0], tiles[1], lane) + both_west(tiles[2], tiles[3], lane)
        mid_n, mid_s = shifted_rows(tiles)
        east_n, east_s = shifted_rows(east)
        west_n, west_s = shifted_rows(west)
        around = (east, west, mid_n, mid_s, east_n, west_n, east_s, west_s)
        return [sum(entry[i] * values[i] for entry, values in zip(couplings, around)) for i in range(4)]

    found = [[rhs[i] * inverse[i] for i in range(4)]]
    found.append(spread_out(found[0]))
    for _ in range(2, ITERS + 1):
        ahead = spread_out(found[-1])
        found.append([2.0 * ahead[i] - found[-2][i] for i in range(4)])
    for j in range(ITERS + 1):
        vectors[j] = found[j][0]
    diagonal[...] = diag[0]
    right_side[...] = rhs[0]
    weighted = [diag[0] * found[j][0] for j in range(ITERS + 1)]
    sums = [weighted[j] * found[j][0] for j in range(ITERS + 1)]
    sums += [weighted[j] * found[j + 1][0] for j in range(ITERS)]
    row = jnp.zeros((1, COLS), jnp.float32)
    for j, entry in enumerate(sums):
        row = jnp.where(lane[:1, :] == j, jnp.sum(entry, keepdims=True), row)
    partial[...] = jnp.broadcast_to(row, partial.shape)


def combine_kernel(moments, vectors, diagonal, pressure, residual, good):
    size = ITERS + 1
    sums = jnp.sum(moments[...], axis=0, keepdims=True)

    def lane_of(j):
        return jnp.broadcast_to(sums[:, j : j + 1], (ROWS, COLS))

    even = [lane_of(j) for j in range(size)]
    odd = [lane_of(size + j) for j in range(ITERS)]
    mu = []
    for j in range(size):
        mu.append(even[0] if j == 0 else 2.0 * even[j] - even[0])
        if j < ITERS:
            mu.append(odd[0] if j == 0 else 2.0 * odd[j] - odd[0])

    def mass(i, j):
        return 0.5 * (mu[i + j] + mu[abs(i - j)])

    def stiffness(i, j):
        i, j = min(i, j), max(i, j)
        if j == 0:
            return mu[0] - mu[1]
        return mass(i, j) - 0.5 * (mass(i, j + 1) + mass(i, j - 1))

    def form(values, entry):
        out = None
        for i in range(len(values)):
            inner = values[i] * entry(i, i)
            for j in range(i + 1, len(values)):
                inner = inner + 2.0 * values[j] * entry(i, j)
            out = values[i] * inner if out is None else out + values[i] * inner
        return out

    def applied(values):
        out = [value for value in values] + [jnp.zeros_like(values[0])]
        out[1] = out[1] - values[0]
        for j in range(1, len(values)):
            out[j + 1] = out[j + 1] - 0.5 * values[j]
            out[j - 1] = out[j - 1] - 0.5 * values[j]
        return out

    def amplified(values, result):
        total = sum(jnp.abs(value) for value in values)
        return total * total * mu[0] / result

    scaled = [jnp.ones((ROWS, COLS), jnp.float32)]
    direction = list(scaled)
    solution_at = []
    energy = mu[0]
    fine = energy > 0.0
    for step in range(ITERS):
        image = applied(direction)
        curvature = form(direction, stiffness)
        step_size = energy / curvature
        fine = fine & (amplified(direction, curvature) <= SCALAR_BOUND) & (curvature > 0.0)
        solution_at = [
            step_size * value + (solution_at[j] if j < len(solution_at) else 0.0) for j, value in enumerate(direction)
        ]
        scaled = [
            (scaled[j] if j < len(scaled) else 0.0) - step_size * value for j, value in enumerate(image)
        ]
        energy_new = form(scaled, mass)
        bound = SCALAR_BOUND if step + 1 < ITERS else FIELD_BOUND
        fine = fine & (amplified(scaled, energy_new) <= bound) & (energy_new > 0.0)
        if step + 1 < ITERS:
            ratio = energy_new / energy
            direction = [
                scaled[j] + (ratio * direction[j] if j < len(direction) else 0.0) for j in range(len(scaled))
            ]
            energy = energy_new
    pressure[...] = sum(solution_at[j] * vectors[j] for j in range(len(solution_at)))
    residual[...] = diagonal[...] * sum(scaled[j] * vectors[j] for j in range(len(scaled)))
    good[0] = jnp.min(jnp.where(fine, 1, 0).astype(jnp.int32))


def tracers_kernel(
    fold_map, tracer, east_vel, north_vel, diffusion, mixing, count, from_east, from_west, near, far, extra,
    mixed,
    north_rows, south_rows, factors,
):
    lane, sub = lanes(), sublanes()
    levels = count[...]
    group = pl.program_id(0)

    @pl.when(group == 0)
    def _():
        halo_rows(fold_map, near, far, extra, north_rows, south_rows)
        c_prev = jnp.zeros((ROWS, COLS), jnp.float32)
        a_prev = jnp.zeros((ROWS, COLS), jnp.float32)
        for k in range(LEVELS):
            wet = jnp.where(k < levels, 1.0, 0.0)
            u, v, spread = 0.5 * wet * east_vel[k], 0.5 * wet * north_vel[k], wet * diffusion[k]
            a = jnp.where(k + 1 < levels, mixing[k], 0.0)
            inverse = 1.0 / (1.0 + a_prev + a + a_prev * c_prev)
            c_prev = -a * inverse
            factors[0, k] = 1.0 - 4.0 * spread
            factors[1, k] = spread - u
            factors[2, k] = spread + u
            factors[3, k] = spread - v
            factors[4, k] = spread + v
            factors[5, k] = inverse
            factors[6, k] = a_prev
            factors[7, k] = c_prev
            a_prev = a

    row = pl.multiple_of(group * ROWS, ROWS)
    columns_east = from_east[pl.ds(row, ROWS), :]
    columns_west = from_west[pl.ds(row, ROWS), :]
    r_prev = [jnp.zeros((ROWS, COLS), jnp.float32)] * GROUP
    for k in range(LEVELS):
        centre, to_e, to_w, to_n, to_s, inverse, above = (factors[j, k] for j in range(7))
        wet = k < levels
        for t in range(GROUP):
            cell = jnp.where(wet, tracer[t, k], 0.0)
            at = t * LEVELS + k
            halo_row = group * (GROUP * LEVELS) + at
            east = east_of(cell, roll(columns_east, -at, 1), lane)
            west = west_of(cell, roll(columns_west, COLS - 1 - at, 1), lane)
            north = north_of(cell, north_rows[pl.ds(halo_row, 1), :], sub)
            south = south_of(cell, south_rows[pl.ds(halo_row, 1), :], sub)
            explicit = centre * cell + to_e * east + to_w * west + to_n * north + to_s * south
            r_prev[t] = (explicit + above * r_prev[t]) * inverse
            mixed[t, k] = r_prev[t]
    x_next = r_prev
    for k in range(LEVELS - 2, -1, -1):
        below = factors[7, k]
        for t in range(GROUP):
            x_next[t] = mixed[t, k] - below * x_next[t]
            mixed[t, k] = x_next[t]


def extended(cells, sides, width):
    for axis, dim in sides:
        count = lax.axis_size(axis)
        head = lax.slice_in_dim(cells, 0, width, axis=dim)
        tail = lax.slice_in_dim(cells, cells.shape[dim] - width, cells.shape[dim], axis=dim)
        cells = jnp.concatenate(
            [
                lax.ppermute(tail, axis, [(i, (i + 1) % count) for i in range(count)]),
                cells,
                lax.ppermute(head, axis, [((i + 1) % count, i) for i in range(count)]),
            ],
            axis=dim,
        )
    return cells


def extend(field, fold_map):
    rows, cols = field.shape
    padded = extended(field, (("gx", 1), ("gy", 0)), 1)
    total_cols = fold_map.shape[0]
    whole_row = lax.all_gather(field[rows - 1, :], "gx", axis=0, tiled=True)
    start = lax.axis_index("gx") * cols
    wanted = (start - 1 + jnp.arange(cols + 2, dtype=jnp.int32)) % total_cols
    folded = jnp.take(whole_row, jnp.take(fold_map, wanted), axis=0)
    row_index = lax.axis_index("gy")
    upper = jnp.where(row_index == lax.axis_size("gy") - 1, folded, padded[rows + 1, :])
    lower = jnp.where(row_index == 0, 0.0, padded[0, :])
    return jnp.concatenate([lower[None, :], padded[1 : rows + 1, :], upper[None, :]], axis=0)


def window(padded, row_off, col_off):
    rows = padded.shape[0] - 2
    cols = padded.shape[1] - 2
    return padded[1 + row_off : 1 + row_off + rows, 1 + col_off : 1 + col_off + cols]


def total_of(value):
    return lax.psum(jnp.sum(value), BOTH)


def direct_gradients(rhs, level_count, fold_map, surface_term):
    levels = jnp.arange(LEVELS, dtype=jnp.int32)[:, None, None]
    level_mask = (levels < level_count[None]).astype(jnp.float32)
    thick = (0.5 + 1.5 * jnp.arange(LEVELS).astype(jnp.float32) / (LEVELS - 1))[:, None, None]
    depth = jnp.sum(thick * level_mask, axis=0) / LEVELS
    wet_cells = level_count > 0
    depth_pad = extend(depth, fold_map)
    couplings = [
        weight * jnp.minimum(depth, window(depth_pad, row_off, col_off)) for row_off, col_off, weight in NEIGHBOURS
    ]
    diag = jnp.where(wet_cells, surface_term + sum(couplings), 1.0)

    def step(_, state):
        pressure, residual, direction, energy = state
        field_pad = extend(direction, fold_map)
        summed = jnp.zeros_like(direction)
        for entry, (row_off, col_off, _weight) in zip(couplings, NEIGHBOURS):
            summed = summed + entry * window(field_pad, row_off, col_off)
        image = jnp.where(wet_cells, diag * direction - summed, direction)
        step_size = energy / total_of(direction * image)
        pressure = pressure + step_size * direction
        residual = residual - step_size * image
        scaled = residual / diag
        energy_new = total_of(residual * scaled)
        return pressure, residual, scaled + energy_new / energy * direction, energy_new

    scaled = rhs / diag
    state = (jnp.zeros_like(rhs), rhs, scaled, total_of(rhs * scaled))
    state = lax.fori_loop(0, ITERS, step, state)
    return state[0], state[1]


def kernel(body, limit=VMEM_LIMIT, **rest):
    return pl.pallas_call(body, compiler_params=params(limit), **rest)


def shape(*dims):
    return jax.ShapeDtypeStruct(dims, jnp.float32)


def vmem(*dims):
    return pltpu.VMEM(dims, jnp.float32)


def block_of(dims, at=0):
    return pl.BlockSpec(dims, lambda i: (at,) + (0,) * (len(dims) - 1))


def all_of(array):
    return block_of(array.shape)


def shards(sizes, tracer, east_vel, north_vel, diffusion, mixing, count, fold_map, surface):
    nx, ny = sizes
    hbm = pl.BlockSpec(memory_space=pltpu.HBM)
    smem = pl.BlockSpec(memory_space=pltpu.SMEM)
    fields = (east_vel, north_vel, diffusion, mixing)

    def device(x, y):
        return (x % nx) * ny + y

    flat = tracer.reshape(EDGE * ROWS, COLS)
    scratch = [
        vmem(EDGE * ROWS, COLS),
        vmem(4, LEVELS, ROWS, COLS),
        pltpu.VMEM((ROWS, COLS), jnp.int32),
        vmem(ROWS, COLS),
        pltpu.SemaphoreType.DMA((GROUPS + 6,)),
    ]
    to_west, to_east = kernel(
        columns_kernel,
        limit=PACK_VMEM_LIMIT,
        out_shape=(shape(COL_SIZE, COLS), shape(COL_SIZE, COLS)),
        in_specs=[hbm] * 7,
        out_specs=(whole(),) * 2,
        scratch_shapes=scratch,
        name="pack_columns",
    )(flat, *fields, count, surface)

    from_east = lax.ppermute(to_west, BOTH, [(device(x + 1, y), device(x, y)) for x in range(nx) for y in range(ny)])
    from_west = lax.ppermute(to_east, BOTH, [(device(x - 1, y), device(x, y)) for x in range(nx) for y in range(ny)])

    near, far, difference, block = kernel(
        rows_kernel,
        limit=PACK_VMEM_LIMIT,
        out_shape=(
            shape(ROW_SIZE, COLS),
            shape(ROW_SIZE, COLS),
            shape(LEVELS, ROWS, COLS),
            jax.ShapeDtypeStruct((1,), jnp.int32),
        ),
        in_specs=[smem] + [hbm] * 7,
        out_specs=(whole(),) * 3 + (smem,),
        scratch_shapes=scratch,
        cost_estimate=pl.CostEstimate(flops=4000000, bytes_accessed=8000000, transcendentals=0),
        name="pack_rows",
    )(fold_map, flat, *fields, count, surface)

    columns = block_of((COL_SIZE, COLS))
    corner = block_of((ROW_DIFF - ROW_EAST, COLS), ROW_EAST // (ROW_DIFF - ROW_EAST))
    near, far = kernel(
        corners_kernel,
        grid=(1,),
        out_shape=(shape(ROW_SIZE, COLS), shape(ROW_SIZE, COLS)),
        in_specs=[columns, columns] + [pl.BlockSpec(memory_space=pl.ANY)] * 2,
        out_specs=(corner, corner),
        input_output_aliases={2: 0, 3: 1},
        name="put_corners",
    )(from_east, from_west, near, far)
    near = lax.ppermute(near, BOTH, [(device(x, y ^ 1), device(x, y)) for x in range(nx) for y in range(ny)])
    inner = [(device(x, y + 1 if y % 2 else y - 1), device(x, y)) for x in range(nx) for y in range(1, ny - 1)]

    def across(turn):
        return [(device(turn - x, ny - 1), device(x, ny - 1)) for x in range(nx)]

    def exchange(at, rows):
        even, odd = (at, at - 1) if at % 2 == 0 else (at - 1, at)
        return lax.ppermute(rows, BOTH, inner + across(even)), lax.ppermute(rows, BOTH, across(odd))

    far, extra = lax.switch(block[0], [functools.partial(exchange, at) for at in range(nx)], far)

    vectors, diagonal, rhs, partial = kernel(
        krylov_kernel,
        out_shape=(shape(ITERS + 1, ROWS, COLS), shape(ROWS, COLS), shape(ROWS, COLS), shape(nx * ny, COLS)),
        in_specs=[smem] + [whole()] * 12,
        out_specs=(whole(),) * 4,
        scratch_shapes=[vmem(DEEP_SIZE, COLS), vmem(DEEP_SIZE, COLS)],
        name="krylov",
    )(fold_map, difference, *fields, count, surface, from_east, from_west, near, far, extra)

    moments = lax.all_to_all(partial, BOTH, 0, 0)

    batch = pl.BlockSpec((GROUP, LEVELS, ROWS, COLS), lambda i: (i, 0, 0, 0))
    mixed = kernel(
        tracers_kernel,
        grid=(GROUPS,),
        out_shape=shape(TRACERS, LEVELS, ROWS, COLS),
        in_specs=[smem, batch]
        + [all_of(array) for array in (*fields, count)]
        + [block_of((COL_DEEP, COLS))] * 2
        + [block_of((EDGE, COLS))] * 3,
        out_specs=batch,
        scratch_shapes=[vmem(EDGE, COLS), vmem(EDGE, COLS), vmem(8, LEVELS, ROWS, COLS)],
        name="tracers",
    )(fold_map, tracer, *fields, count, from_east, from_west, near, far, extra)

    pressure, residual, good = kernel(
        combine_kernel,
        out_shape=(shape(ROWS, COLS), shape(ROWS, COLS), jax.ShapeDtypeStruct((1,), jnp.int32)),
        in_specs=[whole()] * 3,
        out_specs=(whole(), whole(), smem),
        name="combine",
    )(moments, vectors, diagonal)
    pressure, residual = lax.cond(
        good[0] == 1,
        lambda pressure, residual, rhs, count, surface, fold: (pressure, residual),
        lambda pressure, residual, rhs, count, surface, fold: direct_gradients(rhs, count, fold, surface),
        pressure,
        residual,
        rhs,
        count,
        surface,
        fold_map,
    )
    return mixed, pressure, residual


def solution(mesh):
    in_specs = (
        P(None, None, "gy", "gx"),
        P(None, "gy", "gx"),
        P(None, "gy", "gx"),
        P(None, "gy", "gx"),
        P(None, "gy", "gx"),
        P("gy", "gx"),
        P(),
        P("gy", "gx"),
    )
    out_specs = (P(None, None, "gy", "gx"), P("gy", "gx"), P("gy", "gx"))
    body = functools.partial(shards, (mesh.shape["gx"], mesh.shape["gy"]))
    return jax.shard_map(body, mesh=mesh, in_specs=in_specs, out_specs=out_specs, check_vma=False)
```

```python
import functools

import jax
import jax.numpy as jnp
from jax import lax
from jax.experimental import pallas as pl
from jax.experimental.pallas import tpu as pltpu
from jax.sharding import PartitionSpec as P

ITERS = 4
TRACERS, LEVELS, ROWS, COLS = 16, 20, 8, 128
GROUP = 4
GROUPS = TRACERS // GROUP
DEPTH = 5
EDGE = TRACERS * LEVELS
BOTH = ("gx", "gy")
VMEM_LIMIT = 40 * 1024 * 1024
PACK_VMEM_LIMIT = 63 * 1024 * 1024

COL_DEEP, COL_SIZE = GROUPS * ROWS, (GROUPS + 5) * ROWS
COUNT_LANE, SURFACE_LANE = 100, 105
ROW_EAST, ROW_WEST, ROW_DIFF, ROW_FIELD, ROW_COUNT, ROW_SURFACE, ROW_SIZE = 320, 360, 400, 560, 880, 888, 896
DEEP_SIZE = ROW_SIZE - ROW_EAST

SCALAR_BOUND, FIELD_BOUND = 1500.0, 1.0e5

NEIGHBOURS = [
    (0, 1, 1.0),
    (0, -1, 1.0),
    (1, 0, 1.0),
    (-1, 0, 1.0),
    (1, 1, 0.5),
    (1, -1, 0.5),
    (-1, 1, 0.5),
    (-1, -1, 0.5),
]


def params(limit=VMEM_LIMIT):
    return pltpu.CompilerParams(vmem_limit_bytes=limit)


def whole():
    return pl.BlockSpec(memory_space=pltpu.VMEM)


def lanes():
    return lax.broadcasted_iota(jnp.int32, (ROWS, COLS), 1)


def sublanes():
    return lax.broadcasted_iota(jnp.int32, (ROWS, COLS), 0)


def roll(tile, shift, axis):
    size = tile.shape[axis]
    shift = shift % size
    return tile if shift == 0 else pltpu.roll(tile, shift, axis)


def east_of(tile, beyond, lane):
    return roll(jnp.where(lane == 0, beyond, tile), -1, 1)


def west_of(tile, beyond, lane):
    return roll(jnp.where(lane == COLS - 1, beyond, tile), 1, 1)


def north_of(tile, beyond, sub):
    return roll(jnp.where(sub == 0, beyond, tile), -1, 0)


def south_of(tile, beyond, sub):
    return roll(jnp.where(sub == ROWS - 1, beyond, tile), 1, 0)


def thickness(level):
    return 0.5 + 1.5 * level / (LEVELS - 1)


def turned(tile):
    return jnp.take_along_axis(tile, ROWS - 1 - sublanes(), axis=0)


def start_copies(pairs, ready):
    copies = [pltpu.make_async_copy(source, target, ready.at[i]) for i, (source, target) in enumerate(pairs)]
    for copy in copies:
        copy.start()
    return copies


def pack_kernel(
    tracer, east_vel, north_vel, diffusion, mixing, count, surface, fold_map,
    one, two, near_rows, far_rows, difference, fields, branches,
    cells, levels_ref, surface_ref, fold_ref, ready,
):
    lane = lanes()
    low = sublanes() < ROWS // 2
    size = GROUP * LEVELS * ROWS
    pairs = [(count, levels_ref), (surface, surface_ref)]
    pairs += [(tracer.at[pl.ds(g * size, size)], cells.at[pl.ds(g * size, size)]) for g in range(GROUPS)]
    pairs += [(field, fields.at[f]) for f, field in enumerate((east_vel, north_vel, diffusion, mixing))]
    pairs += [(fold_map, fold_ref)]
    copies = start_copies(pairs, ready)
    here = lax.axis_index("gy")
    even = here % 2 == 0
    is_top = here == lax.axis_size("gy") - 1
    eastward = lax.axis_index("gx") % 2 == 0

    def put(row, items):
        west = jnp.zeros((ROWS, COLS), jnp.float32)
        east = jnp.zeros((ROWS, COLS), jnp.float32)
        for tile, width, first in items:
            chosen = lane == first if width == 1 else (lane >= first) & (lane < first + width)
            west = jnp.where(chosen, roll(tile, first, 1), west)
            east = jnp.where(chosen, roll(tile, first + width, 1), east)
        one[row : row + ROWS, :] = jnp.where(eastward, east, west)
        two[row : row + ROWS, :] = jnp.where(eastward, west, east)

    copies[0].wait()
    copies[1].wait()
    levels, surfaces = levels_ref[...], surface_ref[...]
    depths = levels.astype(jnp.float32)
    per = 2 * LEVELS
    level_row = lax.broadcasted_iota(jnp.int32, (per, COLS), 0)
    level_row = jnp.where(level_row >= LEVELS, level_row - LEVELS, level_row)
    wet_south = level_row < jnp.broadcast_to(levels[:1, :], (per, COLS))
    wet_north = level_row < jnp.broadcast_to(levels[ROWS - 1 :, :], (per, COLS))

    def cell(t, k):
        row = (t * LEVELS + k) * ROWS
        return jnp.where(k < levels, cells[row : row + ROWS, :], 0.0)

    for g in range(GROUPS):
        copies[2 + g].wait()
        put(g * ROWS, [(cell(g * GROUP + t, k), 1, t * LEVELS + k) for t in range(GROUP) for k in range(LEVELS)])
        if g == 0:
            for k in range(LEVELS):
                difference[k] = cell(0, k) - cell(1, k)
            items = [(difference[k], 5, 5 * k) for k in range(LEVELS)]
            put(COL_DEEP, items + [(depths, 5, COUNT_LANE), (surfaces, 4, SURFACE_LANE)])
        for at in range(g * GROUP * LEVELS, (g + 1) * GROUP * LEVELS, per):
            south = jnp.where(wet_south, cells[pl.ds(at * ROWS, per, stride=ROWS), :], 0.0)
            north = jnp.where(wet_north, cells[pl.ds(at * ROWS + ROWS - 1, per, stride=ROWS), :], 0.0)
            near_rows[at : at + per, :] = jnp.where(even, north, south)
            far_rows[at : at + per, :] = jnp.where(even, south, north)
    for f in range(4):
        copies[2 + GROUPS + f].wait()
        put(COL_DEEP + (1 + f) * ROWS, [(fields[f, k], 4, 4 * k) for k in range(LEVELS)])
    copies[-1].wait()
    pole = pole_of(fold_ref)
    offset, block = pole & (COLS - 1), pole >> (COLS.bit_length() - 1)
    inside = (offset >= DEPTH) & (offset < COLS - DEPTH + 1)
    branches[0] = block
    branches[1] = jnp.where(inside, lax.axis_size("gx"), block)

    def pack(kind, out):
        turn = turned if kind == "fold" else (lambda tile: tile)
        for k in range(LEVELS):
            out[ROW_DIFF + ROWS * k : ROW_DIFF + ROWS * (k + 1), :] = turn(difference[k])
        for f in range(4):
            for m in range(LEVELS // 2):
                first, second = turn(fields[f, 2 * m]), turn(fields[f, 2 * m + 1])
                if kind == "north":
                    tile = jnp.where(low, roll(first, 4, 0), second)
                else:
                    tile = jnp.where(low, first, roll(second, 4, 0))
                row = ROW_FIELD + ROWS * (f * (LEVELS // 2) + m)
                out[row : row + ROWS, :] = tile
        out[ROW_COUNT : ROW_COUNT + ROWS, :] = turn(depths)
        out[ROW_SURFACE : ROW_SURFACE + ROWS, :] = turn(surfaces)

    @pl.when(even)
    def _():
        pack("north", near_rows)
        pack("south", far_rows)

    @pl.when(jnp.logical_not(even))
    def _():
        pack("south", near_rows)

    @pl.when(jnp.logical_not(even) & jnp.logical_not(is_top))
    def _():
        pack("north", far_rows)

    @pl.when(is_top)
    def _():
        pack("fold", far_rows)


def sides(one, two, row):
    first, second = one[pl.ds(row, ROWS), :], two[pl.ds(row, ROWS), :]
    eastward = lax.axis_index("gx") % 2 == 0
    return jnp.where(eastward, first, second), jnp.where(eastward, second, first)


def corners_kernel(one, two, near_in, far_in, far_fold, extra_fold, near, far, packed):
    del near_in, far_in, far_fold, extra_fold
    half = ROW_WEST - ROW_EAST
    for row in range(0, half, ROWS):
        for base, value in zip((0, half), sides(one, two, COL_DEEP + row)):
            near[base + row : base + row + ROWS, :] = value
            far[base + row : base + row + ROWS, :] = value
            packed[base + row : base + row + ROWS, :] = turned(value)


def pole_of(fold_map):
    return (fold_map[0] + 1) & (COLS * lax.axis_size("gx") - 1)


def halo_rows(fold_map, near, far, far_fold, extra_fold, north_rows, south_rows):
    here = lax.axis_index("gy")
    top = lax.axis_size("gy") - 1

    @pl.when(here % 2 == 0)
    def _():
        north_rows[...] = near[...]
        south_rows[...] = far[...]

    @pl.when(here % 2 == 1)
    def _():
        south_rows[...] = near[...]

    @pl.when((here % 2 == 1) & (here != top))
    def _():
        north_rows[...] = far[...]

    @pl.when(here == top)
    def _():
        lane = lanes()
        pole = pole_of(fold_map)
        offset = pole & (COLS - 1)
        index = (offset - 1 - lane) & (COLS - 1)
        within_far = (lane >= offset) == ((pole & COLS) != 0)
        for row in range(0, north_rows.shape[0], ROWS):
            rows = jnp.where(within_far, far_fold[row : row + ROWS, :], extra_fold[row : row + ROWS, :])
            north_rows[row : row + ROWS, :] = jnp.take_along_axis(rows, index, axis=1)


def unfold(offset, first_in_far, far, extra, far_packed, extra_packed, out):
    lane = lanes()
    index = (offset - 1 - lane) & (COLS - 1)
    within_far = (lane >= offset) == first_in_far
    zero = jnp.zeros((ROWS, COLS), jnp.float32)

    def store(row, value):
        out[row - ROW_EAST : row - ROW_EAST + ROWS, :] = value

    def flipped(row, sign):
        a, b = far[row : row + ROWS, :], extra[row : row + ROWS, :]
        store(row, sign * jnp.take_along_axis(jnp.where(within_far, a, b), index, axis=1))
        return sign * jnp.take_along_axis(jnp.where(within_far, b, a), index, axis=1)

    def collect(packed, tile, width, at):
        chosen = (lane >= at) & (lane < at + width)
        return jnp.where(chosen, roll(tile, at, 1), packed[0]), jnp.where(chosen, roll(tile, at + width, 1), packed[1])

    def beside_of(first, row):
        row = row - ROW_EAST
        a, b = far_packed[row : row + ROWS, :], extra_packed[row : row + ROWS, :]
        return jnp.where(first_in_far == first, a, b)

    def finish(row, packed, sign, width, within):
        beside = (lane + (offset - 1) + width - 2 * within) & (COLS - 1)
        right = sign * jnp.take_along_axis(beside_of(True, ROW_WEST + row), beside, axis=1)
        beside = (lane + (offset - 1 - COLS) + width - 2 * within) & (COLS - 1)
        left = sign * jnp.take_along_axis(beside_of(False, ROW_EAST + row), beside, axis=1)
        store(ROW_EAST + row, jnp.where(within < offset, packed[0], right))
        store(ROW_WEST + row, jnp.where(within >= offset + width - COLS, packed[1], left))

    packed = (zero, zero)
    for k in range(LEVELS):
        packed = collect(packed, flipped(ROW_DIFF + ROWS * k, 1.0), 5, 5 * k)
    packed = collect(packed, flipped(ROW_COUNT, 1.0), 5, COUNT_LANE)
    packed = collect(packed, flipped(ROW_SURFACE, 1.0), 4, SURFACE_LANE)
    fifth = lane - 5 * ((lane * 205) >> 10)
    finish(0, packed, 1.0, jnp.where(lane >= SURFACE_LANE, 4, 5), fifth)
    for f in range(4):
        sign = -1.0 if f < 2 else 1.0
        packed = (zero, zero)
        for m in range(LEVELS // 2):
            tile = flipped(ROW_FIELD + ROWS * (f * (LEVELS // 2) + m), sign)
            packed = collect(packed, tile, 4, 8 * m)
            packed = collect(packed, roll(tile, 4, 0), 4, 8 * m + 4)
        finish((1 + f) * ROWS, packed, sign, 4, lane & 3)


def unpack(east, west, first, width, lane):
    right = roll(east, -first, 1)
    left = roll(west, -width - first, 1)
    return jnp.where(lane < width, right, jnp.where(lane >= COLS - width, left, 0.0))


def both_east(one, two, lane):
    return east_of(one, two, lane), east_of(two, one, lane)


def both_west(one, two, lane):
    return west_of(one, two, lane), west_of(two, one, lane)


def krylov_kernel(
    fold_map, difference, fields, count, surface, one, two, near, far, far_fold, extra_fold, far_packed, extra_packed,
    vectors, diagonal, right_side, partial,
    north_buf, south_buf,
):
    here = lax.axis_index("gy")
    top = lax.axis_size("gy") - 1
    lane, sub = lanes(), sublanes()
    low = sub < 4
    @pl.when(here % 2 == 0)
    def _():
        north_buf[...] = near[ROW_EAST:, :]
        south_buf[...] = far[ROW_EAST:, :]

    @pl.when(here % 2 == 1)
    def _():
        south_buf[...] = near[ROW_EAST:, :]

    @pl.when((here % 2 == 1) & (here != top))
    def _():
        north_buf[...] = far[ROW_EAST:, :]

    @pl.when(here == top)
    def _():
        pole = pole_of(fold_map)
        unfold(pole & (COLS - 1), (pole & COLS) != 0, far_fold, extra_fold, far_packed, extra_packed, north_buf)

    def at(ref, row):
        return ref[row - ROW_EAST : row - ROW_EAST + ROWS, :]

    def field_tile(ref, f, k):
        return at(ref, ROW_FIELD + ROWS * (f * (LEVELS // 2) + k // 2))

    def halo_main(f, k):
        north, south = field_tile(north_buf, f, k), field_tile(south_buf, f, k)
        return jnp.where(low, roll(north, 4 * (k % 2), 0), roll(south, 4 * (1 - k % 2), 0))

    def side(ref, f, first, width):
        return unpack(at(ref, ROW_EAST + ROWS * f), at(ref, ROW_WEST + ROWS * f), first, width, lane)

    halo_packed = [
        [
            jnp.where(low, at(north_buf, base + ROWS * (1 + f)), at(south_buf, base + ROWS * (1 + f)))
            for base in (ROW_EAST, ROW_WEST)
        ]
        for f in range(4)
    ]

    columns = [sides(one, two, COL_DEEP + ROWS * f) for f in range(5)]

    def column(f):
        return columns[f]

    def neighbours_across(own, north, south):
        up, up_n, up_s = roll(own, -1, 0), roll(north, -1, 0), roll(south, -1, 0)
        down, down_n, down_s = roll(own, 1, 0), roll(north, 1, 0), roll(south, 1, 0)
        return (
            jnp.where(sub == 7, up_n, up),
            jnp.where(low, up_n, jnp.where(sub == 7, up, up_s)),
            jnp.where(sub == 0, down_s, down),
            jnp.where(sub == 0, down, jnp.where(low, down_n, down_s)),
        )

    def halo(pair):
        return jnp.where(low, pair[0], pair[1])

    counts_own = (count[...].astype(jnp.float32), unpack(*column(0), COUNT_LANE, 5, lane))
    counts_north = (at(north_buf, ROW_COUNT), side(north_buf, 0, COUNT_LANE, 5))
    counts_south = (at(south_buf, ROW_COUNT), side(south_buf, 0, COUNT_LANE, 5))
    counts = (counts_own[0], counts_own[1], halo((counts_north[0], counts_south[0])), halo((counts_north[1], counts_south[1])))
    surfaces = (
        surface[...],
        unpack(*column(0), SURFACE_LANE, 4, lane),
        halo((at(north_buf, ROW_SURFACE), at(south_buf, ROW_SURFACE))),
        halo((side(north_buf, 0, SURFACE_LANE, 4), side(south_buf, 0, SURFACE_LANE, 4))),
    )

    zero = jnp.zeros((ROWS, COLS), jnp.float32)
    c_prev, r_prev, a_prev = [zero] * 4, [zero] * 4, [zero] * 4
    c_list, r_list = [], []
    for k in range(LEVELS):
        own = (difference[k], unpack(*column(0), 5 * k, 5, lane))
        north = (at(north_buf, ROW_DIFF + ROWS * k), side(north_buf, 0, 5 * k, 5))
        south = (at(south_buf, ROW_DIFF + ROWS * k), side(south_buf, 0, 5 * k, 5))
        halos = (halo((north[0], south[0])), halo((north[1], south[1])))
        centre = (own[0], own[1], halos[0], halos[1])
        easts = both_east(*own, lane) + both_east(*halos, lane)
        wests = both_west(*own, lane) + both_west(*halos, lane)
        first = neighbours_across(own[0], north[0], south[0])
        second = neighbours_across(own[1], north[1], south[1])
        norths = (first[0], second[0], first[1], second[1])
        souths = (first[2], second[2], first[3], second[3])
        values = [
            (fields[f, k], unpack(*column(1 + f), 4 * k, 4, lane), halo_main(f, k), unpack(*halo_packed[f], 4 * k, 4, lane))
            for f in range(4)
        ]
        c_now, r_now, a_now = [], [], []
        for i in range(4):
            u, v, spread, mix = (value[i] for value in values)
            change = (
                -0.5 * u * (easts[i] - wests[i])
                - 0.5 * v * (norths[i] - souths[i])
                + spread * (easts[i] + wests[i] + norths[i] + souths[i] - 4.0 * centre[i])
            )
            explicit = centre[i] + jnp.where(k < counts[i], change, 0.0)
            a = jnp.where(k + 1 < counts[i], mix, 0.0)
            inverse = 1.0 / (1.0 + a_prev[i] + a + a_prev[i] * c_prev[i])
            c_now.append(-a * inverse)
            r_now.append((explicit + a_prev[i] * r_prev[i]) * inverse)
            a_now.append(a)
        c_prev, r_prev, a_prev = c_now, r_now, a_now
        c_list.append(c_now)
        r_list.append(r_now)
    total, x_next = [zero] * 4, [zero] * 4
    for k in range(LEVELS - 1, -1, -1):
        x_next = [r_list[k][i] - c_list[k][i] * x_next[i] for i in range(4)]
        total = [total[i] + thickness(k) * x_next[i] for i in range(4)]
    rhs = [jnp.where(counts[i] > 0, 0.25 * total[i], 0.0) for i in range(4)]

    def depth_of(levels):
        depth = zero
        for k in range(LEVELS):
            depth = depth + jnp.where(k < levels, thickness(k), 0.0)
        return depth / LEVELS

    own = tuple(depth_of(levels) for levels in counts_own)
    north = tuple(depth_of(levels) for levels in counts_north)
    south = tuple(depth_of(levels) for levels in counts_south)
    depths = (own[0], own[1], halo((north[0], south[0])), halo((north[1], south[1])))

    def rows_of(own, north, south):
        first = neighbours_across(own[0], north[0], south[0])
        second = neighbours_across(own[1], north[1], south[1])
        return (first[0], second[0], first[1], second[1]), (first[2], second[2], first[3], second[3])

    def coupled(others, weight):
        return [weight * jnp.minimum(depths[i], others[i]) for i in range(4)]

    own_e, north_e, south_e = (both_east(*pair, lane) for pair in (own, north, south))
    own_w, north_w, south_w = (both_west(*pair, lane) for pair in (own, north, south))
    halo_e = (halo((north_e[0], south_e[0])), halo((north_e[1], south_e[1])))
    halo_w = (halo((north_w[0], south_w[0])), halo((north_w[1], south_w[1])))
    mid = rows_of(own, north, south)
    mid_e = rows_of(own_e, north_e, south_e)
    mid_w = rows_of(own_w, north_w, south_w)
    couplings = [
        coupled(own_e + halo_e, 1.0),
        coupled(own_w + halo_w, 1.0),
        coupled(mid[0], 1.0),
        coupled(mid[1], 1.0),
        coupled(mid_e[0], 0.5),
        coupled(mid_w[0], 0.5),
        coupled(mid_e[1], 0.5),
        coupled(mid_w[1], 0.5),
    ]
    diag = [
        jnp.where(counts[i] > 0, surfaces[i] + sum(entry[i] for entry in couplings), 1.0) for i in range(4)
    ]
    inverse = [1.0 / diag[i] for i in range(4)]
    couplings = [[entry[i] * inverse[i] for i in range(4)] for entry in couplings]

    def shifted_rows(tiles):
        north, south = [None] * 4, [None] * 4
        for i in range(2):
            a, b = roll(tiles[i], -1, 0), roll(tiles[i + 2], -1, 0)
            north[i], north[i + 2] = jnp.where(sub == 7, b, a), jnp.where(sub == 7, a, b)
            a, b = roll(tiles[i], 1, 0), roll(tiles[i + 2], 1, 0)
            south[i], south[i + 2] = jnp.where(sub == 0, b, a), jnp.where(sub == 0, a, b)
        return north, south

    def spread_out(tiles):
        east = both_east(tiles[0], tiles[1], lane) + both_east(tiles[2], tiles[3], lane)
        west = both_west(tiles[0], tiles[1], lane) + both_west(tiles[2], tiles[3], lane)
        mid_n, mid_s = shifted_rows(tiles)
        east_n, east_s = shifted_rows(east)
        west_n, west_s = shifted_rows(west)
        around = (east, west, mid_n, mid_s, east_n, west_n, east_s, west_s)
        return [sum(entry[i] * values[i] for entry, values in zip(couplings, around)) for i in range(4)]

    found = [[rhs[i] * inverse[i] for i in range(4)]]
    found.append(spread_out(found[0]))
    for _ in range(2, ITERS + 1):
        ahead = spread_out(found[-1])
        found.append([2.0 * ahead[i] - found[-2][i] for i in range(4)])
    for j in range(ITERS + 1):
        vectors[j] = found[j][0]
    diagonal[...] = diag[0]
    right_side[...] = rhs[0]
    weighted = [diag[0] * found[j][0] for j in range(ITERS + 1)]
    sums = [weighted[j] * found[j][0] for j in range(ITERS + 1)]
    sums += [weighted[j] * found[j + 1][0] for j in range(ITERS)]
    row = jnp.zeros((1, COLS), jnp.float32)
    for j, entry in enumerate(sums):
        row = jnp.where(lane[:1, :] == j, jnp.sum(entry, keepdims=True), row)
    partial[...] = jnp.broadcast_to(row, partial.shape)


def combine_kernel(moments, vectors, diagonal, pressure, residual, good):
    size = ITERS + 1
    sums = jnp.sum(moments[...], axis=0, keepdims=True)

    def lane_of(j):
        return jnp.broadcast_to(sums[:, j : j + 1], (ROWS, COLS))

    even = [lane_of(j) for j in range(size)]
    odd = [lane_of(size + j) for j in range(ITERS)]
    mu = []
    for j in range(size):
        mu.append(even[0] if j == 0 else 2.0 * even[j] - even[0])
        if j < ITERS:
            mu.append(odd[0] if j == 0 else 2.0 * odd[j] - odd[0])

    def mass(i, j):
        return 0.5 * (mu[i + j] + mu[abs(i - j)])

    def stiffness(i, j):
        i, j = min(i, j), max(i, j)
        if j == 0:
            return mu[0] - mu[1]
        return mass(i, j) - 0.5 * (mass(i, j + 1) + mass(i, j - 1))

    def form(values, entry):
        out = None
        for i in range(len(values)):
            inner = values[i] * entry(i, i)
            for j in range(i + 1, len(values)):
                inner = inner + 2.0 * values[j] * entry(i, j)
            out = values[i] * inner if out is None else out + values[i] * inner
        return out

    def applied(values):
        out = [value for value in values] + [jnp.zeros_like(values[0])]
        out[1] = out[1] - values[0]
        for j in range(1, len(values)):
            out[j + 1] = out[j + 1] - 0.5 * values[j]
            out[j - 1] = out[j - 1] - 0.5 * values[j]
        return out

    def amplified(values, result):
        total = sum(jnp.abs(value) for value in values)
        return total * total * mu[0] / result

    scaled = [jnp.ones((ROWS, COLS), jnp.float32)]
    direction = list(scaled)
    solution_at = []
    energy = mu[0]
    fine = energy > 0.0
    for step in range(ITERS):
        image = applied(direction)
        curvature = form(direction, stiffness)
        step_size = energy / curvature
        fine = fine & (amplified(direction, curvature) <= SCALAR_BOUND) & (curvature > 0.0)
        solution_at = [
            step_size * value + (solution_at[j] if j < len(solution_at) else 0.0) for j, value in enumerate(direction)
        ]
        scaled = [
            (scaled[j] if j < len(scaled) else 0.0) - step_size * value for j, value in enumerate(image)
        ]
        energy_new = form(scaled, mass)
        bound = SCALAR_BOUND if step + 1 < ITERS else FIELD_BOUND
        fine = fine & (amplified(scaled, energy_new) <= bound) & (energy_new > 0.0)
        if step + 1 < ITERS:
            ratio = energy_new / energy
            direction = [
                scaled[j] + (ratio * direction[j] if j < len(direction) else 0.0) for j in range(len(scaled))
            ]
            energy = energy_new
    pressure[...] = sum(solution_at[j] * vectors[j] for j in range(len(solution_at)))
    residual[...] = diagonal[...] * sum(scaled[j] * vectors[j] for j in range(len(scaled)))
    good[0] = jnp.min(jnp.where(fine, 1, 0).astype(jnp.int32))


def tracers_kernel(
    fold_map, tracer, fields, count, one, two, near, far, far_fold, extra_fold,
    mixed,
    north_rows, south_rows, factors,
):
    lane, sub = lanes(), sublanes()
    levels = count[...]
    group = pl.program_id(0)

    @pl.when(group == 0)
    def _():
        halo_rows(fold_map, near, far, far_fold, extra_fold, north_rows, south_rows)
        c_prev = jnp.zeros((ROWS, COLS), jnp.float32)
        a_prev = jnp.zeros((ROWS, COLS), jnp.float32)
        for k in range(LEVELS):
            wet = jnp.where(k < levels, 1.0, 0.0)
            u, v, spread = 0.5 * wet * fields[0, k], 0.5 * wet * fields[1, k], wet * fields[2, k]
            a = jnp.where(k + 1 < levels, fields[3, k], 0.0)
            inverse = 1.0 / (1.0 + a_prev + a + a_prev * c_prev)
            c_prev = -a * inverse
            factors[0, k] = 1.0 - 4.0 * spread
            factors[1, k] = spread - u
            factors[2, k] = spread + u
            factors[3, k] = spread - v
            factors[4, k] = spread + v
            factors[5, k] = inverse
            factors[6, k] = a_prev
            factors[7, k] = c_prev
            a_prev = a

    row = pl.multiple_of(group * ROWS, ROWS)
    columns_east, columns_west = sides(one, two, row)
    r_prev = [jnp.zeros((ROWS, COLS), jnp.float32)] * GROUP
    for k in range(LEVELS):
        centre, to_e, to_w, to_n, to_s, inverse, above = (factors[j, k] for j in range(7))
        wet = k < levels
        for t in range(GROUP):
            cell = jnp.where(wet, tracer[t, k], 0.0)
            at = t * LEVELS + k
            halo_row = group * (GROUP * LEVELS) + at
            east = east_of(cell, roll(columns_east, -at, 1), lane)
            west = west_of(cell, roll(columns_west, COLS - 1 - at, 1), lane)
            north = north_of(cell, north_rows[pl.ds(halo_row, 1), :], sub)
            south = south_of(cell, south_rows[pl.ds(halo_row, 1), :], sub)
            explicit = centre * cell + to_e * east + to_w * west + to_n * north + to_s * south
            r_prev[t] = (explicit + above * r_prev[t]) * inverse
            mixed[t, k] = r_prev[t]
    x_next = r_prev
    for k in range(LEVELS - 2, -1, -1):
        below = factors[7, k]
        for t in range(GROUP):
            x_next[t] = mixed[t, k] - below * x_next[t]
            mixed[t, k] = x_next[t]


def extended(cells, sides, width):
    for axis, dim in sides:
        count = lax.axis_size(axis)
        head = lax.slice_in_dim(cells, 0, width, axis=dim)
        tail = lax.slice_in_dim(cells, cells.shape[dim] - width, cells.shape[dim], axis=dim)
        cells = jnp.concatenate(
            [
                lax.ppermute(tail, axis, [(i, (i + 1) % count) for i in range(count)]),
                cells,
                lax.ppermute(head, axis, [((i + 1) % count, i) for i in range(count)]),
            ],
            axis=dim,
        )
    return cells


def extend(field, fold_map):
    rows, cols = field.shape
    padded = extended(field, (("gx", 1), ("gy", 0)), 1)
    total_cols = fold_map.shape[0]
    whole_row = lax.all_gather(field[rows - 1, :], "gx", axis=0, tiled=True)
    start = lax.axis_index("gx") * cols
    wanted = (start - 1 + jnp.arange(cols + 2, dtype=jnp.int32)) % total_cols
    folded = jnp.take(whole_row, jnp.take(fold_map, wanted), axis=0)
    row_index = lax.axis_index("gy")
    upper = jnp.where(row_index == lax.axis_size("gy") - 1, folded, padded[rows + 1, :])
    lower = jnp.where(row_index == 0, 0.0, padded[0, :])
    return jnp.concatenate([lower[None, :], padded[1 : rows + 1, :], upper[None, :]], axis=0)


def window(padded, row_off, col_off):
    rows = padded.shape[0] - 2
    cols = padded.shape[1] - 2
    return padded[1 + row_off : 1 + row_off + rows, 1 + col_off : 1 + col_off + cols]


def total_of(value):
    return lax.psum(jnp.sum(value), BOTH)


def direct_gradients(rhs, level_count, fold_map, surface_term):
    levels = jnp.arange(LEVELS, dtype=jnp.int32)[:, None, None]
    level_mask = (levels < level_count[None]).astype(jnp.float32)
    thick = (0.5 + 1.5 * jnp.arange(LEVELS).astype(jnp.float32) / (LEVELS - 1))[:, None, None]
    depth = jnp.sum(thick * level_mask, axis=0) / LEVELS
    wet_cells = level_count > 0
    depth_pad = extend(depth, fold_map)
    couplings = [
        weight * jnp.minimum(depth, window(depth_pad, row_off, col_off)) for row_off, col_off, weight in NEIGHBOURS
    ]
    diag = jnp.where(wet_cells, surface_term + sum(couplings), 1.0)

    def step(_, state):
        pressure, residual, direction, energy = state
        field_pad = extend(direction, fold_map)
        summed = jnp.zeros_like(direction)
        for entry, (row_off, col_off, _weight) in zip(couplings, NEIGHBOURS):
            summed = summed + entry * window(field_pad, row_off, col_off)
        image = jnp.where(wet_cells, diag * direction - summed, direction)
        step_size = energy / total_of(direction * image)
        pressure = pressure + step_size * direction
        residual = residual - step_size * image
        scaled = residual / diag
        energy_new = total_of(residual * scaled)
        return pressure, residual, scaled + energy_new / energy * direction, energy_new

    scaled = rhs / diag
    state = (jnp.zeros_like(rhs), rhs, scaled, total_of(rhs * scaled))
    state = lax.fori_loop(0, ITERS, step, state)
    return state[0], state[1]


def kernel(body, limit=VMEM_LIMIT, **rest):
    return pl.pallas_call(body, compiler_params=params(limit), **rest)


def shape(*dims):
    return jax.ShapeDtypeStruct(dims, jnp.float32)


def vmem(*dims):
    return pltpu.VMEM(dims, jnp.float32)


def block_of(dims, at=0):
    return pl.BlockSpec(dims, lambda i: (at,) + (0,) * (len(dims) - 1))


def all_of(array):
    return block_of(array.shape)


def shards(sizes, tracer, east_vel, north_vel, diffusion, mixing, count, fold_map, surface):
    nx, ny = sizes
    hbm = pl.BlockSpec(memory_space=pltpu.HBM)
    smem = pl.BlockSpec(memory_space=pltpu.SMEM)
    fields = (east_vel, north_vel, diffusion, mixing)

    def device(x, y):
        return (x % nx) * ny + y

    one, two, near, far, difference, coefficients, branches = kernel(
        pack_kernel,
        limit=PACK_VMEM_LIMIT,
        out_shape=(
            shape(COL_SIZE, COLS),
            shape(COL_SIZE, COLS),
            shape(ROW_SIZE, COLS),
            shape(ROW_SIZE, COLS),
            shape(LEVELS, ROWS, COLS),
            shape(4, LEVELS, ROWS, COLS),
            jax.ShapeDtypeStruct((2,), jnp.int32),
        ),
        in_specs=[hbm] * 8,
        out_specs=(whole(),) * 6 + (smem,),
        scratch_shapes=[
            vmem(EDGE * ROWS, COLS),
            pltpu.VMEM((ROWS, COLS), jnp.int32),
            vmem(ROWS, COLS),
            pltpu.SMEM(fold_map.shape, jnp.int32),
            pltpu.SemaphoreType.DMA((GROUPS + 7,)),
        ],
        name="pack",
    )(tracer.reshape(EDGE * ROWS, COLS), *fields, count, surface, fold_map)

    def across(turn, rows):
        return lax.ppermute(rows, BOTH, [(device(turn - x, ny - 1), device(x, ny - 1)) for x in range(nx)])

    def over_fold(at, rows):
        even, odd = (at, at - 1) if at % 2 == 0 else (at - 1, at)
        return across(even, rows), across(odd, rows)

    def nothing(rows):
        return jnp.zeros_like(rows), jnp.zeros_like(rows)

    exchanges = [functools.partial(over_fold, at) for at in range(nx)]
    one = lax.ppermute(one, BOTH, [(device(x ^ 1, y), device(x, y)) for x in range(nx) for y in range(ny)])
    two = lax.ppermute(
        two, BOTH, [(device(x + 1 if x % 2 else x - 1, y), device(x, y)) for x in range(nx) for y in range(ny)]
    )
    far_fold, extra_fold = lax.switch(branches[0], exchanges, far)

    columns = block_of((COL_SIZE, COLS))
    corner = block_of((ROW_DIFF - ROW_EAST, COLS), ROW_EAST // (ROW_DIFF - ROW_EAST))
    near, far, packed = kernel(
        corners_kernel,
        grid=(1,),
        out_shape=(shape(ROW_SIZE, COLS), shape(ROW_SIZE, COLS), shape(ROW_DIFF - ROW_EAST, COLS)),
        in_specs=[columns, columns] + [pl.BlockSpec(memory_space=pl.ANY)] * 4,
        out_specs=(corner, corner, block_of((ROW_DIFF - ROW_EAST, COLS))),
        input_output_aliases={2: 0, 3: 1},
        name="put_corners",
    )(one, two, near, far, far_fold, extra_fold)
    near = lax.ppermute(near, BOTH, [(device(x, y ^ 1), device(x, y)) for x in range(nx) for y in range(ny)])
    far = lax.ppermute(
        far, BOTH, [(device(x, y + 1 if y % 2 else y - 1), device(x, y)) for x in range(nx) for y in range(1, ny - 1)]
    )
    far_packed, extra_packed = lax.switch(branches[1], exchanges + [nothing], packed)

    vectors, diagonal, rhs, partial = kernel(
        krylov_kernel,
        out_shape=(shape(ITERS + 1, ROWS, COLS), shape(ROWS, COLS), shape(ROWS, COLS), shape(nx * ny, COLS)),
        in_specs=[smem] + [whole()] * 12,
        out_specs=(whole(),) * 4,
        scratch_shapes=[vmem(DEEP_SIZE, COLS), vmem(DEEP_SIZE, COLS)],
        name="krylov",
    )(
        fold_map, difference, coefficients, count, surface, one, two, near, far,
        far_fold, extra_fold, far_packed, extra_packed,
    )

    moments = lax.all_to_all(partial, BOTH, 0, 0)

    batch = pl.BlockSpec((GROUP, LEVELS, ROWS, COLS), lambda i: (i, 0, 0, 0))
    mixed = kernel(
        tracers_kernel,
        grid=(GROUPS,),
        out_shape=shape(TRACERS, LEVELS, ROWS, COLS),
        in_specs=[smem, batch, all_of(coefficients), all_of(count)]
        + [block_of((COL_DEEP, COLS))] * 2
        + [block_of((EDGE, COLS))] * 4,
        out_specs=batch,
        scratch_shapes=[vmem(EDGE, COLS), vmem(EDGE, COLS), vmem(8, LEVELS, ROWS, COLS)],
        name="tracers",
    )(fold_map, tracer, coefficients, count, one, two, near, far, far_fold, extra_fold)

    pressure, residual, good = kernel(
        combine_kernel,
        out_shape=(shape(ROWS, COLS), shape(ROWS, COLS), jax.ShapeDtypeStruct((1,), jnp.int32)),
        in_specs=[whole()] * 3,
        out_specs=(whole(), whole(), smem),
        name="combine",
    )(moments, vectors, diagonal)
    pressure, residual = lax.cond(
        good[0] == 1,
        lambda pressure, residual, rhs, count, surface, fold: (pressure, residual),
        lambda pressure, residual, rhs, count, surface, fold: direct_gradients(rhs, count, fold, surface),
        pressure,
        residual,
        rhs,
        count,
        surface,
        fold_map,
    )
    return mixed, pressure, residual


def solution(mesh):
    in_specs = (
        P(None, None, "gy", "gx"),
        P(None, "gy", "gx"),
        P(None, "gy", "gx"),
        P(None, "gy", "gx"),
        P(None, "gy", "gx"),
        P("gy", "gx"),
        P(),
        P("gy", "gx"),
    )
    out_specs = (P(None, None, "gy", "gx"), P("gy", "gx"), P("gy", "gx"))
    body = functools.partial(shards, (mesh.shape["gx"], mesh.shape["gy"]))
    return jax.shard_map(body, mesh=mesh, in_specs=in_specs, out_specs=out_specs, check_vma=False)
```

```python
import functools

import jax
import jax.numpy as jnp
from jax import lax
from jax.experimental import pallas as pl
from jax.experimental.pallas import tpu as pltpu
from jax.sharding import PartitionSpec as P

ITERS = 4
TRACERS, LEVELS, ROWS, COLS = 16, 20, 8, 128
GROUP = 4
GROUPS = TRACERS // GROUP
DEPTH = 5
EDGE = TRACERS * LEVELS
BOTH = ("gx", "gy")
VMEM_LIMIT = 40 * 1024 * 1024
PACK_VMEM_LIMIT = 63 * 1024 * 1024

COL_DEEP, COL_SIZE = GROUPS * ROWS, (GROUPS + 5) * ROWS
COUNT_LANE, SURFACE_LANE = 100, 105
ROW_EAST, ROW_WEST, ROW_DIFF, ROW_FIELD, ROW_COUNT, ROW_SURFACE, ROW_SIZE = 320, 360, 400, 560, 880, 888, 896
DEEP_SIZE = ROW_SIZE - ROW_EAST

SCALAR_BOUND, FIELD_BOUND = 1500.0, 1.0e5

NEIGHBOURS = [
    (0, 1, 1.0),
    (0, -1, 1.0),
    (1, 0, 1.0),
    (-1, 0, 1.0),
    (1, 1, 0.5),
    (1, -1, 0.5),
    (-1, 1, 0.5),
    (-1, -1, 0.5),
]


def params(limit=VMEM_LIMIT):
    return pltpu.CompilerParams(vmem_limit_bytes=limit)


def whole():
    return pl.BlockSpec(memory_space=pltpu.VMEM)


def lanes():
    return lax.broadcasted_iota(jnp.int32, (ROWS, COLS), 1)


def sublanes():
    return lax.broadcasted_iota(jnp.int32, (ROWS, COLS), 0)


def roll(tile, shift, axis):
    size = tile.shape[axis]
    shift = shift % size
    return tile if shift == 0 else pltpu.roll(tile, shift, axis)


def east_of(tile, beyond, lane):
    return roll(jnp.where(lane == 0, beyond, tile), -1, 1)


def west_of(tile, beyond, lane):
    return roll(jnp.where(lane == COLS - 1, beyond, tile), 1, 1)


def north_of(tile, beyond, sub):
    return roll(jnp.where(sub == 0, beyond, tile), -1, 0)


def south_of(tile, beyond, sub):
    return roll(jnp.where(sub == ROWS - 1, beyond, tile), 1, 0)


def thickness(level):
    return 0.5 + 1.5 * level / (LEVELS - 1)


def turned(tile):
    return jnp.take_along_axis(tile, ROWS - 1 - sublanes(), axis=0)


def start_copies(pairs, ready):
    copies = [pltpu.make_async_copy(source, target, ready.at[i]) for i, (source, target) in enumerate(pairs)]
    for copy in copies:
        copy.start()
    return copies


def pack_kernel(
    tracer, east_vel, north_vel, diffusion, mixing, count, surface, fold_map,
    one, two, near_rows, far_rows, fold_rows, difference, fields, branches,
    cells, levels_ref, surface_ref, fold_ref, ready,
):
    lane = lanes()
    low = sublanes() < ROWS // 2
    size = GROUP * LEVELS * ROWS
    pairs = [(count, levels_ref), (surface, surface_ref)]
    pairs += [(tracer.at[pl.ds(g * size, size)], cells.at[pl.ds(g * size, size)]) for g in range(GROUPS)]
    pairs += [(field, fields.at[f]) for f, field in enumerate((east_vel, north_vel, diffusion, mixing))]
    pairs += [(fold_map, fold_ref)]
    copies = start_copies(pairs, ready)
    here = lax.axis_index("gy")
    even = here % 2 == 0
    is_top = here == lax.axis_size("gy") - 1
    eastward = lax.axis_index("gx") % 2 == 0

    def put(row, items):
        west = jnp.zeros((ROWS, COLS), jnp.float32)
        east = jnp.zeros((ROWS, COLS), jnp.float32)
        for tile, width, first in items:
            chosen = lane == first if width == 1 else (lane >= first) & (lane < first + width)
            west = jnp.where(chosen, roll(tile, first, 1), west)
            east = jnp.where(chosen, roll(tile, first + width, 1), east)
        one[row : row + ROWS, :] = jnp.where(eastward, east, west)
        two[row : row + ROWS, :] = jnp.where(eastward, west, east)

    copies[0].wait()
    copies[1].wait()
    levels, surfaces = levels_ref[...], surface_ref[...]
    depths = levels.astype(jnp.float32)
    per = 2 * LEVELS
    level_row = lax.broadcasted_iota(jnp.int32, (per, COLS), 0)
    level_row = jnp.where(level_row >= LEVELS, level_row - LEVELS, level_row)
    wet_south = level_row < jnp.broadcast_to(levels[:1, :], (per, COLS))
    wet_north = level_row < jnp.broadcast_to(levels[ROWS - 1 :, :], (per, COLS))

    def cell(t, k):
        row = (t * LEVELS + k) * ROWS
        return jnp.where(k < levels, cells[row : row + ROWS, :], 0.0)

    for g in range(GROUPS):
        copies[2 + g].wait()
        put(g * ROWS, [(cell(g * GROUP + t, k), 1, t * LEVELS + k) for t in range(GROUP) for k in range(LEVELS)])
        if g == 0:
            for k in range(LEVELS):
                difference[k] = cell(0, k) - cell(1, k)
            items = [(difference[k], 5, 5 * k) for k in range(LEVELS)]
            put(COL_DEEP, items + [(depths, 5, COUNT_LANE), (surfaces, 4, SURFACE_LANE)])
        for at in range(g * GROUP * LEVELS, (g + 1) * GROUP * LEVELS, per):
            south = jnp.where(wet_south, cells[pl.ds(at * ROWS, per, stride=ROWS), :], 0.0)
            north = jnp.where(wet_north, cells[pl.ds(at * ROWS + ROWS - 1, per, stride=ROWS), :], 0.0)
            near_rows[at : at + per, :] = jnp.where(even, north, south)
            far_rows[at : at + per, :] = jnp.where(even, south, north)
    for f in range(4):
        copies[2 + GROUPS + f].wait()
        put(COL_DEEP + (1 + f) * ROWS, [(fields[f, k], 4, 4 * k) for k in range(LEVELS)])
    copies[-1].wait()
    pole = pole_of(fold_ref)
    offset, block = pole & (COLS - 1), pole >> (COLS.bit_length() - 1)
    inside = (offset >= DEPTH) & (offset < COLS - DEPTH + 1)
    branches[0] = jnp.where(inside, block, block + lax.axis_size("gx"))

    def pack(kind, out):
        turn = turned if kind == "fold" else (lambda tile: tile)
        for k in range(LEVELS):
            out[ROW_DIFF + ROWS * k : ROW_DIFF + ROWS * (k + 1), :] = turn(difference[k])
        for f in range(4):
            for m in range(LEVELS // 2):
                first, second = turn(fields[f, 2 * m]), turn(fields[f, 2 * m + 1])
                if kind == "north":
                    tile = jnp.where(low, roll(first, 4, 0), second)
                else:
                    tile = jnp.where(low, first, roll(second, 4, 0))
                row = ROW_FIELD + ROWS * (f * (LEVELS // 2) + m)
                out[row : row + ROWS, :] = tile
        out[ROW_COUNT : ROW_COUNT + ROWS, :] = turn(depths)
        out[ROW_SURFACE : ROW_SURFACE + ROWS, :] = turn(surfaces)

    @pl.when(even)
    def _():
        pack("north", near_rows)
        pack("south", far_rows)

    @pl.when(jnp.logical_not(even))
    def _():
        pack("south", near_rows)

    @pl.when(jnp.logical_not(even) & jnp.logical_not(is_top))
    def _():
        pack("north", far_rows)

    @pl.when(is_top)
    def _():
        fold_rows[:ROW_EAST, :] = far_rows[:ROW_EAST, :]
        pack("fold", fold_rows)


def sides(one, two, row):
    first, second = one[pl.ds(row, ROWS), :], two[pl.ds(row, ROWS), :]
    eastward = lax.axis_index("gx") % 2 == 0
    return jnp.where(eastward, first, second), jnp.where(eastward, second, first)


def corners_kernel(one, two, near_in, far_in, near, far, packed):
    del near_in, far_in
    half = ROW_WEST - ROW_EAST
    for row in range(0, half, ROWS):
        for base, value in zip((0, half), sides(one, two, COL_DEEP + row)):
            near[base + row : base + row + ROWS, :] = value
            far[base + row : base + row + ROWS, :] = value
            packed[base + row : base + row + ROWS, :] = turned(value)


def pole_of(fold_map):
    return (fold_map[0] + 1) & (COLS * lax.axis_size("gx") - 1)


def halo_rows(fold_map, near, far, far_fold, extra_fold, north_rows, south_rows):
    here = lax.axis_index("gy")
    top = lax.axis_size("gy") - 1

    @pl.when(here % 2 == 0)
    def _():
        north_rows[...] = near[...]
        south_rows[...] = far[...]

    @pl.when(here % 2 == 1)
    def _():
        south_rows[...] = near[...]

    @pl.when((here % 2 == 1) & (here != top))
    def _():
        north_rows[...] = far[...]

    @pl.when(here == top)
    def _():
        lane = lanes()
        pole = pole_of(fold_map)
        offset = pole & (COLS - 1)
        index = (offset - 1 - lane) & (COLS - 1)
        within_far = (lane >= offset) == ((pole & COLS) != 0)
        for row in range(0, north_rows.shape[0], ROWS):
            rows = jnp.where(within_far, far_fold[row : row + ROWS, :], extra_fold[row : row + ROWS, :])
            north_rows[row : row + ROWS, :] = jnp.take_along_axis(rows, index, axis=1)


def unfold(offset, first_in_far, far, extra, fold_packed, out):
    lane = lanes()
    index = (offset - 1 - lane) & (COLS - 1)
    within_far = (lane >= offset) == first_in_far
    zero = jnp.zeros((ROWS, COLS), jnp.float32)

    def store(row, value):
        out[row - ROW_EAST : row - ROW_EAST + ROWS, :] = value

    def flipped(row, sign):
        a, b = far[row : row + ROWS, :], extra[row : row + ROWS, :]
        store(row, sign * jnp.take_along_axis(jnp.where(within_far, a, b), index, axis=1))
        return sign * jnp.take_along_axis(jnp.where(within_far, b, a), index, axis=1)

    def collect(packed, tile, width, at):
        chosen = (lane >= at) & (lane < at + width)
        return jnp.where(chosen, roll(tile, at, 1), packed[0]), jnp.where(chosen, roll(tile, at + width, 1), packed[1])

    def beside_of(first, row):
        row = row - ROW_EAST
        half = ROW_DIFF - ROW_EAST
        a, b = fold_packed[row : row + ROWS, :], fold_packed[half + row : half + row + ROWS, :]
        return jnp.where(first_in_far == first, a, b)

    def finish(row, packed, sign, width, within):
        beside = (lane + (offset - 1) + width - 2 * within) & (COLS - 1)
        right = sign * jnp.take_along_axis(beside_of(True, ROW_WEST + row), beside, axis=1)
        beside = (lane + (offset - 1 - COLS) + width - 2 * within) & (COLS - 1)
        left = sign * jnp.take_along_axis(beside_of(False, ROW_EAST + row), beside, axis=1)
        store(ROW_EAST + row, jnp.where(within < offset, packed[0], right))
        store(ROW_WEST + row, jnp.where(within >= offset + width - COLS, packed[1], left))

    packed = (zero, zero)
    for k in range(LEVELS):
        packed = collect(packed, flipped(ROW_DIFF + ROWS * k, 1.0), 5, 5 * k)
    packed = collect(packed, flipped(ROW_COUNT, 1.0), 5, COUNT_LANE)
    packed = collect(packed, flipped(ROW_SURFACE, 1.0), 4, SURFACE_LANE)
    fifth = lane - 5 * ((lane * 205) >> 10)
    finish(0, packed, 1.0, jnp.where(lane >= SURFACE_LANE, 4, 5), fifth)
    for f in range(4):
        sign = -1.0 if f < 2 else 1.0
        packed = (zero, zero)
        for m in range(LEVELS // 2):
            tile = flipped(ROW_FIELD + ROWS * (f * (LEVELS // 2) + m), sign)
            packed = collect(packed, tile, 4, 8 * m)
            packed = collect(packed, roll(tile, 4, 0), 4, 8 * m + 4)
        finish((1 + f) * ROWS, packed, sign, 4, lane & 3)


def unpack(east, west, first, width, lane):
    right = roll(east, -first, 1)
    left = roll(west, -width - first, 1)
    return jnp.where(lane < width, right, jnp.where(lane >= COLS - width, left, 0.0))


def both_east(one, two, lane):
    return east_of(one, two, lane), east_of(two, one, lane)


def both_west(one, two, lane):
    return west_of(one, two, lane), west_of(two, one, lane)


def krylov_kernel(
    fold_map, difference, fields, count, surface, one, two, near, far, far_fold, extra_fold, fold_packed,
    vectors, diagonal, right_side, partial,
    north_buf, south_buf,
):
    here = lax.axis_index("gy")
    top = lax.axis_size("gy") - 1
    lane, sub = lanes(), sublanes()
    low = sub < 4
    @pl.when(here % 2 == 0)
    def _():
        north_buf[...] = near[ROW_EAST:, :]
        south_buf[...] = far[ROW_EAST:, :]

    @pl.when(here % 2 == 1)
    def _():
        south_buf[...] = near[ROW_EAST:, :]

    @pl.when((here % 2 == 1) & (here != top))
    def _():
        north_buf[...] = far[ROW_EAST:, :]

    @pl.when(here == top)
    def _():
        pole = pole_of(fold_map)
        unfold(pole & (COLS - 1), (pole & COLS) != 0, far_fold, extra_fold, fold_packed, north_buf)

    def at(ref, row):
        return ref[row - ROW_EAST : row - ROW_EAST + ROWS, :]

    def field_tile(ref, f, k):
        return at(ref, ROW_FIELD + ROWS * (f * (LEVELS // 2) + k // 2))

    def halo_main(f, k):
        north, south = field_tile(north_buf, f, k), field_tile(south_buf, f, k)
        return jnp.where(low, roll(north, 4 * (k % 2), 0), roll(south, 4 * (1 - k % 2), 0))

    def side(ref, f, first, width):
        return unpack(at(ref, ROW_EAST + ROWS * f), at(ref, ROW_WEST + ROWS * f), first, width, lane)

    halo_packed = [
        [
            jnp.where(low, at(north_buf, base + ROWS * (1 + f)), at(south_buf, base + ROWS * (1 + f)))
            for base in (ROW_EAST, ROW_WEST)
        ]
        for f in range(4)
    ]

    columns = [sides(one, two, COL_DEEP + ROWS * f) for f in range(5)]

    def column(f):
        return columns[f]

    def neighbours_across(own, north, south):
        up, up_n, up_s = roll(own, -1, 0), roll(north, -1, 0), roll(south, -1, 0)
        down, down_n, down_s = roll(own, 1, 0), roll(north, 1, 0), roll(south, 1, 0)
        return (
            jnp.where(sub == 7, up_n, up),
            jnp.where(low, up_n, jnp.where(sub == 7, up, up_s)),
            jnp.where(sub == 0, down_s, down),
            jnp.where(sub == 0, down, jnp.where(low, down_n, down_s)),
        )

    def halo(pair):
        return jnp.where(low, pair[0], pair[1])

    counts_own = (count[...].astype(jnp.float32), unpack(*column(0), COUNT_LANE, 5, lane))
    counts_north = (at(north_buf, ROW_COUNT), side(north_buf, 0, COUNT_LANE, 5))
    counts_south = (at(south_buf, ROW_COUNT), side(south_buf, 0, COUNT_LANE, 5))
    counts = (counts_own[0], counts_own[1], halo((counts_north[0], counts_south[0])), halo((counts_north[1], counts_south[1])))
    surfaces = (
        surface[...],
        unpack(*column(0), SURFACE_LANE, 4, lane),
        halo((at(north_buf, ROW_SURFACE), at(south_buf, ROW_SURFACE))),
        halo((side(north_buf, 0, SURFACE_LANE, 4), side(south_buf, 0, SURFACE_LANE, 4))),
    )

    zero = jnp.zeros((ROWS, COLS), jnp.float32)
    c_prev, r_prev, a_prev = [zero] * 4, [zero] * 4, [zero] * 4
    c_list, r_list = [], []
    for k in range(LEVELS):
        own = (difference[k], unpack(*column(0), 5 * k, 5, lane))
        north = (at(north_buf, ROW_DIFF + ROWS * k), side(north_buf, 0, 5 * k, 5))
        south = (at(south_buf, ROW_DIFF + ROWS * k), side(south_buf, 0, 5 * k, 5))
        halos = (halo((north[0], south[0])), halo((north[1], south[1])))
        centre = (own[0], own[1], halos[0], halos[1])
        easts = both_east(*own, lane) + both_east(*halos, lane)
        wests = both_west(*own, lane) + both_west(*halos, lane)
        first = neighbours_across(own[0], north[0], south[0])
        second = neighbours_across(own[1], north[1], south[1])
        norths = (first[0], second[0], first[1], second[1])
        souths = (first[2], second[2], first[3], second[3])
        values = [
            (fields[f, k], unpack(*column(1 + f), 4 * k, 4, lane), halo_main(f, k), unpack(*halo_packed[f], 4 * k, 4, lane))
            for f in range(4)
        ]
        c_now, r_now, a_now = [], [], []
        for i in range(4):
            u, v, spread, mix = (value[i] for value in values)
            change = (
                -0.5 * u * (easts[i] - wests[i])
                - 0.5 * v * (norths[i] - souths[i])
                + spread * (easts[i] + wests[i] + norths[i] + souths[i] - 4.0 * centre[i])
            )
            explicit = centre[i] + jnp.where(k < counts[i], change, 0.0)
            a = jnp.where(k + 1 < counts[i], mix, 0.0)
            inverse = 1.0 / (1.0 + a_prev[i] + a + a_prev[i] * c_prev[i])
            c_now.append(-a * inverse)
            r_now.append((explicit + a_prev[i] * r_prev[i]) * inverse)
            a_now.append(a)
        c_prev, r_prev, a_prev = c_now, r_now, a_now
        c_list.append(c_now)
        r_list.append(r_now)
    total, x_next = [zero] * 4, [zero] * 4
    for k in range(LEVELS - 1, -1, -1):
        x_next = [r_list[k][i] - c_list[k][i] * x_next[i] for i in range(4)]
        total = [total[i] + thickness(k) * x_next[i] for i in range(4)]
    rhs = [jnp.where(counts[i] > 0, 0.25 * total[i], 0.0) for i in range(4)]

    def depth_of(levels):
        depth = zero
        for k in range(LEVELS):
            depth = depth + jnp.where(k < levels, thickness(k), 0.0)
        return depth / LEVELS

    own = tuple(depth_of(levels) for levels in counts_own)
    north = tuple(depth_of(levels) for levels in counts_north)
    south = tuple(depth_of(levels) for levels in counts_south)
    depths = (own[0], own[1], halo((north[0], south[0])), halo((north[1], south[1])))

    def rows_of(own, north, south):
        first = neighbours_across(own[0], north[0], south[0])
        second = neighbours_across(own[1], north[1], south[1])
        return (first[0], second[0], first[1], second[1]), (first[2], second[2], first[3], second[3])

    def coupled(others, weight):
        return [weight * jnp.minimum(depths[i], others[i]) for i in range(4)]

    own_e, north_e, south_e = (both_east(*pair, lane) for pair in (own, north, south))
    own_w, north_w, south_w = (both_west(*pair, lane) for pair in (own, north, south))
    halo_e = (halo((north_e[0], south_e[0])), halo((north_e[1], south_e[1])))
    halo_w = (halo((north_w[0], south_w[0])), halo((north_w[1], south_w[1])))
    mid = rows_of(own, north, south)
    mid_e = rows_of(own_e, north_e, south_e)
    mid_w = rows_of(own_w, north_w, south_w)
    couplings = [
        coupled(own_e + halo_e, 1.0),
        coupled(own_w + halo_w, 1.0),
        coupled(mid[0], 1.0),
        coupled(mid[1], 1.0),
        coupled(mid_e[0], 0.5),
        coupled(mid_w[0], 0.5),
        coupled(mid_e[1], 0.5),
        coupled(mid_w[1], 0.5),
    ]
    diag = [
        jnp.where(counts[i] > 0, surfaces[i] + sum(entry[i] for entry in couplings), 1.0) for i in range(4)
    ]
    inverse = [1.0 / diag[i] for i in range(4)]
    couplings = [[entry[i] * inverse[i] for i in range(4)] for entry in couplings]

    def shifted_rows(tiles):
        north, south = [None] * 4, [None] * 4
        for i in range(2):
            a, b = roll(tiles[i], -1, 0), roll(tiles[i + 2], -1, 0)
            north[i], north[i + 2] = jnp.where(sub == 7, b, a), jnp.where(sub == 7, a, b)
            a, b = roll(tiles[i], 1, 0), roll(tiles[i + 2], 1, 0)
            south[i], south[i + 2] = jnp.where(sub == 0, b, a), jnp.where(sub == 0, a, b)
        return north, south

    def spread_out(tiles):
        east = both_east(tiles[0], tiles[1], lane) + both_east(tiles[2], tiles[3], lane)
        west = both_west(tiles[0], tiles[1], lane) + both_west(tiles[2], tiles[3], lane)
        mid_n, mid_s = shifted_rows(tiles)
        east_n, east_s = shifted_rows(east)
        west_n, west_s = shifted_rows(west)
        around = (east, west, mid_n, mid_s, east_n, west_n, east_s, west_s)
        return [sum(entry[i] * values[i] for entry, values in zip(couplings, around)) for i in range(4)]

    found = [[rhs[i] * inverse[i] for i in range(4)]]
    found.append(spread_out(found[0]))
    for _ in range(2, ITERS + 1):
        ahead = spread_out(found[-1])
        found.append([2.0 * ahead[i] - found[-2][i] for i in range(4)])
    for j in range(ITERS + 1):
        vectors[j] = found[j][0]
    diagonal[...] = diag[0]
    right_side[...] = rhs[0]
    weighted = [diag[0] * found[j][0] for j in range(ITERS + 1)]
    sums = [weighted[j] * found[j][0] for j in range(ITERS + 1)]
    sums += [weighted[j] * found[j + 1][0] for j in range(ITERS)]
    row = jnp.zeros((1, COLS), jnp.float32)
    for j, entry in enumerate(sums):
        row = jnp.where(lane[:1, :] == j, jnp.sum(entry, keepdims=True), row)
    partial[...] = jnp.broadcast_to(row, partial.shape)


def combine_kernel(moments, vectors, diagonal, pressure, residual, good):
    size = ITERS + 1
    sums = jnp.sum(moments[...], axis=0, keepdims=True)

    def lane_of(j):
        return jnp.broadcast_to(sums[:, j : j + 1], (ROWS, COLS))

    even = [lane_of(j) for j in range(size)]
    odd = [lane_of(size + j) for j in range(ITERS)]
    mu = []
    for j in range(size):
        mu.append(even[0] if j == 0 else 2.0 * even[j] - even[0])
        if j < ITERS:
            mu.append(odd[0] if j == 0 else 2.0 * odd[j] - odd[0])

    def mass(i, j):
        return 0.5 * (mu[i + j] + mu[abs(i - j)])

    def stiffness(i, j):
        i, j = min(i, j), max(i, j)
        if j == 0:
            return mu[0] - mu[1]
        return mass(i, j) - 0.5 * (mass(i, j + 1) + mass(i, j - 1))

    def form(values, entry):
        out = None
        for i in range(len(values)):
            inner = values[i] * entry(i, i)
            for j in range(i + 1, len(values)):
                inner = inner + 2.0 * values[j] * entry(i, j)
            out = values[i] * inner if out is None else out + values[i] * inner
        return out

    def applied(values):
        out = [value for value in values] + [jnp.zeros_like(values[0])]
        out[1] = out[1] - values[0]
        for j in range(1, len(values)):
            out[j + 1] = out[j + 1] - 0.5 * values[j]
            out[j - 1] = out[j - 1] - 0.5 * values[j]
        return out

    def amplified(values, result):
        total = sum(jnp.abs(value) for value in values)
        return total * total * mu[0] / result

    scaled = [jnp.ones((ROWS, COLS), jnp.float32)]
    direction = list(scaled)
    solution_at = []
    energy = mu[0]
    fine = energy > 0.0
    for step in range(ITERS):
        image = applied(direction)
        curvature = form(direction, stiffness)
        step_size = energy / curvature
        fine = fine & (amplified(direction, curvature) <= SCALAR_BOUND) & (curvature > 0.0)
        solution_at = [
            step_size * value + (solution_at[j] if j < len(solution_at) else 0.0) for j, value in enumerate(direction)
        ]
        scaled = [
            (scaled[j] if j < len(scaled) else 0.0) - step_size * value for j, value in enumerate(image)
        ]
        energy_new = form(scaled, mass)
        bound = SCALAR_BOUND if step + 1 < ITERS else FIELD_BOUND
        fine = fine & (amplified(scaled, energy_new) <= bound) & (energy_new > 0.0)
        if step + 1 < ITERS:
            ratio = energy_new / energy
            direction = [
                scaled[j] + (ratio * direction[j] if j < len(direction) else 0.0) for j in range(len(scaled))
            ]
            energy = energy_new
    pressure[...] = sum(solution_at[j] * vectors[j] for j in range(len(solution_at)))
    residual[...] = diagonal[...] * sum(scaled[j] * vectors[j] for j in range(len(scaled)))
    good[0] = jnp.min(jnp.where(fine, 1, 0).astype(jnp.int32))


def tracers_kernel(
    fold_map, tracer, fields, count, one, two, near, far, far_fold, extra_fold,
    mixed,
    north_rows, south_rows, factors,
):
    lane, sub = lanes(), sublanes()
    levels = count[...]
    group = pl.program_id(0)

    @pl.when(group == 0)
    def _():
        halo_rows(fold_map, near, far, far_fold, extra_fold, north_rows, south_rows)
        c_prev = jnp.zeros((ROWS, COLS), jnp.float32)
        a_prev = jnp.zeros((ROWS, COLS), jnp.float32)
        for k in range(LEVELS):
            wet = jnp.where(k < levels, 1.0, 0.0)
            u, v, spread = 0.5 * wet * fields[0, k], 0.5 * wet * fields[1, k], wet * fields[2, k]
            a = jnp.where(k + 1 < levels, fields[3, k], 0.0)
            inverse = 1.0 / (1.0 + a_prev + a + a_prev * c_prev)
            c_prev = -a * inverse
            factors[0, k] = 1.0 - 4.0 * spread
            factors[1, k] = spread - u
            factors[2, k] = spread + u
            factors[3, k] = spread - v
            factors[4, k] = spread + v
            factors[5, k] = inverse
            factors[6, k] = a_prev
            factors[7, k] = c_prev
            a_prev = a

    row = pl.multiple_of(group * ROWS, ROWS)
    columns_east, columns_west = sides(one, two, row)
    r_prev = [jnp.zeros((ROWS, COLS), jnp.float32)] * GROUP
    for k in range(LEVELS):
        centre, to_e, to_w, to_n, to_s, inverse, above = (factors[j, k] for j in range(7))
        wet = k < levels
        for t in range(GROUP):
            cell = jnp.where(wet, tracer[t, k], 0.0)
            at = t * LEVELS + k
            halo_row = group * (GROUP * LEVELS) + at
            east = east_of(cell, roll(columns_east, -at, 1), lane)
            west = west_of(cell, roll(columns_west, COLS - 1 - at, 1), lane)
            north = north_of(cell, north_rows[pl.ds(halo_row, 1), :], sub)
            south = south_of(cell, south_rows[pl.ds(halo_row, 1), :], sub)
            explicit = centre * cell + to_e * east + to_w * west + to_n * north + to_s * south
            r_prev[t] = (explicit + above * r_prev[t]) * inverse
            mixed[t, k] = r_prev[t]
    x_next = r_prev
    for k in range(LEVELS - 2, -1, -1):
        below = factors[7, k]
        for t in range(GROUP):
            x_next[t] = mixed[t, k] - below * x_next[t]
            mixed[t, k] = x_next[t]


def extended(cells, sides, width):
    for axis, dim in sides:
        count = lax.axis_size(axis)
        head = lax.slice_in_dim(cells, 0, width, axis=dim)
        tail = lax.slice_in_dim(cells, cells.shape[dim] - width, cells.shape[dim], axis=dim)
        cells = jnp.concatenate(
            [
                lax.ppermute(tail, axis, [(i, (i + 1) % count) for i in range(count)]),
                cells,
                lax.ppermute(head, axis, [((i + 1) % count, i) for i in range(count)]),
            ],
            axis=dim,
        )
    return cells


def extend(field, fold_map):
    rows, cols = field.shape
    padded = extended(field, (("gx", 1), ("gy", 0)), 1)
    total_cols = fold_map.shape[0]
    whole_row = lax.all_gather(field[rows - 1, :], "gx", axis=0, tiled=True)
    start = lax.axis_index("gx") * cols
    wanted = (start - 1 + jnp.arange(cols + 2, dtype=jnp.int32)) % total_cols
    folded = jnp.take(whole_row, jnp.take(fold_map, wanted), axis=0)
    row_index = lax.axis_index("gy")
    upper = jnp.where(row_index == lax.axis_size("gy") - 1, folded, padded[rows + 1, :])
    lower = jnp.where(row_index == 0, 0.0, padded[0, :])
    return jnp.concatenate([lower[None, :], padded[1 : rows + 1, :], upper[None, :]], axis=0)


def window(padded, row_off, col_off):
    rows = padded.shape[0] - 2
    cols = padded.shape[1] - 2
    return padded[1 + row_off : 1 + row_off + rows, 1 + col_off : 1 + col_off + cols]


def total_of(value):
    return lax.psum(jnp.sum(value), BOTH)


def direct_gradients(rhs, level_count, fold_map, surface_term):
    levels = jnp.arange(LEVELS, dtype=jnp.int32)[:, None, None]
    level_mask = (levels < level_count[None]).astype(jnp.float32)
    thick = (0.5 + 1.5 * jnp.arange(LEVELS).astype(jnp.float32) / (LEVELS - 1))[:, None, None]
    depth = jnp.sum(thick * level_mask, axis=0) / LEVELS
    wet_cells = level_count > 0
    depth_pad = extend(depth, fold_map)
    couplings = [
        weight * jnp.minimum(depth, window(depth_pad, row_off, col_off)) for row_off, col_off, weight in NEIGHBOURS
    ]
    diag = jnp.where(wet_cells, surface_term + sum(couplings), 1.0)

    def step(_, state):
        pressure, residual, direction, energy = state
        field_pad = extend(direction, fold_map)
        summed = jnp.zeros_like(direction)
        for entry, (row_off, col_off, _weight) in zip(couplings, NEIGHBOURS):
            summed = summed + entry * window(field_pad, row_off, col_off)
        image = jnp.where(wet_cells, diag * direction - summed, direction)
        step_size = energy / total_of(direction * image)
        pressure = pressure + step_size * direction
        residual = residual - step_size * image
        scaled = residual / diag
        energy_new = total_of(residual * scaled)
        return pressure, residual, scaled + energy_new / energy * direction, energy_new

    scaled = rhs / diag
    state = (jnp.zeros_like(rhs), rhs, scaled, total_of(rhs * scaled))
    state = lax.fori_loop(0, ITERS, step, state)
    return state[0], state[1]


def kernel(body, limit=VMEM_LIMIT, **rest):
    return pl.pallas_call(body, compiler_params=params(limit), **rest)


def shape(*dims):
    return jax.ShapeDtypeStruct(dims, jnp.float32)


def vmem(*dims):
    return pltpu.VMEM(dims, jnp.float32)


def block_of(dims, at=0):
    return pl.BlockSpec(dims, lambda i: (at,) + (0,) * (len(dims) - 1))


def all_of(array):
    return block_of(array.shape)


def shards(sizes, tracer, east_vel, north_vel, diffusion, mixing, count, fold_map, surface):
    nx, ny = sizes
    hbm = pl.BlockSpec(memory_space=pltpu.HBM)
    smem = pl.BlockSpec(memory_space=pltpu.SMEM)
    fields = (east_vel, north_vel, diffusion, mixing)

    def device(x, y):
        return (x % nx) * ny + y

    one, two, near, far, fold, difference, coefficients, branches = kernel(
        pack_kernel,
        limit=PACK_VMEM_LIMIT,
        out_shape=(
            shape(COL_SIZE, COLS),
            shape(COL_SIZE, COLS),
            shape(ROW_SIZE, COLS),
            shape(ROW_SIZE, COLS),
            shape(ROW_SIZE, COLS),
            shape(LEVELS, ROWS, COLS),
            shape(4, LEVELS, ROWS, COLS),
            jax.ShapeDtypeStruct((1,), jnp.int32),
        ),
        in_specs=[hbm] * 8,
        out_specs=(whole(),) * 7 + (smem,),
        scratch_shapes=[
            vmem(EDGE * ROWS, COLS),
            pltpu.VMEM((ROWS, COLS), jnp.int32),
            vmem(ROWS, COLS),
            pltpu.SMEM(fold_map.shape, jnp.int32),
            pltpu.SemaphoreType.DMA((GROUPS + 7,)),
        ],
        name="pack",
    )(tracer.reshape(EDGE * ROWS, COLS), *fields, count, surface, fold_map)

    swap = [(device(x ^ 1, y), device(x, y)) for x in range(nx) for y in range(ny)]
    shift = [(device(x + 1 if x % 2 else x - 1, y), device(x, y)) for x in range(nx) for y in range(ny)]
    pairs = [(device(x, y ^ 1), device(x, y)) for x in range(nx) for y in range(ny)]
    inner = [(device(x, y + 1 if y % 2 else y - 1), device(x, y)) for x in range(nx) for y in range(1, ny - 1)]
    half = ROW_DIFF - ROW_EAST

    def over_fold(at, rows):
        even, odd = (at, at - 1) if at % 2 == 0 else (at - 1, at)
        return tuple(
            lax.ppermute(rows, BOTH, [(device(turn - x, ny - 1), device(x, ny - 1)) for x in range(nx)])
            for turn in (even, odd)
        )

    def exchange(at, beside, one, two, near, far, fold):
        one, two = lax.ppermute(one, BOTH, swap), lax.ppermute(two, BOTH, shift)
        across = over_fold(at, fold)
        columns = block_of((COL_SIZE, COLS))
        corner = block_of((half, COLS), ROW_EAST // half)
        near, far, packed = kernel(
            corners_kernel,
            grid=(1,),
            out_shape=(shape(ROW_SIZE, COLS), shape(ROW_SIZE, COLS), shape(2 * half, COLS)),
            in_specs=[columns, columns] + [pl.BlockSpec(memory_space=pl.ANY)] * 2,
            out_specs=(corner, corner, block_of((2 * half, COLS))),
            input_output_aliases={2: 0, 3: 1},
            name="put_corners",
        )(one, two, near, far)
        near, far = lax.ppermute(near, BOTH, pairs), lax.ppermute(far, BOTH, inner)
        if beside:
            packed = jnp.concatenate(over_fold(at, packed[:half]), axis=0)
        return one, two, near, far, *across, packed

    one, two, near, far, far_fold, extra_fold, fold_packed = lax.switch(
        branches[0],
        [functools.partial(exchange, at, beside) for beside in (False, True) for at in range(nx)],
        one, two, near, far, fold,
    )

    vectors, diagonal, rhs, partial = kernel(
        krylov_kernel,
        out_shape=(shape(ITERS + 1, ROWS, COLS), shape(ROWS, COLS), shape(ROWS, COLS), shape(nx * ny, COLS)),
        in_specs=[smem] + [whole()] * 11,
        out_specs=(whole(),) * 4,
        scratch_shapes=[vmem(DEEP_SIZE, COLS), vmem(DEEP_SIZE, COLS)],
        name="krylov",
    )(
        fold_map, difference, coefficients, count, surface, one, two, near, far,
        far_fold, extra_fold, fold_packed,
    )

    moments = lax.all_to_all(partial, BOTH, 0, 0)

    batch = pl.BlockSpec((GROUP, LEVELS, ROWS, COLS), lambda i: (i, 0, 0, 0))
    mixed = kernel(
        tracers_kernel,
        grid=(GROUPS,),
        out_shape=shape(TRACERS, LEVELS, ROWS, COLS),
        in_specs=[smem, batch, all_of(coefficients), all_of(count)]
        + [block_of((COL_DEEP, COLS))] * 2
        + [block_of((EDGE, COLS))] * 4,
        out_specs=batch,
        scratch_shapes=[vmem(EDGE, COLS), vmem(EDGE, COLS), vmem(8, LEVELS, ROWS, COLS)],
        name="tracers",
    )(fold_map, tracer, coefficients, count, one, two, near, far, far_fold, extra_fold)

    pressure, residual, good = kernel(
        combine_kernel,
        out_shape=(shape(ROWS, COLS), shape(ROWS, COLS), jax.ShapeDtypeStruct((1,), jnp.int32)),
        in_specs=[whole()] * 3,
        out_specs=(whole(), whole(), smem),
        name="combine",
    )(moments, vectors, diagonal)
    pressure, residual = lax.cond(
        good[0] == 1,
        lambda pressure, residual, rhs, count, surface, fold: (pressure, residual),
        lambda pressure, residual, rhs, count, surface, fold: direct_gradients(rhs, count, fold, surface),
        pressure,
        residual,
        rhs,
        count,
        surface,
        fold_map,
    )
    return mixed, pressure, residual


def solution(mesh):
    in_specs = (
        P(None, None, "gy", "gx"),
        P(None, "gy", "gx"),
        P(None, "gy", "gx"),
        P(None, "gy", "gx"),
        P(None, "gy", "gx"),
        P("gy", "gx"),
        P(),
        P("gy", "gx"),
    )
    out_specs = (P(None, None, "gy", "gx"), P("gy", "gx"), P("gy", "gx"))
    body = functools.partial(shards, (mesh.shape["gx"], mesh.shape["gy"]))
    return jax.shard_map(body, mesh=mesh, in_specs=in_specs, out_specs=out_specs, check_vma=False)
```

```python
import functools

import jax
import jax.numpy as jnp
from jax import lax
from jax.experimental import pallas as pl
from jax.experimental.pallas import tpu as pltpu
from jax.sharding import PartitionSpec as P

ITERS = 4
TRACERS, LEVELS, ROWS, COLS = 16, 20, 8, 128
GROUP = 4
GROUPS = TRACERS // GROUP
DEPTH = 5
EDGE = TRACERS * LEVELS
BOTH = ("gx", "gy")
VMEM_LIMIT = 40 * 1024 * 1024
PACK_VMEM_LIMIT = 63 * 1024 * 1024

COL_DEEP, COL_SIZE = GROUPS * ROWS, (GROUPS + 5) * ROWS
COUNT_LANE, SURFACE_LANE = 100, 105
ROW_DIFF, ROW_FIELD, ROW_COUNT, ROW_SURFACE, ROW_SIZE = 320, 480, 800, 808, 816
ROW_EAST, ROW_WEST, DEEP_SIZE, SET = 816, 856, 576, 40

SCALAR_BOUND, FIELD_BOUND = 1500.0, 1.0e5

NEIGHBOURS = [
    (0, 1, 1.0),
    (0, -1, 1.0),
    (1, 0, 1.0),
    (-1, 0, 1.0),
    (1, 1, 0.5),
    (1, -1, 0.5),
    (-1, 1, 0.5),
    (-1, -1, 0.5),
]


def params(limit=VMEM_LIMIT):
    return pltpu.CompilerParams(vmem_limit_bytes=limit)


def whole():
    return pl.BlockSpec(memory_space=pltpu.VMEM)


def lanes():
    return lax.broadcasted_iota(jnp.int32, (ROWS, COLS), 1)


def sublanes():
    return lax.broadcasted_iota(jnp.int32, (ROWS, COLS), 0)


def roll(tile, shift, axis):
    size = tile.shape[axis]
    shift = shift % size
    return tile if shift == 0 else pltpu.roll(tile, shift, axis)


def east_of(tile, beyond, lane):
    return roll(jnp.where(lane == 0, beyond, tile), -1, 1)


def west_of(tile, beyond, lane):
    return roll(jnp.where(lane == COLS - 1, beyond, tile), 1, 1)


def north_of(tile, beyond, sub):
    return roll(jnp.where(sub == 0, beyond, tile), -1, 0)


def south_of(tile, beyond, sub):
    return roll(jnp.where(sub == ROWS - 1, beyond, tile), 1, 0)


def thickness(level):
    return 0.5 + 1.5 * level / (LEVELS - 1)


def turned(tile):
    return jnp.take_along_axis(tile, ROWS - 1 - sublanes(), axis=0)


def start_copies(pairs, ready):
    copies = [pltpu.make_async_copy(source, target, ready.at[i]) for i, (source, target) in enumerate(pairs)]
    for copy in copies:
        copy.start()
    return copies


def pack_kernel(
    tracer, east_vel, north_vel, diffusion, mixing, count, surface, fold_map,
    one, two, near_rows, far_rows, fold_rows, fold_columns, difference, fields, branches,
    cells, levels_ref, surface_ref, fold_ref, ready,
):
    lane = lanes()
    low = sublanes() < ROWS // 2
    size = GROUP * LEVELS * ROWS
    pairs = [(count, levels_ref), (surface, surface_ref)]
    pairs += [(tracer.at[pl.ds(g * size, size)], cells.at[pl.ds(g * size, size)]) for g in range(GROUPS)]
    pairs += [(field, fields.at[f]) for f, field in enumerate((east_vel, north_vel, diffusion, mixing))]
    pairs += [(fold_map, fold_ref)]
    copies = start_copies(pairs, ready)
    here = lax.axis_index("gy")
    even = here % 2 == 0
    is_top = here == lax.axis_size("gy") - 1
    eastward = lax.axis_index("gx") % 2 == 0

    def put(row, items):
        west = jnp.zeros((ROWS, COLS), jnp.float32)
        east = jnp.zeros((ROWS, COLS), jnp.float32)
        for tile, width, first in items:
            chosen = lane == first if width == 1 else (lane >= first) & (lane < first + width)
            west = jnp.where(chosen, roll(tile, first, 1), west)
            east = jnp.where(chosen, roll(tile, first + width, 1), east)
        one[row : row + ROWS, :] = jnp.where(eastward, east, west)
        two[row : row + ROWS, :] = jnp.where(eastward, west, east)
        if row >= COL_DEEP:
            fold_columns[row - COL_DEEP : row - COL_DEEP + ROWS, :] = turned(east)
            fold_columns[SET + row - COL_DEEP : SET + row - COL_DEEP + ROWS, :] = turned(west)

    copies[0].wait()
    copies[1].wait()
    levels, surfaces = levels_ref[...], surface_ref[...]
    depths = levels.astype(jnp.float32)
    per = 2 * LEVELS
    level_row = lax.broadcasted_iota(jnp.int32, (per, COLS), 0)
    level_row = jnp.where(level_row >= LEVELS, level_row - LEVELS, level_row)
    wet_south = level_row < jnp.broadcast_to(levels[:1, :], (per, COLS))
    wet_north = level_row < jnp.broadcast_to(levels[ROWS - 1 :, :], (per, COLS))

    def cell(t, k):
        row = (t * LEVELS + k) * ROWS
        return jnp.where(k < levels, cells[row : row + ROWS, :], 0.0)

    for g in range(GROUPS):
        copies[2 + g].wait()
        put(g * ROWS, [(cell(g * GROUP + t, k), 1, t * LEVELS + k) for t in range(GROUP) for k in range(LEVELS)])
        if g == 0:
            for k in range(LEVELS):
                difference[k] = cell(0, k) - cell(1, k)
            items = [(difference[k], 5, 5 * k) for k in range(LEVELS)]
            put(COL_DEEP, items + [(depths, 5, COUNT_LANE), (surfaces, 4, SURFACE_LANE)])
        for at in range(g * GROUP * LEVELS, (g + 1) * GROUP * LEVELS, per):
            south = jnp.where(wet_south, cells[pl.ds(at * ROWS, per, stride=ROWS), :], 0.0)
            north = jnp.where(wet_north, cells[pl.ds(at * ROWS + ROWS - 1, per, stride=ROWS), :], 0.0)
            near_rows[at : at + per, :] = jnp.where(even, north, south)
            far_rows[at : at + per, :] = jnp.where(even, south, north)
    for f in range(4):
        copies[2 + GROUPS + f].wait()
        put(COL_DEEP + (1 + f) * ROWS, [(fields[f, k], 4, 4 * k) for k in range(LEVELS)])
    copies[-1].wait()
    pole = pole_of(fold_ref)
    offset, block = pole & (COLS - 1), pole >> (COLS.bit_length() - 1)
    beyond = jnp.where(offset < DEPTH, 1, jnp.where(offset > COLS - DEPTH, 2, 0))
    branches[0] = block + beyond * lax.axis_size("gx")

    def pack(kind, out):
        turn = turned if kind == "fold" else (lambda tile: tile)
        for k in range(LEVELS):
            out[ROW_DIFF + ROWS * k : ROW_DIFF + ROWS * (k + 1), :] = turn(difference[k])
        for f in range(4):
            for m in range(LEVELS // 2):
                first, second = turn(fields[f, 2 * m]), turn(fields[f, 2 * m + 1])
                if kind == "north":
                    tile = jnp.where(low, roll(first, 4, 0), second)
                else:
                    tile = jnp.where(low, first, roll(second, 4, 0))
                row = ROW_FIELD + ROWS * (f * (LEVELS // 2) + m)
                out[row : row + ROWS, :] = tile
        out[ROW_COUNT : ROW_COUNT + ROWS, :] = turn(depths)
        out[ROW_SURFACE : ROW_SURFACE + ROWS, :] = turn(surfaces)

    @pl.when(even)
    def _():
        pack("north", near_rows)
        pack("south", far_rows)

    @pl.when(jnp.logical_not(even))
    def _():
        pack("south", near_rows)

    @pl.when(jnp.logical_not(even) & jnp.logical_not(is_top))
    def _():
        pack("north", far_rows)

    @pl.when(is_top)
    def _():
        fold_rows[:ROW_DIFF, :] = far_rows[:ROW_DIFF, :]
        pack("fold", fold_rows)


def sides(one, two, row):
    first, second = one[pl.ds(row, ROWS), :], two[pl.ds(row, ROWS), :]
    eastward = lax.axis_index("gx") % 2 == 0
    return jnp.where(eastward, first, second), jnp.where(eastward, second, first)


def pole_of(fold_map):
    return (fold_map[0] + 1) & (COLS * lax.axis_size("gx") - 1)


def halo_rows(fold_map, near, far, far_fold, extra_fold, north_rows, south_rows):
    here = lax.axis_index("gy")
    top = lax.axis_size("gy") - 1

    @pl.when(here % 2 == 0)
    def _():
        north_rows[...] = near[...]
        south_rows[...] = far[...]

    @pl.when(here % 2 == 1)
    def _():
        south_rows[...] = near[...]

    @pl.when((here % 2 == 1) & (here != top))
    def _():
        north_rows[...] = far[...]

    @pl.when(here == top)
    def _():
        lane = lanes()
        pole = pole_of(fold_map)
        offset = pole & (COLS - 1)
        index = (offset - 1 - lane) & (COLS - 1)
        within_far = (lane >= offset) == ((pole & COLS) != 0)
        for row in range(0, north_rows.shape[0], ROWS):
            rows = jnp.where(within_far, far_fold[row : row + ROWS, :], extra_fold[row : row + ROWS, :])
            north_rows[row : row + ROWS, :] = jnp.take_along_axis(rows, index, axis=1)


def unfold(offset, first_in_far, far, extra, third, out):
    lane = lanes()
    index = (offset - 1 - lane) & (COLS - 1)
    within_far = (lane >= offset) == first_in_far
    zero = jnp.zeros((ROWS, COLS), jnp.float32)

    def store(row, value):
        out[row - ROW_DIFF : row - ROW_DIFF + ROWS, :] = value

    def flipped(row, sign):
        a, b = far[row : row + ROWS, :], extra[row : row + ROWS, :]
        store(row, sign * jnp.take_along_axis(jnp.where(within_far, a, b), index, axis=1))
        return sign * jnp.take_along_axis(jnp.where(within_far, b, a), index, axis=1)

    def collect(packed, tile, width, at):
        chosen = (lane >= at) & (lane < at + width)
        return jnp.where(chosen, roll(tile, at, 1), packed[0]), jnp.where(chosen, roll(tile, at + width, 1), packed[1])

    def finish(row, packed, sign, width, within):
        beside = (lane + (offset - 1) + width - 2 * within) & (COLS - 1)
        right = sign * jnp.take_along_axis(third[row : row + ROWS, :], beside, axis=1)
        beside = (lane + (offset - 1 - COLS) + width - 2 * within) & (COLS - 1)
        left = sign * jnp.take_along_axis(third[SET + row : SET + row + ROWS, :], beside, axis=1)
        store(ROW_EAST + row, jnp.where(within < offset, packed[0], right))
        store(ROW_WEST + row, jnp.where(within >= offset + width - COLS, packed[1], left))

    packed = (zero, zero)
    for k in range(LEVELS):
        packed = collect(packed, flipped(ROW_DIFF + ROWS * k, 1.0), 5, 5 * k)
    packed = collect(packed, flipped(ROW_COUNT, 1.0), 5, COUNT_LANE)
    packed = collect(packed, flipped(ROW_SURFACE, 1.0), 4, SURFACE_LANE)
    fifth = lane - 5 * ((lane * 205) >> 10)
    finish(0, packed, 1.0, jnp.where(lane >= SURFACE_LANE, 4, 5), fifth)
    for f in range(4):
        sign = -1.0 if f < 2 else 1.0
        packed = (zero, zero)
        for m in range(LEVELS // 2):
            tile = flipped(ROW_FIELD + ROWS * (f * (LEVELS // 2) + m), sign)
            packed = collect(packed, tile, 4, 8 * m)
            packed = collect(packed, roll(tile, 4, 0), 4, 8 * m + 4)
        finish((1 + f) * ROWS, packed, sign, 4, lane & 3)


def unpack(east, west, first, width, lane):
    right = roll(east, -first, 1)
    left = roll(west, -width - first, 1)
    return jnp.where(lane < width, right, jnp.where(lane >= COLS - width, left, 0.0))


def both_east(one, two, lane):
    return east_of(one, two, lane), east_of(two, one, lane)


def both_west(one, two, lane):
    return west_of(one, two, lane), west_of(two, one, lane)


def krylov_kernel(
    fold_map, difference, fields, count, surface, one, two, near, far, near_columns, far_columns,
    far_fold, extra_fold, third,
    vectors, diagonal, right_side, partial,
    north_buf, south_buf,
):
    here = lax.axis_index("gy")
    top = lax.axis_size("gy") - 1
    lane, sub = lanes(), sublanes()
    low = sub < 4
    def fill(out, rows, columns):
        out[: ROW_SIZE - ROW_DIFF, :] = rows[ROW_DIFF:, :]
        out[ROW_SIZE - ROW_DIFF :, :] = columns[...]

    @pl.when(here % 2 == 0)
    def _():
        fill(north_buf, near, near_columns)
        fill(south_buf, far, far_columns)

    @pl.when(here % 2 == 1)
    def _():
        fill(south_buf, near, near_columns)

    @pl.when((here % 2 == 1) & (here != top))
    def _():
        fill(north_buf, far, far_columns)

    @pl.when(here == top)
    def _():
        pole = pole_of(fold_map)
        unfold(pole & (COLS - 1), (pole & COLS) != 0, far_fold, extra_fold, third, north_buf)

    def at(ref, row):
        return ref[row - ROW_DIFF : row - ROW_DIFF + ROWS, :]

    def field_tile(ref, f, k):
        return at(ref, ROW_FIELD + ROWS * (f * (LEVELS // 2) + k // 2))

    def halo_main(f, k):
        north, south = field_tile(north_buf, f, k), field_tile(south_buf, f, k)
        return jnp.where(low, roll(north, 4 * (k % 2), 0), roll(south, 4 * (1 - k % 2), 0))

    def side(ref, f, first, width):
        return unpack(at(ref, ROW_EAST + ROWS * f), at(ref, ROW_WEST + ROWS * f), first, width, lane)

    halo_packed = [
        [
            jnp.where(low, at(north_buf, base + ROWS * (1 + f)), at(south_buf, base + ROWS * (1 + f)))
            for base in (ROW_EAST, ROW_WEST)
        ]
        for f in range(4)
    ]

    columns = [sides(one, two, COL_DEEP + ROWS * f) for f in range(5)]

    def column(f):
        return columns[f]

    def neighbours_across(own, north, south):
        up, up_n, up_s = roll(own, -1, 0), roll(north, -1, 0), roll(south, -1, 0)
        down, down_n, down_s = roll(own, 1, 0), roll(north, 1, 0), roll(south, 1, 0)
        return (
            jnp.where(sub == 7, up_n, up),
            jnp.where(low, up_n, jnp.where(sub == 7, up, up_s)),
            jnp.where(sub == 0, down_s, down),
            jnp.where(sub == 0, down, jnp.where(low, down_n, down_s)),
        )

    def halo(pair):
        return jnp.where(low, pair[0], pair[1])

    counts_own = (count[...].astype(jnp.float32), unpack(*column(0), COUNT_LANE, 5, lane))
    counts_north = (at(north_buf, ROW_COUNT), side(north_buf, 0, COUNT_LANE, 5))
    counts_south = (at(south_buf, ROW_COUNT), side(south_buf, 0, COUNT_LANE, 5))
    counts = (counts_own[0], counts_own[1], halo((counts_north[0], counts_south[0])), halo((counts_north[1], counts_south[1])))
    surfaces = (
        surface[...],
        unpack(*column(0), SURFACE_LANE, 4, lane),
        halo((at(north_buf, ROW_SURFACE), at(south_buf, ROW_SURFACE))),
        halo((side(north_buf, 0, SURFACE_LANE, 4), side(south_buf, 0, SURFACE_LANE, 4))),
    )

    zero = jnp.zeros((ROWS, COLS), jnp.float32)
    c_prev, r_prev, a_prev = [zero] * 4, [zero] * 4, [zero] * 4
    c_list, r_list = [], []
    for k in range(LEVELS):
        own = (difference[k], unpack(*column(0), 5 * k, 5, lane))
        north = (at(north_buf, ROW_DIFF + ROWS * k), side(north_buf, 0, 5 * k, 5))
        south = (at(south_buf, ROW_DIFF + ROWS * k), side(south_buf, 0, 5 * k, 5))
        halos = (halo((north[0], south[0])), halo((north[1], south[1])))
        centre = (own[0], own[1], halos[0], halos[1])
        easts = both_east(*own, lane) + both_east(*halos, lane)
        wests = both_west(*own, lane) + both_west(*halos, lane)
        first = neighbours_across(own[0], north[0], south[0])
        second = neighbours_across(own[1], north[1], south[1])
        norths = (first[0], second[0], first[1], second[1])
        souths = (first[2], second[2], first[3], second[3])
        values = [
            (fields[f, k], unpack(*column(1 + f), 4 * k, 4, lane), halo_main(f, k), unpack(*halo_packed[f], 4 * k, 4, lane))
            for f in range(4)
        ]
        c_now, r_now, a_now = [], [], []
        for i in range(4):
            u, v, spread, mix = (value[i] for value in values)
            change = (
                -0.5 * u * (easts[i] - wests[i])
                - 0.5 * v * (norths[i] - souths[i])
                + spread * (easts[i] + wests[i] + norths[i] + souths[i] - 4.0 * centre[i])
            )
            explicit = centre[i] + jnp.where(k < counts[i], change, 0.0)
            a = jnp.where(k + 1 < counts[i], mix, 0.0)
            inverse = 1.0 / (1.0 + a_prev[i] + a + a_prev[i] * c_prev[i])
            c_now.append(-a * inverse)
            r_now.append((explicit + a_prev[i] * r_prev[i]) * inverse)
            a_now.append(a)
        c_prev, r_prev, a_prev = c_now, r_now, a_now
        c_list.append(c_now)
        r_list.append(r_now)
    total, x_next = [zero] * 4, [zero] * 4
    for k in range(LEVELS - 1, -1, -1):
        x_next = [r_list[k][i] - c_list[k][i] * x_next[i] for i in range(4)]
        total = [total[i] + thickness(k) * x_next[i] for i in range(4)]
    rhs = [jnp.where(counts[i] > 0, 0.25 * total[i], 0.0) for i in range(4)]

    def depth_of(levels):
        depth = zero
        for k in range(LEVELS):
            depth = depth + jnp.where(k < levels, thickness(k), 0.0)
        return depth / LEVELS

    own = tuple(depth_of(levels) for levels in counts_own)
    north = tuple(depth_of(levels) for levels in counts_north)
    south = tuple(depth_of(levels) for levels in counts_south)
    depths = (own[0], own[1], halo((north[0], south[0])), halo((north[1], south[1])))

    def rows_of(own, north, south):
        first = neighbours_across(own[0], north[0], south[0])
        second = neighbours_across(own[1], north[1], south[1])
        return (first[0], second[0], first[1], second[1]), (first[2], second[2], first[3], second[3])

    def coupled(others, weight):
        return [weight * jnp.minimum(depths[i], others[i]) for i in range(4)]

    own_e, north_e, south_e = (both_east(*pair, lane) for pair in (own, north, south))
    own_w, north_w, south_w = (both_west(*pair, lane) for pair in (own, north, south))
    halo_e = (halo((north_e[0], south_e[0])), halo((north_e[1], south_e[1])))
    halo_w = (halo((north_w[0], south_w[0])), halo((north_w[1], south_w[1])))
    mid = rows_of(own, north, south)
    mid_e = rows_of(own_e, north_e, south_e)
    mid_w = rows_of(own_w, north_w, south_w)
    couplings = [
        coupled(own_e + halo_e, 1.0),
        coupled(own_w + halo_w, 1.0),
        coupled(mid[0], 1.0),
        coupled(mid[1], 1.0),
        coupled(mid_e[0], 0.5),
        coupled(mid_w[0], 0.5),
        coupled(mid_e[1], 0.5),
        coupled(mid_w[1], 0.5),
    ]
    diag = [
        jnp.where(counts[i] > 0, surfaces[i] + sum(entry[i] for entry in couplings), 1.0) for i in range(4)
    ]
    inverse = [1.0 / diag[i] for i in range(4)]
    couplings = [[entry[i] * inverse[i] for i in range(4)] for entry in couplings]

    def shifted_rows(tiles):
        north, south = [None] * 4, [None] * 4
        for i in range(2):
            a, b = roll(tiles[i], -1, 0), roll(tiles[i + 2], -1, 0)
            north[i], north[i + 2] = jnp.where(sub == 7, b, a), jnp.where(sub == 7, a, b)
            a, b = roll(tiles[i], 1, 0), roll(tiles[i + 2], 1, 0)
            south[i], south[i + 2] = jnp.where(sub == 0, b, a), jnp.where(sub == 0, a, b)
        return north, south

    def spread_out(tiles):
        east = both_east(tiles[0], tiles[1], lane) + both_east(tiles[2], tiles[3], lane)
        west = both_west(tiles[0], tiles[1], lane) + both_west(tiles[2], tiles[3], lane)
        mid_n, mid_s = shifted_rows(tiles)
        east_n, east_s = shifted_rows(east)
        west_n, west_s = shifted_rows(west)
        around = (east, west, mid_n, mid_s, east_n, west_n, east_s, west_s)
        return [sum(entry[i] * values[i] for entry, values in zip(couplings, around)) for i in range(4)]

    found = [[rhs[i] * inverse[i] for i in range(4)]]
    found.append(spread_out(found[0]))
    for _ in range(2, ITERS + 1):
        ahead = spread_out(found[-1])
        found.append([2.0 * ahead[i] - found[-2][i] for i in range(4)])
    for j in range(ITERS + 1):
        vectors[j] = found[j][0]
    diagonal[...] = diag[0]
    right_side[...] = rhs[0]
    weighted = [diag[0] * found[j][0] for j in range(ITERS + 1)]
    sums = [weighted[j] * found[j][0] for j in range(ITERS + 1)]
    sums += [weighted[j] * found[j + 1][0] for j in range(ITERS)]
    row = jnp.zeros((1, COLS), jnp.float32)
    for j, entry in enumerate(sums):
        row = jnp.where(lane[:1, :] == j, jnp.sum(entry, keepdims=True), row)
    partial[...] = jnp.broadcast_to(row, partial.shape)


def combine_kernel(moments, vectors, diagonal, pressure, residual, good):
    size = ITERS + 1
    sums = jnp.sum(moments[...], axis=0, keepdims=True)

    def lane_of(j):
        return jnp.broadcast_to(sums[:, j : j + 1], (ROWS, COLS))

    even = [lane_of(j) for j in range(size)]
    odd = [lane_of(size + j) for j in range(ITERS)]
    mu = []
    for j in range(size):
        mu.append(even[0] if j == 0 else 2.0 * even[j] - even[0])
        if j < ITERS:
            mu.append(odd[0] if j == 0 else 2.0 * odd[j] - odd[0])

    def mass(i, j):
        return 0.5 * (mu[i + j] + mu[abs(i - j)])

    def stiffness(i, j):
        i, j = min(i, j), max(i, j)
        if j == 0:
            return mu[0] - mu[1]
        return mass(i, j) - 0.5 * (mass(i, j + 1) + mass(i, j - 1))

    def form(values, entry):
        out = None
        for i in range(len(values)):
            inner = values[i] * entry(i, i)
            for j in range(i + 1, len(values)):
                inner = inner + 2.0 * values[j] * entry(i, j)
            out = values[i] * inner if out is None else out + values[i] * inner
        return out

    def applied(values):
        out = [value for value in values] + [jnp.zeros_like(values[0])]
        out[1] = out[1] - values[0]
        for j in range(1, len(values)):
            out[j + 1] = out[j + 1] - 0.5 * values[j]
            out[j - 1] = out[j - 1] - 0.5 * values[j]
        return out

    def amplified(values, result):
        total = sum(jnp.abs(value) for value in values)
        return total * total * mu[0] / result

    scaled = [jnp.ones((ROWS, COLS), jnp.float32)]
    direction = list(scaled)
    solution_at = []
    energy = mu[0]
    fine = energy > 0.0
    for step in range(ITERS):
        image = applied(direction)
        curvature = form(direction, stiffness)
        step_size = energy / curvature
        fine = fine & (amplified(direction, curvature) <= SCALAR_BOUND) & (curvature > 0.0)
        solution_at = [
            step_size * value + (solution_at[j] if j < len(solution_at) else 0.0) for j, value in enumerate(direction)
        ]
        scaled = [
            (scaled[j] if j < len(scaled) else 0.0) - step_size * value for j, value in enumerate(image)
        ]
        energy_new = form(scaled, mass)
        bound = SCALAR_BOUND if step + 1 < ITERS else FIELD_BOUND
        fine = fine & (amplified(scaled, energy_new) <= bound) & (energy_new > 0.0)
        if step + 1 < ITERS:
            ratio = energy_new / energy
            direction = [
                scaled[j] + (ratio * direction[j] if j < len(direction) else 0.0) for j in range(len(scaled))
            ]
            energy = energy_new
    pressure[...] = sum(solution_at[j] * vectors[j] for j in range(len(solution_at)))
    residual[...] = diagonal[...] * sum(scaled[j] * vectors[j] for j in range(len(scaled)))
    good[0] = jnp.min(jnp.where(fine, 1, 0).astype(jnp.int32))


def tracers_kernel(
    fold_map, tracer, fields, count, one, two, near, far, far_fold, extra_fold,
    mixed,
    north_rows, south_rows, factors,
):
    lane, sub = lanes(), sublanes()
    levels = count[...]
    group = pl.program_id(0)

    @pl.when(group == 0)
    def _():
        halo_rows(fold_map, near, far, far_fold, extra_fold, north_rows, south_rows)
        c_prev = jnp.zeros((ROWS, COLS), jnp.float32)
        a_prev = jnp.zeros((ROWS, COLS), jnp.float32)
        for k in range(LEVELS):
            wet = jnp.where(k < levels, 1.0, 0.0)
            u, v, spread = 0.5 * wet * fields[0, k], 0.5 * wet * fields[1, k], wet * fields[2, k]
            a = jnp.where(k + 1 < levels, fields[3, k], 0.0)
            inverse = 1.0 / (1.0 + a_prev + a + a_prev * c_prev)
            c_prev = -a * inverse
            factors[0, k] = 1.0 - 4.0 * spread
            factors[1, k] = spread - u
            factors[2, k] = spread + u
            factors[3, k] = spread - v
            factors[4, k] = spread + v
            factors[5, k] = inverse
            factors[6, k] = a_prev
            factors[7, k] = c_prev
            a_prev = a

    row = pl.multiple_of(group * ROWS, ROWS)
    columns_east, columns_west = sides(one, two, row)
    r_prev = [jnp.zeros((ROWS, COLS), jnp.float32)] * GROUP
    for k in range(LEVELS):
        centre, to_e, to_w, to_n, to_s, inverse, above = (factors[j, k] for j in range(7))
        wet = k < levels
        for t in range(GROUP):
            cell = jnp.where(wet, tracer[t, k], 0.0)
            at = t * LEVELS + k
            halo_row = group * (GROUP * LEVELS) + at
            east = east_of(cell, roll(columns_east, -at, 1), lane)
            west = west_of(cell, roll(columns_west, COLS - 1 - at, 1), lane)
            north = north_of(cell, north_rows[pl.ds(halo_row, 1), :], sub)
            south = south_of(cell, south_rows[pl.ds(halo_row, 1), :], sub)
            explicit = centre * cell + to_e * east + to_w * west + to_n * north + to_s * south
            r_prev[t] = (explicit + above * r_prev[t]) * inverse
            mixed[t, k] = r_prev[t]
    x_next = r_prev
    for k in range(LEVELS - 2, -1, -1):
        below = factors[7, k]
        for t in range(GROUP):
            x_next[t] = mixed[t, k] - below * x_next[t]
            mixed[t, k] = x_next[t]


def extended(cells, sides, width):
    for axis, dim in sides:
        count = lax.axis_size(axis)
        head = lax.slice_in_dim(cells, 0, width, axis=dim)
        tail = lax.slice_in_dim(cells, cells.shape[dim] - width, cells.shape[dim], axis=dim)
        cells = jnp.concatenate(
            [
                lax.ppermute(tail, axis, [(i, (i + 1) % count) for i in range(count)]),
                cells,
                lax.ppermute(head, axis, [((i + 1) % count, i) for i in range(count)]),
            ],
            axis=dim,
        )
    return cells


def extend(field, fold_map):
    rows, cols = field.shape
    padded = extended(field, (("gx", 1), ("gy", 0)), 1)
    total_cols = fold_map.shape[0]
    whole_row = lax.all_gather(field[rows - 1, :], "gx", axis=0, tiled=True)
    start = lax.axis_index("gx") * cols
    wanted = (start - 1 + jnp.arange(cols + 2, dtype=jnp.int32)) % total_cols
    folded = jnp.take(whole_row, jnp.take(fold_map, wanted), axis=0)
    row_index = lax.axis_index("gy")
    upper = jnp.where(row_index == lax.axis_size("gy") - 1, folded, padded[rows + 1, :])
    lower = jnp.where(row_index == 0, 0.0, padded[0, :])
    return jnp.concatenate([lower[None, :], padded[1 : rows + 1, :], upper[None, :]], axis=0)


def window(padded, row_off, col_off):
    rows = padded.shape[0] - 2
    cols = padded.shape[1] - 2
    return padded[1 + row_off : 1 + row_off + rows, 1 + col_off : 1 + col_off + cols]


def total_of(value):
    return lax.psum(jnp.sum(value), BOTH)


def direct_gradients(rhs, level_count, fold_map, surface_term):
    levels = jnp.arange(LEVELS, dtype=jnp.int32)[:, None, None]
    level_mask = (levels < level_count[None]).astype(jnp.float32)
    thick = (0.5 + 1.5 * jnp.arange(LEVELS).astype(jnp.float32) / (LEVELS - 1))[:, None, None]
    depth = jnp.sum(thick * level_mask, axis=0) / LEVELS
    wet_cells = level_count > 0
    depth_pad = extend(depth, fold_map)
    couplings = [
        weight * jnp.minimum(depth, window(depth_pad, row_off, col_off)) for row_off, col_off, weight in NEIGHBOURS
    ]
    diag = jnp.where(wet_cells, surface_term + sum(couplings), 1.0)

    def step(_, state):
        pressure, residual, direction, energy = state
        field_pad = extend(direction, fold_map)
        summed = jnp.zeros_like(direction)
        for entry, (row_off, col_off, _weight) in zip(couplings, NEIGHBOURS):
            summed = summed + entry * window(field_pad, row_off, col_off)
        image = jnp.where(wet_cells, diag * direction - summed, direction)
        step_size = energy / total_of(direction * image)
        pressure = pressure + step_size * direction
        residual = residual - step_size * image
        scaled = residual / diag
        energy_new = total_of(residual * scaled)
        return pressure, residual, scaled + energy_new / energy * direction, energy_new

    scaled = rhs / diag
    state = (jnp.zeros_like(rhs), rhs, scaled, total_of(rhs * scaled))
    state = lax.fori_loop(0, ITERS, step, state)
    return state[0], state[1]


def kernel(body, limit=VMEM_LIMIT, **rest):
    return pl.pallas_call(body, compiler_params=params(limit), **rest)


def shape(*dims):
    return jax.ShapeDtypeStruct(dims, jnp.float32)


def vmem(*dims):
    return pltpu.VMEM(dims, jnp.float32)


def block_of(dims, at=0):
    return pl.BlockSpec(dims, lambda i: (at,) + (0,) * (len(dims) - 1))


def all_of(array):
    return block_of(array.shape)


def shards(sizes, tracer, east_vel, north_vel, diffusion, mixing, count, fold_map, surface):
    nx, ny = sizes
    hbm = pl.BlockSpec(memory_space=pltpu.HBM)
    smem = pl.BlockSpec(memory_space=pltpu.SMEM)
    fields = (east_vel, north_vel, diffusion, mixing)

    def device(x, y):
        return (x % nx) * ny + y

    one, two, near, far, fold, fold_columns, difference, coefficients, branches = kernel(
        pack_kernel,
        limit=PACK_VMEM_LIMIT,
        out_shape=(
            shape(COL_SIZE, COLS),
            shape(COL_SIZE, COLS),
            shape(ROW_SIZE, COLS),
            shape(ROW_SIZE, COLS),
            shape(ROW_SIZE, COLS),
            shape(2 * SET, COLS),
            shape(LEVELS, ROWS, COLS),
            shape(4, LEVELS, ROWS, COLS),
            jax.ShapeDtypeStruct((1,), jnp.int32),
        ),
        in_specs=[hbm] * 8,
        out_specs=(whole(),) * 8 + (smem,),
        scratch_shapes=[
            vmem(EDGE * ROWS, COLS),
            pltpu.VMEM((ROWS, COLS), jnp.int32),
            vmem(ROWS, COLS),
            pltpu.SMEM(fold_map.shape, jnp.int32),
            pltpu.SemaphoreType.DMA((GROUPS + 7,)),
        ],
        name="pack",
    )(tracer.reshape(EDGE * ROWS, COLS), *fields, count, surface, fold_map)

    swap = [(device(x ^ 1, y), device(x, y)) for x in range(nx) for y in range(ny)]
    shift = [(device(x + 1 if x % 2 else x - 1, y), device(x, y)) for x in range(nx) for y in range(ny)]
    pairs = [(device(x, y ^ 1), device(x, y)) for x in range(nx) for y in range(ny)]
    inner = [(device(x, y + 1 if y % 2 else y - 1), device(x, y)) for x in range(nx) for y in range(1, ny - 1)]

    def across(turn, rows):
        return lax.ppermute(rows, BOTH, [(device(turn - x, ny - 1), device(x, ny - 1)) for x in range(nx)])

    def exchange(at, beyond, one, two, near, far, fold, fold_columns):
        even, odd = (at, at - 1) if at % 2 == 0 else (at - 1, at)
        one, two = lax.ppermute(one, BOTH, swap), lax.ppermute(two, BOTH, shift)
        far, near = lax.ppermute(far, BOTH, inner), lax.ppermute(near, BOTH, pairs)
        far_fold, extra_fold = across(even, fold), across(odd, fold)
        third = across(at - 2 if beyond == 1 else at + 1, fold_columns) if beyond else fold_columns
        eastward = lax.axis_index("gx") % 2 == 0
        columns = jnp.concatenate(
            [jnp.where(eastward, one, two)[COL_DEEP:], jnp.where(eastward, two, one)[COL_DEEP:]], axis=0
        )
        far_columns, near_columns = lax.ppermute(columns, BOTH, inner), lax.ppermute(columns, BOTH, pairs)
        return one, two, near, far, near_columns, far_columns, far_fold, extra_fold, third

    one, two, near, far, near_columns, far_columns, far_fold, extra_fold, third = lax.switch(
        branches[0],
        [functools.partial(exchange, at, beyond) for beyond in range(3) for at in range(nx)],
        one, two, near, far, fold, fold_columns,
    )

    vectors, diagonal, rhs, partial = kernel(
        krylov_kernel,
        out_shape=(shape(ITERS + 1, ROWS, COLS), shape(ROWS, COLS), shape(ROWS, COLS), shape(nx * ny, COLS)),
        in_specs=[smem] + [whole()] * 13,
        out_specs=(whole(),) * 4,
        scratch_shapes=[vmem(DEEP_SIZE, COLS), vmem(DEEP_SIZE, COLS)],
        name="krylov",
    )(
        fold_map, difference, coefficients, count, surface, one, two, near, far, near_columns, far_columns,
        far_fold, extra_fold, third,
    )

    moments = lax.all_to_all(partial, BOTH, 0, 0)

    batch = pl.BlockSpec((GROUP, LEVELS, ROWS, COLS), lambda i: (i, 0, 0, 0))
    mixed = kernel(
        tracers_kernel,
        grid=(GROUPS,),
        out_shape=shape(TRACERS, LEVELS, ROWS, COLS),
        in_specs=[smem, batch, all_of(coefficients), all_of(count)]
        + [block_of((COL_DEEP, COLS))] * 2
        + [block_of((EDGE, COLS))] * 4,
        out_specs=batch,
        scratch_shapes=[vmem(EDGE, COLS), vmem(EDGE, COLS), vmem(8, LEVELS, ROWS, COLS)],
        name="tracers",
    )(fold_map, tracer, coefficients, count, one, two, near, far, far_fold, extra_fold)

    pressure, residual, good = kernel(
        combine_kernel,
        out_shape=(shape(ROWS, COLS), shape(ROWS, COLS), jax.ShapeDtypeStruct((1,), jnp.int32)),
        in_specs=[whole()] * 3,
        out_specs=(whole(), whole(), smem),
        name="combine",
    )(moments, vectors, diagonal)
    pressure, residual = lax.cond(
        good[0] == 1,
        lambda pressure, residual, rhs, count, surface, fold: (pressure, residual),
        lambda pressure, residual, rhs, count, surface, fold: direct_gradients(rhs, count, fold, surface),
        pressure,
        residual,
        rhs,
        count,
        surface,
        fold_map,
    )
    return mixed, pressure, residual


def solution(mesh):
    in_specs = (
        P(None, None, "gy", "gx"),
        P(None, "gy", "gx"),
        P(None, "gy", "gx"),
        P(None, "gy", "gx"),
        P(None, "gy", "gx"),
        P("gy", "gx"),
        P(),
        P("gy", "gx"),
    )
    out_specs = (P(None, None, "gy", "gx"), P("gy", "gx"), P("gy", "gx"))
    body = functools.partial(shards, (mesh.shape["gx"], mesh.shape["gy"]))
    return jax.shard_map(body, mesh=mesh, in_specs=in_specs, out_specs=out_specs, check_vma=False)
```

```python
import functools

import jax
import jax.numpy as jnp
from jax import lax
from jax.experimental import pallas as pl
from jax.experimental.pallas import tpu as pltpu
from jax.sharding import PartitionSpec as P

ITERS = 4
TRACERS, LEVELS, ROWS, COLS = 16, 20, 8, 128
GROUP = 4
GROUPS = TRACERS // GROUP
DEPTH = 5
EDGE = TRACERS * LEVELS
BOTH = ("gx", "gy")
VMEM_LIMIT = 40 * 1024 * 1024
PACK_VMEM_LIMIT = 63 * 1024 * 1024

COL_DEEP, COL_SIZE = GROUPS * ROWS, (GROUPS + 5) * ROWS
COUNT_LANE, SURFACE_LANE = 100, 105
ROW_DIFF, ROW_FIELD, ROW_COUNT, ROW_SURFACE, ROW_SIZE = 320, 480, 800, 808, 816
ROW_EAST, ROW_WEST, DEEP_SIZE, SET = 816, 856, 576, 40

SCALAR_BOUND, FIELD_BOUND = 1500.0, 1.0e5

NEIGHBOURS = [
    (0, 1, 1.0),
    (0, -1, 1.0),
    (1, 0, 1.0),
    (-1, 0, 1.0),
    (1, 1, 0.5),
    (1, -1, 0.5),
    (-1, 1, 0.5),
    (-1, -1, 0.5),
]


def params(limit=VMEM_LIMIT):
    return pltpu.CompilerParams(vmem_limit_bytes=limit)


def whole():
    return pl.BlockSpec(memory_space=pltpu.VMEM)


def lanes():
    return lax.broadcasted_iota(jnp.int32, (ROWS, COLS), 1)


def sublanes():
    return lax.broadcasted_iota(jnp.int32, (ROWS, COLS), 0)


def roll(tile, shift, axis):
    size = tile.shape[axis]
    shift = shift % size
    return tile if shift == 0 else pltpu.roll(tile, shift, axis)


def east_of(tile, beyond, lane):
    return roll(jnp.where(lane == 0, beyond, tile), -1, 1)


def west_of(tile, beyond, lane):
    return roll(jnp.where(lane == COLS - 1, beyond, tile), 1, 1)


def north_of(tile, beyond, sub):
    return roll(jnp.where(sub == 0, beyond, tile), -1, 0)


def south_of(tile, beyond, sub):
    return roll(jnp.where(sub == ROWS - 1, beyond, tile), 1, 0)


def thickness(level):
    return 0.5 + 1.5 * level / (LEVELS - 1)


def turned(tile):
    return jnp.take_along_axis(tile, ROWS - 1 - sublanes(), axis=0)


def start_copies(pairs, ready):
    copies = [pltpu.make_async_copy(source, target, ready.at[i]) for i, (source, target) in enumerate(pairs)]
    for copy in copies:
        copy.start()
    return copies


def pack_kernel(
    tracer, east_vel, north_vel, diffusion, mixing, count, surface, fold_map,
    one, two, near_rows, far_rows, fold_rows, fold_columns, difference, fields, branches,
    cells, levels_ref, surface_ref, fold_ref, ready,
):
    lane = lanes()
    low = sublanes() < ROWS // 2
    size = GROUP * LEVELS * ROWS
    pairs = [(count, levels_ref), (surface, surface_ref)]
    pairs += [(tracer.at[pl.ds(g * size, size)], cells.at[pl.ds(g * size, size)]) for g in range(GROUPS)]
    pairs += [(field, fields.at[f]) for f, field in enumerate((east_vel, north_vel, diffusion, mixing))]
    pairs += [(fold_map, fold_ref)]
    copies = start_copies(pairs, ready)
    here = lax.axis_index("gy")
    even = here % 2 == 0
    is_top = here == lax.axis_size("gy") - 1
    eastward = lax.axis_index("gx") % 2 == 0

    def put(row, items):
        west = jnp.zeros((ROWS, COLS), jnp.float32)
        east = jnp.zeros((ROWS, COLS), jnp.float32)
        for tile, width, first in items:
            chosen = lane == first if width == 1 else (lane >= first) & (lane < first + width)
            west = jnp.where(chosen, roll(tile, first, 1), west)
            east = jnp.where(chosen, roll(tile, first + width, 1), east)
        one[row : row + ROWS, :] = jnp.where(eastward, east, west)
        two[row : row + ROWS, :] = jnp.where(eastward, west, east)
        if row >= COL_DEEP:
            fold_columns[row - COL_DEEP : row - COL_DEEP + ROWS, :] = turned(east)
            fold_columns[SET + row - COL_DEEP : SET + row - COL_DEEP + ROWS, :] = turned(west)

    copies[0].wait()
    copies[1].wait()
    levels, surfaces = levels_ref[...], surface_ref[...]
    depths = levels.astype(jnp.float32)
    per = 2 * LEVELS
    level_row = lax.broadcasted_iota(jnp.int32, (per, COLS), 0)
    level_row = jnp.where(level_row >= LEVELS, level_row - LEVELS, level_row)
    wet_south = level_row < jnp.broadcast_to(levels[:1, :], (per, COLS))
    wet_north = level_row < jnp.broadcast_to(levels[ROWS - 1 :, :], (per, COLS))

    def cell(t, k):
        row = (t * LEVELS + k) * ROWS
        return jnp.where(k < levels, cells[row : row + ROWS, :], 0.0)

    for g in range(GROUPS):
        copies[2 + g].wait()
        put(g * ROWS, [(cell(g * GROUP + t, k), 1, t * LEVELS + k) for t in range(GROUP) for k in range(LEVELS)])
        if g == 0:
            for k in range(LEVELS):
                difference[k] = cell(0, k) - cell(1, k)
            items = [(difference[k], 5, 5 * k) for k in range(LEVELS)]
            put(COL_DEEP, items + [(depths, 5, COUNT_LANE), (surfaces, 4, SURFACE_LANE)])
        for at in range(g * GROUP * LEVELS, (g + 1) * GROUP * LEVELS, per):
            south = jnp.where(wet_south, cells[pl.ds(at * ROWS, per, stride=ROWS), :], 0.0)
            north = jnp.where(wet_north, cells[pl.ds(at * ROWS + ROWS - 1, per, stride=ROWS), :], 0.0)
            near_rows[at : at + per, :] = jnp.where(even, north, south)
            far_rows[at : at + per, :] = jnp.where(even, south, north)
    for f in range(4):
        copies[2 + GROUPS + f].wait()
        put(COL_DEEP + (1 + f) * ROWS, [(fields[f, k], 4, 4 * k) for k in range(LEVELS)])
    copies[-1].wait()
    pole = pole_of(fold_ref)
    offset, block = pole & (COLS - 1), pole >> (COLS.bit_length() - 1)
    blocks = lax.axis_size("gx")
    branches[0] = block
    third = jnp.where(offset < DEPTH, block - 2, block + 1) & (blocks - 1)
    branches[1] = jnp.where((offset < DEPTH) | (offset > COLS - DEPTH), third, blocks)

    def pack(kind, out):
        turn = turned if kind == "fold" else (lambda tile: tile)
        for k in range(LEVELS):
            out[ROW_DIFF + ROWS * k : ROW_DIFF + ROWS * (k + 1), :] = turn(difference[k])
        for f in range(4):
            for m in range(LEVELS // 2):
                first, second = turn(fields[f, 2 * m]), turn(fields[f, 2 * m + 1])
                if kind == "north":
                    tile = jnp.where(low, roll(first, 4, 0), second)
                else:
                    tile = jnp.where(low, first, roll(second, 4, 0))
                row = ROW_FIELD + ROWS * (f * (LEVELS // 2) + m)
                out[row : row + ROWS, :] = tile
        out[ROW_COUNT : ROW_COUNT + ROWS, :] = turn(depths)
        out[ROW_SURFACE : ROW_SURFACE + ROWS, :] = turn(surfaces)

    @pl.when(even)
    def _():
        pack("north", near_rows)
        pack("south", far_rows)

    @pl.when(jnp.logical_not(even))
    def _():
        pack("south", near_rows)

    @pl.when(jnp.logical_not(even) & jnp.logical_not(is_top))
    def _():
        pack("north", far_rows)

    @pl.when(is_top)
    def _():
        fold_rows[:ROW_DIFF, :] = far_rows[:ROW_DIFF, :]
        pack("fold", fold_rows)


def sides(one, two, row):
    first, second = one[pl.ds(row, ROWS), :], two[pl.ds(row, ROWS), :]
    eastward = lax.axis_index("gx") % 2 == 0
    return jnp.where(eastward, first, second), jnp.where(eastward, second, first)


def beside_kernel(one, two, near, far, far_fold, extra_fold, columns):
    del near, far, far_fold, extra_fold
    for row in range(0, SET, ROWS):
        east, west = sides(one, two, COL_DEEP + row)
        columns[row : row + ROWS, :] = east
        columns[SET + row : SET + row + ROWS, :] = west


def pole_of(fold_map):
    return (fold_map[0] + 1) & (COLS * lax.axis_size("gx") - 1)


def halo_rows(fold_map, near, far, far_fold, extra_fold, north_rows, south_rows):
    here = lax.axis_index("gy")
    top = lax.axis_size("gy") - 1

    @pl.when(here % 2 == 0)
    def _():
        north_rows[...] = near[...]
        south_rows[...] = far[...]

    @pl.when(here % 2 == 1)
    def _():
        south_rows[...] = near[...]

    @pl.when((here % 2 == 1) & (here != top))
    def _():
        north_rows[...] = far[...]

    @pl.when(here == top)
    def _():
        lane = lanes()
        pole = pole_of(fold_map)
        offset = pole & (COLS - 1)
        index = (offset - 1 - lane) & (COLS - 1)
        within_far = (lane >= offset) == ((pole & COLS) != 0)
        for row in range(0, north_rows.shape[0], ROWS):
            rows = jnp.where(within_far, far_fold[row : row + ROWS, :], extra_fold[row : row + ROWS, :])
            north_rows[row : row + ROWS, :] = jnp.take_along_axis(rows, index, axis=1)


def unfold(offset, first_in_far, far, extra, third, out):
    lane = lanes()
    index = (offset - 1 - lane) & (COLS - 1)
    within_far = (lane >= offset) == first_in_far
    zero = jnp.zeros((ROWS, COLS), jnp.float32)

    def store(row, value):
        out[row - ROW_DIFF : row - ROW_DIFF + ROWS, :] = value

    def flipped(row, sign):
        a, b = far[row : row + ROWS, :], extra[row : row + ROWS, :]
        store(row, sign * jnp.take_along_axis(jnp.where(within_far, a, b), index, axis=1))
        return sign * jnp.take_along_axis(jnp.where(within_far, b, a), index, axis=1)

    def collect(packed, tile, width, at):
        chosen = (lane >= at) & (lane < at + width)
        return jnp.where(chosen, roll(tile, at, 1), packed[0]), jnp.where(chosen, roll(tile, at + width, 1), packed[1])

    def finish(row, packed, sign, width, within):
        beside = (lane + (offset - 1) + width - 2 * within) & (COLS - 1)
        right = sign * jnp.take_along_axis(third[row : row + ROWS, :], beside, axis=1)
        beside = (lane + (offset - 1 - COLS) + width - 2 * within) & (COLS - 1)
        left = sign * jnp.take_along_axis(third[SET + row : SET + row + ROWS, :], beside, axis=1)
        store(ROW_EAST + row, jnp.where(within < offset, packed[0], right))
        store(ROW_WEST + row, jnp.where(within >= offset + width - COLS, packed[1], left))

    packed = (zero, zero)
    for k in range(LEVELS):
        packed = collect(packed, flipped(ROW_DIFF + ROWS * k, 1.0), 5, 5 * k)
    packed = collect(packed, flipped(ROW_COUNT, 1.0), 5, COUNT_LANE)
    packed = collect(packed, flipped(ROW_SURFACE, 1.0), 4, SURFACE_LANE)
    fifth = lane - 5 * ((lane * 205) >> 10)
    finish(0, packed, 1.0, jnp.where(lane >= SURFACE_LANE, 4, 5), fifth)
    for f in range(4):
        sign = -1.0 if f < 2 else 1.0
        packed = (zero, zero)
        for m in range(LEVELS // 2):
            tile = flipped(ROW_FIELD + ROWS * (f * (LEVELS // 2) + m), sign)
            packed = collect(packed, tile, 4, 8 * m)
            packed = collect(packed, roll(tile, 4, 0), 4, 8 * m + 4)
        finish((1 + f) * ROWS, packed, sign, 4, lane & 3)


def unpack(east, west, first, width, lane):
    right = roll(east, -first, 1)
    left = roll(west, -width - first, 1)
    return jnp.where(lane < width, right, jnp.where(lane >= COLS - width, left, 0.0))


def both_east(one, two, lane):
    return east_of(one, two, lane), east_of(two, one, lane)


def both_west(one, two, lane):
    return west_of(one, two, lane), west_of(two, one, lane)


def krylov_kernel(
    fold_map, difference, fields, count, surface, one, two, near, far, near_columns, far_columns,
    far_fold, extra_fold, third,
    vectors, diagonal, right_side, partial,
    north_buf, south_buf,
):
    here = lax.axis_index("gy")
    top = lax.axis_size("gy") - 1
    lane, sub = lanes(), sublanes()
    low = sub < 4
    def fill(out, rows, columns):
        out[: ROW_SIZE - ROW_DIFF, :] = rows[ROW_DIFF:, :]
        out[ROW_SIZE - ROW_DIFF :, :] = columns[...]

    @pl.when(here % 2 == 0)
    def _():
        fill(north_buf, near, near_columns)
        fill(south_buf, far, far_columns)

    @pl.when(here % 2 == 1)
    def _():
        fill(south_buf, near, near_columns)

    @pl.when((here % 2 == 1) & (here != top))
    def _():
        fill(north_buf, far, far_columns)

    @pl.when(here == top)
    def _():
        pole = pole_of(fold_map)
        unfold(pole & (COLS - 1), (pole & COLS) != 0, far_fold, extra_fold, third, north_buf)

    def at(ref, row):
        return ref[row - ROW_DIFF : row - ROW_DIFF + ROWS, :]

    def field_tile(ref, f, k):
        return at(ref, ROW_FIELD + ROWS * (f * (LEVELS // 2) + k // 2))

    def halo_main(f, k):
        north, south = field_tile(north_buf, f, k), field_tile(south_buf, f, k)
        return jnp.where(low, roll(north, 4 * (k % 2), 0), roll(south, 4 * (1 - k % 2), 0))

    def side(ref, f, first, width):
        return unpack(at(ref, ROW_EAST + ROWS * f), at(ref, ROW_WEST + ROWS * f), first, width, lane)

    halo_packed = [
        [
            jnp.where(low, at(north_buf, base + ROWS * (1 + f)), at(south_buf, base + ROWS * (1 + f)))
            for base in (ROW_EAST, ROW_WEST)
        ]
        for f in range(4)
    ]

    columns = [sides(one, two, COL_DEEP + ROWS * f) for f in range(5)]

    def column(f):
        return columns[f]

    def neighbours_across(own, north, south):
        up, up_n, up_s = roll(own, -1, 0), roll(north, -1, 0), roll(south, -1, 0)
        down, down_n, down_s = roll(own, 1, 0), roll(north, 1, 0), roll(south, 1, 0)
        return (
            jnp.where(sub == 7, up_n, up),
            jnp.where(low, up_n, jnp.where(sub == 7, up, up_s)),
            jnp.where(sub == 0, down_s, down),
            jnp.where(sub == 0, down, jnp.where(low, down_n, down_s)),
        )

    def halo(pair):
        return jnp.where(low, pair[0], pair[1])

    counts_own = (count[...].astype(jnp.float32), unpack(*column(0), COUNT_LANE, 5, lane))
    counts_north = (at(north_buf, ROW_COUNT), side(north_buf, 0, COUNT_LANE, 5))
    counts_south = (at(south_buf, ROW_COUNT), side(south_buf, 0, COUNT_LANE, 5))
    counts = (counts_own[0], counts_own[1], halo((counts_north[0], counts_south[0])), halo((counts_north[1], counts_south[1])))
    surfaces = (
        surface[...],
        unpack(*column(0), SURFACE_LANE, 4, lane),
        halo((at(north_buf, ROW_SURFACE), at(south_buf, ROW_SURFACE))),
        halo((side(north_buf, 0, SURFACE_LANE, 4), side(south_buf, 0, SURFACE_LANE, 4))),
    )

    zero = jnp.zeros((ROWS, COLS), jnp.float32)
    c_prev, r_prev, a_prev = [zero] * 4, [zero] * 4, [zero] * 4
    c_list, r_list = [], []
    for k in range(LEVELS):
        own = (difference[k], unpack(*column(0), 5 * k, 5, lane))
        north = (at(north_buf, ROW_DIFF + ROWS * k), side(north_buf, 0, 5 * k, 5))
        south = (at(south_buf, ROW_DIFF + ROWS * k), side(south_buf, 0, 5 * k, 5))
        halos = (halo((north[0], south[0])), halo((north[1], south[1])))
        centre = (own[0], own[1], halos[0], halos[1])
        easts = both_east(*own, lane) + both_east(*halos, lane)
        wests = both_west(*own, lane) + both_west(*halos, lane)
        first = neighbours_across(own[0], north[0], south[0])
        second = neighbours_across(own[1], north[1], south[1])
        norths = (first[0], second[0], first[1], second[1])
        souths = (first[2], second[2], first[3], second[3])
        values = [
            (fields[f, k], unpack(*column(1 + f), 4 * k, 4, lane), halo_main(f, k), unpack(*halo_packed[f], 4 * k, 4, lane))
            for f in range(4)
        ]
        c_now, r_now, a_now = [], [], []
        for i in range(4):
            u, v, spread, mix = (value[i] for value in values)
            change = (
                -0.5 * u * (easts[i] - wests[i])
                - 0.5 * v * (norths[i] - souths[i])
                + spread * (easts[i] + wests[i] + norths[i] + souths[i] - 4.0 * centre[i])
            )
            explicit = centre[i] + jnp.where(k < counts[i], change, 0.0)
            a = jnp.where(k + 1 < counts[i], mix, 0.0)
            inverse = 1.0 / (1.0 + a_prev[i] + a + a_prev[i] * c_prev[i])
            c_now.append(-a * inverse)
            r_now.append((explicit + a_prev[i] * r_prev[i]) * inverse)
            a_now.append(a)
        c_prev, r_prev, a_prev = c_now, r_now, a_now
        c_list.append(c_now)
        r_list.append(r_now)
    total, x_next = [zero] * 4, [zero] * 4
    for k in range(LEVELS - 1, -1, -1):
        x_next = [r_list[k][i] - c_list[k][i] * x_next[i] for i in range(4)]
        total = [total[i] + thickness(k) * x_next[i] for i in range(4)]
    rhs = [jnp.where(counts[i] > 0, 0.25 * total[i], 0.0) for i in range(4)]

    def depth_of(levels):
        depth = zero
        for k in range(LEVELS):
            depth = depth + jnp.where(k < levels, thickness(k), 0.0)
        return depth / LEVELS

    own = tuple(depth_of(levels) for levels in counts_own)
    north = tuple(depth_of(levels) for levels in counts_north)
    south = tuple(depth_of(levels) for levels in counts_south)
    depths = (own[0], own[1], halo((north[0], south[0])), halo((north[1], south[1])))

    def rows_of(own, north, south):
        first = neighbours_across(own[0], north[0], south[0])
        second = neighbours_across(own[1], north[1], south[1])
        return (first[0], second[0], first[1], second[1]), (first[2], second[2], first[3], second[3])

    def coupled(others, weight):
        return [weight * jnp.minimum(depths[i], others[i]) for i in range(4)]

    own_e, north_e, south_e = (both_east(*pair, lane) for pair in (own, north, south))
    own_w, north_w, south_w = (both_west(*pair, lane) for pair in (own, north, south))
    halo_e = (halo((north_e[0], south_e[0])), halo((north_e[1], south_e[1])))
    halo_w = (halo((north_w[0], south_w[0])), halo((north_w[1], south_w[1])))
    mid = rows_of(own, north, south)
    mid_e = rows_of(own_e, north_e, south_e)
    mid_w = rows_of(own_w, north_w, south_w)
    couplings = [
        coupled(own_e + halo_e, 1.0),
        coupled(own_w + halo_w, 1.0),
        coupled(mid[0], 1.0),
        coupled(mid[1], 1.0),
        coupled(mid_e[0], 0.5),
        coupled(mid_w[0], 0.5),
        coupled(mid_e[1], 0.5),
        coupled(mid_w[1], 0.5),
    ]
    diag = [
        jnp.where(counts[i] > 0, surfaces[i] + sum(entry[i] for entry in couplings), 1.0) for i in range(4)
    ]
    inverse = [1.0 / diag[i] for i in range(4)]
    couplings = [[entry[i] * inverse[i] for i in range(4)] for entry in couplings]

    def shifted_rows(tiles):
        north, south = [None] * 4, [None] * 4
        for i in range(2):
            a, b = roll(tiles[i], -1, 0), roll(tiles[i + 2], -1, 0)
            north[i], north[i + 2] = jnp.where(sub == 7, b, a), jnp.where(sub == 7, a, b)
            a, b = roll(tiles[i], 1, 0), roll(tiles[i + 2], 1, 0)
            south[i], south[i + 2] = jnp.where(sub == 0, b, a), jnp.where(sub == 0, a, b)
        return north, south

    def spread_out(tiles):
        east = both_east(tiles[0], tiles[1], lane) + both_east(tiles[2], tiles[3], lane)
        west = both_west(tiles[0], tiles[1], lane) + both_west(tiles[2], tiles[3], lane)
        mid_n, mid_s = shifted_rows(tiles)
        east_n, east_s = shifted_rows(east)
        west_n, west_s = shifted_rows(west)
        around = (east, west, mid_n, mid_s, east_n, west_n, east_s, west_s)
        return [sum(entry[i] * values[i] for entry, values in zip(couplings, around)) for i in range(4)]

    found = [[rhs[i] * inverse[i] for i in range(4)]]
    found.append(spread_out(found[0]))
    for _ in range(2, ITERS + 1):
        ahead = spread_out(found[-1])
        found.append([2.0 * ahead[i] - found[-2][i] for i in range(4)])
    for j in range(ITERS + 1):
        vectors[j] = found[j][0]
    diagonal[...] = diag[0]
    right_side[...] = rhs[0]
    weighted = [diag[0] * found[j][0] for j in range(ITERS + 1)]
    sums = [weighted[j] * found[j][0] for j in range(ITERS + 1)]
    sums += [weighted[j] * found[j + 1][0] for j in range(ITERS)]
    row = jnp.zeros((1, COLS), jnp.float32)
    for j, entry in enumerate(sums):
        row = jnp.where(lane[:1, :] == j, jnp.sum(entry, keepdims=True), row)
    partial[...] = jnp.broadcast_to(row, partial.shape)


def combine_kernel(moments, vectors, diagonal, pressure, residual, good):
    size = ITERS + 1
    sums = jnp.sum(moments[...], axis=0, keepdims=True)

    def lane_of(j):
        return jnp.broadcast_to(sums[:, j : j + 1], (ROWS, COLS))

    even = [lane_of(j) for j in range(size)]
    odd = [lane_of(size + j) for j in range(ITERS)]
    mu = []
    for j in range(size):
        mu.append(even[0] if j == 0 else 2.0 * even[j] - even[0])
        if j < ITERS:
            mu.append(odd[0] if j == 0 else 2.0 * odd[j] - odd[0])

    def mass(i, j):
        return 0.5 * (mu[i + j] + mu[abs(i - j)])

    def stiffness(i, j):
        i, j = min(i, j), max(i, j)
        if j == 0:
            return mu[0] - mu[1]
        return mass(i, j) - 0.5 * (mass(i, j + 1) + mass(i, j - 1))

    def form(values, entry):
        out = None
        for i in range(len(values)):
            inner = values[i] * entry(i, i)
            for j in range(i + 1, len(values)):
                inner = inner + 2.0 * values[j] * entry(i, j)
            out = values[i] * inner if out is None else out + values[i] * inner
        return out

    def applied(values):
        out = [value for value in values] + [jnp.zeros_like(values[0])]
        out[1] = out[1] - values[0]
        for j in range(1, len(values)):
            out[j + 1] = out[j + 1] - 0.5 * values[j]
            out[j - 1] = out[j - 1] - 0.5 * values[j]
        return out

    def amplified(values, result):
        total = sum(jnp.abs(value) for value in values)
        return total * total * mu[0] / result

    scaled = [jnp.ones((ROWS, COLS), jnp.float32)]
    direction = list(scaled)
    solution_at = []
    energy = mu[0]
    fine = energy > 0.0
    for step in range(ITERS):
        image = applied(direction)
        curvature = form(direction, stiffness)
        step_size = energy / curvature
        fine = fine & (amplified(direction, curvature) <= SCALAR_BOUND) & (curvature > 0.0)
        solution_at = [
            step_size * value + (solution_at[j] if j < len(solution_at) else 0.0) for j, value in enumerate(direction)
        ]
        scaled = [
            (scaled[j] if j < len(scaled) else 0.0) - step_size * value for j, value in enumerate(image)
        ]
        energy_new = form(scaled, mass)
        bound = SCALAR_BOUND if step + 1 < ITERS else FIELD_BOUND
        fine = fine & (amplified(scaled, energy_new) <= bound) & (energy_new > 0.0)
        if step + 1 < ITERS:
            ratio = energy_new / energy
            direction = [
                scaled[j] + (ratio * direction[j] if j < len(direction) else 0.0) for j in range(len(scaled))
            ]
            energy = energy_new
    pressure[...] = sum(solution_at[j] * vectors[j] for j in range(len(solution_at)))
    residual[...] = diagonal[...] * sum(scaled[j] * vectors[j] for j in range(len(scaled)))
    good[0] = jnp.min(jnp.where(fine, 1, 0).astype(jnp.int32))


def tracers_kernel(
    fold_map, tracer, fields, count, one, two, near, far, far_fold, extra_fold, partial,
    mixed,
    north_rows, south_rows, factors,
):
    del partial
    lane, sub = lanes(), sublanes()
    levels = count[...]
    group = pl.program_id(0)

    @pl.when(group == 0)
    def _():
        halo_rows(fold_map, near, far, far_fold, extra_fold, north_rows, south_rows)
        c_prev = jnp.zeros((ROWS, COLS), jnp.float32)
        a_prev = jnp.zeros((ROWS, COLS), jnp.float32)
        for k in range(LEVELS):
            wet = jnp.where(k < levels, 1.0, 0.0)
            u, v, spread = 0.5 * wet * fields[0, k], 0.5 * wet * fields[1, k], wet * fields[2, k]
            a = jnp.where(k + 1 < levels, fields[3, k], 0.0)
            inverse = 1.0 / (1.0 + a_prev + a + a_prev * c_prev)
            c_prev = -a * inverse
            factors[0, k] = 1.0 - 4.0 * spread
            factors[1, k] = spread - u
            factors[2, k] = spread + u
            factors[3, k] = spread - v
            factors[4, k] = spread + v
            factors[5, k] = inverse
            factors[6, k] = a_prev
            factors[7, k] = c_prev
            a_prev = a

    row = pl.multiple_of(group * ROWS, ROWS)
    columns_east, columns_west = sides(one, two, row)
    r_prev = [jnp.zeros((ROWS, COLS), jnp.float32)] * GROUP
    for k in range(LEVELS):
        centre, to_e, to_w, to_n, to_s, inverse, above = (factors[j, k] for j in range(7))
        wet = k < levels
        for t in range(GROUP):
            cell = jnp.where(wet, tracer[t, k], 0.0)
            at = t * LEVELS + k
            halo_row = group * (GROUP * LEVELS) + at
            east = east_of(cell, roll(columns_east, -at, 1), lane)
            west = west_of(cell, roll(columns_west, COLS - 1 - at, 1), lane)
            north = north_of(cell, north_rows[pl.ds(halo_row, 1), :], sub)
            south = south_of(cell, south_rows[pl.ds(halo_row, 1), :], sub)
            explicit = centre * cell + to_e * east + to_w * west + to_n * north + to_s * south
            r_prev[t] = (explicit + above * r_prev[t]) * inverse
            mixed[t, k] = r_prev[t]
    x_next = r_prev
    for k in range(LEVELS - 2, -1, -1):
        below = factors[7, k]
        for t in range(GROUP):
            x_next[t] = mixed[t, k] - below * x_next[t]
            mixed[t, k] = x_next[t]


def extended(cells, sides, width):
    for axis, dim in sides:
        count = lax.axis_size(axis)
        head = lax.slice_in_dim(cells, 0, width, axis=dim)
        tail = lax.slice_in_dim(cells, cells.shape[dim] - width, cells.shape[dim], axis=dim)
        cells = jnp.concatenate(
            [
                lax.ppermute(tail, axis, [(i, (i + 1) % count) for i in range(count)]),
                cells,
                lax.ppermute(head, axis, [((i + 1) % count, i) for i in range(count)]),
            ],
            axis=dim,
        )
    return cells


def extend(field, fold_map):
    rows, cols = field.shape
    padded = extended(field, (("gx", 1), ("gy", 0)), 1)
    total_cols = fold_map.shape[0]
    whole_row = lax.all_gather(field[rows - 1, :], "gx", axis=0, tiled=True)
    start = lax.axis_index("gx") * cols
    wanted = (start - 1 + jnp.arange(cols + 2, dtype=jnp.int32)) % total_cols
    folded = jnp.take(whole_row, jnp.take(fold_map, wanted), axis=0)
    row_index = lax.axis_index("gy")
    upper = jnp.where(row_index == lax.axis_size("gy") - 1, folded, padded[rows + 1, :])
    lower = jnp.where(row_index == 0, 0.0, padded[0, :])
    return jnp.concatenate([lower[None, :], padded[1 : rows + 1, :], upper[None, :]], axis=0)


def window(padded, row_off, col_off):
    rows = padded.shape[0] - 2
    cols = padded.shape[1] - 2
    return padded[1 + row_off : 1 + row_off + rows, 1 + col_off : 1 + col_off + cols]


def total_of(value):
    return lax.psum(jnp.sum(value), BOTH)


def direct_gradients(rhs, level_count, fold_map, surface_term):
    levels = jnp.arange(LEVELS, dtype=jnp.int32)[:, None, None]
    level_mask = (levels < level_count[None]).astype(jnp.float32)
    thick = (0.5 + 1.5 * jnp.arange(LEVELS).astype(jnp.float32) / (LEVELS - 1))[:, None, None]
    depth = jnp.sum(thick * level_mask, axis=0) / LEVELS
    wet_cells = level_count > 0
    depth_pad = extend(depth, fold_map)
    couplings = [
        weight * jnp.minimum(depth, window(depth_pad, row_off, col_off)) for row_off, col_off, weight in NEIGHBOURS
    ]
    diag = jnp.where(wet_cells, surface_term + sum(couplings), 1.0)

    def step(_, state):
        pressure, residual, direction, energy = state
        field_pad = extend(direction, fold_map)
        summed = jnp.zeros_like(direction)
        for entry, (row_off, col_off, _weight) in zip(couplings, NEIGHBOURS):
            summed = summed + entry * window(field_pad, row_off, col_off)
        image = jnp.where(wet_cells, diag * direction - summed, direction)
        step_size = energy / total_of(direction * image)
        pressure = pressure + step_size * direction
        residual = residual - step_size * image
        scaled = residual / diag
        energy_new = total_of(residual * scaled)
        return pressure, residual, scaled + energy_new / energy * direction, energy_new

    scaled = rhs / diag
    state = (jnp.zeros_like(rhs), rhs, scaled, total_of(rhs * scaled))
    state = lax.fori_loop(0, ITERS, step, state)
    return state[0], state[1]


def kernel(body, limit=VMEM_LIMIT, **rest):
    return pl.pallas_call(body, compiler_params=params(limit), **rest)


def shape(*dims):
    return jax.ShapeDtypeStruct(dims, jnp.float32)


def vmem(*dims):
    return pltpu.VMEM(dims, jnp.float32)


def block_of(dims, at=0):
    return pl.BlockSpec(dims, lambda i: (at,) + (0,) * (len(dims) - 1))


def all_of(array):
    return block_of(array.shape)


def shards(sizes, tracer, east_vel, north_vel, diffusion, mixing, count, fold_map, surface):
    nx, ny = sizes
    hbm = pl.BlockSpec(memory_space=pltpu.HBM)
    smem = pl.BlockSpec(memory_space=pltpu.SMEM)
    fields = (east_vel, north_vel, diffusion, mixing)

    def device(x, y):
        return (x % nx) * ny + y

    one, two, near, far, fold, fold_columns, difference, coefficients, branches = kernel(
        pack_kernel,
        limit=PACK_VMEM_LIMIT,
        out_shape=(
            shape(COL_SIZE, COLS),
            shape(COL_SIZE, COLS),
            shape(ROW_SIZE, COLS),
            shape(ROW_SIZE, COLS),
            shape(ROW_SIZE, COLS),
            shape(2 * SET, COLS),
            shape(LEVELS, ROWS, COLS),
            shape(4, LEVELS, ROWS, COLS),
            jax.ShapeDtypeStruct((2,), jnp.int32),
        ),
        in_specs=[hbm] * 8,
        out_specs=(whole(),) * 8 + (smem,),
        scratch_shapes=[
            vmem(EDGE * ROWS, COLS),
            pltpu.VMEM((ROWS, COLS), jnp.int32),
            vmem(ROWS, COLS),
            pltpu.SMEM(fold_map.shape, jnp.int32),
            pltpu.SemaphoreType.DMA((GROUPS + 7,)),
        ],
        name="pack",
    )(tracer.reshape(EDGE * ROWS, COLS), *fields, count, surface, fold_map)

    swap = [(device(x ^ 1, y), device(x, y)) for x in range(nx) for y in range(ny)]
    shift = [(device(x + 1 if x % 2 else x - 1, y), device(x, y)) for x in range(nx) for y in range(ny)]
    pairs = [(device(x, y ^ 1), device(x, y)) for x in range(nx) for y in range(ny)]
    inner = [(device(x, y + 1 if y % 2 else y - 1), device(x, y)) for x in range(nx) for y in range(1, ny - 1)]

    def across(turn, rows):
        return lax.ppermute(rows, BOTH, [(device(turn - x, ny - 1), device(x, ny - 1)) for x in range(nx)])

    def exchange(at, one, two, rows):
        even, odd = (at, at - 1) if at % 2 == 0 else (at - 1, at)
        one, two = lax.ppermute(one, BOTH, swap), lax.ppermute(two, BOTH, shift)
        return one, two, across(even, rows), across(odd, rows)

    far, near = lax.ppermute(far, BOTH, inner), lax.ppermute(near, BOTH, pairs)
    one, two, far_fold, extra_fold = lax.switch(
        branches[0], [functools.partial(exchange, at) for at in range(nx)], one, two, fold
    )
    columns = kernel(
        beside_kernel,
        grid=(1,),
        out_shape=shape(2 * SET, COLS),
        in_specs=[block_of((COL_SIZE, COLS))] * 2 + [pl.BlockSpec(memory_space=pl.ANY)] * 4,
        out_specs=block_of((2 * SET, COLS)),
        name="beside",
    )(one, two, near, far, far_fold, extra_fold)
    far_columns, near_columns = lax.ppermute(columns, BOTH, inner), lax.ppermute(columns, BOTH, pairs)
    third = lax.switch(
        branches[1], [functools.partial(across, at) for at in range(nx)] + [lambda rows: rows], fold_columns
    )

    vectors, diagonal, rhs, partial = kernel(
        krylov_kernel,
        out_shape=(shape(ITERS + 1, ROWS, COLS), shape(ROWS, COLS), shape(ROWS, COLS), shape(nx * ny, COLS)),
        in_specs=[smem] + [whole()] * 13,
        out_specs=(whole(),) * 4,
        scratch_shapes=[vmem(DEEP_SIZE, COLS), vmem(DEEP_SIZE, COLS)],
        name="krylov",
    )(
        fold_map, difference, coefficients, count, surface, one, two, near, far, near_columns, far_columns,
        far_fold, extra_fold, third,
    )

    moments = lax.all_to_all(partial, BOTH, 0, 0)

    batch = pl.BlockSpec((GROUP, LEVELS, ROWS, COLS), lambda i: (i, 0, 0, 0))
    mixed = kernel(
        tracers_kernel,
        grid=(GROUPS,),
        out_shape=shape(TRACERS, LEVELS, ROWS, COLS),
        in_specs=[smem, batch, all_of(coefficients), all_of(count)]
        + [block_of((COL_DEEP, COLS))] * 2
        + [block_of((EDGE, COLS))] * 4
        + [pl.BlockSpec(memory_space=pl.ANY)],
        out_specs=batch,
        scratch_shapes=[vmem(EDGE, COLS), vmem(EDGE, COLS), vmem(8, LEVELS, ROWS, COLS)],
        name="tracers",
    )(fold_map, tracer, coefficients, count, one, two, near, far, far_fold, extra_fold, partial)

    pressure, residual, good = kernel(
        combine_kernel,
        out_shape=(shape(ROWS, COLS), shape(ROWS, COLS), jax.ShapeDtypeStruct((1,), jnp.int32)),
        in_specs=[whole()] * 3,
        out_specs=(whole(), whole(), smem),
        name="combine",
    )(moments, vectors, diagonal)
    pressure, residual = lax.cond(
        good[0] == 1,
        lambda pressure, residual, rhs, count, surface, fold: (pressure, residual),
        lambda pressure, residual, rhs, count, surface, fold: direct_gradients(rhs, count, fold, surface),
        pressure,
        residual,
        rhs,
        count,
        surface,
        fold_map,
    )
    return mixed, pressure, residual


def solution(mesh):
    in_specs = (
        P(None, None, "gy", "gx"),
        P(None, "gy", "gx"),
        P(None, "gy", "gx"),
        P(None, "gy", "gx"),
        P(None, "gy", "gx"),
        P("gy", "gx"),
        P(),
        P("gy", "gx"),
    )
    out_specs = (P(None, None, "gy", "gx"), P("gy", "gx"), P("gy", "gx"))
    body = functools.partial(shards, (mesh.shape["gx"], mesh.shape["gy"]))
    return jax.shard_map(body, mesh=mesh, in_specs=in_specs, out_specs=out_specs, check_vma=False)
```

```python
import functools

import jax
import jax.numpy as jnp
from jax import lax
from jax.experimental import pallas as pl
from jax.experimental.pallas import tpu as pltpu
from jax.sharding import PartitionSpec as P

ITERS = 4
TRACERS, LEVELS, ROWS, COLS = 16, 20, 8, 128
GROUP = 4
GROUPS = TRACERS // GROUP
EDGE = TRACERS * LEVELS
BOTH = ("gx", "gy")
VMEM_LIMIT = 40 * 1024 * 1024
PACK_VMEM_LIMIT = 63 * 1024 * 1024

COL_DEEP, COL_SIZE = GROUPS * ROWS, (GROUPS + 5) * ROWS
COUNT_LANE, SURFACE_LANE = 100, 105
ROW_EAST, ROW_WEST, ROW_DIFF, ROW_FIELD, ROW_COUNT, ROW_SURFACE, ROW_SIZE = 320, 360, 400, 560, 880, 888, 896
DEEP_SIZE = ROW_SIZE - ROW_EAST

SCALAR_BOUND, FIELD_BOUND = 1500.0, 1.0e5

NEIGHBOURS = [
    (0, 1, 1.0),
    (0, -1, 1.0),
    (1, 0, 1.0),
    (-1, 0, 1.0),
    (1, 1, 0.5),
    (1, -1, 0.5),
    (-1, 1, 0.5),
    (-1, -1, 0.5),
]


def params(limit=VMEM_LIMIT):
    return pltpu.CompilerParams(vmem_limit_bytes=limit)


def whole():
    return pl.BlockSpec(memory_space=pltpu.VMEM)


def lanes():
    return lax.broadcasted_iota(jnp.int32, (ROWS, COLS), 1)


def sublanes():
    return lax.broadcasted_iota(jnp.int32, (ROWS, COLS), 0)


def roll(tile, shift, axis):
    size = tile.shape[axis]
    shift = shift % size
    return tile if shift == 0 else pltpu.roll(tile, shift, axis)


def east_of(tile, beyond, lane):
    return roll(jnp.where(lane == 0, beyond, tile), -1, 1)


def west_of(tile, beyond, lane):
    return roll(jnp.where(lane == COLS - 1, beyond, tile), 1, 1)


def north_of(tile, beyond, sub):
    return roll(jnp.where(sub == 0, beyond, tile), -1, 0)


def south_of(tile, beyond, sub):
    return roll(jnp.where(sub == ROWS - 1, beyond, tile), 1, 0)


def thickness(level):
    return 0.5 + 1.5 * level / (LEVELS - 1)


def turned(tile):
    return jnp.take_along_axis(tile, ROWS - 1 - sublanes(), axis=0)


def start_copies(pairs, ready):
    copies = [pltpu.make_async_copy(source, target, ready.at[i]) for i, (source, target) in enumerate(pairs)]
    for copy in copies:
        copy.start()
    return copies


def pack_kernel(
    tracer, east_vel, north_vel, diffusion, mixing, count, surface, fold_map,
    one, two, near_rows, far_rows, difference, fields, branches,
    cells, levels_ref, surface_ref, fold_ref, ready,
):
    lane = lanes()
    low = sublanes() < ROWS // 2
    size = GROUP * LEVELS * ROWS
    pairs = [(count, levels_ref), (surface, surface_ref)]
    pairs += [(tracer.at[pl.ds(g * size, size)], cells.at[pl.ds(g * size, size)]) for g in range(GROUPS)]
    pairs += [(field, fields.at[f]) for f, field in enumerate((east_vel, north_vel, diffusion, mixing))]
    pairs += [(fold_map, fold_ref)]
    copies = start_copies(pairs, ready)
    here = lax.axis_index("gy")
    even = here % 2 == 0
    is_top = here == lax.axis_size("gy") - 1
    eastward = lax.axis_index("gx") % 2 == 0

    def put(row, items):
        west = jnp.zeros((ROWS, COLS), jnp.float32)
        east = jnp.zeros((ROWS, COLS), jnp.float32)
        for tile, width, first in items:
            chosen = lane == first if width == 1 else (lane >= first) & (lane < first + width)
            west = jnp.where(chosen, roll(tile, first, 1), west)
            east = jnp.where(chosen, roll(tile, first + width, 1), east)
        one[row : row + ROWS, :] = jnp.where(eastward, east, west)
        two[row : row + ROWS, :] = jnp.where(eastward, west, east)

    copies[0].wait()
    copies[1].wait()
    levels, surfaces = levels_ref[...], surface_ref[...]
    depths = levels.astype(jnp.float32)
    per = 2 * LEVELS
    level_row = lax.broadcasted_iota(jnp.int32, (per, COLS), 0)
    level_row = jnp.where(level_row >= LEVELS, level_row - LEVELS, level_row)
    wet_south = level_row < jnp.broadcast_to(levels[:1, :], (per, COLS))
    wet_north = level_row < jnp.broadcast_to(levels[ROWS - 1 :, :], (per, COLS))

    def cell(t, k):
        row = (t * LEVELS + k) * ROWS
        return jnp.where(k < levels, cells[row : row + ROWS, :], 0.0)

    for g in range(GROUPS):
        copies[2 + g].wait()
        put(g * ROWS, [(cell(g * GROUP + t, k), 1, t * LEVELS + k) for t in range(GROUP) for k in range(LEVELS)])
        if g == 0:
            for k in range(LEVELS):
                difference[k] = cell(0, k) - cell(1, k)
            items = [(difference[k], 5, 5 * k) for k in range(LEVELS)]
            put(COL_DEEP, items + [(depths, 5, COUNT_LANE), (surfaces, 4, SURFACE_LANE)])
        for at in range(g * GROUP * LEVELS, (g + 1) * GROUP * LEVELS, per):
            south = jnp.where(wet_south, cells[pl.ds(at * ROWS, per, stride=ROWS), :], 0.0)
            north = jnp.where(wet_north, cells[pl.ds(at * ROWS + ROWS - 1, per, stride=ROWS), :], 0.0)
            near_rows[at : at + per, :] = jnp.where(even, north, south)
            far_rows[at : at + per, :] = jnp.where(even, south, north)
    for f in range(4):
        copies[2 + GROUPS + f].wait()
        put(COL_DEEP + (1 + f) * ROWS, [(fields[f, k], 4, 4 * k) for k in range(LEVELS)])
    copies[-1].wait()
    branches[0] = pole_of(fold_ref) >> (COLS.bit_length() - 1)

    def pack(kind, out):
        turn = turned if kind == "fold" else (lambda tile: tile)
        for k in range(LEVELS):
            out[ROW_DIFF + ROWS * k : ROW_DIFF + ROWS * (k + 1), :] = turn(difference[k])
        for f in range(4):
            for m in range(LEVELS // 2):
                first, second = turn(fields[f, 2 * m]), turn(fields[f, 2 * m + 1])
                if kind == "north":
                    tile = jnp.where(low, roll(first, 4, 0), second)
                else:
                    tile = jnp.where(low, first, roll(second, 4, 0))
                row = ROW_FIELD + ROWS * (f * (LEVELS // 2) + m)
                out[row : row + ROWS, :] = tile
        out[ROW_COUNT : ROW_COUNT + ROWS, :] = turn(depths)
        out[ROW_SURFACE : ROW_SURFACE + ROWS, :] = turn(surfaces)

    @pl.when(even)
    def _():
        pack("north", near_rows)
        pack("south", far_rows)

    @pl.when(jnp.logical_not(even))
    def _():
        pack("south", near_rows)

    @pl.when(jnp.logical_not(even) & jnp.logical_not(is_top))
    def _():
        pack("north", far_rows)

    @pl.when(is_top)
    def _():
        pack("fold", far_rows)


def sides(one, two, row):
    first, second = one[pl.ds(row, ROWS), :], two[pl.ds(row, ROWS), :]
    eastward = lax.axis_index("gx") % 2 == 0
    return jnp.where(eastward, first, second), jnp.where(eastward, second, first)


def corners_kernel(one, two, near_in, far_in, near, far):
    del near_in, far_in
    is_top = lax.axis_index("gy") == lax.axis_size("gy") - 1
    half = ROW_WEST - ROW_EAST
    for row in range(0, half, ROWS):
        for base, value in zip((0, half), sides(one, two, COL_DEEP + row)):
            near[base + row : base + row + ROWS, :] = value
            far[base + row : base + row + ROWS, :] = jnp.where(is_top, turned(value), value)


def pole_of(fold_map):
    return (fold_map[0] + 1) & (COLS * lax.axis_size("gx") - 1)


def halo_rows(fold_map, near, far, extra, north_rows, south_rows):
    here = lax.axis_index("gy")
    top = lax.axis_size("gy") - 1

    @pl.when(here % 2 == 0)
    def _():
        north_rows[...] = near[...]
        south_rows[...] = far[...]

    @pl.when(here % 2 == 1)
    def _():
        south_rows[...] = near[...]

    @pl.when((here % 2 == 1) & (here != top))
    def _():
        north_rows[...] = far[...]

    @pl.when(here == top)
    def _():
        lane = lanes()
        pole = pole_of(fold_map)
        offset = pole & (COLS - 1)
        index = (offset - 1 - lane) & (COLS - 1)
        within_far = (lane >= offset) == ((pole & COLS) != 0)
        for row in range(0, north_rows.shape[0], ROWS):
            rows = jnp.where(within_far, far[row : row + ROWS, :], extra[row : row + ROWS, :])
            north_rows[row : row + ROWS, :] = jnp.take_along_axis(rows, index, axis=1)


def unfold(offset, first_in_far, far, extra, out):
    lane = lanes()
    index = (offset - 1 - lane) & (COLS - 1)
    within_far = (lane >= offset) == first_in_far
    zero = jnp.zeros((ROWS, COLS), jnp.float32)

    def store(row, value):
        out[row - ROW_EAST : row - ROW_EAST + ROWS, :] = value

    def flipped(row, sign):
        a, b = far[row : row + ROWS, :], extra[row : row + ROWS, :]
        store(row, sign * jnp.take_along_axis(jnp.where(within_far, a, b), index, axis=1))
        return sign * jnp.take_along_axis(jnp.where(within_far, b, a), index, axis=1)

    def collect(packed, tile, width, at):
        chosen = (lane >= at) & (lane < at + width)
        return jnp.where(chosen, roll(tile, at, 1), packed[0]), jnp.where(chosen, roll(tile, at + width, 1), packed[1])

    def beside_of(first, row):
        a, b = far[row : row + ROWS, :], extra[row : row + ROWS, :]
        return jnp.where(first_in_far == first, a, b)

    def finish(row, packed, sign, width, within):
        beside = (lane + (offset - 1) + width - 2 * within) & (COLS - 1)
        right = sign * jnp.take_along_axis(beside_of(True, ROW_WEST + row), beside, axis=1)
        beside = (lane + (offset - 1 - COLS) + width - 2 * within) & (COLS - 1)
        left = sign * jnp.take_along_axis(beside_of(False, ROW_EAST + row), beside, axis=1)
        store(ROW_EAST + row, jnp.where(within < offset, packed[0], right))
        store(ROW_WEST + row, jnp.where(within >= offset + width - COLS, packed[1], left))

    packed = (zero, zero)
    for k in range(LEVELS):
        packed = collect(packed, flipped(ROW_DIFF + ROWS * k, 1.0), 5, 5 * k)
    packed = collect(packed, flipped(ROW_COUNT, 1.0), 5, COUNT_LANE)
    packed = collect(packed, flipped(ROW_SURFACE, 1.0), 4, SURFACE_LANE)
    fifth = lane - 5 * ((lane * 205) >> 10)
    finish(0, packed, 1.0, jnp.where(lane >= SURFACE_LANE, 4, 5), fifth)
    for f in range(4):
        sign = -1.0 if f < 2 else 1.0
        packed = (zero, zero)
        for m in range(LEVELS // 2):
            tile = flipped(ROW_FIELD + ROWS * (f * (LEVELS // 2) + m), sign)
            packed = collect(packed, tile, 4, 8 * m)
            packed = collect(packed, roll(tile, 4, 0), 4, 8 * m + 4)
        finish((1 + f) * ROWS, packed, sign, 4, lane & 3)


def unpack(east, west, first, width, lane):
    right = roll(east, -first, 1)
    left = roll(west, -width - first, 1)
    return jnp.where(lane < width, right, jnp.where(lane >= COLS - width, left, 0.0))


def both_east(one, two, lane):
    return east_of(one, two, lane), east_of(two, one, lane)


def both_west(one, two, lane):
    return west_of(one, two, lane), west_of(two, one, lane)


def krylov_kernel(
    fold_map, difference, fields, count, surface, one, two, near, far, extra,
    vectors, diagonal, right_side, partial,
    north_buf, south_buf,
):
    here = lax.axis_index("gy")
    top = lax.axis_size("gy") - 1
    lane, sub = lanes(), sublanes()
    low = sub < 4
    @pl.when(here % 2 == 0)
    def _():
        north_buf[...] = near[ROW_EAST:, :]
        south_buf[...] = far[ROW_EAST:, :]

    @pl.when(here % 2 == 1)
    def _():
        south_buf[...] = near[ROW_EAST:, :]

    @pl.when((here % 2 == 1) & (here != top))
    def _():
        north_buf[...] = far[ROW_EAST:, :]

    @pl.when(here == top)
    def _():
        pole = pole_of(fold_map)
        unfold(pole & (COLS - 1), (pole & COLS) != 0, far, extra, north_buf)

    def at(ref, row):
        return ref[row - ROW_EAST : row - ROW_EAST + ROWS, :]

    def field_tile(ref, f, k):
        return at(ref, ROW_FIELD + ROWS * (f * (LEVELS // 2) + k // 2))

    def halo_main(f, k):
        north, south = field_tile(north_buf, f, k), field_tile(south_buf, f, k)
        return jnp.where(low, roll(north, 4 * (k % 2), 0), roll(south, 4 * (1 - k % 2), 0))

    def side(ref, f, first, width):
        return unpack(at(ref, ROW_EAST + ROWS * f), at(ref, ROW_WEST + ROWS * f), first, width, lane)

    halo_packed = [
        [
            jnp.where(low, at(north_buf, base + ROWS * (1 + f)), at(south_buf, base + ROWS * (1 + f)))
            for base in (ROW_EAST, ROW_WEST)
        ]
        for f in range(4)
    ]

    columns = [sides(one, two, COL_DEEP + ROWS * f) for f in range(5)]

    def column(f):
        return columns[f]

    def neighbours_across(own, north, south):
        up, up_n, up_s = roll(own, -1, 0), roll(north, -1, 0), roll(south, -1, 0)
        down, down_n, down_s = roll(own, 1, 0), roll(north, 1, 0), roll(south, 1, 0)
        return (
            jnp.where(sub == 7, up_n, up),
            jnp.where(low, up_n, jnp.where(sub == 7, up, up_s)),
            jnp.where(sub == 0, down_s, down),
            jnp.where(sub == 0, down, jnp.where(low, down_n, down_s)),
        )

    def halo(pair):
        return jnp.where(low, pair[0], pair[1])

    counts_own = (count[...].astype(jnp.float32), unpack(*column(0), COUNT_LANE, 5, lane))
    counts_north = (at(north_buf, ROW_COUNT), side(north_buf, 0, COUNT_LANE, 5))
    counts_south = (at(south_buf, ROW_COUNT), side(south_buf, 0, COUNT_LANE, 5))
    counts = (counts_own[0], counts_own[1], halo((counts_north[0], counts_south[0])), halo((counts_north[1], counts_south[1])))
    surfaces = (
        surface[...],
        unpack(*column(0), SURFACE_LANE, 4, lane),
        halo((at(north_buf, ROW_SURFACE), at(south_buf, ROW_SURFACE))),
        halo((side(north_buf, 0, SURFACE_LANE, 4), side(south_buf, 0, SURFACE_LANE, 4))),
    )

    zero = jnp.zeros((ROWS, COLS), jnp.float32)
    c_prev, r_prev, a_prev = [zero] * 4, [zero] * 4, [zero] * 4
    c_list, r_list = [], []
    for k in range(LEVELS):
        own = (difference[k], unpack(*column(0), 5 * k, 5, lane))
        north = (at(north_buf, ROW_DIFF + ROWS * k), side(north_buf, 0, 5 * k, 5))
        south = (at(south_buf, ROW_DIFF + ROWS * k), side(south_buf, 0, 5 * k, 5))
        halos = (halo((north[0], south[0])), halo((north[1], south[1])))
        centre = (own[0], own[1], halos[0], halos[1])
        easts = both_east(*own, lane) + both_east(*halos, lane)
        wests = both_west(*own, lane) + both_west(*halos, lane)
        first = neighbours_across(own[0], north[0], south[0])
        second = neighbours_across(own[1], north[1], south[1])
        norths = (first[0], second[0], first[1], second[1])
        souths = (first[2], second[2], first[3], second[3])
        values = [
            (fields[f, k], unpack(*column(1 + f), 4 * k, 4, lane), halo_main(f, k), unpack(*halo_packed[f], 4 * k, 4, lane))
            for f in range(4)
        ]
        c_now, r_now, a_now = [], [], []
        for i in range(4):
            u, v, spread, mix = (value[i] for value in values)
            change = (
                -0.5 * u * (easts[i] - wests[i])
                - 0.5 * v * (norths[i] - souths[i])
                + spread * (easts[i] + wests[i] + norths[i] + souths[i] - 4.0 * centre[i])
            )
            explicit = centre[i] + jnp.where(k < counts[i], change, 0.0)
            a = jnp.where(k + 1 < counts[i], mix, 0.0)
            inverse = 1.0 / (1.0 + a_prev[i] + a + a_prev[i] * c_prev[i])
            c_now.append(-a * inverse)
            r_now.append((explicit + a_prev[i] * r_prev[i]) * inverse)
            a_now.append(a)
        c_prev, r_prev, a_prev = c_now, r_now, a_now
        c_list.append(c_now)
        r_list.append(r_now)
    total, x_next = [zero] * 4, [zero] * 4
    for k in range(LEVELS - 1, -1, -1):
        x_next = [r_list[k][i] - c_list[k][i] * x_next[i] for i in range(4)]
        total = [total[i] + thickness(k) * x_next[i] for i in range(4)]
    rhs = [jnp.where(counts[i] > 0, 0.25 * total[i], 0.0) for i in range(4)]

    def depth_of(levels):
        depth = zero
        for k in range(LEVELS):
            depth = depth + jnp.where(k < levels, thickness(k), 0.0)
        return depth / LEVELS

    own = tuple(depth_of(levels) for levels in counts_own)
    north = tuple(depth_of(levels) for levels in counts_north)
    south = tuple(depth_of(levels) for levels in counts_south)
    depths = (own[0], own[1], halo((north[0], south[0])), halo((north[1], south[1])))

    def rows_of(own, north, south):
        first = neighbours_across(own[0], north[0], south[0])
        second = neighbours_across(own[1], north[1], south[1])
        return (first[0], second[0], first[1], second[1]), (first[2], second[2], first[3], second[3])

    def coupled(others, weight):
        return [weight * jnp.minimum(depths[i], others[i]) for i in range(4)]

    own_e, north_e, south_e = (both_east(*pair, lane) for pair in (own, north, south))
    own_w, north_w, south_w = (both_west(*pair, lane) for pair in (own, north, south))
    halo_e = (halo((north_e[0], south_e[0])), halo((north_e[1], south_e[1])))
    halo_w = (halo((north_w[0], south_w[0])), halo((north_w[1], south_w[1])))
    mid = rows_of(own, north, south)
    mid_e = rows_of(own_e, north_e, south_e)
    mid_w = rows_of(own_w, north_w, south_w)
    couplings = [
        coupled(own_e + halo_e, 1.0),
        coupled(own_w + halo_w, 1.0),
        coupled(mid[0], 1.0),
        coupled(mid[1], 1.0),
        coupled(mid_e[0], 0.5),
        coupled(mid_w[0], 0.5),
        coupled(mid_e[1], 0.5),
        coupled(mid_w[1], 0.5),
    ]
    diag = [
        jnp.where(counts[i] > 0, surfaces[i] + sum(entry[i] for entry in couplings), 1.0) for i in range(4)
    ]
    inverse = [1.0 / diag[i] for i in range(4)]
    couplings = [[entry[i] * inverse[i] for i in range(4)] for entry in couplings]

    def shifted_rows(tiles):
        north, south = [None] * 4, [None] * 4
        for i in range(2):
            a, b = roll(tiles[i], -1, 0), roll(tiles[i + 2], -1, 0)
            north[i], north[i + 2] = jnp.where(sub == 7, b, a), jnp.where(sub == 7, a, b)
            a, b = roll(tiles[i], 1, 0), roll(tiles[i + 2], 1, 0)
            south[i], south[i + 2] = jnp.where(sub == 0, b, a), jnp.where(sub == 0, a, b)
        return north, south

    def spread_out(tiles):
        east = both_east(tiles[0], tiles[1], lane) + both_east(tiles[2], tiles[3], lane)
        west = both_west(tiles[0], tiles[1], lane) + both_west(tiles[2], tiles[3], lane)
        mid_n, mid_s = shifted_rows(tiles)
        east_n, east_s = shifted_rows(east)
        west_n, west_s = shifted_rows(west)
        around = (east, west, mid_n, mid_s, east_n, west_n, east_s, west_s)
        return [sum(entry[i] * values[i] for entry, values in zip(couplings, around)) for i in range(4)]

    found = [[rhs[i] * inverse[i] for i in range(4)]]
    found.append(spread_out(found[0]))
    for _ in range(2, ITERS + 1):
        ahead = spread_out(found[-1])
        found.append([2.0 * ahead[i] - found[-2][i] for i in range(4)])
    for j in range(ITERS + 1):
        vectors[j] = found[j][0]
    diagonal[...] = diag[0]
    right_side[...] = rhs[0]
    weighted = [diag[0] * found[j][0] for j in range(ITERS + 1)]
    sums = [weighted[j] * found[j][0] for j in range(ITERS + 1)]
    sums += [weighted[j] * found[j + 1][0] for j in range(ITERS)]
    row = jnp.zeros((1, COLS), jnp.float32)
    for j, entry in enumerate(sums):
        row = jnp.where(lane[:1, :] == j, jnp.sum(entry, keepdims=True), row)
    partial[...] = jnp.broadcast_to(row, partial.shape)


def combine_kernel(moments, vectors, diagonal, pressure, residual, good):
    size = ITERS + 1
    sums = jnp.sum(moments[...], axis=0, keepdims=True)

    def lane_of(j):
        return jnp.broadcast_to(sums[:, j : j + 1], (ROWS, COLS))

    even = [lane_of(j) for j in range(size)]
    odd = [lane_of(size + j) for j in range(ITERS)]
    mu = []
    for j in range(size):
        mu.append(even[0] if j == 0 else 2.0 * even[j] - even[0])
        if j < ITERS:
            mu.append(odd[0] if j == 0 else 2.0 * odd[j] - odd[0])

    def mass(i, j):
        return 0.5 * (mu[i + j] + mu[abs(i - j)])

    def stiffness(i, j):
        i, j = min(i, j), max(i, j)
        if j == 0:
            return mu[0] - mu[1]
        return mass(i, j) - 0.5 * (mass(i, j + 1) + mass(i, j - 1))

    def form(values, entry):
        out = None
        for i in range(len(values)):
            inner = values[i] * entry(i, i)
            for j in range(i + 1, len(values)):
                inner = inner + 2.0 * values[j] * entry(i, j)
            out = values[i] * inner if out is None else out + values[i] * inner
        return out

    def applied(values):
        out = [value for value in values] + [jnp.zeros_like(values[0])]
        out[1] = out[1] - values[0]
        for j in range(1, len(values)):
            out[j + 1] = out[j + 1] - 0.5 * values[j]
            out[j - 1] = out[j - 1] - 0.5 * values[j]
        return out

    def amplified(values, result):
        total = sum(jnp.abs(value) for value in values)
        return total * total * mu[0] / result

    scaled = [jnp.ones((ROWS, COLS), jnp.float32)]
    direction = list(scaled)
    solution_at = []
    energy = mu[0]
    fine = energy > 0.0
    for step in range(ITERS):
        image = applied(direction)
        curvature = form(direction, stiffness)
        step_size = energy / curvature
        fine = fine & (amplified(direction, curvature) <= SCALAR_BOUND) & (curvature > 0.0)
        solution_at = [
            step_size * value + (solution_at[j] if j < len(solution_at) else 0.0) for j, value in enumerate(direction)
        ]
        scaled = [
            (scaled[j] if j < len(scaled) else 0.0) - step_size * value for j, value in enumerate(image)
        ]
        energy_new = form(scaled, mass)
        bound = SCALAR_BOUND if step + 1 < ITERS else FIELD_BOUND
        fine = fine & (amplified(scaled, energy_new) <= bound) & (energy_new > 0.0)
        if step + 1 < ITERS:
            ratio = energy_new / energy
            direction = [
                scaled[j] + (ratio * direction[j] if j < len(direction) else 0.0) for j in range(len(scaled))
            ]
            energy = energy_new
    pressure[...] = sum(solution_at[j] * vectors[j] for j in range(len(solution_at)))
    residual[...] = diagonal[...] * sum(scaled[j] * vectors[j] for j in range(len(scaled)))
    good[0] = jnp.min(jnp.where(fine, 1, 0).astype(jnp.int32))


def tracers_kernel(
    fold_map, tracer, fields, count, one, two, near, far, extra,
    mixed,
    north_rows, south_rows, factors,
):
    lane, sub = lanes(), sublanes()
    levels = count[...]
    group = pl.program_id(0)

    @pl.when(group == 0)
    def _():
        halo_rows(fold_map, near, far, extra, north_rows, south_rows)
        c_prev = jnp.zeros((ROWS, COLS), jnp.float32)
        a_prev = jnp.zeros((ROWS, COLS), jnp.float32)
        for k in range(LEVELS):
            wet = jnp.where(k < levels, 1.0, 0.0)
            u, v, spread = 0.5 * wet * fields[0, k], 0.5 * wet * fields[1, k], wet * fields[2, k]
            a = jnp.where(k + 1 < levels, fields[3, k], 0.0)
            inverse = 1.0 / (1.0 + a_prev + a + a_prev * c_prev)
            c_prev = -a * inverse
            factors[0, k] = 1.0 - 4.0 * spread
            factors[1, k] = spread - u
            factors[2, k] = spread + u
            factors[3, k] = spread - v
            factors[4, k] = spread + v
            factors[5, k] = inverse
            factors[6, k] = a_prev
            factors[7, k] = c_prev
            a_prev = a

    row = pl.multiple_of(group * ROWS, ROWS)
    columns_east, columns_west = sides(one, two, row)
    r_prev = [jnp.zeros((ROWS, COLS), jnp.float32)] * GROUP
    for k in range(LEVELS):
        centre, to_e, to_w, to_n, to_s, inverse, above = (factors[j, k] for j in range(7))
        wet = k < levels
        for t in range(GROUP):
            cell = jnp.where(wet, tracer[t, k], 0.0)
            at = t * LEVELS + k
            halo_row = group * (GROUP * LEVELS) + at
            east = east_of(cell, roll(columns_east, -at, 1), lane)
            west = west_of(cell, roll(columns_west, COLS - 1 - at, 1), lane)
            north = north_of(cell, north_rows[pl.ds(halo_row, 1), :], sub)
            south = south_of(cell, south_rows[pl.ds(halo_row, 1), :], sub)
            explicit = centre * cell + to_e * east + to_w * west + to_n * north + to_s * south
            r_prev[t] = (explicit + above * r_prev[t]) * inverse
            mixed[t, k] = r_prev[t]
    x_next = r_prev
    for k in range(LEVELS - 2, -1, -1):
        below = factors[7, k]
        for t in range(GROUP):
            x_next[t] = mixed[t, k] - below * x_next[t]
            mixed[t, k] = x_next[t]


def extended(cells, sides, width):
    for axis, dim in sides:
        count = lax.axis_size(axis)
        head = lax.slice_in_dim(cells, 0, width, axis=dim)
        tail = lax.slice_in_dim(cells, cells.shape[dim] - width, cells.shape[dim], axis=dim)
        cells = jnp.concatenate(
            [
                lax.ppermute(tail, axis, [(i, (i + 1) % count) for i in range(count)]),
                cells,
                lax.ppermute(head, axis, [((i + 1) % count, i) for i in range(count)]),
            ],
            axis=dim,
        )
    return cells


def extend(field, fold_map):
    rows, cols = field.shape
    padded = extended(field, (("gx", 1), ("gy", 0)), 1)
    total_cols = fold_map.shape[0]
    whole_row = lax.all_gather(field[rows - 1, :], "gx", axis=0, tiled=True)
    start = lax.axis_index("gx") * cols
    wanted = (start - 1 + jnp.arange(cols + 2, dtype=jnp.int32)) % total_cols
    folded = jnp.take(whole_row, jnp.take(fold_map, wanted), axis=0)
    row_index = lax.axis_index("gy")
    upper = jnp.where(row_index == lax.axis_size("gy") - 1, folded, padded[rows + 1, :])
    lower = jnp.where(row_index == 0, 0.0, padded[0, :])
    return jnp.concatenate([lower[None, :], padded[1 : rows + 1, :], upper[None, :]], axis=0)


def window(padded, row_off, col_off):
    rows = padded.shape[0] - 2
    cols = padded.shape[1] - 2
    return padded[1 + row_off : 1 + row_off + rows, 1 + col_off : 1 + col_off + cols]


def total_of(value):
    return lax.psum(jnp.sum(value), BOTH)


def direct_gradients(rhs, level_count, fold_map, surface_term):
    levels = jnp.arange(LEVELS, dtype=jnp.int32)[:, None, None]
    level_mask = (levels < level_count[None]).astype(jnp.float32)
    thick = (0.5 + 1.5 * jnp.arange(LEVELS).astype(jnp.float32) / (LEVELS - 1))[:, None, None]
    depth = jnp.sum(thick * level_mask, axis=0) / LEVELS
    wet_cells = level_count > 0
    depth_pad = extend(depth, fold_map)
    couplings = [
        weight * jnp.minimum(depth, window(depth_pad, row_off, col_off)) for row_off, col_off, weight in NEIGHBOURS
    ]
    diag = jnp.where(wet_cells, surface_term + sum(couplings), 1.0)

    def step(_, state):
        pressure, residual, direction, energy = state
        field_pad = extend(direction, fold_map)
        summed = jnp.zeros_like(direction)
        for entry, (row_off, col_off, _weight) in zip(couplings, NEIGHBOURS):
            summed = summed + entry * window(field_pad, row_off, col_off)
        image = jnp.where(wet_cells, diag * direction - summed, direction)
        step_size = energy / total_of(direction * image)
        pressure = pressure + step_size * direction
        residual = residual - step_size * image
        scaled = residual / diag
        energy_new = total_of(residual * scaled)
        return pressure, residual, scaled + energy_new / energy * direction, energy_new

    scaled = rhs / diag
    state = (jnp.zeros_like(rhs), rhs, scaled, total_of(rhs * scaled))
    state = lax.fori_loop(0, ITERS, step, state)
    return state[0], state[1]


def kernel(body, limit=VMEM_LIMIT, **rest):
    return pl.pallas_call(body, compiler_params=params(limit), **rest)


def shape(*dims):
    return jax.ShapeDtypeStruct(dims, jnp.float32)


def vmem(*dims):
    return pltpu.VMEM(dims, jnp.float32)


def block_of(dims, at=0):
    return pl.BlockSpec(dims, lambda i: (at,) + (0,) * (len(dims) - 1))


def all_of(array):
    return block_of(array.shape)


def shards(sizes, tracer, east_vel, north_vel, diffusion, mixing, count, fold_map, surface):
    nx, ny = sizes
    hbm = pl.BlockSpec(memory_space=pltpu.HBM)
    smem = pl.BlockSpec(memory_space=pltpu.SMEM)
    fields = (east_vel, north_vel, diffusion, mixing)

    def device(x, y):
        return (x % nx) * ny + y

    one, two, near, far, difference, coefficients, branches = kernel(
        pack_kernel,
        limit=PACK_VMEM_LIMIT,
        out_shape=(
            shape(COL_SIZE, COLS),
            shape(COL_SIZE, COLS),
            shape(ROW_SIZE, COLS),
            shape(ROW_SIZE, COLS),
            shape(LEVELS, ROWS, COLS),
            shape(4, LEVELS, ROWS, COLS),
            jax.ShapeDtypeStruct((1,), jnp.int32),
        ),
        in_specs=[hbm] * 8,
        out_specs=(whole(),) * 6 + (smem,),
        scratch_shapes=[
            vmem(EDGE * ROWS, COLS),
            pltpu.VMEM((ROWS, COLS), jnp.int32),
            vmem(ROWS, COLS),
            pltpu.SMEM(fold_map.shape, jnp.int32),
            pltpu.SemaphoreType.DMA((GROUPS + 7,)),
        ],
        name="pack",
    )(tracer.reshape(EDGE * ROWS, COLS), *fields, count, surface, fold_map)

    one = lax.ppermute(one, BOTH, [(device(x ^ 1, y), device(x, y)) for x in range(nx) for y in range(ny)])
    two = lax.ppermute(
        two, BOTH, [(device(x + 1 if x % 2 else x - 1, y), device(x, y)) for x in range(nx) for y in range(ny)]
    )

    columns = block_of((COL_SIZE, COLS))
    corner = block_of((ROW_DIFF - ROW_EAST, COLS), ROW_EAST // (ROW_DIFF - ROW_EAST))
    near, far = kernel(
        corners_kernel,
        grid=(1,),
        out_shape=(shape(ROW_SIZE, COLS), shape(ROW_SIZE, COLS)),
        in_specs=[columns, columns] + [pl.BlockSpec(memory_space=pl.ANY)] * 2,
        out_specs=(corner, corner),
        input_output_aliases={2: 0, 3: 1},
        name="put_corners",
    )(one, two, near, far)
    near = lax.ppermute(near, BOTH, [(device(x, y ^ 1), device(x, y)) for x in range(nx) for y in range(ny)])
    inner = [(device(x, y + 1 if y % 2 else y - 1), device(x, y)) for x in range(nx) for y in range(1, ny - 1)]

    def across(turn):
        return [(device(turn - x, ny - 1), device(x, ny - 1)) for x in range(nx)]

    def exchange(at, rows):
        even, odd = (at, at - 1) if at % 2 == 0 else (at - 1, at)
        return lax.ppermute(rows, BOTH, inner + across(even)), lax.ppermute(rows, BOTH, across(odd))

    far, extra = lax.switch(branches[0], [functools.partial(exchange, at) for at in range(nx)], far)

    vectors, diagonal, rhs, partial = kernel(
        krylov_kernel,
        out_shape=(shape(ITERS + 1, ROWS, COLS), shape(ROWS, COLS), shape(ROWS, COLS), shape(nx * ny, COLS)),
        in_specs=[smem] + [whole()] * 9,
        out_specs=(whole(),) * 4,
        scratch_shapes=[vmem(DEEP_SIZE, COLS), vmem(DEEP_SIZE, COLS)],
        name="krylov",
    )(fold_map, difference, coefficients, count, surface, one, two, near, far, extra)

    moments = lax.all_to_all(partial, BOTH, 0, 0)

    batch = pl.BlockSpec((GROUP, LEVELS, ROWS, COLS), lambda i: (i, 0, 0, 0))
    mixed = kernel(
        tracers_kernel,
        grid=(GROUPS,),
        out_shape=shape(TRACERS, LEVELS, ROWS, COLS),
        in_specs=[smem, batch, all_of(coefficients), all_of(count)]
        + [block_of((COL_DEEP, COLS))] * 2
        + [block_of((EDGE, COLS))] * 3,
        out_specs=batch,
        scratch_shapes=[vmem(EDGE, COLS), vmem(EDGE, COLS), vmem(8, LEVELS, ROWS, COLS)],
        name="tracers",
    )(fold_map, tracer, coefficients, count, one, two, near, far, extra)

    pressure, residual, good = kernel(
        combine_kernel,
        out_shape=(shape(ROWS, COLS), shape(ROWS, COLS), jax.ShapeDtypeStruct((1,), jnp.int32)),
        in_specs=[whole()] * 3,
        out_specs=(whole(), whole(), smem),
        name="combine",
    )(moments, vectors, diagonal)
    pressure, residual = lax.cond(
        good[0] == 1,
        lambda pressure, residual, rhs, count, surface, fold: (pressure, residual),
        lambda pressure, residual, rhs, count, surface, fold: direct_gradients(rhs, count, fold, surface),
        pressure,
        residual,
        rhs,
        count,
        surface,
        fold_map,
    )
    return mixed, pressure, residual


def solution(mesh):
    in_specs = (
        P(None, None, "gy", "gx"),
        P(None, "gy", "gx"),
        P(None, "gy", "gx"),
        P(None, "gy", "gx"),
        P(None, "gy", "gx"),
        P("gy", "gx"),
        P(),
        P("gy", "gx"),
    )
    out_specs = (P(None, None, "gy", "gx"), P("gy", "gx"), P("gy", "gx"))
    body = functools.partial(shards, (mesh.shape["gx"], mesh.shape["gy"]))
    return jax.shard_map(body, mesh=mesh, in_specs=in_specs, out_specs=out_specs, check_vma=False)
```

```python
import functools

import jax
import jax.numpy as jnp
from jax import lax
from jax.experimental import pallas as pl
from jax.experimental.pallas import tpu as pltpu
from jax.sharding import PartitionSpec as P

ITERS = 4
TRACERS, LEVELS, ROWS, COLS = 16, 20, 8, 128
GROUP = 4
GROUPS = TRACERS // GROUP
EDGE = TRACERS * LEVELS
BOTH = ("gx", "gy")
VMEM_LIMIT = 40 * 1024 * 1024
PACK_VMEM_LIMIT = 63 * 1024 * 1024

COL_DEEP, COL_SIZE = GROUPS * ROWS, (GROUPS + 5) * ROWS
COUNT_LANE, SURFACE_LANE = 100, 105
ROW_EAST, ROW_WEST, ROW_DIFF, ROW_FIELD, ROW_COUNT, ROW_SURFACE, ROW_SIZE = 320, 360, 400, 560, 880, 888, 896
DEEP_SIZE = ROW_SIZE - ROW_EAST

SCALAR_BOUND, FIELD_BOUND = 1500.0, 1.0e5

NEIGHBOURS = [
    (0, 1, 1.0),
    (0, -1, 1.0),
    (1, 0, 1.0),
    (-1, 0, 1.0),
    (1, 1, 0.5),
    (1, -1, 0.5),
    (-1, 1, 0.5),
    (-1, -1, 0.5),
]


def params(limit=VMEM_LIMIT):
    return pltpu.CompilerParams(vmem_limit_bytes=limit)


def whole():
    return pl.BlockSpec(memory_space=pltpu.VMEM)


def lanes():
    return lax.broadcasted_iota(jnp.int32, (ROWS, COLS), 1)


def sublanes():
    return lax.broadcasted_iota(jnp.int32, (ROWS, COLS), 0)


def roll(tile, shift, axis):
    size = tile.shape[axis]
    shift = shift % size
    return tile if shift == 0 else pltpu.roll(tile, shift, axis)


def east_of(tile, beyond, lane):
    return roll(jnp.where(lane == 0, beyond, tile), -1, 1)


def west_of(tile, beyond, lane):
    return roll(jnp.where(lane == COLS - 1, beyond, tile), 1, 1)


def north_of(tile, beyond, sub):
    return roll(jnp.where(sub == 0, beyond, tile), -1, 0)


def south_of(tile, beyond, sub):
    return roll(jnp.where(sub == ROWS - 1, beyond, tile), 1, 0)


def thickness(level):
    return 0.5 + 1.5 * level / (LEVELS - 1)


def turned(tile):
    return jnp.take_along_axis(tile, ROWS - 1 - sublanes(), axis=0)


def start_copies(pairs, ready):
    copies = [pltpu.make_async_copy(source, target, ready.at[i]) for i, (source, target) in enumerate(pairs)]
    for copy in copies:
        copy.start()
    return copies


def pack_kernel(
    tracer, east_vel, north_vel, diffusion, mixing, count, surface, fold_map,
    one, two, near_rows, far_rows, difference, fields, branches,
    cells, levels_ref, surface_ref, fold_ref, ready,
):
    lane = lanes()
    low = sublanes() < ROWS // 2
    size = GROUP * LEVELS * ROWS
    pairs = [(count, levels_ref), (surface, surface_ref)]
    pairs += [(tracer.at[pl.ds(g * size, size)], cells.at[pl.ds(g * size, size)]) for g in range(GROUPS)]
    pairs += [(field, fields.at[f]) for f, field in enumerate((east_vel, north_vel, diffusion, mixing))]
    pairs += [(fold_map, fold_ref)]
    copies = start_copies(pairs, ready)
    here = lax.axis_index("gy")
    even = here % 2 == 0
    is_top = here == lax.axis_size("gy") - 1
    eastward = lax.axis_index("gx") % 2 == 0

    def put(row, items):
        west = jnp.zeros((ROWS, COLS), jnp.float32)
        east = jnp.zeros((ROWS, COLS), jnp.float32)
        for tile, width, first in items:
            chosen = lane == first if width == 1 else (lane >= first) & (lane < first + width)
            west = jnp.where(chosen, roll(tile, first, 1), west)
            east = jnp.where(chosen, roll(tile, first + width, 1), east)
        one[row : row + ROWS, :] = jnp.where(eastward, east, west)
        two[row : row + ROWS, :] = jnp.where(eastward, west, east)

    copies[0].wait()
    copies[1].wait()
    levels, surfaces = levels_ref[...], surface_ref[...]
    depths = levels.astype(jnp.float32)
    per = 2 * LEVELS
    level_row = lax.broadcasted_iota(jnp.int32, (per, COLS), 0)
    level_row = jnp.where(level_row >= LEVELS, level_row - LEVELS, level_row)
    wet_south = level_row < jnp.broadcast_to(levels[:1, :], (per, COLS))
    wet_north = level_row < jnp.broadcast_to(levels[ROWS - 1 :, :], (per, COLS))

    def cell(t, k):
        row = (t * LEVELS + k) * ROWS
        return jnp.where(k < levels, cells[row : row + ROWS, :], 0.0)

    for g in range(GROUPS):
        copies[2 + g].wait()
        put(g * ROWS, [(cell(g * GROUP + t, k), 1, t * LEVELS + k) for t in range(GROUP) for k in range(LEVELS)])
        if g == 0:
            for k in range(LEVELS):
                difference[k] = cell(0, k) - cell(1, k)
            items = [(difference[k], 5, 5 * k) for k in range(LEVELS)]
            put(COL_DEEP, items + [(depths, 5, COUNT_LANE), (surfaces, 4, SURFACE_LANE)])
        for at in range(g * GROUP * LEVELS, (g + 1) * GROUP * LEVELS, per):
            south = jnp.where(wet_south, cells[pl.ds(at * ROWS, per, stride=ROWS), :], 0.0)
            north = jnp.where(wet_north, cells[pl.ds(at * ROWS + ROWS - 1, per, stride=ROWS), :], 0.0)
            near_rows[at : at + per, :] = jnp.where(even, north, south)
            far_rows[at : at + per, :] = jnp.where(even, south, north)
    for f in range(4):
        copies[2 + GROUPS + f].wait()
        put(COL_DEEP + (1 + f) * ROWS, [(fields[f, k], 4, 4 * k) for k in range(LEVELS)])
    copies[-1].wait()
    branches[0] = pole_of(fold_ref) >> (COLS.bit_length() - 1)

    def pack(kind, out):
        turn = turned if kind == "fold" else (lambda tile: tile)
        for k in range(LEVELS):
            out[ROW_DIFF + ROWS * k : ROW_DIFF + ROWS * (k + 1), :] = turn(difference[k])
        for f in range(4):
            for m in range(LEVELS // 2):
                first, second = turn(fields[f, 2 * m]), turn(fields[f, 2 * m + 1])
                if kind == "north":
                    tile = jnp.where(low, roll(first, 4, 0), second)
                else:
                    tile = jnp.where(low, first, roll(second, 4, 0))
                row = ROW_FIELD + ROWS * (f * (LEVELS // 2) + m)
                out[row : row + ROWS, :] = tile
        out[ROW_COUNT : ROW_COUNT + ROWS, :] = turn(depths)
        out[ROW_SURFACE : ROW_SURFACE + ROWS, :] = turn(surfaces)

    @pl.when(even)
    def _():
        pack("north", near_rows)
        pack("south", far_rows)

    @pl.when(jnp.logical_not(even))
    def _():
        pack("south", near_rows)

    @pl.when(jnp.logical_not(even) & jnp.logical_not(is_top))
    def _():
        pack("north", far_rows)

    @pl.when(is_top)
    def _():
        pack("fold", far_rows)


def sides(one, two, row):
    first, second = one[pl.ds(row, ROWS), :], two[pl.ds(row, ROWS), :]
    eastward = lax.axis_index("gx") % 2 == 0
    return jnp.where(eastward, first, second), jnp.where(eastward, second, first)


def corners_kernel(one, two, near_in, far_in, near, far):
    del near_in, far_in
    is_top = lax.axis_index("gy") == lax.axis_size("gy") - 1
    half = ROW_WEST - ROW_EAST
    for row in range(0, half, ROWS):
        for base, value in zip((0, half), sides(one, two, COL_DEEP + row)):
            near[base + row : base + row + ROWS, :] = value
            far[base + row : base + row + ROWS, :] = jnp.where(is_top, turned(value), value)


def pole_of(fold_map):
    return (fold_map[0] + 1) & (COLS * lax.axis_size("gx") - 1)


def halo_rows(fold_map, near, far, extra, north_rows, south_rows):
    here = lax.axis_index("gy")
    top = lax.axis_size("gy") - 1

    @pl.when(here % 2 == 0)
    def _():
        north_rows[...] = near[...]
        south_rows[...] = far[...]

    @pl.when(here % 2 == 1)
    def _():
        south_rows[...] = near[...]

    @pl.when((here % 2 == 1) & (here != top))
    def _():
        north_rows[...] = far[...]

    @pl.when(here == top)
    def _():
        lane = lanes()
        pole = pole_of(fold_map)
        offset = pole & (COLS - 1)
        index = (offset - 1 - lane) & (COLS - 1)
        within_far = (lane >= offset) == ((pole & COLS) != 0)
        for row in range(0, north_rows.shape[0], ROWS):
            rows = jnp.where(within_far, far[row : row + ROWS, :], extra[row : row + ROWS, :])
            north_rows[row : row + ROWS, :] = jnp.take_along_axis(rows, index, axis=1)


def unfold(offset, first_in_far, far, extra, out):
    lane = lanes()
    index = (offset - 1 - lane) & (COLS - 1)
    within_far = (lane >= offset) == first_in_far
    zero = jnp.zeros((ROWS, COLS), jnp.float32)

    def store(row, value):
        out[row - ROW_EAST : row - ROW_EAST + ROWS, :] = value

    def flipped(row, sign):
        a, b = far[row : row + ROWS, :], extra[row : row + ROWS, :]
        store(row, sign * jnp.take_along_axis(jnp.where(within_far, a, b), index, axis=1))
        return sign * jnp.take_along_axis(jnp.where(within_far, b, a), index, axis=1)

    def collect(packed, tile, width, at):
        chosen = (lane >= at) & (lane < at + width)
        return jnp.where(chosen, roll(tile, at, 1), packed[0]), jnp.where(chosen, roll(tile, at + width, 1), packed[1])

    def beside_of(first, row):
        a, b = far[row : row + ROWS, :], extra[row : row + ROWS, :]
        return jnp.where(first_in_far == first, a, b)

    def finish(row, packed, sign, width, within):
        beside = (lane + (offset - 1) + width - 2 * within) & (COLS - 1)
        right = sign * jnp.take_along_axis(beside_of(True, ROW_WEST + row), beside, axis=1)
        beside = (lane + (offset - 1 - COLS) + width - 2 * within) & (COLS - 1)
        left = sign * jnp.take_along_axis(beside_of(False, ROW_EAST + row), beside, axis=1)
        store(ROW_EAST + row, jnp.where(within < offset, packed[0], right))
        store(ROW_WEST + row, jnp.where(within >= offset + width - COLS, packed[1], left))

    packed = (zero, zero)
    for k in range(LEVELS):
        packed = collect(packed, flipped(ROW_DIFF + ROWS * k, 1.0), 5, 5 * k)
    packed = collect(packed, flipped(ROW_COUNT, 1.0), 5, COUNT_LANE)
    packed = collect(packed, flipped(ROW_SURFACE, 1.0), 4, SURFACE_LANE)
    fifth = lane - 5 * ((lane * 205) >> 10)
    finish(0, packed, 1.0, jnp.where(lane >= SURFACE_LANE, 4, 5), fifth)
    for f in range(4):
        sign = -1.0 if f < 2 else 1.0
        packed = (zero, zero)
        for m in range(LEVELS // 2):
            tile = flipped(ROW_FIELD + ROWS * (f * (LEVELS // 2) + m), sign)
            packed = collect(packed, tile, 4, 8 * m)
            packed = collect(packed, roll(tile, 4, 0), 4, 8 * m + 4)
        finish((1 + f) * ROWS, packed, sign, 4, lane & 3)


def unpack(east, west, first, width, lane):
    right = roll(east, -first, 1)
    left = roll(west, -width - first, 1)
    return jnp.where(lane < width, right, jnp.where(lane >= COLS - width, left, 0.0))


def both_east(one, two, lane):
    return east_of(one, two, lane), east_of(two, one, lane)


def both_west(one, two, lane):
    return west_of(one, two, lane), west_of(two, one, lane)


def krylov_kernel(
    fold_map, difference, fields, count, surface, one, two, near, far, extra,
    vectors, diagonal, right_side, partial,
    north_buf, south_buf,
):
    here = lax.axis_index("gy")
    top = lax.axis_size("gy") - 1
    lane, sub = lanes(), sublanes()
    low = sub < 4
    @pl.when(here % 2 == 0)
    def _():
        north_buf[...] = near[ROW_EAST:, :]
        south_buf[...] = far[ROW_EAST:, :]

    @pl.when(here % 2 == 1)
    def _():
        south_buf[...] = near[ROW_EAST:, :]

    @pl.when((here % 2 == 1) & (here != top))
    def _():
        north_buf[...] = far[ROW_EAST:, :]

    @pl.when(here == top)
    def _():
        pole = pole_of(fold_map)
        unfold(pole & (COLS - 1), (pole & COLS) != 0, far, extra, north_buf)

    def at(ref, row):
        return ref[row - ROW_EAST : row - ROW_EAST + ROWS, :]

    def field_tile(ref, f, k):
        return at(ref, ROW_FIELD + ROWS * (f * (LEVELS // 2) + k // 2))

    def halo_main(f, k):
        north, south = field_tile(north_buf, f, k), field_tile(south_buf, f, k)
        return jnp.where(low, roll(north, 4 * (k % 2), 0), roll(south, 4 * (1 - k % 2), 0))

    def side(ref, f, first, width):
        return unpack(at(ref, ROW_EAST + ROWS * f), at(ref, ROW_WEST + ROWS * f), first, width, lane)

    halo_packed = [
        [
            jnp.where(low, at(north_buf, base + ROWS * (1 + f)), at(south_buf, base + ROWS * (1 + f)))
            for base in (ROW_EAST, ROW_WEST)
        ]
        for f in range(4)
    ]

    columns = [sides(one, two, COL_DEEP + ROWS * f) for f in range(5)]

    def column(f):
        return columns[f]

    def neighbours_across(own, north, south):
        up, up_n, up_s = roll(own, -1, 0), roll(north, -1, 0), roll(south, -1, 0)
        down, down_n, down_s = roll(own, 1, 0), roll(north, 1, 0), roll(south, 1, 0)
        return (
            jnp.where(sub == 7, up_n, up),
            jnp.where(low, up_n, jnp.where(sub == 7, up, up_s)),
            jnp.where(sub == 0, down_s, down),
            jnp.where(sub == 0, down, jnp.where(low, down_n, down_s)),
        )

    def halo(pair):
        return jnp.where(low, pair[0], pair[1])

    counts_own = (count[...].astype(jnp.float32), unpack(*column(0), COUNT_LANE, 5, lane))
    counts_north = (at(north_buf, ROW_COUNT), side(north_buf, 0, COUNT_LANE, 5))
    counts_south = (at(south_buf, ROW_COUNT), side(south_buf, 0, COUNT_LANE, 5))
    counts = (counts_own[0], counts_own[1], halo((counts_north[0], counts_south[0])), halo((counts_north[1], counts_south[1])))
    surfaces = (
        surface[...],
        unpack(*column(0), SURFACE_LANE, 4, lane),
        halo((at(north_buf, ROW_SURFACE), at(south_buf, ROW_SURFACE))),
        halo((side(north_buf, 0, SURFACE_LANE, 4), side(south_buf, 0, SURFACE_LANE, 4))),
    )

    zero = jnp.zeros((ROWS, COLS), jnp.float32)
    c_prev, r_prev, a_prev = [zero] * 4, [zero] * 4, [zero] * 4
    c_list, r_list = [], []
    for k in range(LEVELS):
        own = (difference[k], unpack(*column(0), 5 * k, 5, lane))
        north = (at(north_buf, ROW_DIFF + ROWS * k), side(north_buf, 0, 5 * k, 5))
        south = (at(south_buf, ROW_DIFF + ROWS * k), side(south_buf, 0, 5 * k, 5))
        halos = (halo((north[0], south[0])), halo((north[1], south[1])))
        centre = (own[0], own[1], halos[0], halos[1])
        easts = both_east(*own, lane) + both_east(*halos, lane)
        wests = both_west(*own, lane) + both_west(*halos, lane)
        first = neighbours_across(own[0], north[0], south[0])
        second = neighbours_across(own[1], north[1], south[1])
        norths = (first[0], second[0], first[1], second[1])
        souths = (first[2], second[2], first[3], second[3])
        values = [
            (fields[f, k], unpack(*column(1 + f), 4 * k, 4, lane), halo_main(f, k), unpack(*halo_packed[f], 4 * k, 4, lane))
            for f in range(4)
        ]
        c_now, r_now, a_now = [], [], []
        for i in range(4):
            u, v, spread, mix = (value[i] for value in values)
            change = (
                -0.5 * u * (easts[i] - wests[i])
                - 0.5 * v * (norths[i] - souths[i])
                + spread * (easts[i] + wests[i] + norths[i] + souths[i] - 4.0 * centre[i])
            )
            explicit = centre[i] + jnp.where(k < counts[i], change, 0.0)
            a = jnp.where(k + 1 < counts[i], mix, 0.0)
            inverse = 1.0 / (1.0 + a_prev[i] + a + a_prev[i] * c_prev[i])
            c_now.append(-a * inverse)
            r_now.append((explicit + a_prev[i] * r_prev[i]) * inverse)
            a_now.append(a)
        c_prev, r_prev, a_prev = c_now, r_now, a_now
        c_list.append(c_now)
        r_list.append(r_now)
    total, x_next = [zero] * 4, [zero] * 4
    for k in range(LEVELS - 1, -1, -1):
        x_next = [r_list[k][i] - c_list[k][i] * x_next[i] for i in range(4)]
        total = [total[i] + thickness(k) * x_next[i] for i in range(4)]
    rhs = [jnp.where(counts[i] > 0, 0.25 * total[i], 0.0) for i in range(4)]

    def depth_of(levels):
        depth = zero
        for k in range(LEVELS):
            depth = depth + jnp.where(k < levels, thickness(k), 0.0)
        return depth / LEVELS

    own = tuple(depth_of(levels) for levels in counts_own)
    north = tuple(depth_of(levels) for levels in counts_north)
    south = tuple(depth_of(levels) for levels in counts_south)
    depths = (own[0], own[1], halo((north[0], south[0])), halo((north[1], south[1])))

    def rows_of(own, north, south):
        first = neighbours_across(own[0], north[0], south[0])
        second = neighbours_across(own[1], north[1], south[1])
        return (first[0], second[0], first[1], second[1]), (first[2], second[2], first[3], second[3])

    def coupled(others, weight):
        return [weight * jnp.minimum(depths[i], others[i]) for i in range(4)]

    own_e, north_e, south_e = (both_east(*pair, lane) for pair in (own, north, south))
    own_w, north_w, south_w = (both_west(*pair, lane) for pair in (own, north, south))
    halo_e = (halo((north_e[0], south_e[0])), halo((north_e[1], south_e[1])))
    halo_w = (halo((north_w[0], south_w[0])), halo((north_w[1], south_w[1])))
    mid = rows_of(own, north, south)
    mid_e = rows_of(own_e, north_e, south_e)
    mid_w = rows_of(own_w, north_w, south_w)
    couplings = [
        coupled(own_e + halo_e, 1.0),
        coupled(own_w + halo_w, 1.0),
        coupled(mid[0], 1.0),
        coupled(mid[1], 1.0),
        coupled(mid_e[0], 0.5),
        coupled(mid_w[0], 0.5),
        coupled(mid_e[1], 0.5),
        coupled(mid_w[1], 0.5),
    ]
    diag = [
        jnp.where(counts[i] > 0, surfaces[i] + sum(entry[i] for entry in couplings), 1.0) for i in range(4)
    ]
    inverse = [1.0 / diag[i] for i in range(4)]
    couplings = [[entry[i] * inverse[i] for i in range(4)] for entry in couplings]

    def shifted_rows(tiles):
        north, south = [None] * 4, [None] * 4
        for i in range(2):
            a, b = roll(tiles[i], -1, 0), roll(tiles[i + 2], -1, 0)
            north[i], north[i + 2] = jnp.where(sub == 7, b, a), jnp.where(sub == 7, a, b)
            a, b = roll(tiles[i], 1, 0), roll(tiles[i + 2], 1, 0)
            south[i], south[i + 2] = jnp.where(sub == 0, b, a), jnp.where(sub == 0, a, b)
        return north, south

    def spread_out(tiles):
        east = both_east(tiles[0], tiles[1], lane) + both_east(tiles[2], tiles[3], lane)
        west = both_west(tiles[0], tiles[1], lane) + both_west(tiles[2], tiles[3], lane)
        mid_n, mid_s = shifted_rows(tiles)
        east_n, east_s = shifted_rows(east)
        west_n, west_s = shifted_rows(west)
        around = (east, west, mid_n, mid_s, east_n, west_n, east_s, west_s)
        return [sum(entry[i] * values[i] for entry, values in zip(couplings, around)) for i in range(4)]

    found = [[rhs[i] * inverse[i] for i in range(4)]]
    found.append(spread_out(found[0]))
    for _ in range(2, ITERS + 1):
        ahead = spread_out(found[-1])
        found.append([2.0 * ahead[i] - found[-2][i] for i in range(4)])
    for j in range(ITERS + 1):
        vectors[j] = found[j][0]
    diagonal[...] = diag[0]
    right_side[...] = rhs[0]
    weighted = [diag[0] * found[j][0] for j in range(ITERS + 1)]
    sums = [weighted[j] * found[j][0] for j in range(ITERS + 1)]
    sums += [weighted[j] * found[j + 1][0] for j in range(ITERS)]
    row = jnp.zeros((1, COLS), jnp.float32)
    for j, entry in enumerate(sums):
        row = jnp.where(lane[:1, :] == j, jnp.sum(entry, keepdims=True), row)
    partial[...] = jnp.broadcast_to(row, partial.shape)


def combine_kernel(moments, vectors, diagonal, pressure, residual, good):
    size = ITERS + 1
    sums = jnp.sum(moments[...], axis=0, keepdims=True)

    def lane_of(j):
        return jnp.broadcast_to(sums[:, j : j + 1], (ROWS, COLS))

    even = [lane_of(j) for j in range(size)]
    odd = [lane_of(size + j) for j in range(ITERS)]
    mu = []
    for j in range(size):
        mu.append(even[0] if j == 0 else 2.0 * even[j] - even[0])
        if j < ITERS:
            mu.append(odd[0] if j == 0 else 2.0 * odd[j] - odd[0])

    def mass(i, j):
        return 0.5 * (mu[i + j] + mu[abs(i - j)])

    def stiffness(i, j):
        i, j = min(i, j), max(i, j)
        if j == 0:
            return mu[0] - mu[1]
        return mass(i, j) - 0.5 * (mass(i, j + 1) + mass(i, j - 1))

    def form(values, entry):
        out = None
        for i in range(len(values)):
            inner = values[i] * entry(i, i)
            for j in range(i + 1, len(values)):
                inner = inner + 2.0 * values[j] * entry(i, j)
            out = values[i] * inner if out is None else out + values[i] * inner
        return out

    def applied(values):
        out = [value for value in values] + [jnp.zeros_like(values[0])]
        out[1] = out[1] - values[0]
        for j in range(1, len(values)):
            out[j + 1] = out[j + 1] - 0.5 * values[j]
            out[j - 1] = out[j - 1] - 0.5 * values[j]
        return out

    def amplified(values, result):
        total = sum(jnp.abs(value) for value in values)
        return total * total * mu[0] / result

    scaled = [jnp.ones((ROWS, COLS), jnp.float32)]
    direction = list(scaled)
    solution_at = []
    energy = mu[0]
    fine = energy > 0.0
    for step in range(ITERS):
        image = applied(direction)
        curvature = form(direction, stiffness)
        step_size = energy / curvature
        fine = fine & (amplified(direction, curvature) <= SCALAR_BOUND) & (curvature > 0.0)
        solution_at = [
            step_size * value + (solution_at[j] if j < len(solution_at) else 0.0) for j, value in enumerate(direction)
        ]
        scaled = [
            (scaled[j] if j < len(scaled) else 0.0) - step_size * value for j, value in enumerate(image)
        ]
        energy_new = form(scaled, mass)
        bound = SCALAR_BOUND if step + 1 < ITERS else FIELD_BOUND
        fine = fine & (amplified(scaled, energy_new) <= bound) & (energy_new > 0.0)
        if step + 1 < ITERS:
            ratio = energy_new / energy
            direction = [
                scaled[j] + (ratio * direction[j] if j < len(direction) else 0.0) for j in range(len(scaled))
            ]
            energy = energy_new
    pressure[...] = sum(solution_at[j] * vectors[j] for j in range(len(solution_at)))
    residual[...] = diagonal[...] * sum(scaled[j] * vectors[j] for j in range(len(scaled)))
    good[0] = jnp.min(jnp.where(fine, 1, 0).astype(jnp.int32))


def tracers_kernel(
    fold_map, tracer, fields, count, one, two, near, far, extra,
    mixed,
    north_rows, south_rows, factors,
):
    lane, sub = lanes(), sublanes()
    levels = count[...]
    group = pl.program_id(0)

    @pl.when(group == 0)
    def _():
        halo_rows(fold_map, near, far, extra, north_rows, south_rows)
        c_prev = jnp.zeros((ROWS, COLS), jnp.float32)
        a_prev = jnp.zeros((ROWS, COLS), jnp.float32)
        for k in range(LEVELS):
            wet = jnp.where(k < levels, 1.0, 0.0)
            u, v, spread = 0.5 * wet * fields[0, k], 0.5 * wet * fields[1, k], wet * fields[2, k]
            a = jnp.where(k + 1 < levels, fields[3, k], 0.0)
            inverse = 1.0 / (1.0 + a_prev + a + a_prev * c_prev)
            c_prev = -a * inverse
            factors[0, k] = 1.0 - 4.0 * spread
            factors[1, k] = spread - u
            factors[2, k] = spread + u
            factors[3, k] = spread - v
            factors[4, k] = spread + v
            factors[5, k] = inverse
            factors[6, k] = a_prev
            factors[7, k] = c_prev
            a_prev = a

    row = pl.multiple_of(group * ROWS, ROWS)
    columns_east, columns_west = sides(one, two, row)
    r_prev = [jnp.zeros((ROWS, COLS), jnp.float32)] * GROUP
    for k in range(LEVELS):
        centre, to_e, to_w, to_n, to_s, inverse, above = (factors[j, k] for j in range(7))
        wet = k < levels
        for t in range(GROUP):
            cell = jnp.where(wet, tracer[t, k], 0.0)
            at = t * LEVELS + k
            halo_row = group * (GROUP * LEVELS) + at
            east = east_of(cell, roll(columns_east, -at, 1), lane)
            west = west_of(cell, roll(columns_west, COLS - 1 - at, 1), lane)
            north = north_of(cell, north_rows[pl.ds(halo_row, 1), :], sub)
            south = south_of(cell, south_rows[pl.ds(halo_row, 1), :], sub)
            explicit = centre * cell + to_e * east + to_w * west + to_n * north + to_s * south
            r_prev[t] = (explicit + above * r_prev[t]) * inverse
            mixed[t, k] = r_prev[t]
    x_next = r_prev
    for k in range(LEVELS - 2, -1, -1):
        below = factors[7, k]
        for t in range(GROUP):
            x_next[t] = mixed[t, k] - below * x_next[t]
            mixed[t, k] = x_next[t]


def extended(cells, sides, width):
    for axis, dim in sides:
        count = lax.axis_size(axis)
        head = lax.slice_in_dim(cells, 0, width, axis=dim)
        tail = lax.slice_in_dim(cells, cells.shape[dim] - width, cells.shape[dim], axis=dim)
        cells = jnp.concatenate(
            [
                lax.ppermute(tail, axis, [(i, (i + 1) % count) for i in range(count)]),
                cells,
                lax.ppermute(head, axis, [((i + 1) % count, i) for i in range(count)]),
            ],
            axis=dim,
        )
    return cells


def extend(field, fold_map):
    rows, cols = field.shape
    padded = extended(field, (("gx", 1), ("gy", 0)), 1)
    total_cols = fold_map.shape[0]
    whole_row = lax.all_gather(field[rows - 1, :], "gx", axis=0, tiled=True)
    start = lax.axis_index("gx") * cols
    wanted = (start - 1 + jnp.arange(cols + 2, dtype=jnp.int32)) % total_cols
    folded = jnp.take(whole_row, jnp.take(fold_map, wanted), axis=0)
    row_index = lax.axis_index("gy")
    upper = jnp.where(row_index == lax.axis_size("gy") - 1, folded, padded[rows + 1, :])
    lower = jnp.where(row_index == 0, 0.0, padded[0, :])
    return jnp.concatenate([lower[None, :], padded[1 : rows + 1, :], upper[None, :]], axis=0)


def window(padded, row_off, col_off):
    rows = padded.shape[0] - 2
    cols = padded.shape[1] - 2
    return padded[1 + row_off : 1 + row_off + rows, 1 + col_off : 1 + col_off + cols]


def total_of(value):
    return lax.psum(jnp.sum(value), BOTH)


def direct_gradients(rhs, level_count, fold_map, surface_term):
    levels = jnp.arange(LEVELS, dtype=jnp.int32)[:, None, None]
    level_mask = (levels < level_count[None]).astype(jnp.float32)
    thick = (0.5 + 1.5 * jnp.arange(LEVELS).astype(jnp.float32) / (LEVELS - 1))[:, None, None]
    depth = jnp.sum(thick * level_mask, axis=0) / LEVELS
    wet_cells = level_count > 0
    depth_pad = extend(depth, fold_map)
    couplings = [
        weight * jnp.minimum(depth, window(depth_pad, row_off, col_off)) for row_off, col_off, weight in NEIGHBOURS
    ]
    diag = jnp.where(wet_cells, surface_term + sum(couplings), 1.0)

    def step(_, state):
        pressure, residual, direction, energy = state
        field_pad = extend(direction, fold_map)
        summed = jnp.zeros_like(direction)
        for entry, (row_off, col_off, _weight) in zip(couplings, NEIGHBOURS):
            summed = summed + entry * window(field_pad, row_off, col_off)
        image = jnp.where(wet_cells, diag * direction - summed, direction)
        step_size = energy / total_of(direction * image)
        pressure = pressure + step_size * direction
        residual = residual - step_size * image
        scaled = residual / diag
        energy_new = total_of(residual * scaled)
        return pressure, residual, scaled + energy_new / energy * direction, energy_new

    scaled = rhs / diag
    state = (jnp.zeros_like(rhs), rhs, scaled, total_of(rhs * scaled))
    state = lax.fori_loop(0, ITERS, step, state)
    return state[0], state[1]


def kernel(body, limit=VMEM_LIMIT, **rest):
    return pl.pallas_call(body, compiler_params=params(limit), **rest)


def shape(*dims):
    return jax.ShapeDtypeStruct(dims, jnp.float32)


def vmem(*dims):
    return pltpu.VMEM(dims, jnp.float32)


def block_of(dims, at=0):
    return pl.BlockSpec(dims, lambda i: (at,) + (0,) * (len(dims) - 1))


def all_of(array):
    return block_of(array.shape)


def shards(sizes, tracer, east_vel, north_vel, diffusion, mixing, count, fold_map, surface):
    nx, ny = sizes
    hbm = pl.BlockSpec(memory_space=pltpu.HBM)
    smem = pl.BlockSpec(memory_space=pltpu.SMEM)
    fields = (east_vel, north_vel, diffusion, mixing)

    def device(x, y):
        return (x % nx) * ny + y

    one, two, near, far, difference, coefficients, branches = kernel(
        pack_kernel,
        limit=PACK_VMEM_LIMIT,
        out_shape=(
            shape(COL_SIZE, COLS),
            shape(COL_SIZE, COLS),
            shape(ROW_SIZE, COLS),
            shape(ROW_SIZE, COLS),
            shape(LEVELS, ROWS, COLS),
            shape(4, LEVELS, ROWS, COLS),
            jax.ShapeDtypeStruct((1,), jnp.int32),
        ),
        in_specs=[hbm] * 8,
        out_specs=(whole(),) * 6 + (smem,),
        scratch_shapes=[
            vmem(EDGE * ROWS, COLS),
            pltpu.VMEM((ROWS, COLS), jnp.int32),
            vmem(ROWS, COLS),
            pltpu.SMEM(fold_map.shape, jnp.int32),
            pltpu.SemaphoreType.DMA((GROUPS + 7,)),
        ],
        name="pack",
    )(tracer.reshape(EDGE * ROWS, COLS), *fields, count, surface, fold_map)

    one = lax.ppermute(one, BOTH, [(device(x ^ 1, y), device(x, y)) for x in range(nx) for y in range(ny)])
    two = lax.ppermute(
        two, BOTH, [(device(x + 1 if x % 2 else x - 1, y), device(x, y)) for x in range(nx) for y in range(ny)]
    )

    columns = block_of((COL_SIZE, COLS))
    corner = block_of((ROW_DIFF - ROW_EAST, COLS), ROW_EAST // (ROW_DIFF - ROW_EAST))
    near, far = kernel(
        corners_kernel,
        grid=(1,),
        out_shape=(shape(ROW_SIZE, COLS), shape(ROW_SIZE, COLS)),
        in_specs=[columns, columns] + [pl.BlockSpec(memory_space=pl.ANY)] * 2,
        out_specs=(corner, corner),
        input_output_aliases={2: 0, 3: 1},
        name="put_corners",
    )(one, two, near, far)
    near = lax.ppermute(near, BOTH, [(device(x, y ^ 1), device(x, y)) for x in range(nx) for y in range(ny)])
    inner = [(device(x, y + 1 if y % 2 else y - 1), device(x, y)) for x in range(nx) for y in range(1, ny - 1)]

    def across(turn):
        return [(device(turn - x, ny - 1), device(x, ny - 1)) for x in range(nx)]

    def exchange(at, rows):
        even, odd = (at, at - 1) if at % 2 == 0 else (at - 1, at)
        return lax.ppermute(rows, BOTH, inner + across(even)), lax.ppermute(rows, BOTH, across(odd))

    far, extra = lax.switch(branches[0], [functools.partial(exchange, at) for at in range(nx)], far)

    rest = (difference, coefficients, count, surface, one, two, near, far, extra)
    vectors, diagonal, rhs, partial = kernel(
        krylov_kernel,
        grid=(1,),
        out_shape=(shape(ITERS + 1, ROWS, COLS), shape(ROWS, COLS), shape(ROWS, COLS), shape(nx * ny, COLS)),
        in_specs=[smem] + [all_of(array) for array in rest],
        out_specs=(
            block_of((ITERS + 1, ROWS, COLS)),
            block_of((ROWS, COLS)),
            block_of((ROWS, COLS)),
            block_of((nx * ny, COLS)),
        ),
        scratch_shapes=[vmem(DEEP_SIZE, COLS), vmem(DEEP_SIZE, COLS)],
        name="krylov",
    )(fold_map, *rest)

    moments = lax.all_to_all(partial, BOTH, 0, 0)

    batch = pl.BlockSpec((GROUP, LEVELS, ROWS, COLS), lambda i: (i, 0, 0, 0))
    mixed = kernel(
        tracers_kernel,
        grid=(GROUPS,),
        out_shape=shape(TRACERS, LEVELS, ROWS, COLS),
        in_specs=[smem, batch, all_of(coefficients), all_of(count)]
        + [block_of((COL_DEEP, COLS))] * 2
        + [block_of((EDGE, COLS))] * 3,
        out_specs=batch,
        scratch_shapes=[vmem(EDGE, COLS), vmem(EDGE, COLS), vmem(8, LEVELS, ROWS, COLS)],
        name="tracers",
    )(fold_map, tracer, coefficients, count, one, two, near, far, extra)

    pressure, residual, good = kernel(
        combine_kernel,
        out_shape=(shape(ROWS, COLS), shape(ROWS, COLS), jax.ShapeDtypeStruct((1,), jnp.int32)),
        in_specs=[whole()] * 3,
        out_specs=(whole(), whole(), smem),
        name="combine",
    )(moments, vectors, diagonal)
    pressure, residual = lax.cond(
        good[0] == 1,
        lambda pressure, residual, rhs, count, surface, fold: (pressure, residual),
        lambda pressure, residual, rhs, count, surface, fold: direct_gradients(rhs, count, fold, surface),
        pressure,
        residual,
        rhs,
        count,
        surface,
        fold_map,
    )
    return mixed, pressure, residual


def solution(mesh):
    in_specs = (
        P(None, None, "gy", "gx"),
        P(None, "gy", "gx"),
        P(None, "gy", "gx"),
        P(None, "gy", "gx"),
        P(None, "gy", "gx"),
        P("gy", "gx"),
        P(),
        P("gy", "gx"),
    )
    out_specs = (P(None, None, "gy", "gx"), P("gy", "gx"), P("gy", "gx"))
    body = functools.partial(shards, (mesh.shape["gx"], mesh.shape["gy"]))
    return jax.shard_map(body, mesh=mesh, in_specs=in_specs, out_specs=out_specs, check_vma=False)
```
